32 devices in a mesh: groups: 2 (over y), tile: 4 (over z), shot: 4 (over x, core).
Axes of the slice: x: 2, y: 2, z: 4, core: 2. Of those that a mesh axis runs over, the one named last changes fastest.
Arguments:
- src_prev: float32 [8, 8, 64, 128], P(('groups', 'shot'), None, 'tile'), parts along dimension 0, may hold values from -6 to 6
- src_now: float32 [8, 8, 64, 128], P(('groups', 'shot'), None, 'tile'), parts along dimension 0, may hold values from -6 to 6
- rec_prev: float32 [8, 8, 64, 128], P(('groups', 'shot'), None, 'tile'), parts along dimension 0, may hold values from -6 to 6
- rec_now: float32 [8, 8, 64, 128], P(('groups', 'shot'), None, 'tile'), parts along dimension 0, may hold values from -6 to 6
- speed_table: float32 [32], P('groups'), parts along dimension 0, may hold values from 0.05 to 0.2
- region_ids: int32 [8, 128, 128], P(None, ('groups', 'tile')), parts along dimension 1, may hold values from 0 to 15
- source_cell: int32 [8], P(('groups', 'shot')), parts along dimension 0, may hold values from 0 to 65535
- wavelet: float32 [8, 2], P(('groups', 'shot')), parts along dimension 0, may hold values from -12 to 12
- receiver_cell: int32 [8, 128], P(('groups', 'shot'), 'tile'), parts along dimension 0, may hold values from 0 to 2047
- receiver_data: float32 [8, 2, 128], P(('groups', 'shot'), None, 'tile'), parts along dimension 0, may hold values from -12 to 12
Outputs:
- src_next: float32 [8, 8, 64, 128], P(('groups', 'shot'), None, 'tile'), parts along dimension 0
- rec_next: float32 [8, 8, 64, 128], P(('groups', 'shot'), None, 'tile'), parts along dimension 0
- offset_image: float32 [33, 8, 128, 128], P(None, 'shot', ('groups', 'tile')), parts along dimension 2
The draws below stay inside these ranges and needn't reach their ends.
There are 2 independent parts, one for each index of `groups`. The reference program is written for one: setup_inputs(seed, part) draws one part's arguments, and reference() takes and returns one part's arrays. A program takes and returns all parts, laid end to end along the dimension named above; each array names one. Nothing has to cross between parts.
Inputs may be any that keep to these rules, and one draw needn't show every extreme that they name: `receiver_cell`: receivers may share a cell; their traces then add.
All inputs are finite; a program needn't handle non-finite values.
Results may differ from the reference program's by a relative error of at most 0.0001.
Values sent between devices are 32-bit elements; how exact they have to be, the bound alone decides.
No kernel may reach another device: no remote copies, remote signals or barrier semaphores. Data moves between devices by JAX's collectives and lax.ppermute only.
A program may use at most 64 MiB of HBM per device.

```python
import math
import jax
import jax.numpy as jnp

NZ = 8
CX = 16
NY = 128
OFFS = 33
REGIONS = 16
RECV_DEV = 32
NX = 64
SHOTS = 4
RECVS = 128


def set_ends(drawn, own_key, smallest, top_value):
    dims = drawn.shape
    spot = [jax.random.randint(jax.random.fold_in(own_key, axis), (), 0, dims[axis]) for axis in range(len(dims))]
    drawn = drawn.at[tuple(spot)].set(smallest)
    longest = dims.index(max(dims))
    spot[longest] = (spot[longest] + 1) % dims[longest]
    return drawn.at[tuple(spot)].set(top_value)


def shard_levels(key, dims, pieces, low, high):
    def one(dim, shards_of):
        draws = jax.random.uniform(jax.random.fold_in(jax.random.fold_in(key, 6), dim), (shards_of,), jnp.float32, low / len(pieces), high / len(pieces))
        return jnp.repeat(jnp.exp(draws), dims[dim] // shards_of).reshape((-1,) + (1,) * (len(dims) - dim - 1))

    loudness = one(*pieces[0])
    for cut in pieces[1:]:
        loudness = loudness * one(*cut)
    return loudness


def bell_draw(own_key, shape, width, most, pieces=(), kind=jnp.bfloat16):
    values = width * jax.random.normal(own_key, shape, jnp.float32)
    if pieces:
        values = values * shard_levels(own_key, shape, pieces, -0.22, 0.18)
    return jnp.clip(values, -most, most).astype(kind)


def setup_inputs(seed: int = 0, part: int = 0) -> dict:
    arg_keys = jax.random.split(jax.random.key(seed), 11)
    own_keys = jax.random.split(jax.random.fold_in(arg_keys[10], part), 11)
    return {
        "src_prev": bell_draw(own_keys[0], (SHOTS, NZ, NX, NY), 1.0, 6.0, ((0, 4), (2, 4)), jnp.float32),
        "src_now": bell_draw(own_keys[1], (SHOTS, NZ, NX, NY), 1.0, 6.0, ((0, 4), (2, 4)), jnp.float32),
        "rec_prev": bell_draw(own_keys[2], (SHOTS, NZ, NX, NY), 1.0, 6.0, ((0, 4), (2, 4)), jnp.float32),
        "rec_now": bell_draw(own_keys[3], (SHOTS, NZ, NX, NY), 1.0, 6.0, ((0, 4), (2, 4)), jnp.float32),
        "speed_table": jnp.clip(jnp.exp(jax.random.uniform(own_keys[4], (REGIONS,), jnp.float32, math.log(0.05), math.log(0.2))), 0.05, 0.2),
        "region_ids": set_ends(jax.random.randint(own_keys[5], (NZ, NX, NY), 0, REGIONS), jax.random.fold_in(own_keys[5], 1), 0, REGIONS - 1).astype(jnp.int32),
        "source_cell": set_ends(jax.random.randint(own_keys[6], (SHOTS,), 0, NZ * NX * NY), jax.random.fold_in(own_keys[6], 1), 0, (NZ * NX * NY) - 1).astype(jnp.int32),
        "wavelet": bell_draw(own_keys[7], (SHOTS, 2), 3.0, 12.0, ((0, 4),), jnp.float32),
        "receiver_cell": set_ends(jax.random.randint(own_keys[8], (SHOTS, RECVS), 0, CX * NY), jax.random.fold_in(own_keys[8], 1), 0, (CX * NY) - 1).astype(jnp.int32),
        "receiver_data": bell_draw(own_keys[9], (SHOTS, 2, RECVS), 2.0, 12.0, ((0, 4), (2, 4)), jnp.float32),
    }


COEFS = (-205.0 / 72.0, 8.0 / 5.0, -1.0 / 5.0, 8.0 / 315.0, -1.0 / 560.0)


def laplace(field):
    levels, extent, across = field.shape[1], field.shape[2], field.shape[3]
    padded = jnp.pad(field, ((0, 0), (4, 4), (4, 4), (4, 4)))
    total = 3.0 * COEFS[0] * field
    for stride in range(1, 5):
        beside = padded[:, 4 + stride:4 + stride + levels, 4:4 + extent, 4:4 + across] + padded[:, 4 - stride:4 - stride + levels, 4:4 + extent, 4:4 + across]
        beside = beside + padded[:, 4:4 + levels, 4 + stride:4 + stride + extent, 4:4 + across] + padded[:, 4:4 + levels, 4 - stride:4 - stride + extent, 4:4 + across]
        beside = beside + padded[:, 4:4 + levels, 4:4 + extent, 4 + stride:4 + stride + across] + padded[:, 4:4 + levels, 4:4 + extent, 4 - stride:4 - stride + across]
        total = total + COEFS[stride] * beside
    return total


def reference(src_prev, src_now, rec_prev, rec_now, speed_table, region_ids, source_cell, wavelet, receiver_cell, receiver_data):
    coef = speed_table[region_ids]
    shot_rows = jnp.arange(SHOTS).astype(jnp.int32)
    tile_start = (jnp.arange(RECVS).astype(jnp.int32) // RECV_DEV) * (CX * NY)
    columns = tile_start[None, :] + receiver_cell
    row_index = jnp.broadcast_to(shot_rows[:, None], columns.shape)

    def inject_source(field, amps):
        flat = jnp.zeros((SHOTS, NZ * NX * NY), jnp.float32).at[shot_rows, source_cell].add(amps)
        return field + flat.reshape(field.shape)

    def inject_receivers(field, values):
        plane = jnp.zeros((SHOTS, NX * NY), jnp.float32).at[row_index, columns].add(values)
        return field.at[:, 0].add(plane.reshape(SHOTS, NX, NY))

    def advance(prev, now, step, source_side):
        base = (2.0 * now - prev) + coef * laplace(now)
        if source_side:
            return inject_source(base, wavelet[:, step])
        return inject_receivers(base, receiver_data[:, step])

    src_mid = advance(src_prev, src_now, 0, True)
    src_next = advance(src_now, src_mid, 1, True)
    rec_mid = advance(rec_prev, rec_now, 0, False)
    rec_next = advance(rec_now, rec_mid, 1, False)
    reach = OFFS // 2
    src_wide = jnp.pad(src_next, ((0, 0), (0, 0), (reach, reach), (0, 0)))
    rec_wide = jnp.pad(rec_next, ((0, 0), (0, 0), (reach, reach), (0, 0)))
    gathers = []
    for offset in range(OFFS):
        product = src_wide[:, :, 2 * reach - offset:2 * reach - offset + NX] * rec_wide[:, :, offset:offset + NX]
        gathers.append(jnp.sum(product, axis=0))
    offset_image = jnp.stack(gathers) * (1.0 / SHOTS)
    return src_next, rec_next, offset_image
```

```python
import functools

import jax
import jax.numpy as jnp
from jax import lax
from jax.experimental import pallas as pl
from jax.experimental.pallas import tpu as pltpu
from jax.sharding import PartitionSpec as P

OFFS = 33
REACH = OFFS // 2
HALO = 4
LEAD = 8

COEFS = (-205.0 / 72.0, 8.0 / 5.0, -1.0 / 5.0, 8.0 / 315.0, -1.0 / 560.0)

VMEM = pl.BlockSpec(memory_space=pltpu.VMEM)
SMEM = pl.BlockSpec(memory_space=pltpu.SMEM)
LIMIT = 16 * 1024 * 1024


def lane_weights(shape):
    lane = lax.broadcasted_iota(jnp.int32, shape, 1)
    across = shape[1]
    after = [jnp.where(lane < across - k, COEFS[k], 0.0) for k in range(1, HALO + 1)]
    before = [jnp.where(lane >= k, COEFS[k], 0.0) for k in range(1, HALO + 1)]
    return after, before


def laplace_level(wide, field, level, levels, extent, weights):
    after, before = weights
    centre = wide[field, level, LEAD : LEAD + extent, :]
    across = centre.shape[1]
    total = 3.0 * COEFS[0] * centre
    for k in range(1, HALO + 1):
        beside = (
            wide[field, level, LEAD + k : LEAD + k + extent, :]
            + wide[field, level, LEAD - k : LEAD - k + extent, :]
        )
        if level + k < levels:
            beside = beside + wide[field, level + k, LEAD : LEAD + extent, :]
        if level - k >= 0:
            beside = beside + wide[field, level - k, LEAD : LEAD + extent, :]
        total = total + COEFS[k] * beside
        total = total + after[k - 1] * pltpu.roll(centre, across - k, 1)
        total = total + before[k - 1] * pltpu.roll(centre, k, 1)
    return total


def source_hit(cell, level, width, first, shape):
    across = shape[1]
    flat = lax.broadcasted_iota(jnp.int32, shape, 0) * across + lax.broadcasted_iota(
        jnp.int32, shape, 1
    )
    return flat == cell - (level * width + first) * across


def own_part(
    width,
    first_ref,
    cell_ref,
    amps_ref,
    src_prev,
    src_now,
    rec_prev,
    rec_now,
    table_ref,
    ids_ref,
    spots_ref,
    traces_ref,
    part_ref,
    coef_ref,
    plane_ref,
    low_ref,
    high_ref,
    wide,
    table,
):
    levels, extent, across = src_now.shape[1:]
    shape = (extent, across)
    regions = table_ref.shape[1]

    table[...] = jnp.zeros_like(table)
    table[0:1, 0:regions] = table_ref[...]
    speeds = jnp.broadcast_to(table[0:1, :], (8, across))
    for level in range(levels):
        for row in range(0, extent, 8):
            ids = ids_ref[level, row : row + 8, :]
            coef_ref[level, row : row + 8, :] = jnp.take_along_axis(
                speeds, ids, axis=1, mode="promise_in_bounds"
            )

    spots = spots_ref[...]
    column = lax.broadcasted_iota(jnp.int32, (extent, spots.shape[1]), 0) * across
    in_column = (spots >= column) & (spots < column + across)
    lane = lax.broadcasted_iota(jnp.int32, (across, spots.shape[1]), 0)
    in_row = jnp.where(lax.rem(spots, across) == lane, 1.0, 0.0)
    traces = jnp.concatenate(
        [jnp.where(in_column, traces_ref[0, t : t + 1, :], 0.0) for t in range(2)], axis=0
    )
    planes = lax.dot_general(
        traces,
        in_row,
        (((1,), (1,)), ((), ())),
        precision=lax.Precision.HIGHEST,
        preferred_element_type=jnp.float32,
    )
    plane_ref[...] = planes[extent:, :]

    first = first_ref[0]
    for field, now in enumerate((src_now, rec_now)):
        for level in range(levels):
            zeros = jnp.zeros((LEAD, across), jnp.float32)
            wide[field, level, 0:LEAD, :] = zeros
            wide[field, level, LEAD + extent : 2 * LEAD + extent, :] = zeros
            wide[field, level, LEAD : LEAD + extent, :] = now[0, level]
    weights = lane_weights(shape)
    for field, (prev, now) in enumerate(((src_prev, src_now), (rec_prev, rec_now))):
        for level in range(levels):
            total = laplace_level(wide, field, level, levels, extent, weights)
            value = 2.0 * now[0, level] - prev[0, level] + coef_ref[level] * total
            if field == 0:
                hit = source_hit(cell_ref[0], level, width, first, shape)
                value = value + jnp.where(hit, amps_ref[0, 0], 0.0)
            elif level == 0:
                value = value + planes[:extent, :]
            part_ref[field, level] = value
            place = field * levels + level
            low_ref[place, 0:HALO, :] = now[0, level, 0:HALO, :]
            low_ref[place, HALO : 2 * HALO, :] = value[0:HALO, :]
            high_ref[place, 0:HALO, :] = now[0, level, extent - HALO : extent, :]
            high_ref[place, HALO : 2 * HALO, :] = value[extent - HALO : extent, :]
    for level in range(levels):
        place = 2 * levels + level // 2
        rows = pl.ds(level % 2 * HALO, HALO)
        low_ref[place, rows, :] = coef_ref[level, 0:HALO, :]
        high_ref[place, rows, :] = coef_ref[level, extent - HALO : extent, :]


def both_steps(
    width,
    first_ref,
    cell_ref,
    amps_ref,
    src_now,
    rec_now,
    part_ref,
    coef_ref,
    plane_ref,
    low_ref,
    high_ref,
    src_next,
    rec_next,
    packed_ref,
    own,
    other,
    middle,
):
    levels, extent, across = src_now.shape[1:]
    shape = (extent, across)
    share = packed_ref.shape[2]
    zeros = jnp.zeros((LEAD, across), jnp.float32)
    end = LEAD + extent
    for field, now in enumerate((src_now, rec_now)):
        for level in range(levels):
            place = field * levels + level
            own[field, level, 0:LEAD, :] = zeros
            own[field, level, end : end + LEAD, :] = zeros
            own[field, level, LEAD:end, :] = now[0, level]
            other[field, level, LEAD:end, :] = jnp.zeros(shape, jnp.float32)
            other[field, level, LEAD - HALO : LEAD, :] = low_ref[place, 0:HALO, :]
            other[field, level, end : end + HALO, :] = high_ref[place, 0:HALO, :]
    for field in range(2):
        for level in range(levels):
            place = field * levels + level
            pair = 2 * levels + level // 2
            rows = pl.ds(level % 2 * HALO, HALO)
            below = jnp.zeros((HALO, across), jnp.float32)
            above = jnp.zeros((HALO, across), jnp.float32)
            left = jnp.zeros((8, across), jnp.float32)
            right = jnp.zeros((8, across), jnp.float32)
            for k in range(1, HALO + 1):
                begin = LEAD - HALO + k
                below = below + COEFS[k] * own[field, level, begin : begin + HALO, :]
                above = above + COEFS[k] * own[field, level, end - k : end - k + HALO, :]
                left = left + COEFS[k] * other[field, level, LEAD - k : LEAD - k + 8, :]
                right = right + COEFS[k] * other[field, level, end - 8 + k : end + k, :]
            middle[field, level, LEAD - HALO : LEAD, :] = (
                low_ref[place, HALO : 2 * HALO, :] + low_ref[pair, rows, :] * below
            )
            middle[field, level, end : end + HALO, :] = (
                high_ref[place, HALO : 2 * HALO, :] + high_ref[pair, rows, :] * above
            )
            middle[field, level, LEAD : LEAD + 8, :] = (
                part_ref[field, level, 0:8, :] + coef_ref[level, 0:8, :] * left
            )
            middle[field, level, end - 8 : end, :] = (
                part_ref[field, level, extent - 8 : extent, :]
                + coef_ref[level, extent - 8 : extent, :] * right
            )
    first = first_ref[0]
    weights = lane_weights(shape)
    for field, (now, after) in enumerate(((src_now, src_next), (rec_now, rec_next))):
        for level in range(levels):
            total = laplace_level(middle, field, level, levels, extent, weights)
            value = 2.0 * middle[field, level, LEAD:end, :] - now[0, level]
            value = value + coef_ref[level] * total
            if field == 0:
                hit = source_hit(cell_ref[0], level, width, first, shape)
                value = value + jnp.where(hit, amps_ref[0, 1], 0.0)
            elif level == 0:
                value = value + plane_ref[...]
            after[0, level] = value
            packed_ref[level // share, field, level % share] = value


def image_products(weight, mine_ref, low_ref, high_ref, image_ref, wide):
    shots, _, share, extent, across = mine_ref.shape
    for shot in range(shots):
        for field in range(2):
            for level in range(share):
                scale = weight if field == 0 else 1.0
                wide[shot, field, level, 0:REACH, :] = (
                    scale * low_ref[shot, field, level, extent - REACH : extent, :]
                )
                wide[shot, field, level, REACH : REACH + extent, :] = (
                    scale * mine_ref[shot, field, level]
                )
                wide[shot, field, level, REACH + extent : 2 * REACH + extent, :] = (
                    scale * high_ref[shot, field, level, 0:REACH, :]
                )
    for level in range(share):
        for offset in range(OFFS):
            total = jnp.zeros((extent, across), jnp.float32)
            for shot in range(shots):
                begin = 2 * REACH - offset
                total = total + (
                    wide[shot, 0, level, begin : begin + extent, :]
                    * wide[shot, 1, level, offset : offset + extent, :]
                )
            image_ref[offset, level] = total


def swap_sides(low, high):
    count = lax.axis_size("tile")
    forward = [(i, i + 1) for i in range(count - 1)]
    backward = [(target, source) for source, target in forward]
    return lax.ppermute(high, "tile", forward), lax.ppermute(low, "tile", backward)


def per_device(
    src_prev,
    src_now,
    rec_prev,
    rec_now,
    speed_table,
    region_ids,
    source_cell,
    wavelet,
    receiver_cell,
    receiver_data,
):
    _, levels, extent, across = src_now.shape
    width = extent * lax.axis_size("tile")
    shots = lax.axis_size("shot")
    share = levels // shots
    first = (lax.axis_index("tile") * extent).reshape(1)
    params = pltpu.CompilerParams(vmem_limit_bytes=LIMIT)

    def struct(*shape):
        return jax.ShapeDtypeStruct(shape, jnp.float32)

    wide = pltpu.VMEM((2, levels, extent + 2 * LEAD, across), jnp.float32)
    message = struct(2 * levels + levels // 2, 2 * HALO, across)
    part, coef, plane, low, high = pl.pallas_call(
        functools.partial(own_part, width),
        out_shape=(
            struct(2, levels, extent, across),
            struct(levels, extent, across),
            struct(extent, across),
            message,
            message,
        ),
        in_specs=[SMEM] * 3 + [VMEM] * 8,
        out_specs=[VMEM] * 5,
        scratch_shapes=[wide, pltpu.VMEM((8, across), jnp.float32)],
        compiler_params=params,
        name="own_part",
    )(
        first,
        source_cell,
        wavelet,
        src_prev,
        src_now,
        rec_prev,
        rec_now,
        speed_table.reshape(1, -1),
        region_ids,
        receiver_cell,
        receiver_data,
    )
    from_low, from_high = swap_sides(low, high)
    src_next, rec_next, packed = pl.pallas_call(
        functools.partial(both_steps, width),
        out_shape=(
            struct(1, levels, extent, across),
            struct(1, levels, extent, across),
            struct(shots, 2, share, extent, across),
        ),
        in_specs=[SMEM] * 3 + [VMEM] * 7,
        out_specs=[VMEM] * 3,
        scratch_shapes=[wide, wide, wide],
        compiler_params=params,
        name="both_steps",
    )(first, source_cell, wavelet, src_now, rec_now, part, coef, plane, from_low, from_high)
    mine = lax.all_to_all(packed, "shot", 0, 0, tiled=True)
    low_fields, high_fields = swap_sides(mine, mine)
    image = pl.pallas_call(
        functools.partial(image_products, 1.0 / shots),
        out_shape=struct(OFFS, share, extent, across),
        in_specs=[VMEM] * 3,
        out_specs=VMEM,
        scratch_shapes=[pltpu.VMEM((shots, 2, share, extent + 2 * REACH, across), jnp.float32)],
        compiler_params=params,
        name="image_products",
    )(mine, low_fields, high_fields)
    return src_next, rec_next, image


def solution(mesh):
    field = P(("groups", "shot"), None, "tile", None)
    return jax.shard_map(
        per_device,
        mesh=mesh,
        in_specs=(
            field,
            field,
            field,
            field,
            P("groups"),
            P(None, ("groups", "tile"), None),
            P(("groups", "shot")),
            P(("groups", "shot"), None),
            P(("groups", "shot"), "tile"),
            P(("groups", "shot"), None, "tile"),
        ),
        out_specs=(field, field, P(None, "shot", ("groups", "tile"), None)),
        check_vma=False,
    )
```

```python
import functools

import jax
import jax.numpy as jnp
from jax import lax
from jax.experimental import pallas as pl
from jax.experimental.pallas import tpu as pltpu
from jax.sharding import PartitionSpec as P

OFFS = 33
REACH = OFFS // 2
HALO = 4
LEAD = 8

COEFS = (-205.0 / 72.0, 8.0 / 5.0, -1.0 / 5.0, 8.0 / 315.0, -1.0 / 560.0)

VMEM = pl.BlockSpec(memory_space=pltpu.VMEM)
HBM = pl.BlockSpec(memory_space=pltpu.HBM)
LIMIT = 16 * 1024 * 1024


def lane_weights(shape):
    lane = lax.broadcasted_iota(jnp.int32, shape, 1)
    across = shape[1]
    after = [jnp.where(lane < across - k, COEFS[k], 0.0) for k in range(1, HALO + 1)]
    before = [jnp.where(lane >= k, COEFS[k], 0.0) for k in range(1, HALO + 1)]
    return after, before


def laplace_level(wide, field, level, levels, extent, weights):
    after, before = weights
    centre = wide[field, level, LEAD : LEAD + extent, :]
    across = centre.shape[1]
    total = 3.0 * COEFS[0] * centre
    for k in range(1, HALO + 1):
        beside = (
            wide[field, level, LEAD + k : LEAD + k + extent, :]
            + wide[field, level, LEAD - k : LEAD - k + extent, :]
        )
        if level + k < levels:
            beside = beside + wide[field, level + k, LEAD : LEAD + extent, :]
        if level - k >= 0:
            beside = beside + wide[field, level - k, LEAD : LEAD + extent, :]
        total = total + COEFS[k] * beside
        total = total + after[k - 1] * pltpu.roll(centre, across - k, 1)
        total = total + before[k - 1] * pltpu.roll(centre, k, 1)
    return total


def source_hit(cell, level, width, first, shape):
    across = shape[1]
    flat = lax.broadcasted_iota(jnp.int32, shape, 0) * across + lax.broadcasted_iota(
        jnp.int32, shape, 1
    )
    return flat == cell - (level * width + first) * across


def own_part(
    width,
    table_hbm,
    spots_hbm,
    traces_hbm,
    cell_hbm,
    amps_hbm,
    ids_hbm,
    src_now,
    rec_now,
    src_prev,
    rec_prev,
    wide,
    part_ref,
    later_ref,
    coef_ref,
    low_ref,
    high_ref,
    table,
    spots_ref,
    traces_ref,
    cell_ref,
    amps_ref,
    ids_ref,
    prev_ref,
    sems,
):
    levels, extent, across = ids_ref.shape
    shape = (extent, across)
    regions = table_hbm.shape[1]
    end = LEAD + extent
    moves = (
        (table_hbm, table),
        (ids_hbm, ids_ref),
        (spots_hbm, spots_ref),
        (traces_hbm, traces_ref),
        (cell_hbm, cell_ref),
        (amps_hbm, amps_ref),
        (src_now.at[0], wide.at[0, :, pl.ds(LEAD, extent), :]),
        (src_prev.at[0], prev_ref.at[0]),
        (rec_now.at[0], wide.at[1, :, pl.ds(LEAD, extent), :]),
        (rec_prev.at[0], prev_ref.at[1]),
    )
    copies = [
        pltpu.make_async_copy(here, there, sems.at[i]) for i, (here, there) in enumerate(moves)
    ]
    for copy in copies:
        copy.start()
    zeros = jnp.zeros((LEAD, across), jnp.float32)
    for field in range(2):
        for level in range(levels):
            wide[field, level, 0:LEAD, :] = zeros
            wide[field, level, end : end + LEAD, :] = zeros
    weights = lane_weights(shape)

    for copy in copies[2:4]:
        copy.wait()
    spots = spots_ref[...]
    column = lax.broadcasted_iota(jnp.int32, (extent, spots.shape[1]), 0) * across
    in_column = (spots >= column) & (spots < column + across)
    lane = lax.broadcasted_iota(jnp.int32, (across, spots.shape[1]), 0)
    in_row = jnp.where(lax.rem(spots, across) == lane, 1.0, 0.0)
    traces = jnp.concatenate(
        [jnp.where(in_column, traces_ref[0, t : t + 1, :], 0.0) for t in range(2)], axis=0
    )
    planes = lax.dot_general(
        traces,
        in_row,
        (((1,), (1,)), ((), ())),
        precision=lax.Precision.HIGHEST,
        preferred_element_type=jnp.float32,
    )

    copies[0].wait()
    copies[1].wait()
    speeds = jnp.concatenate(
        [table[...], jnp.zeros((1, across - regions), jnp.float32)], axis=1
    )
    speeds = jnp.broadcast_to(speeds, (8, across))
    for level in range(levels):
        for row in range(0, extent, 8):
            ids = ids_ref[level, row : row + 8, :]
            coef_ref[level, row : row + 8, :] = jnp.take_along_axis(
                speeds, ids, axis=1, mode="promise_in_bounds"
            )
        place = 2 * levels + level // 2
        rows = pl.ds(level % 2 * HALO, HALO)
        low_ref[place, rows, :] = coef_ref[level, 0:HALO, :]
        high_ref[place, rows, :] = coef_ref[level, extent - HALO : extent, :]

    copies[4].wait()
    copies[5].wait()
    first = lax.axis_index("tile") * extent
    for field in range(2):
        copies[6 + 2 * field].wait()
        copies[7 + 2 * field].wait()
        for level in range(levels):
            total = laplace_level(wide, field, level, levels, extent, weights)
            now = wide[field, level, LEAD:end, :]
            value = 2.0 * now - prev_ref[field, level] + coef_ref[level] * total
            later = -now
            if field == 0:
                hit = source_hit(cell_ref[0], level, width, first, shape)
                value = value + jnp.where(hit, amps_ref[0, 0], 0.0)
                later = later + jnp.where(hit, amps_ref[0, 1], 0.0)
            elif level == 0:
                value = value + planes[:extent, :]
                later = later + planes[extent:, :]
            part_ref[field, level] = value
            later_ref[field, level] = later
            place = field * levels + level
            low_ref[place, 0:HALO, :] = now[0:HALO, :]
            low_ref[place, HALO : 2 * HALO, :] = value[0:HALO, :]
            high_ref[place, 0:HALO, :] = now[extent - HALO : extent, :]
            high_ref[place, HALO : 2 * HALO, :] = value[extent - HALO : extent, :]


def both_steps(
    own,
    part_ref,
    later_ref,
    coef_ref,
    low_ref,
    high_ref,
    packed_ref,
    other,
    middle,
):
    levels, extent, across = coef_ref.shape
    shape = (extent, across)
    share = packed_ref.shape[2]
    end = LEAD + extent
    for field in range(2):
        for level in range(levels):
            place = field * levels + level
            other[field, level, LEAD:end, :] = jnp.zeros(shape, jnp.float32)
            other[field, level, LEAD - HALO : LEAD, :] = low_ref[place, 0:HALO, :]
            other[field, level, end : end + HALO, :] = high_ref[place, 0:HALO, :]
    for field in range(2):
        for level in range(levels):
            place = field * levels + level
            pair = 2 * levels + level // 2
            rows = pl.ds(level % 2 * HALO, HALO)
            below = jnp.zeros((HALO, across), jnp.float32)
            above = jnp.zeros((HALO, across), jnp.float32)
            left = jnp.zeros((8, across), jnp.float32)
            right = jnp.zeros((8, across), jnp.float32)
            for k in range(1, HALO + 1):
                begin = LEAD - HALO + k
                below = below + COEFS[k] * own[field, level, begin : begin + HALO, :]
                above = above + COEFS[k] * own[field, level, end - k : end - k + HALO, :]
                left = left + COEFS[k] * other[field, level, LEAD - k : LEAD - k + 8, :]
                right = right + COEFS[k] * other[field, level, end - 8 + k : end + k, :]
            middle[field, level, LEAD - HALO : LEAD, :] = (
                low_ref[place, HALO : 2 * HALO, :] + low_ref[pair, rows, :] * below
            )
            middle[field, level, end : end + HALO, :] = (
                high_ref[place, HALO : 2 * HALO, :] + high_ref[pair, rows, :] * above
            )
            middle[field, level, LEAD : LEAD + 8, :] = (
                part_ref[field, level, 0:8, :] + coef_ref[level, 0:8, :] * left
            )
            middle[field, level, end - 8 : end, :] = (
                part_ref[field, level, extent - 8 : extent, :]
                + coef_ref[level, extent - 8 : extent, :] * right
            )
    weights = lane_weights(shape)
    for field in range(2):
        for level in range(levels):
            total = laplace_level(middle, field, level, levels, extent, weights)
            value = 2.0 * middle[field, level, LEAD:end, :] + later_ref[field, level]
            packed_ref[level // share, field, level % share] = value + coef_ref[level] * total


def image_products(
    weight,
    final_ref,
    mine_ref,
    low_ref,
    high_ref,
    src_hbm,
    rec_hbm,
    image_hbm,
    wide,
    image_ref,
    field_sems,
    image_sems,
):
    shots, _, share, extent, across = mine_ref.shape
    copies = []
    for field, out in enumerate((src_hbm, rec_hbm)):
        for shot in range(shots):
            copies.append(
                pltpu.make_async_copy(
                    final_ref.at[shot, field],
                    out.at[0, pl.ds(shot * share, share)],
                    field_sems.at[field, shot],
                )
            )
    for copy in copies:
        copy.start()
    for shot in range(shots):
        for field in range(2):
            for level in range(share):
                scale = weight if field == 0 else 1.0
                wide[shot, field, level, 0:REACH, :] = (
                    scale * low_ref[shot, field, level, extent - REACH : extent, :]
                )
                wide[shot, field, level, REACH : REACH + extent, :] = (
                    scale * mine_ref[shot, field, level]
                )
                wide[shot, field, level, REACH + extent : 2 * REACH + extent, :] = (
                    scale * high_ref[shot, field, level, 0:REACH, :]
                )
    parts = image_sems.shape[0]
    for piece in range(parts):
        offsets = range(piece * OFFS // parts, (piece + 1) * OFFS // parts)
        for offset in offsets:
            for level in range(share):
                total = jnp.zeros((extent, across), jnp.float32)
                for shot in range(shots):
                    begin = 2 * REACH - offset
                    total = total + (
                        wide[shot, 0, level, begin : begin + extent, :]
                        * wide[shot, 1, level, offset : offset + extent, :]
                    )
                image_ref[offset, level] = total
        rows = pl.ds(offsets[0], len(offsets))
        copy = pltpu.make_async_copy(image_ref.at[rows], image_hbm.at[rows], image_sems.at[piece])
        copy.start()
        copies.append(copy)
    for copy in copies:
        copy.wait()


def swap_sides(low, high):
    count = lax.axis_size("tile")
    forward = [(i, i + 1) for i in range(count - 1)]
    backward = [(target, source) for source, target in forward]
    return lax.ppermute(high, "tile", forward), lax.ppermute(low, "tile", backward)


def per_device(
    src_prev,
    src_now,
    rec_prev,
    rec_now,
    speed_table,
    region_ids,
    source_cell,
    wavelet,
    receiver_cell,
    receiver_data,
):
    _, levels, extent, across = src_now.shape
    width = extent * lax.axis_size("tile")
    shots = lax.axis_size("shot")
    share = levels // shots
    params = pltpu.CompilerParams(vmem_limit_bytes=LIMIT)

    def struct(*shape):
        return jax.ShapeDtypeStruct(shape, jnp.float32)

    def scratch(*shape, dtype=jnp.float32):
        return pltpu.VMEM(shape, dtype)

    wide_shape = (2, levels, extent + 2 * LEAD, across)
    message = struct(2 * levels + levels // 2, 2 * HALO, across)
    own, part, later, coef, low, high = pl.pallas_call(
        functools.partial(own_part, width),
        out_shape=(
            struct(*wide_shape),
            struct(2, levels, extent, across),
            struct(2, levels, extent, across),
            struct(levels, extent, across),
            message,
            message,
        ),
        in_specs=[HBM] * 10,
        out_specs=[VMEM] * 6,
        scratch_shapes=[
            scratch(1, speed_table.shape[0]),
            scratch(*receiver_cell.shape, dtype=jnp.int32),
            scratch(*receiver_data.shape),
            pltpu.SMEM(source_cell.shape, jnp.int32),
            pltpu.SMEM(wavelet.shape, jnp.float32),
            scratch(levels, extent, across, dtype=jnp.int32),
            scratch(2, levels, extent, across),
            pltpu.SemaphoreType.DMA((10,)),
        ],
        compiler_params=params,
        name="own_part",
    )(
        speed_table.reshape(1, -1),
        receiver_cell,
        receiver_data,
        source_cell,
        wavelet,
        region_ids,
        src_now,
        rec_now,
        src_prev,
        rec_prev,
    )
    from_low, from_high = swap_sides(low, high)
    packed = pl.pallas_call(
        both_steps,
        out_shape=struct(shots, 2, share, extent, across),
        in_specs=[VMEM] * 6,
        out_specs=VMEM,
        scratch_shapes=[scratch(*wide_shape), scratch(*wide_shape)],
        compiler_params=params,
        name="both_steps",
    )(own, part, later, coef, from_low, from_high)
    mine = lax.all_to_all(packed, "shot", 0, 0, tiled=True)
    low_fields, high_fields = swap_sides(mine, mine)
    return pl.pallas_call(
        functools.partial(image_products, 1.0 / shots),
        out_shape=(
            struct(1, levels, extent, across),
            struct(1, levels, extent, across),
            struct(OFFS, share, extent, across),
        ),
        in_specs=[VMEM] * 4,
        out_specs=[HBM] * 3,
        scratch_shapes=[
            scratch(shots, 2, share, extent + 2 * REACH, across),
            scratch(OFFS, share, extent, across),
            pltpu.SemaphoreType.DMA((2, shots)),
            pltpu.SemaphoreType.DMA((3,)),
        ],
        compiler_params=params,
        name="image_products",
    )(packed, mine, low_fields, high_fields)


def solution(mesh):
    field = P(("groups", "shot"), None, "tile", None)
    return jax.shard_map(
        per_device,
        mesh=mesh,
        in_specs=(
            field,
            field,
            field,
            field,
            P("groups"),
            P(None, ("groups", "tile"), None),
            P(("groups", "shot")),
            P(("groups", "shot"), None),
            P(("groups", "shot"), "tile"),
            P(("groups", "shot"), None, "tile"),
        ),
        out_specs=(field, field, P(None, "shot", ("groups", "tile"), None)),
        check_vma=False,
    )
```

```python
import functools

import jax
import jax.numpy as jnp
from jax import lax
from jax.experimental import pallas as pl
from jax.experimental.pallas import tpu as pltpu
from jax.sharding import PartitionSpec as P

OFFS = 33
REACH = OFFS // 2
HALO = 4
LEAD = 8

COEFS = (-205.0 / 72.0, 8.0 / 5.0, -1.0 / 5.0, 8.0 / 315.0, -1.0 / 560.0)

VMEM = pl.BlockSpec(memory_space=pltpu.VMEM)
HBM = pl.BlockSpec(memory_space=pltpu.HBM)
SMEM = pl.BlockSpec(memory_space=pltpu.SMEM)
LIMIT = 16 * 1024 * 1024


def lane_weights(shape):
    lane = lax.broadcasted_iota(jnp.int32, shape, 1)
    across = shape[1]
    after = [jnp.where(lane < across - k, COEFS[k], 0.0) for k in range(1, HALO + 1)]
    before = [jnp.where(lane >= k, COEFS[k], 0.0) for k in range(1, HALO + 1)]
    return after, before


def laplace_level(wide, field, level, levels, extent, weights):
    after, before = weights
    centre = wide[field, level, LEAD : LEAD + extent, :]
    across = centre.shape[1]
    total = 3.0 * COEFS[0] * centre
    for k in range(1, HALO + 1):
        beside = (
            wide[field, level, LEAD + k : LEAD + k + extent, :]
            + wide[field, level, LEAD - k : LEAD - k + extent, :]
        )
        if level + k < levels:
            beside = beside + wide[field, level + k, LEAD : LEAD + extent, :]
        if level - k >= 0:
            beside = beside + wide[field, level - k, LEAD : LEAD + extent, :]
        total = total + COEFS[k] * beside
        total = total + after[k - 1] * pltpu.roll(centre, across - k, 1)
        total = total + before[k - 1] * pltpu.roll(centre, k, 1)
    return total


def own_part(
    table_hbm,
    spots_hbm,
    traces_hbm,
    amps_hbm,
    ids_hbm,
    src_now,
    rec_now,
    src_prev,
    rec_prev,
    amps_ref,
    wide,
    part_ref,
    later_ref,
    coef_ref,
    low_ref,
    high_ref,
    table,
    spots_ref,
    traces_ref,
    ids_ref,
    prev_ref,
    sems,
):
    levels, extent, across = ids_ref.shape
    shape = (extent, across)
    regions = table_hbm.shape[1]
    end = LEAD + extent
    moves = (
        (table_hbm, table),
        (ids_hbm, ids_ref),
        (spots_hbm, spots_ref),
        (traces_hbm, traces_ref),
        (src_now.at[0], wide.at[0, :, pl.ds(LEAD, extent), :]),
        (src_prev.at[0], prev_ref.at[0]),
        (rec_now.at[0], wide.at[1, :, pl.ds(LEAD, extent), :]),
        (rec_prev.at[0], prev_ref.at[1]),
        (amps_hbm, amps_ref),
    )
    copies = [
        pltpu.make_async_copy(here, there, sems.at[i]) for i, (here, there) in enumerate(moves)
    ]
    for copy in copies:
        copy.start()
    zeros = jnp.zeros((LEAD, across), jnp.float32)
    for field in range(2):
        for level in range(levels):
            wide[field, level, 0:LEAD, :] = zeros
            wide[field, level, end : end + LEAD, :] = zeros
    weights = lane_weights(shape)

    for copy in copies[2:4]:
        copy.wait()
    spots = spots_ref[...]
    column = lax.broadcasted_iota(jnp.int32, (extent, spots.shape[1]), 0) * across
    in_column = (spots >= column) & (spots < column + across)
    lane = lax.broadcasted_iota(jnp.int32, (across, spots.shape[1]), 0)
    in_row = jnp.where(lax.rem(spots, across) == lane, 1.0, 0.0)
    traces = jnp.concatenate(
        [jnp.where(in_column, traces_ref[0, t : t + 1, :], 0.0) for t in range(2)], axis=0
    )
    planes = lax.dot_general(
        traces,
        in_row,
        (((1,), (1,)), ((), ())),
        precision=lax.Precision.HIGHEST,
        preferred_element_type=jnp.float32,
    )

    copies[0].wait()
    copies[1].wait()
    speeds = jnp.concatenate(
        [table[...], jnp.zeros((1, across - regions), jnp.float32)], axis=1
    )
    speeds = jnp.broadcast_to(speeds, (8, across))
    for level in range(levels):
        for row in range(0, extent, 8):
            ids = ids_ref[level, row : row + 8, :]
            coef_ref[level, row : row + 8, :] = jnp.take_along_axis(
                speeds, ids, axis=1, mode="promise_in_bounds"
            )
        place = 2 * levels + level // 2
        rows = pl.ds(level % 2 * HALO, HALO)
        low_ref[place, rows, :] = coef_ref[level, 0:HALO, :]
        high_ref[place, rows, :] = coef_ref[level, extent - HALO : extent, :]

    for field in range(2):
        copies[4 + 2 * field].wait()
        copies[5 + 2 * field].wait()
        for level in range(levels):
            total = laplace_level(wide, field, level, levels, extent, weights)
            now = wide[field, level, LEAD:end, :]
            value = 2.0 * now - prev_ref[field, level] + coef_ref[level] * total
            later = -now
            if field == 1 and level == 0:
                value = value + planes[:extent, :]
                later = later + planes[extent:, :]
            part_ref[field, level] = value
            later_ref[field, level] = later
            place = field * levels + level
            low_ref[place, 0:HALO, :] = now[0:HALO, :]
            low_ref[place, HALO : 2 * HALO, :] = value[0:HALO, :]
            high_ref[place, 0:HALO, :] = now[extent - HALO : extent, :]
            high_ref[place, HALO : 2 * HALO, :] = value[extent - HALO : extent, :]
    copies[8].wait()


def both_steps(
    width,
    cell_ref,
    amps_ref,
    own,
    part_ref,
    later_ref,
    coef_ref,
    low_ref,
    high_ref,
    packed_ref,
    other,
    middle,
):
    levels, extent, across = coef_ref.shape
    shape = (extent, across)
    shots, share = packed_ref.shape[0] // 2, packed_ref.shape[2]
    end = LEAD + extent
    for field in range(2):
        for level in range(levels):
            place = field * levels + level
            other[field, level, LEAD:end, :] = jnp.zeros(shape, jnp.float32)
            other[field, level, LEAD - HALO : LEAD, :] = low_ref[place, 0:HALO, :]
            other[field, level, end : end + HALO, :] = high_ref[place, 0:HALO, :]
    for field in range(2):
        for level in range(levels):
            place = field * levels + level
            pair = 2 * levels + level // 2
            rows = pl.ds(level % 2 * HALO, HALO)
            below = jnp.zeros((HALO, across), jnp.float32)
            above = jnp.zeros((HALO, across), jnp.float32)
            left = jnp.zeros((8, across), jnp.float32)
            right = jnp.zeros((8, across), jnp.float32)
            for k in range(1, HALO + 1):
                begin = LEAD - HALO + k
                below = below + COEFS[k] * own[field, level, begin : begin + HALO, :]
                above = above + COEFS[k] * own[field, level, end - k : end - k + HALO, :]
                left = left + COEFS[k] * other[field, level, LEAD - k : LEAD - k + 8, :]
                right = right + COEFS[k] * other[field, level, end - 8 + k : end + k, :]
            middle[field, level, LEAD - HALO : LEAD, :] = (
                low_ref[place, HALO : 2 * HALO, :] + low_ref[pair, rows, :] * below
            )
            middle[field, level, end : end + HALO, :] = (
                high_ref[place, HALO : 2 * HALO, :] + high_ref[pair, rows, :] * above
            )
            middle[field, level, LEAD : LEAD + 8, :] = (
                part_ref[field, level, 0:8, :] + coef_ref[level, 0:8, :] * left
            )
            middle[field, level, end - 8 : end, :] = (
                part_ref[field, level, extent - 8 : extent, :]
                + coef_ref[level, extent - 8 : extent, :] * right
            )
    cell = cell_ref[0]
    deep = lax.div(cell, width * across)
    row = lax.rem(lax.div(cell, across), width) - lax.axis_index("tile") * extent
    lane = lax.broadcasted_iota(jnp.int32, (1, across), 1)
    at_cell = lane == lax.rem(cell, across)
    inject = [jnp.where(at_cell, amps_ref[0:1, t : t + 1], 0.0) for t in range(2)]

    @pl.when((row >= -HALO) & (row < extent + HALO))
    def _():
        middle[0, deep, pl.ds(row + LEAD, 1), :] += inject[0]

    weights = lane_weights(shape)
    for field in range(2):
        for level in range(levels):
            total = laplace_level(middle, field, level, levels, extent, weights)
            value = 2.0 * middle[field, level, LEAD:end, :] + later_ref[field, level]
            value = value + coef_ref[level] * total
            for half in range(2):
                packed_ref[half * shots + level // share, field, level % share] = value

    @pl.when((row >= 0) & (row < extent))
    def _():
        for half in range(2):
            place = half * shots + lax.div(deep, share)
            packed_ref[place, 0, lax.rem(deep, share), pl.ds(row, 1), :] += inject[1]


def image_products(
    weight,
    final_ref,
    pair_ref,
    beyond_ref,
    src_hbm,
    rec_hbm,
    image_hbm,
    wide,
    image_ref,
    field_sems,
    image_sems,
):
    shots, _, share, extent, across = beyond_ref.shape
    copies = []
    for field, out in enumerate((src_hbm, rec_hbm)):
        for shot in range(shots):
            copies.append(
                pltpu.make_async_copy(
                    final_ref.at[shot, field],
                    out.at[0, pl.ds(shot * share, share)],
                    field_sems.at[field, shot],
                )
            )
    for copy in copies:
        copy.start()
    odd = lax.rem(lax.axis_index("tile"), 2)
    places = [pl.multiple_of((1 - odd + half) * extent, extent) for half in range(2)]
    outside = pl.multiple_of(odd * 2 * extent, extent)
    for shot in range(shots):
        for field in range(2):
            for level in range(share):
                scale = weight if field == 0 else 1.0
                for half in range(2):
                    wide[shot, field, level, pl.ds(places[half], extent), :] = (
                        scale * pair_ref[half * shots + shot, field, level]
                    )
                wide[shot, field, level, pl.ds(outside, extent), :] = (
                    scale * beyond_ref[shot, field, level]
                )
    parts = image_sems.shape[0]
    for piece in range(parts):
        offsets = range(piece * OFFS // parts, (piece + 1) * OFFS // parts)
        for offset in offsets:
            for level in range(share):
                total = jnp.zeros((extent, across), jnp.float32)
                for shot in range(shots):
                    lower = extent + REACH - offset
                    upper = extent - REACH + offset
                    total = total + (
                        wide[shot, 0, level, lower : lower + extent, :]
                        * wide[shot, 1, level, upper : upper + extent, :]
                    )
                image_ref[offset, level] = total
        rows = pl.ds(offsets[0], len(offsets))
        copy = pltpu.make_async_copy(image_ref.at[rows], image_hbm.at[rows], image_sems.at[piece])
        copy.start()
        copies.append(copy)
    for copy in copies:
        copy.wait()


def swap_sides(low, high):
    count = lax.axis_size("tile")
    forward = [(i, i + 1) for i in range(count - 1)]
    backward = [(target, source) for source, target in forward]
    return lax.ppermute(high, "tile", forward), lax.ppermute(low, "tile", backward)


def per_device(
    src_prev,
    src_now,
    rec_prev,
    rec_now,
    speed_table,
    region_ids,
    source_cell,
    wavelet,
    receiver_cell,
    receiver_data,
):
    _, levels, extent, across = src_now.shape
    tiles = lax.axis_size("tile")
    width = extent * tiles
    shots = lax.axis_size("shot")
    share = levels // shots
    params = pltpu.CompilerParams(vmem_limit_bytes=LIMIT)

    def struct(*shape):
        return jax.ShapeDtypeStruct(shape, jnp.float32)

    def scratch(*shape, dtype=jnp.float32):
        return pltpu.VMEM(shape, dtype)

    wide_shape = (2, levels, extent + 2 * LEAD, across)
    message = struct(2 * levels + levels // 2, 2 * HALO, across)
    amps, own, part, later, coef, low, high = pl.pallas_call(
        own_part,
        out_shape=(
            struct(*wavelet.shape),
            struct(*wide_shape),
            struct(2, levels, extent, across),
            struct(2, levels, extent, across),
            struct(levels, extent, across),
            message,
            message,
        ),
        in_specs=[HBM] * 9,
        out_specs=[VMEM] * 7,
        scratch_shapes=[
            scratch(1, speed_table.shape[0]),
            scratch(*receiver_cell.shape, dtype=jnp.int32),
            scratch(*receiver_data.shape),
            scratch(levels, extent, across, dtype=jnp.int32),
            scratch(2, levels, extent, across),
            pltpu.SemaphoreType.DMA((9,)),
        ],
        compiler_params=params,
        name="own_part",
    )(
        *(
            pltpu.with_memory_space_constraint(array, pltpu.HBM)
            for array in (
                speed_table.reshape(1, -1),
                receiver_cell,
                receiver_data,
                wavelet,
                region_ids,
                src_now,
                rec_now,
                src_prev,
                rec_prev,
            )
        )
    )
    from_low, from_high = swap_sides(low, high)
    packed = pl.pallas_call(
        functools.partial(both_steps, width),
        out_shape=struct(2 * shots, 2, share, extent, across),
        in_specs=[SMEM] + [VMEM] * 7,
        out_specs=VMEM,
        scratch_shapes=[scratch(*wide_shape), scratch(*wide_shape)],
        compiler_params=params,
        name="both_steps",
    )(source_cell, amps, own, part, later, coef, from_low, from_high)
    groups = [
        [tile * shots + shot for tile in (first, first + 1) for shot in range(shots)]
        for first in range(0, tiles, 2)
    ]
    pair = lax.all_to_all(
        packed, ("tile", "shot"), 0, 0, axis_index_groups=groups, tiled=True
    )
    mine = lax.dynamic_slice_in_dim(pair, lax.axis_index("tile") % 2 * shots, shots, 0)
    across_pairs = [(i, i + 1) for i in range(1, tiles - 1, 2)]
    beyond = lax.ppermute(mine, "tile", across_pairs + [(b, a) for a, b in across_pairs])
    return pl.pallas_call(
        functools.partial(image_products, 1.0 / shots),
        out_shape=(
            struct(1, levels, extent, across),
            struct(1, levels, extent, across),
            struct(OFFS, share, extent, across),
        ),
        in_specs=[VMEM] * 3,
        out_specs=[HBM] * 3,
        scratch_shapes=[
            scratch(shots, 2, share, 3 * extent, across),
            scratch(OFFS, share, extent, across),
            pltpu.SemaphoreType.DMA((2, shots)),
            pltpu.SemaphoreType.DMA((3,)),
        ],
        compiler_params=params,
        name="image_products",
    )(packed, pair, beyond)


def solution(mesh):
    field = P(("groups", "shot"), None, "tile", None)
    return jax.shard_map(
        per_device,
        mesh=mesh,
        in_specs=(
            field,
            field,
            field,
            field,
            P("groups"),
            P(None, ("groups", "tile"), None),
            P(("groups", "shot")),
            P(("groups", "shot"), None),
            P(("groups", "shot"), "tile"),
            P(("groups", "shot"), None, "tile"),
        ),
        out_specs=(field, field, P(None, "shot", ("groups", "tile"), None)),
        check_vma=False,
    )
```

```python
import functools

import jax
import jax.numpy as jnp
from jax import lax
from jax.experimental import pallas as pl
from jax.experimental.pallas import tpu as pltpu
from jax.sharding import PartitionSpec as P

OFFS = 33
REACH = OFFS // 2
HALO = 4
LEAD = 8

COEFS = (-205.0 / 72.0, 8.0 / 5.0, -1.0 / 5.0, 8.0 / 315.0, -1.0 / 560.0)

VMEM = pl.BlockSpec(memory_space=pltpu.VMEM)
HBM = pl.BlockSpec(memory_space=pltpu.HBM)
SMEM = pl.BlockSpec(memory_space=pltpu.SMEM)
LIMIT = 16 * 1024 * 1024


def lane_weights(shape):
    lane = lax.broadcasted_iota(jnp.int32, shape, 1)
    across = shape[1]
    after = [jnp.where(lane < across - k, COEFS[k], 0.0) for k in range(1, HALO + 1)]
    before = [jnp.where(lane >= k, COEFS[k], 0.0) for k in range(1, HALO + 1)]
    return after, before


def laplace_level(wide, field, level, levels, extent, weights):
    after, before = weights
    centre = wide[field, level, LEAD : LEAD + extent, :]
    across = centre.shape[1]
    total = 3.0 * COEFS[0] * centre
    for k in range(1, HALO + 1):
        beside = (
            wide[field, level, LEAD + k : LEAD + k + extent, :]
            + wide[field, level, LEAD - k : LEAD - k + extent, :]
        )
        if level + k < levels:
            beside = beside + wide[field, level + k, LEAD : LEAD + extent, :]
        if level - k >= 0:
            beside = beside + wide[field, level - k, LEAD : LEAD + extent, :]
        total = total + COEFS[k] * beside
        total = total + after[k - 1] * pltpu.roll(centre, across - k, 1)
        total = total + before[k - 1] * pltpu.roll(centre, k, 1)
    return total


def goes_up_first():
    return lax.rem(lax.axis_index("tile") + lax.axis_index("shot"), 2) == 0


def source_and_order(
    width, cell_ref, amps_ref, later_ref, source_ref, source_later_ref, up_first_ref
):
    levels, extent, across = source_later_ref.shape
    cell = cell_ref[0]
    deep = lax.div(cell, width * across)
    row = lax.rem(lax.div(cell, across), width) - lax.axis_index("tile") * extent + LEAD
    shape = (extent + 2 * LEAD, across)
    rows = lax.broadcasted_iota(jnp.int32, shape, 0)
    lanes = lax.broadcasted_iota(jnp.int32, shape, 1)
    hit = jnp.where((rows == row) & (lanes == lax.rem(cell, across)), 1.0, 0.0)
    for level in range(levels):
        here = hit * jnp.where(deep == level, 1.0, 0.0)
        source_ref[level] = here * amps_ref[0:1, 0:1]
        source_later_ref[level] = (
            later_ref[0, level] + here[LEAD : LEAD + extent, :] * amps_ref[0:1, 1:2]
        )
    up_first_ref[...] = jnp.full(
        up_first_ref.shape, jnp.where(goes_up_first(), 1, 0), dtype=jnp.int32
    )


def own_part(
    table_hbm,
    spots_hbm,
    traces_hbm,
    amps_hbm,
    ids_hbm,
    src_now,
    rec_now,
    src_prev,
    rec_prev,
    amps_ref,
    wide,
    part_ref,
    later_ref,
    coef_ref,
    sent_first_ref,
    sent_last_ref,
    table,
    spots_ref,
    traces_ref,
    ids_ref,
    prev_ref,
    sems,
):
    levels, extent, across = ids_ref.shape
    shape = (extent, across)
    regions = table_hbm.shape[1]
    end = LEAD + extent
    moves = (
        (table_hbm, table),
        (ids_hbm, ids_ref),
        (spots_hbm, spots_ref),
        (traces_hbm, traces_ref),
        (src_now.at[0], wide.at[0, :, pl.ds(LEAD, extent), :]),
        (src_prev.at[0], prev_ref.at[0]),
        (rec_now.at[0], wide.at[1, :, pl.ds(LEAD, extent), :]),
        (rec_prev.at[0], prev_ref.at[1]),
        (amps_hbm, amps_ref),
    )
    copies = [
        pltpu.make_async_copy(here, there, sems.at[i]) for i, (here, there) in enumerate(moves)
    ]
    for copy in copies:
        copy.start()
    zeros = jnp.zeros((LEAD, across), jnp.float32)
    for field in range(2):
        for level in range(levels):
            wide[field, level, 0:LEAD, :] = zeros
            wide[field, level, end : end + LEAD, :] = zeros
    weights = lane_weights(shape)

    for copy in copies[2:4]:
        copy.wait()
    spots = spots_ref[...]
    column = lax.broadcasted_iota(jnp.int32, (extent, spots.shape[1]), 0) * across
    in_column = (spots >= column) & (spots < column + across)
    lane = lax.broadcasted_iota(jnp.int32, (across, spots.shape[1]), 0)
    in_row = jnp.where(lax.rem(spots, across) == lane, 1.0, 0.0)
    traces = jnp.concatenate(
        [jnp.where(in_column, traces_ref[0, t : t + 1, :], 0.0) for t in range(2)], axis=0
    )
    planes = lax.dot_general(
        traces,
        in_row,
        (((1,), (1,)), ((), ())),
        precision=lax.Precision.HIGHEST,
        preferred_element_type=jnp.float32,
    )

    up_first = goes_up_first()

    def send(place, rows, value):
        low = value[0:HALO, :]
        high = value[extent - HALO : extent, :]
        sent_first_ref[place, rows, :] = jnp.where(up_first, high, low)
        sent_last_ref[place, rows, :] = jnp.where(up_first, low, high)

    copies[0].wait()
    copies[1].wait()
    speeds = jnp.concatenate(
        [table[...], jnp.zeros((1, across - regions), jnp.float32)], axis=1
    )
    speeds = jnp.broadcast_to(speeds, (8, across))
    for level in range(levels):
        for row in range(0, extent, 8):
            ids = ids_ref[level, row : row + 8, :]
            coef_ref[level, row : row + 8, :] = jnp.take_along_axis(
                speeds, ids, axis=1, mode="promise_in_bounds"
            )
        send(2 * levels + level // 2, pl.ds(level % 2 * HALO, HALO), coef_ref[level])

    for field in range(2):
        copies[4 + 2 * field].wait()
        copies[5 + 2 * field].wait()
        for level in range(levels):
            total = laplace_level(wide, field, level, levels, extent, weights)
            now = wide[field, level, LEAD:end, :]
            value = 2.0 * now - prev_ref[field, level] + coef_ref[level] * total
            later = -now
            if field == 1 and level == 0:
                value = value + planes[:extent, :]
                later = later + planes[extent:, :]
            part_ref[field, level] = value
            later_ref[field, level] = later
            place = field * levels + level
            send(place, pl.ds(0, HALO), now)
            send(place, pl.ds(HALO, HALO), value)
    copies[8].wait()


def both_steps(
    up_first_ref,
    own,
    part_ref,
    later_ref,
    source_ref,
    source_later_ref,
    coef_ref,
    came_first_ref,
    came_last_ref,
    packed_ref,
    other,
    middle,
):
    levels, extent, across = coef_ref.shape
    shape = (extent, across)
    share = packed_ref.shape[2]
    end = LEAD + extent
    up_first = up_first_ref[0:HALO, :] != 0

    def received(place, rows):
        first = came_first_ref[place, rows, :]
        last = came_last_ref[place, rows, :]
        return jnp.where(up_first, last, first), jnp.where(up_first, first, last)

    for field in range(2):
        for level in range(levels):
            low, high = received(field * levels + level, pl.ds(0, HALO))
            other[field, level, LEAD:end, :] = jnp.zeros(shape, jnp.float32)
            other[field, level, LEAD - HALO : LEAD, :] = low
            other[field, level, end : end + HALO, :] = high
    for field in range(2):
        for level in range(levels):
            below = jnp.zeros((HALO, across), jnp.float32)
            above = jnp.zeros((HALO, across), jnp.float32)
            left = jnp.zeros((8, across), jnp.float32)
            right = jnp.zeros((8, across), jnp.float32)
            for k in range(1, HALO + 1):
                begin = LEAD - HALO + k
                below = below + COEFS[k] * own[field, level, begin : begin + HALO, :]
                above = above + COEFS[k] * own[field, level, end - k : end - k + HALO, :]
                left = left + COEFS[k] * other[field, level, LEAD - k : LEAD - k + 8, :]
                right = right + COEFS[k] * other[field, level, end - 8 + k : end + k, :]
            low, high = received(field * levels + level, pl.ds(HALO, HALO))
            low_coef, high_coef = received(
                2 * levels + level // 2, pl.ds(level % 2 * HALO, HALO)
            )
            low = low + low_coef * below
            high = high + high_coef * above
            left = part_ref[field, level, 0:8, :] + coef_ref[level, 0:8, :] * left
            right = (
                part_ref[field, level, extent - 8 : extent, :]
                + coef_ref[level, extent - 8 : extent, :] * right
            )
            if field == 0:
                low = low + source_ref[level, LEAD - HALO : LEAD, :]
                left = left + source_ref[level, LEAD : LEAD + 8, :]
                right = right + source_ref[level, end - 8 : end, :]
                high = high + source_ref[level, end : end + HALO, :]
            middle[field, level, LEAD - HALO : LEAD, :] = low
            middle[field, level, LEAD : LEAD + 8, :] = left
            middle[field, level, end - 8 : end, :] = right
            middle[field, level, end : end + HALO, :] = high
    weights = lane_weights(shape)
    for field in range(2):
        for level in range(levels):
            total = laplace_level(middle, field, level, levels, extent, weights)
            later = source_later_ref[level] if field == 0 else later_ref[field, level]
            value = 2.0 * middle[field, level, LEAD:end, :] + later
            packed_ref[level // share, field, level % share] = value + coef_ref[level] * total


def image_products(
    weight,
    up_first_ref,
    final_ref,
    mine_ref,
    came_first_ref,
    came_last_ref,
    src_hbm,
    rec_hbm,
    image_hbm,
    wide,
    image_ref,
    field_sems,
    image_sems,
):
    shots, _, share, extent, across = mine_ref.shape
    copies = []
    for field, out in enumerate((src_hbm, rec_hbm)):
        for shot in range(shots):
            copies.append(
                pltpu.make_async_copy(
                    final_ref.at[shot, field],
                    out.at[0, pl.ds(shot * share, share)],
                    field_sems.at[field, shot],
                )
            )
    for copy in copies:
        copy.start()
    up_first = jnp.concatenate([up_first_ref[...]] * (extent // 8), axis=0) != 0
    for shot in range(shots):
        for field in range(2):
            for level in range(share):
                scale = weight if field == 0 else 1.0
                first = scale * came_first_ref[shot, field, level]
                last = scale * came_last_ref[shot, field, level]
                wide[shot, field, level, 0:extent, :] = jnp.where(up_first, last, first)
                wide[shot, field, level, extent : 2 * extent, :] = (
                    scale * mine_ref[shot, field, level]
                )
                wide[shot, field, level, 2 * extent : 3 * extent, :] = jnp.where(
                    up_first, first, last
                )
    parts = image_sems.shape[0]
    for piece in range(parts):
        offsets = range(piece * OFFS // parts, (piece + 1) * OFFS // parts)
        for offset in offsets:
            for level in range(share):
                total = jnp.zeros((extent, across), jnp.float32)
                for shot in range(shots):
                    lower = extent + REACH - offset
                    upper = extent - REACH + offset
                    total = total + (
                        wide[shot, 0, level, lower : lower + extent, :]
                        * wide[shot, 1, level, upper : upper + extent, :]
                    )
                image_ref[offset, level] = total
        rows = pl.ds(offsets[0], len(offsets))
        copy = pltpu.make_async_copy(image_ref.at[rows], image_hbm.at[rows], image_sems.at[piece])
        copy.start()
        copies.append(copy)
    for copy in copies:
        copy.wait()


def swap_sides(first, last):
    tiles, shots = lax.axis_size("tile"), lax.axis_size("shot")
    rounds = [[], []]
    for tile in range(tiles - 1):
        for shot in range(shots):
            here, there = tile * shots + shot, (tile + 1) * shots + shot
            rounds[(tile + shot) % 2] += [(here, there), (there, here)]
    axes = ("tile", "shot")
    return lax.ppermute(first, axes, rounds[0]), lax.ppermute(last, axes, rounds[1])


def per_device(
    src_prev,
    src_now,
    rec_prev,
    rec_now,
    speed_table,
    region_ids,
    source_cell,
    wavelet,
    receiver_cell,
    receiver_data,
):
    _, levels, extent, across = src_now.shape
    tiles = lax.axis_size("tile")
    width = extent * tiles
    shots = lax.axis_size("shot")
    share = levels // shots
    params = pltpu.CompilerParams(vmem_limit_bytes=LIMIT)

    def struct(*shape):
        return jax.ShapeDtypeStruct(shape, jnp.float32)

    def scratch(*shape, dtype=jnp.float32):
        return pltpu.VMEM(shape, dtype)

    wide_shape = (2, levels, extent + 2 * LEAD, across)
    message = struct(2 * levels + levels // 2, 2 * HALO, across)
    amps, own, part, later, coef, first, last = pl.pallas_call(
        own_part,
        out_shape=(
            struct(*wavelet.shape),
            struct(*wide_shape),
            struct(2, levels, extent, across),
            struct(2, levels, extent, across),
            struct(levels, extent, across),
            message,
            message,
        ),
        in_specs=[HBM] * 9,
        out_specs=[VMEM] * 7,
        scratch_shapes=[
            scratch(1, speed_table.shape[0]),
            scratch(*receiver_cell.shape, dtype=jnp.int32),
            scratch(*receiver_data.shape),
            scratch(levels, extent, across, dtype=jnp.int32),
            scratch(2, levels, extent, across),
            pltpu.SemaphoreType.DMA((9,)),
        ],
        compiler_params=params,
        name="own_part",
    )(
        *(
            pltpu.with_memory_space_constraint(array, pltpu.HBM)
            for array in (
                speed_table.reshape(1, -1),
                receiver_cell,
                receiver_data,
                wavelet,
                region_ids,
                src_now,
                rec_now,
                src_prev,
                rec_prev,
            )
        )
    )
    came_first, came_last = swap_sides(first, last)
    source, source_later, up_first = pl.pallas_call(
        functools.partial(source_and_order, width),
        out_shape=(
            struct(levels, extent + 2 * LEAD, across),
            struct(levels, extent, across),
            jax.ShapeDtypeStruct((8, across), jnp.int32),
        ),
        in_specs=[SMEM] + [VMEM] * 2,
        out_specs=[VMEM] * 3,
        compiler_params=params,
        name="source_and_order",
    )(source_cell, amps, later)
    packed = pl.pallas_call(
        both_steps,
        out_shape=struct(shots, 2, share, extent, across),
        in_specs=[VMEM] * 9,
        out_specs=VMEM,
        scratch_shapes=[scratch(*wide_shape), scratch(*wide_shape)],
        compiler_params=params,
        name="both_steps",
    )(up_first, own, part, later, source, source_later, coef, came_first, came_last)
    mine = lax.all_to_all(packed, "shot", 0, 0, tiled=True)
    fields_first, fields_last = swap_sides(mine, mine)
    return pl.pallas_call(
        functools.partial(image_products, 1.0 / shots),
        out_shape=(
            struct(1, levels, extent, across),
            struct(1, levels, extent, across),
            struct(OFFS, share, extent, across),
        ),
        in_specs=[VMEM] * 5,
        out_specs=[HBM] * 3,
        scratch_shapes=[
            scratch(shots, 2, share, 3 * extent, across),
            scratch(OFFS, share, extent, across),
            pltpu.SemaphoreType.DMA((2, shots)),
            pltpu.SemaphoreType.DMA((3,)),
        ],
        compiler_params=params,
        name="image_products",
    )(up_first, packed, mine, fields_first, fields_last)


def solution(mesh):
    field = P(("groups", "shot"), None, "tile", None)
    return jax.shard_map(
        per_device,
        mesh=mesh,
        in_specs=(
            field,
            field,
            field,
            field,
            P("groups"),
            P(None, ("groups", "tile"), None),
            P(("groups", "shot")),
            P(("groups", "shot"), None),
            P(("groups", "shot"), "tile"),
            P(("groups", "shot"), None, "tile"),
        ),
        out_specs=(field, field, P(None, "shot", ("groups", "tile"), None)),
        check_vma=False,
    )
```

```python
import functools

import jax
import jax.numpy as jnp
from jax import lax
from jax.experimental import pallas as pl
from jax.experimental.pallas import tpu as pltpu
from jax.sharding import PartitionSpec as P

OFFS = 33
REACH = OFFS // 2
HALO = 4
LEAD = 8

COEFS = (-205.0 / 72.0, 8.0 / 5.0, -1.0 / 5.0, 8.0 / 315.0, -1.0 / 560.0)

VMEM = pl.BlockSpec(memory_space=pltpu.VMEM)
HBM = pl.BlockSpec(memory_space=pltpu.HBM)
SMEM = pl.BlockSpec(memory_space=pltpu.SMEM)
LIMIT = 16 * 1024 * 1024


def lane_weights(shape):
    lane = lax.broadcasted_iota(jnp.int32, shape, 1)
    across = shape[1]
    after = [jnp.where(lane < across - k, COEFS[k], 0.0) for k in range(1, HALO + 1)]
    before = [jnp.where(lane >= k, COEFS[k], 0.0) for k in range(1, HALO + 1)]
    return after, before


def laplace_level(wide, field, level, levels, extent, weights):
    after, before = weights
    centre = wide[field, level, LEAD : LEAD + extent, :]
    across = centre.shape[1]
    total = 3.0 * COEFS[0] * centre
    for k in range(1, HALO + 1):
        beside = (
            wide[field, level, LEAD + k : LEAD + k + extent, :]
            + wide[field, level, LEAD - k : LEAD - k + extent, :]
        )
        if level + k < levels:
            beside = beside + wide[field, level + k, LEAD : LEAD + extent, :]
        if level - k >= 0:
            beside = beside + wide[field, level - k, LEAD : LEAD + extent, :]
        total = total + COEFS[k] * beside
        total = total + after[k - 1] * pltpu.roll(centre, across - k, 1)
        total = total + before[k - 1] * pltpu.roll(centre, k, 1)
    return total


def goes_up_first():
    return lax.rem(lax.axis_index("tile"), 2) == 0


def source_and_order(
    width, cell_ref, amps_ref, later_ref, source_ref, source_later_ref, up_first_ref
):
    levels, extent, across = source_later_ref.shape
    cell = cell_ref[0]
    deep = lax.div(cell, width * across)
    row = lax.rem(lax.div(cell, across), width) - lax.axis_index("tile") * extent + LEAD
    shape = (extent + 2 * LEAD, across)
    rows = lax.broadcasted_iota(jnp.int32, shape, 0)
    lanes = lax.broadcasted_iota(jnp.int32, shape, 1)
    hit = jnp.where((rows == row) & (lanes == lax.rem(cell, across)), 1.0, 0.0)
    for level in range(levels):
        here = hit * jnp.where(deep == level, 1.0, 0.0)
        source_ref[level] = here * amps_ref[0:1, 0:1]
        source_later_ref[level] = (
            later_ref[0, level] + here[LEAD : LEAD + extent, :] * amps_ref[0:1, 1:2]
        )
    up_first_ref[...] = jnp.full(
        up_first_ref.shape, jnp.where(goes_up_first(), 1, 0), dtype=jnp.int32
    )


def own_part(
    table_hbm,
    spots_hbm,
    traces_hbm,
    amps_hbm,
    ids_hbm,
    src_now,
    rec_now,
    src_prev,
    rec_prev,
    amps_ref,
    wide,
    part_ref,
    later_ref,
    coef_ref,
    sent_first_ref,
    sent_last_ref,
    table,
    spots_ref,
    traces_ref,
    ids_ref,
    prev_ref,
    sems,
):
    levels, extent, across = ids_ref.shape
    shape = (extent, across)
    regions = table_hbm.shape[1]
    end = LEAD + extent
    moves = (
        (table_hbm, table),
        (ids_hbm, ids_ref),
        (spots_hbm, spots_ref),
        (traces_hbm, traces_ref),
        (src_now.at[0], wide.at[0, :, pl.ds(LEAD, extent), :]),
        (src_prev.at[0], prev_ref.at[0]),
        (rec_now.at[0], wide.at[1, :, pl.ds(LEAD, extent), :]),
        (rec_prev.at[0], prev_ref.at[1]),
        (amps_hbm, amps_ref),
    )
    copies = [
        pltpu.make_async_copy(here, there, sems.at[i]) for i, (here, there) in enumerate(moves)
    ]
    for copy in copies:
        copy.start()
    zeros = jnp.zeros((LEAD, across), jnp.float32)
    for field in range(2):
        for level in range(levels):
            wide[field, level, 0:LEAD, :] = zeros
            wide[field, level, end : end + LEAD, :] = zeros
    weights = lane_weights(shape)

    for copy in copies[2:4]:
        copy.wait()
    spots = spots_ref[...]
    column = lax.broadcasted_iota(jnp.int32, (extent, spots.shape[1]), 0) * across
    in_column = (spots >= column) & (spots < column + across)
    lane = lax.broadcasted_iota(jnp.int32, (across, spots.shape[1]), 0)
    in_row = jnp.where(lax.rem(spots, across) == lane, 1.0, 0.0)
    traces = jnp.concatenate(
        [jnp.where(in_column, traces_ref[0, t : t + 1, :], 0.0) for t in range(2)], axis=0
    )
    planes = lax.dot_general(
        traces,
        in_row,
        (((1,), (1,)), ((), ())),
        precision=lax.Precision.HIGHEST,
        preferred_element_type=jnp.float32,
    )

    up_first = goes_up_first()

    def send(place, rows, value):
        low = value[0:HALO, :]
        high = value[extent - HALO : extent, :]
        sent_first_ref[place, rows, :] = jnp.where(up_first, high, low)
        sent_last_ref[place, rows, :] = jnp.where(up_first, low, high)

    copies[0].wait()
    copies[1].wait()
    speeds = jnp.concatenate(
        [table[...], jnp.zeros((1, across - regions), jnp.float32)], axis=1
    )
    speeds = jnp.broadcast_to(speeds, (8, across))
    for level in range(levels):
        for row in range(0, extent, 8):
            ids = ids_ref[level, row : row + 8, :]
            coef_ref[level, row : row + 8, :] = jnp.take_along_axis(
                speeds, ids, axis=1, mode="promise_in_bounds"
            )
        send(2 * levels + level // 2, pl.ds(level % 2 * HALO, HALO), coef_ref[level])

    for field in range(2):
        copies[4 + 2 * field].wait()
        copies[5 + 2 * field].wait()
        for level in range(levels):
            total = laplace_level(wide, field, level, levels, extent, weights)
            now = wide[field, level, LEAD:end, :]
            value = 2.0 * now - prev_ref[field, level] + coef_ref[level] * total
            later = -now
            if field == 1 and level == 0:
                value = value + planes[:extent, :]
                later = later + planes[extent:, :]
            part_ref[field, level] = value
            later_ref[field, level] = later
            place = field * levels + level
            send(place, pl.ds(0, HALO), now)
            send(place, pl.ds(HALO, HALO), value)
    copies[8].wait()


def both_steps(
    up_first_ref,
    own,
    part_ref,
    later_ref,
    source_ref,
    source_later_ref,
    coef_ref,
    came_first_ref,
    came_last_ref,
    packed_ref,
    other,
    middle,
):
    levels, extent, across = coef_ref.shape
    shape = (extent, across)
    share = packed_ref.shape[2]
    end = LEAD + extent
    up_first = up_first_ref[0:HALO, :] != 0

    def received(place, rows):
        first = came_first_ref[place, rows, :]
        last = came_last_ref[place, rows, :]
        return jnp.where(up_first, last, first), jnp.where(up_first, first, last)

    for field in range(2):
        for level in range(levels):
            low, high = received(field * levels + level, pl.ds(0, HALO))
            other[field, level, LEAD:end, :] = jnp.zeros(shape, jnp.float32)
            other[field, level, LEAD - HALO : LEAD, :] = low
            other[field, level, end : end + HALO, :] = high
    for field in range(2):
        for level in range(levels):
            below = jnp.zeros((HALO, across), jnp.float32)
            above = jnp.zeros((HALO, across), jnp.float32)
            left = jnp.zeros((8, across), jnp.float32)
            right = jnp.zeros((8, across), jnp.float32)
            for k in range(1, HALO + 1):
                begin = LEAD - HALO + k
                below = below + COEFS[k] * own[field, level, begin : begin + HALO, :]
                above = above + COEFS[k] * own[field, level, end - k : end - k + HALO, :]
                left = left + COEFS[k] * other[field, level, LEAD - k : LEAD - k + 8, :]
                right = right + COEFS[k] * other[field, level, end - 8 + k : end + k, :]
            low, high = received(field * levels + level, pl.ds(HALO, HALO))
            low_coef, high_coef = received(
                2 * levels + level // 2, pl.ds(level % 2 * HALO, HALO)
            )
            low = low + low_coef * below
            high = high + high_coef * above
            left = part_ref[field, level, 0:8, :] + coef_ref[level, 0:8, :] * left
            right = (
                part_ref[field, level, extent - 8 : extent, :]
                + coef_ref[level, extent - 8 : extent, :] * right
            )
            if field == 0:
                low = low + source_ref[level, LEAD - HALO : LEAD, :]
                left = left + source_ref[level, LEAD : LEAD + 8, :]
                right = right + source_ref[level, end - 8 : end, :]
                high = high + source_ref[level, end : end + HALO, :]
            middle[field, level, LEAD - HALO : LEAD, :] = low
            middle[field, level, LEAD : LEAD + 8, :] = left
            middle[field, level, end - 8 : end, :] = right
            middle[field, level, end : end + HALO, :] = high
    weights = lane_weights(shape)
    for field in range(2):
        for level in range(levels):
            total = laplace_level(middle, field, level, levels, extent, weights)
            later = source_later_ref[level] if field == 0 else later_ref[field, level]
            value = 2.0 * middle[field, level, LEAD:end, :] + later
            packed_ref[level // share, field, level % share] = value + coef_ref[level] * total


def image_products(
    weight,
    up_first_ref,
    final_ref,
    mine_ref,
    came_last_ref,
    came_first_ref,
    src_hbm,
    rec_hbm,
    image_hbm,
    wide,
    image_ref,
    field_sems,
    image_sems,
):
    shots, _, share, extent, across = mine_ref.shape
    copies = []
    for field, out in enumerate((src_hbm, rec_hbm)):
        for shot in range(shots):
            copies.append(
                pltpu.make_async_copy(
                    final_ref.at[shot, field],
                    out.at[0, pl.ds(shot * share, share)],
                    field_sems.at[field, shot],
                )
            )
    for copy in copies:
        copy.start()
    up_first = jnp.concatenate([up_first_ref[...]] * (extent // 8), axis=0) != 0
    for shot in range(shots):
        for field in range(2):
            for level in range(share):
                scale = weight if field == 0 else 1.0
                first = scale * came_first_ref[shot, field, level]
                last = scale * came_last_ref[shot, field, level]
                wide[shot, field, level, 0:extent, :] = jnp.where(up_first, last, first)
                wide[shot, field, level, extent : 2 * extent, :] = (
                    scale * mine_ref[shot, field, level]
                )
                wide[shot, field, level, 2 * extent : 3 * extent, :] = jnp.where(
                    up_first, first, last
                )
    parts = image_sems.shape[0]
    for piece in range(parts):
        offsets = range(piece * OFFS // parts, (piece + 1) * OFFS // parts)
        for offset in offsets:
            for level in range(share):
                total = jnp.zeros((extent, across), jnp.float32)
                for shot in range(shots):
                    lower = extent + REACH - offset
                    upper = extent - REACH + offset
                    total = total + (
                        wide[shot, 0, level, lower : lower + extent, :]
                        * wide[shot, 1, level, upper : upper + extent, :]
                    )
                image_ref[offset, level] = total
        rows = pl.ds(offsets[0], len(offsets))
        copy = pltpu.make_async_copy(image_ref.at[rows], image_hbm.at[rows], image_sems.at[piece])
        copy.start()
        copies.append(copy)
    for copy in copies:
        copy.wait()


def swap_sides(first, last):
    rounds = [
        [pair for here in range(begin, lax.axis_size("tile") - 1, 2) for pair in both_ways(here)]
        for begin in range(2)
    ]
    came_last = lax.ppermute(last, "tile", rounds[1])
    came_first = lax.ppermute(first, "tile", rounds[0])
    return came_first, came_last


def both_ways(tile):
    return (tile, tile + 1), (tile + 1, tile)


def per_device(
    src_prev,
    src_now,
    rec_prev,
    rec_now,
    speed_table,
    region_ids,
    source_cell,
    wavelet,
    receiver_cell,
    receiver_data,
):
    _, levels, extent, across = src_now.shape
    tiles = lax.axis_size("tile")
    width = extent * tiles
    shots = lax.axis_size("shot")
    share = levels // shots
    params = pltpu.CompilerParams(vmem_limit_bytes=LIMIT)

    def struct(*shape):
        return jax.ShapeDtypeStruct(shape, jnp.float32)

    def scratch(*shape, dtype=jnp.float32):
        return pltpu.VMEM(shape, dtype)

    wide_shape = (2, levels, extent + 2 * LEAD, across)
    message = struct(2 * levels + levels // 2, 2 * HALO, across)
    amps, own, part, later, coef, first, last = pl.pallas_call(
        own_part,
        out_shape=(
            struct(*wavelet.shape),
            struct(*wide_shape),
            struct(2, levels, extent, across),
            struct(2, levels, extent, across),
            struct(levels, extent, across),
            message,
            message,
        ),
        in_specs=[HBM] * 9,
        out_specs=[VMEM] * 7,
        scratch_shapes=[
            scratch(1, speed_table.shape[0]),
            scratch(*receiver_cell.shape, dtype=jnp.int32),
            scratch(*receiver_data.shape),
            scratch(levels, extent, across, dtype=jnp.int32),
            scratch(2, levels, extent, across),
            pltpu.SemaphoreType.DMA((9,)),
        ],
        compiler_params=params,
        name="own_part",
    )(
        *(
            pltpu.with_memory_space_constraint(array, pltpu.HBM)
            for array in (
                speed_table.reshape(1, -1),
                receiver_cell,
                receiver_data,
                wavelet,
                region_ids,
                src_now,
                rec_now,
                src_prev,
                rec_prev,
            )
        )
    )
    came_first, came_last = swap_sides(first, last)
    source, source_later, up_first = pl.pallas_call(
        functools.partial(source_and_order, width),
        out_shape=(
            struct(levels, extent + 2 * LEAD, across),
            struct(levels, extent, across),
            jax.ShapeDtypeStruct((8, across), jnp.int32),
        ),
        in_specs=[SMEM] + [VMEM] * 2,
        out_specs=[VMEM] * 3,
        compiler_params=params,
        name="source_and_order",
    )(source_cell, amps, later)
    packed = pl.pallas_call(
        both_steps,
        out_shape=struct(shots, 2, share, extent, across),
        in_specs=[VMEM] * 9,
        out_specs=VMEM,
        scratch_shapes=[scratch(*wide_shape), scratch(*wide_shape)],
        compiler_params=params,
        name="both_steps",
    )(up_first, own, part, later, source, source_later, coef, came_first, came_last)
    mine = lax.all_to_all(packed, "shot", 0, 0, tiled=True)
    fields_first, fields_last = swap_sides(mine, mine)
    return pl.pallas_call(
        functools.partial(image_products, 1.0 / shots),
        out_shape=(
            struct(1, levels, extent, across),
            struct(1, levels, extent, across),
            struct(OFFS, share, extent, across),
        ),
        in_specs=[VMEM] * 5,
        out_specs=[HBM] * 3,
        scratch_shapes=[
            scratch(shots, 2, share, 3 * extent, across),
            scratch(OFFS, share, extent, across),
            pltpu.SemaphoreType.DMA((2, shots)),
            pltpu.SemaphoreType.DMA((3,)),
        ],
        compiler_params=params,
        name="image_products",
    )(up_first, packed, mine, fields_last, fields_first)


def solution(mesh):
    field = P(("groups", "shot"), None, "tile", None)
    return jax.shard_map(
        per_device,
        mesh=mesh,
        in_specs=(
            field,
            field,
            field,
            field,
            P("groups"),
            P(None, ("groups", "tile"), None),
            P(("groups", "shot")),
            P(("groups", "shot"), None),
            P(("groups", "shot"), "tile"),
            P(("groups", "shot"), None, "tile"),
        ),
        out_specs=(field, field, P(None, "shot", ("groups", "tile"), None)),
        check_vma=False,
    )
```

```python
import functools

import jax
import jax.numpy as jnp
from jax import lax
from jax.experimental import pallas as pl
from jax.experimental.pallas import tpu as pltpu
from jax.sharding import PartitionSpec as P

OFFS = 33
REACH = OFFS // 2
HALO = 4
LEAD = 8

COEFS = (-205.0 / 72.0, 8.0 / 5.0, -1.0 / 5.0, 8.0 / 315.0, -1.0 / 560.0)

VMEM = pl.BlockSpec(memory_space=pltpu.VMEM)
HBM = pl.BlockSpec(memory_space=pltpu.HBM)
SMEM = pl.BlockSpec(memory_space=pltpu.SMEM)
LIMIT = 16 * 1024 * 1024


def lane_weights(shape):
    lane = lax.broadcasted_iota(jnp.int32, shape, 1)
    across = shape[1]
    after = [jnp.where(lane < across - k, COEFS[k], 0.0) for k in range(1, HALO + 1)]
    before = [jnp.where(lane >= k, COEFS[k], 0.0) for k in range(1, HALO + 1)]
    return after, before


def laplace_level(wide, field, level, levels, extent, weights):
    after, before = weights
    centre = wide[field, level, LEAD : LEAD + extent, :]
    across = centre.shape[1]
    total = 3.0 * COEFS[0] * centre
    for k in range(1, HALO + 1):
        beside = (
            wide[field, level, LEAD + k : LEAD + k + extent, :]
            + wide[field, level, LEAD - k : LEAD - k + extent, :]
        )
        if level + k < levels:
            beside = beside + wide[field, level + k, LEAD : LEAD + extent, :]
        if level - k >= 0:
            beside = beside + wide[field, level - k, LEAD : LEAD + extent, :]
        total = total + COEFS[k] * beside
        total = total + after[k - 1] * pltpu.roll(centre, across - k, 1)
        total = total + before[k - 1] * pltpu.roll(centre, k, 1)
    return total


def goes_up_first():
    return lax.rem(lax.axis_index("tile"), 2) == 0


def source_and_order(
    width, cell_ref, amps_ref, later_ref, source_ref, source_later_ref, up_first_ref, inside_ref
):
    levels, extent, across = source_later_ref.shape
    cell = cell_ref[0]
    deep = lax.div(cell, width * across)
    row = lax.rem(lax.div(cell, across), width) - lax.axis_index("tile") * extent + LEAD
    shape = (extent + 2 * LEAD, across)
    rows = lax.broadcasted_iota(jnp.int32, shape, 0)
    lanes = lax.broadcasted_iota(jnp.int32, shape, 1)
    hit = jnp.where((rows == row) & (lanes == lax.rem(cell, across)), 1.0, 0.0)
    for level in range(levels):
        here = hit * jnp.where(deep == level, 1.0, 0.0)
        source_ref[level] = here * amps_ref[0:1, 0:1]
        source_later_ref[level] = (
            later_ref[0, level] + here[LEAD : LEAD + extent, :] * amps_ref[0:1, 1:2]
        )
    up_first_ref[...] = jnp.full(
        up_first_ref.shape, jnp.where(goes_up_first(), 1, 0), dtype=jnp.int32
    )
    tile = lax.axis_index("tile")
    inside = (tile > 0) & (tile < lax.axis_size("tile") - 1)
    inside_ref[...] = jnp.full(inside_ref.shape, jnp.where(inside, 1, 0), dtype=jnp.int32)


def own_part(
    table_hbm,
    spots_hbm,
    traces_hbm,
    amps_hbm,
    ids_hbm,
    src_now,
    rec_now,
    src_prev,
    rec_prev,
    amps_ref,
    wide,
    part_ref,
    later_ref,
    coef_ref,
    sent_first_ref,
    sent_last_ref,
    table,
    spots_ref,
    traces_ref,
    ids_ref,
    prev_ref,
    sems,
):
    levels, extent, across = ids_ref.shape
    shape = (extent, across)
    regions = table_hbm.shape[1]
    end = LEAD + extent
    moves = (
        (table_hbm, table),
        (ids_hbm, ids_ref),
        (spots_hbm, spots_ref),
        (traces_hbm, traces_ref),
        (src_now.at[0], wide.at[0, :, pl.ds(LEAD, extent), :]),
        (src_prev.at[0], prev_ref.at[0]),
        (rec_now.at[0], wide.at[1, :, pl.ds(LEAD, extent), :]),
        (rec_prev.at[0], prev_ref.at[1]),
        (amps_hbm, amps_ref),
    )
    copies = [
        pltpu.make_async_copy(here, there, sems.at[i]) for i, (here, there) in enumerate(moves)
    ]
    for copy in copies:
        copy.start()
    zeros = jnp.zeros((LEAD, across), jnp.float32)
    for field in range(2):
        for level in range(levels):
            wide[field, level, 0:LEAD, :] = zeros
            wide[field, level, end : end + LEAD, :] = zeros
    weights = lane_weights(shape)

    for copy in copies[2:4]:
        copy.wait()
    spots = spots_ref[...]
    column = lax.broadcasted_iota(jnp.int32, (extent, spots.shape[1]), 0) * across
    in_column = (spots >= column) & (spots < column + across)
    lane = lax.broadcasted_iota(jnp.int32, (across, spots.shape[1]), 0)
    in_row = jnp.where(lax.rem(spots, across) == lane, 1.0, 0.0)
    traces = jnp.concatenate(
        [jnp.where(in_column, traces_ref[0, t : t + 1, :], 0.0) for t in range(2)], axis=0
    )
    planes = lax.dot_general(
        traces,
        in_row,
        (((1,), (1,)), ((), ())),
        precision=lax.Precision.HIGHEST,
        preferred_element_type=jnp.float32,
    )

    up_first = goes_up_first()

    def send(place, rows, value):
        low = value[0:HALO, :]
        high = value[extent - HALO : extent, :]
        sent_first_ref[place, rows, :] = jnp.where(up_first, high, low)
        sent_last_ref[place, rows, :] = jnp.where(up_first, low, high)

    copies[0].wait()
    copies[1].wait()
    speeds = jnp.concatenate(
        [table[...], jnp.zeros((1, across - regions), jnp.float32)], axis=1
    )
    speeds = jnp.broadcast_to(speeds, (8, across))
    for level in range(levels):
        for row in range(0, extent, 8):
            ids = ids_ref[level, row : row + 8, :]
            coef_ref[level, row : row + 8, :] = jnp.take_along_axis(
                speeds, ids, axis=1, mode="promise_in_bounds"
            )
        send(2 * levels + level // 2, pl.ds(level % 2 * HALO, HALO), coef_ref[level])

    for field in range(2):
        copies[4 + 2 * field].wait()
        copies[5 + 2 * field].wait()
        for level in range(levels):
            total = laplace_level(wide, field, level, levels, extent, weights)
            now = wide[field, level, LEAD:end, :]
            value = 2.0 * now - prev_ref[field, level] + coef_ref[level] * total
            later = -now
            if field == 1 and level == 0:
                value = value + planes[:extent, :]
                later = later + planes[extent:, :]
            part_ref[field, level] = value
            later_ref[field, level] = later
            place = field * levels + level
            send(place, pl.ds(0, HALO), now)
            send(place, pl.ds(HALO, HALO), value)
    copies[8].wait()


def both_steps(
    up_first_ref,
    inside_ref,
    own,
    part_ref,
    later_ref,
    source_ref,
    source_later_ref,
    coef_ref,
    came_first_ref,
    came_last_ref,
    packed_ref,
    other,
    middle,
):
    levels, extent, across = coef_ref.shape
    shape = (extent, across)
    share = packed_ref.shape[2]
    end = LEAD + extent
    up_first = up_first_ref[0:HALO, :] != 0
    inside = inside_ref[0:HALO, :] != 0

    def received(place, rows):
        first = came_first_ref[place, rows, :]
        last = jnp.where(inside, came_last_ref[place, rows, :], 0.0)
        return jnp.where(up_first, last, first), jnp.where(up_first, first, last)

    for field in range(2):
        for level in range(levels):
            low, high = received(field * levels + level, pl.ds(0, HALO))
            other[field, level, LEAD:end, :] = jnp.zeros(shape, jnp.float32)
            other[field, level, LEAD - HALO : LEAD, :] = low
            other[field, level, end : end + HALO, :] = high
    for field in range(2):
        for level in range(levels):
            below = jnp.zeros((HALO, across), jnp.float32)
            above = jnp.zeros((HALO, across), jnp.float32)
            left = jnp.zeros((8, across), jnp.float32)
            right = jnp.zeros((8, across), jnp.float32)
            for k in range(1, HALO + 1):
                begin = LEAD - HALO + k
                below = below + COEFS[k] * own[field, level, begin : begin + HALO, :]
                above = above + COEFS[k] * own[field, level, end - k : end - k + HALO, :]
                left = left + COEFS[k] * other[field, level, LEAD - k : LEAD - k + 8, :]
                right = right + COEFS[k] * other[field, level, end - 8 + k : end + k, :]
            low, high = received(field * levels + level, pl.ds(HALO, HALO))
            low_coef, high_coef = received(
                2 * levels + level // 2, pl.ds(level % 2 * HALO, HALO)
            )
            low = low + low_coef * below
            high = high + high_coef * above
            left = part_ref[field, level, 0:8, :] + coef_ref[level, 0:8, :] * left
            right = (
                part_ref[field, level, extent - 8 : extent, :]
                + coef_ref[level, extent - 8 : extent, :] * right
            )
            if field == 0:
                low = low + source_ref[level, LEAD - HALO : LEAD, :]
                left = left + source_ref[level, LEAD : LEAD + 8, :]
                right = right + source_ref[level, end - 8 : end, :]
                high = high + source_ref[level, end : end + HALO, :]
            middle[field, level, LEAD - HALO : LEAD, :] = low
            middle[field, level, LEAD : LEAD + 8, :] = left
            middle[field, level, end - 8 : end, :] = right
            middle[field, level, end : end + HALO, :] = high
    weights = lane_weights(shape)
    for field in range(2):
        for level in range(levels):
            total = laplace_level(middle, field, level, levels, extent, weights)
            later = source_later_ref[level] if field == 0 else later_ref[field, level]
            value = 2.0 * middle[field, level, LEAD:end, :] + later
            packed_ref[level // share, field, level % share] = value + coef_ref[level] * total


def image_products(
    weight,
    up_first_ref,
    inside_ref,
    final_ref,
    mine_ref,
    came_last_ref,
    came_first_ref,
    src_hbm,
    rec_hbm,
    image_hbm,
    wide,
    image_ref,
    field_sems,
    image_sems,
):
    shots, _, share, extent, across = mine_ref.shape
    copies = []
    for field, out in enumerate((src_hbm, rec_hbm)):
        for shot in range(shots):
            copies.append(
                pltpu.make_async_copy(
                    final_ref.at[shot, field],
                    out.at[0, pl.ds(shot * share, share)],
                    field_sems.at[field, shot],
                )
            )
    for copy in copies:
        copy.start()
    up_first = jnp.concatenate([up_first_ref[...]] * (extent // 8), axis=0) != 0
    inside = jnp.concatenate([inside_ref[...]] * (extent // 8), axis=0) != 0
    for shot in range(shots):
        for field in range(2):
            for level in range(share):
                scale = weight if field == 0 else 1.0
                first = scale * came_first_ref[shot, field, level]
                last = jnp.where(inside, scale * came_last_ref[shot, field, level], 0.0)
                wide[shot, field, level, 0:extent, :] = jnp.where(up_first, last, first)
                wide[shot, field, level, extent : 2 * extent, :] = (
                    scale * mine_ref[shot, field, level]
                )
                wide[shot, field, level, 2 * extent : 3 * extent, :] = jnp.where(
                    up_first, first, last
                )
    parts = image_sems.shape[0]
    for piece in range(parts):
        offsets = range(piece * OFFS // parts, (piece + 1) * OFFS // parts)
        for offset in offsets:
            for level in range(share):
                total = jnp.zeros((extent, across), jnp.float32)
                for shot in range(shots):
                    lower = extent + REACH - offset
                    upper = extent - REACH + offset
                    total = total + (
                        wide[shot, 0, level, lower : lower + extent, :]
                        * wide[shot, 1, level, upper : upper + extent, :]
                    )
                image_ref[offset, level] = total
        rows = pl.ds(offsets[0], len(offsets))
        copy = pltpu.make_async_copy(image_ref.at[rows], image_hbm.at[rows], image_sems.at[piece])
        copy.start()
        copies.append(copy)
    for copy in copies:
        copy.wait()


def swap_sides(first, last):
    tiles = lax.axis_size("tile")

    def swap(value, begin):
        partner = list(range(tiles))
        for tile in range(begin, tiles - 1, 2):
            partner[tile], partner[tile + 1] = tile + 1, tile
        return lax.ppermute(value, "tile", list(enumerate(partner)))

    came_last = swap(last, 1)
    return swap(first, 0), came_last


def per_device(
    src_prev,
    src_now,
    rec_prev,
    rec_now,
    speed_table,
    region_ids,
    source_cell,
    wavelet,
    receiver_cell,
    receiver_data,
):
    _, levels, extent, across = src_now.shape
    tiles = lax.axis_size("tile")
    width = extent * tiles
    shots = lax.axis_size("shot")
    share = levels // shots
    params = pltpu.CompilerParams(vmem_limit_bytes=LIMIT)

    def struct(*shape):
        return jax.ShapeDtypeStruct(shape, jnp.float32)

    def scratch(*shape, dtype=jnp.float32):
        return pltpu.VMEM(shape, dtype)

    wide_shape = (2, levels, extent + 2 * LEAD, across)
    message = struct(2 * levels + levels // 2, 2 * HALO, across)
    amps, own, part, later, coef, first, last = pl.pallas_call(
        own_part,
        out_shape=(
            struct(*wavelet.shape),
            struct(*wide_shape),
            struct(2, levels, extent, across),
            struct(2, levels, extent, across),
            struct(levels, extent, across),
            message,
            message,
        ),
        in_specs=[HBM] * 9,
        out_specs=[VMEM] * 7,
        scratch_shapes=[
            scratch(1, speed_table.shape[0]),
            scratch(*receiver_cell.shape, dtype=jnp.int32),
            scratch(*receiver_data.shape),
            scratch(levels, extent, across, dtype=jnp.int32),
            scratch(2, levels, extent, across),
            pltpu.SemaphoreType.DMA((9,)),
        ],
        compiler_params=params,
        name="own_part",
    )(
        *(
            pltpu.with_memory_space_constraint(array, pltpu.HBM)
            for array in (
                speed_table.reshape(1, -1),
                receiver_cell,
                receiver_data,
                wavelet,
                region_ids,
                src_now,
                rec_now,
                src_prev,
                rec_prev,
            )
        )
    )
    came_first, came_last = swap_sides(first, last)
    source, source_later, up_first, inside = pl.pallas_call(
        functools.partial(source_and_order, width),
        out_shape=(
            struct(levels, extent + 2 * LEAD, across),
            struct(levels, extent, across),
            jax.ShapeDtypeStruct((8, across), jnp.int32),
            jax.ShapeDtypeStruct((8, across), jnp.int32),
        ),
        in_specs=[SMEM] + [VMEM] * 2,
        out_specs=[VMEM] * 4,
        compiler_params=params,
        name="source_and_order",
    )(source_cell, amps, later)
    packed = pl.pallas_call(
        both_steps,
        out_shape=struct(shots, 2, share, extent, across),
        in_specs=[VMEM] * 10,
        out_specs=VMEM,
        scratch_shapes=[scratch(*wide_shape), scratch(*wide_shape)],
        compiler_params=params,
        name="both_steps",
    )(up_first, inside, own, part, later, source, source_later, coef, came_first, came_last)
    mine = lax.all_to_all(packed, "shot", 0, 0, tiled=True)
    fields_first, fields_last = swap_sides(mine, mine)
    return pl.pallas_call(
        functools.partial(image_products, 1.0 / shots),
        out_shape=(
            struct(1, levels, extent, across),
            struct(1, levels, extent, across),
            struct(OFFS, share, extent, across),
        ),
        in_specs=[VMEM] * 6,
        out_specs=[HBM] * 3,
        scratch_shapes=[
            scratch(shots, 2, share, 3 * extent, across),
            scratch(OFFS, share, extent, across),
            pltpu.SemaphoreType.DMA((2, shots)),
            pltpu.SemaphoreType.DMA((3,)),
        ],
        compiler_params=params,
        name="image_products",
    )(up_first, inside, packed, mine, fields_last, fields_first)


def solution(mesh):
    field = P(("groups", "shot"), None, "tile", None)
    return jax.shard_map(
        per_device,
        mesh=mesh,
        in_specs=(
            field,
            field,
            field,
            field,
            P("groups"),
            P(None, ("groups", "tile"), None),
            P(("groups", "shot")),
            P(("groups", "shot"), None),
            P(("groups", "shot"), "tile"),
            P(("groups", "shot"), None, "tile"),
        ),
        out_specs=(field, field, P(None, "shot", ("groups", "tile"), None)),
        check_vma=False,
    )
```

```python
import functools

import jax
import jax.numpy as jnp
from jax import lax
from jax.experimental import pallas as pl
from jax.experimental.pallas import tpu as pltpu
from jax.sharding import PartitionSpec as P

OFFS = 33
REACH = OFFS // 2
HALO = 4
LEAD = 8

COEFS = (-205.0 / 72.0, 8.0 / 5.0, -1.0 / 5.0, 8.0 / 315.0, -1.0 / 560.0)

VMEM = pl.BlockSpec(memory_space=pltpu.VMEM)
HBM = pl.BlockSpec(memory_space=pltpu.HBM)
SMEM = pl.BlockSpec(memory_space=pltpu.SMEM)
LIMIT = 16 * 1024 * 1024


def lane_weights(shape):
    lane = lax.broadcasted_iota(jnp.int32, shape, 1)
    across = shape[1]
    after = [jnp.where(lane < across - k, COEFS[k], 0.0) for k in range(1, HALO + 1)]
    before = [jnp.where(lane >= k, COEFS[k], 0.0) for k in range(1, HALO + 1)]
    return after, before


def laplace_level(wide, field, level, levels, extent, weights):
    after, before = weights
    centre = wide[field, level, LEAD : LEAD + extent, :]
    across = centre.shape[1]
    total = 3.0 * COEFS[0] * centre
    for k in range(1, HALO + 1):
        beside = (
            wide[field, level, LEAD + k : LEAD + k + extent, :]
            + wide[field, level, LEAD - k : LEAD - k + extent, :]
        )
        if level + k < levels:
            beside = beside + wide[field, level + k, LEAD : LEAD + extent, :]
        if level - k >= 0:
            beside = beside + wide[field, level - k, LEAD : LEAD + extent, :]
        total = total + COEFS[k] * beside
        total = total + after[k - 1] * pltpu.roll(centre, across - k, 1)
        total = total + before[k - 1] * pltpu.roll(centre, k, 1)
    return total


def goes_up_first():
    return lax.rem(lax.axis_index("tile"), 2) == 0


def source_and_order(
    width, cell_ref, amps_ref, later_ref, source_ref, source_later_ref, up_first_ref, inside_ref, bits_ref
):
    levels, extent, across = source_later_ref.shape
    cell = cell_ref[0]
    deep = lax.div(cell, width * across)
    row = lax.rem(lax.div(cell, across), width) - lax.axis_index("tile") * extent + LEAD
    shape = (extent + 2 * LEAD, across)
    rows = lax.broadcasted_iota(jnp.int32, shape, 0)
    lanes = lax.broadcasted_iota(jnp.int32, shape, 1)
    hit = jnp.where((rows == row) & (lanes == lax.rem(cell, across)), 1.0, 0.0)
    for level in range(levels):
        here = hit * jnp.where(deep == level, 1.0, 0.0)
        source_ref[level] = here * amps_ref[0:1, 0:1]
        source_later_ref[level] = (
            later_ref[0, level] + here[LEAD : LEAD + extent, :] * amps_ref[0:1, 1:2]
        )
    up_first_ref[...] = jnp.full(
        up_first_ref.shape, jnp.where(goes_up_first(), 1, 0), dtype=jnp.int32
    )
    tile = lax.axis_index("tile")
    inside = (tile > 0) & (tile < lax.axis_size("tile") - 1)
    inside_ref[...] = jnp.full(inside_ref.shape, jnp.where(inside, 1, 0), dtype=jnp.int32)
    shot = jnp.full(bits_ref.shape[1:], lax.axis_index("shot"), dtype=jnp.int32)
    for bit in range(bits_ref.shape[0]):
        bits_ref[bit] = shot & (1 << bit)


def own_part(
    table_hbm,
    spots_hbm,
    traces_hbm,
    amps_hbm,
    ids_hbm,
    src_now,
    rec_now,
    src_prev,
    rec_prev,
    amps_ref,
    wide,
    part_ref,
    later_ref,
    coef_ref,
    sent_first_ref,
    sent_last_ref,
    table,
    spots_ref,
    traces_ref,
    ids_ref,
    prev_ref,
    sems,
):
    levels, extent, across = ids_ref.shape
    shape = (extent, across)
    regions = table_hbm.shape[1]
    end = LEAD + extent
    moves = (
        (table_hbm, table),
        (ids_hbm, ids_ref),
        (spots_hbm, spots_ref),
        (traces_hbm, traces_ref),
        (src_now.at[0], wide.at[0, :, pl.ds(LEAD, extent), :]),
        (src_prev.at[0], prev_ref.at[0]),
        (rec_now.at[0], wide.at[1, :, pl.ds(LEAD, extent), :]),
        (rec_prev.at[0], prev_ref.at[1]),
        (amps_hbm, amps_ref),
    )
    copies = [
        pltpu.make_async_copy(here, there, sems.at[i]) for i, (here, there) in enumerate(moves)
    ]
    for copy in copies:
        copy.start()
    zeros = jnp.zeros((LEAD, across), jnp.float32)
    for field in range(2):
        for level in range(levels):
            wide[field, level, 0:LEAD, :] = zeros
            wide[field, level, end : end + LEAD, :] = zeros
    weights = lane_weights(shape)

    for copy in copies[2:4]:
        copy.wait()
    spots = spots_ref[...]
    column = lax.broadcasted_iota(jnp.int32, (extent, spots.shape[1]), 0) * across
    in_column = (spots >= column) & (spots < column + across)
    lane = lax.broadcasted_iota(jnp.int32, (across, spots.shape[1]), 0)
    in_row = jnp.where(lax.rem(spots, across) == lane, 1.0, 0.0)
    traces = jnp.concatenate(
        [jnp.where(in_column, traces_ref[0, t : t + 1, :], 0.0) for t in range(2)], axis=0
    )
    planes = lax.dot_general(
        traces,
        in_row,
        (((1,), (1,)), ((), ())),
        precision=lax.Precision.HIGHEST,
        preferred_element_type=jnp.float32,
    )

    up_first = goes_up_first()

    def send(place, rows, value):
        low = value[0:HALO, :]
        high = value[extent - HALO : extent, :]
        sent_first_ref[place, rows, :] = jnp.where(up_first, high, low)
        sent_last_ref[place, rows, :] = jnp.where(up_first, low, high)

    copies[0].wait()
    copies[1].wait()
    speeds = jnp.concatenate(
        [table[...], jnp.zeros((1, across - regions), jnp.float32)], axis=1
    )
    speeds = jnp.broadcast_to(speeds, (8, across))
    for level in range(levels):
        for row in range(0, extent, 8):
            ids = ids_ref[level, row : row + 8, :]
            coef_ref[level, row : row + 8, :] = jnp.take_along_axis(
                speeds, ids, axis=1, mode="promise_in_bounds"
            )
        send(2 * levels + level // 2, pl.ds(level % 2 * HALO, HALO), coef_ref[level])

    for field in range(2):
        copies[4 + 2 * field].wait()
        copies[5 + 2 * field].wait()
        for level in range(levels):
            total = laplace_level(wide, field, level, levels, extent, weights)
            now = wide[field, level, LEAD:end, :]
            value = 2.0 * now - prev_ref[field, level] + coef_ref[level] * total
            later = -now
            if field == 1 and level == 0:
                value = value + planes[:extent, :]
                later = later + planes[extent:, :]
            part_ref[field, level] = value
            later_ref[field, level] = later
            place = field * levels + level
            send(place, pl.ds(0, HALO), now)
            send(place, pl.ds(HALO, HALO), value)
    copies[8].wait()


def both_steps(
    up_first_ref,
    inside_ref,
    bits_ref,
    own,
    part_ref,
    later_ref,
    source_ref,
    source_later_ref,
    coef_ref,
    came_first_ref,
    came_last_ref,
    final_ref,
    mine_ref,
    *rest,
):
    *theirs, other, middle = rest
    blocks = [mine_ref, *theirs]
    levels, extent, across = coef_ref.shape
    shape = (extent, across)
    share = mine_ref.shape[1]
    end = LEAD + extent
    up_first = up_first_ref[0:HALO, :] != 0
    inside = inside_ref[0:HALO, :] != 0

    def received(place, rows):
        first = came_first_ref[place, rows, :]
        last = jnp.where(inside, came_last_ref[place, rows, :], 0.0)
        return jnp.where(up_first, last, first), jnp.where(up_first, first, last)

    for field in range(2):
        for level in range(levels):
            low, high = received(field * levels + level, pl.ds(0, HALO))
            other[field, level, LEAD:end, :] = jnp.zeros(shape, jnp.float32)
            other[field, level, LEAD - HALO : LEAD, :] = low
            other[field, level, end : end + HALO, :] = high
    for field in range(2):
        for level in range(levels):
            below = jnp.zeros((HALO, across), jnp.float32)
            above = jnp.zeros((HALO, across), jnp.float32)
            left = jnp.zeros((8, across), jnp.float32)
            right = jnp.zeros((8, across), jnp.float32)
            for k in range(1, HALO + 1):
                begin = LEAD - HALO + k
                below = below + COEFS[k] * own[field, level, begin : begin + HALO, :]
                above = above + COEFS[k] * own[field, level, end - k : end - k + HALO, :]
                left = left + COEFS[k] * other[field, level, LEAD - k : LEAD - k + 8, :]
                right = right + COEFS[k] * other[field, level, end - 8 + k : end + k, :]
            low, high = received(field * levels + level, pl.ds(HALO, HALO))
            low_coef, high_coef = received(
                2 * levels + level // 2, pl.ds(level % 2 * HALO, HALO)
            )
            low = low + low_coef * below
            high = high + high_coef * above
            left = part_ref[field, level, 0:8, :] + coef_ref[level, 0:8, :] * left
            right = (
                part_ref[field, level, extent - 8 : extent, :]
                + coef_ref[level, extent - 8 : extent, :] * right
            )
            if field == 0:
                low = low + source_ref[level, LEAD - HALO : LEAD, :]
                left = left + source_ref[level, LEAD : LEAD + 8, :]
                right = right + source_ref[level, end - 8 : end, :]
                high = high + source_ref[level, end : end + HALO, :]
            middle[field, level, LEAD - HALO : LEAD, :] = low
            middle[field, level, LEAD : LEAD + 8, :] = left
            middle[field, level, end - 8 : end, :] = right
            middle[field, level, end : end + HALO, :] = high
    weights = lane_weights(shape)
    for field in range(2):
        for level in range(levels):
            total = laplace_level(middle, field, level, levels, extent, weights)
            later = source_later_ref[level] if field == 0 else later_ref[field, level]
            value = 2.0 * middle[field, level, LEAD:end, :] + later
            final_ref[field, level] = value + coef_ref[level] * total
    masks = [
        jnp.concatenate([bits_ref[bit]] * (extent // 8), axis=0) != 0
        for bit in range(bits_ref.shape[0])
    ]
    for field in range(2):
        for level in range(share):
            parts = [final_ref[field, place * share + level] for place in range(len(blocks))]
            for bit, mask in enumerate(masks):
                parts = [
                    jnp.where(mask, parts[place ^ (1 << bit)], parts[place])
                    for place in range(len(blocks))
                ]
            for block, part in zip(blocks, parts):
                block[field, level] = part


def image_products(
    weight,
    up_first_ref,
    inside_ref,
    final_ref,
    mine_ref,
    came_last_ref,
    came_first_ref,
    src_hbm,
    rec_hbm,
    image_hbm,
    wide,
    image_ref,
    field_sems,
    image_sems,
):
    shots, _, share, extent, across = mine_ref.shape
    copies = []
    for field, out in enumerate((src_hbm, rec_hbm)):
        copies.append(
            pltpu.make_async_copy(final_ref.at[field], out.at[0], field_sems.at[field])
        )
    for copy in copies:
        copy.start()
    up_first = jnp.concatenate([up_first_ref[...]] * (extent // 8), axis=0) != 0
    inside = jnp.concatenate([inside_ref[...]] * (extent // 8), axis=0) != 0
    for shot in range(shots):
        for field in range(2):
            for level in range(share):
                scale = weight if field == 0 else 1.0
                first = scale * came_first_ref[shot, field, level]
                last = jnp.where(inside, scale * came_last_ref[shot, field, level], 0.0)
                wide[shot, field, level, 0:extent, :] = jnp.where(up_first, last, first)
                wide[shot, field, level, extent : 2 * extent, :] = (
                    scale * mine_ref[shot, field, level]
                )
                wide[shot, field, level, 2 * extent : 3 * extent, :] = jnp.where(
                    up_first, first, last
                )
    parts = image_sems.shape[0]
    for piece in range(parts):
        offsets = range(piece * OFFS // parts, (piece + 1) * OFFS // parts)
        for offset in offsets:
            for level in range(share):
                total = jnp.zeros((extent, across), jnp.float32)
                for shot in range(shots):
                    lower = extent + REACH - offset
                    upper = extent - REACH + offset
                    total = total + (
                        wide[shot, 0, level, lower : lower + extent, :]
                        * wide[shot, 1, level, upper : upper + extent, :]
                    )
                image_ref[offset, level] = total
        rows = pl.ds(offsets[0], len(offsets))
        copy = pltpu.make_async_copy(image_ref.at[rows], image_hbm.at[rows], image_sems.at[piece])
        copy.start()
        copies.append(copy)
    for copy in copies:
        copy.wait()


def swap_sides(first, last):
    tiles = lax.axis_size("tile")

    def swap(value, begin):
        partner = list(range(tiles))
        for tile in range(begin, tiles - 1 + begin, 2):
            after = (tile + 1) % tiles
            partner[tile], partner[after] = after, tile
        return lax.ppermute(value, "tile", list(enumerate(partner)))

    came_last = swap(last, 1)
    return swap(first, 0), came_last


def per_device(
    src_prev,
    src_now,
    rec_prev,
    rec_now,
    speed_table,
    region_ids,
    source_cell,
    wavelet,
    receiver_cell,
    receiver_data,
):
    _, levels, extent, across = src_now.shape
    tiles = lax.axis_size("tile")
    width = extent * tiles
    shots = lax.axis_size("shot")
    share = levels // shots
    params = pltpu.CompilerParams(vmem_limit_bytes=LIMIT)

    def struct(*shape):
        return jax.ShapeDtypeStruct(shape, jnp.float32)

    def scratch(*shape, dtype=jnp.float32):
        return pltpu.VMEM(shape, dtype)

    wide_shape = (2, levels, extent + 2 * LEAD, across)
    message = struct(2 * levels + levels // 2, 2 * HALO, across)
    amps, own, part, later, coef, first, last = pl.pallas_call(
        own_part,
        out_shape=(
            struct(*wavelet.shape),
            struct(*wide_shape),
            struct(2, levels, extent, across),
            struct(2, levels, extent, across),
            struct(levels, extent, across),
            message,
            message,
        ),
        in_specs=[HBM] * 9,
        out_specs=[VMEM] * 7,
        scratch_shapes=[
            scratch(1, speed_table.shape[0]),
            scratch(*receiver_cell.shape, dtype=jnp.int32),
            scratch(*receiver_data.shape),
            scratch(levels, extent, across, dtype=jnp.int32),
            scratch(2, levels, extent, across),
            pltpu.SemaphoreType.DMA((9,)),
        ],
        compiler_params=params,
        name="own_part",
    )(
        *(
            pltpu.with_memory_space_constraint(array, pltpu.HBM)
            for array in (
                speed_table.reshape(1, -1),
                receiver_cell,
                receiver_data,
                wavelet,
                region_ids,
                src_now,
                rec_now,
                src_prev,
                rec_prev,
            )
        )
    )
    came_first, came_last = swap_sides(first, last)
    source, source_later, up_first, inside, bits = pl.pallas_call(
        functools.partial(source_and_order, width),
        out_shape=(
            struct(levels, extent + 2 * LEAD, across),
            struct(levels, extent, across),
            jax.ShapeDtypeStruct((8, across), jnp.int32),
            jax.ShapeDtypeStruct((8, across), jnp.int32),
            jax.ShapeDtypeStruct((shots.bit_length() - 1, 8, across), jnp.int32),
        ),
        in_specs=[SMEM] + [VMEM] * 2,
        out_specs=[VMEM] * 5,
        compiler_params=params,
        name="source_and_order",
    )(source_cell, amps, later)
    block = struct(2, share, extent, across)
    final, own_block, *blocks = pl.pallas_call(
        both_steps,
        out_shape=(struct(2, levels, extent, across), *([block] * shots)),
        in_specs=[VMEM] * 11,
        out_specs=[VMEM] * (1 + shots),
        scratch_shapes=[scratch(*wide_shape), scratch(*wide_shape)],
        compiler_params=params,
        name="both_steps",
    )(up_first, inside, bits, own, part, later, source, source_later, coef, came_first, came_last)
    came = [
        lax.ppermute(sent, "shot", [(shot, shot ^ (1 + i)) for shot in range(shots)])
        for i, sent in enumerate(blocks)
    ]
    mine = jnp.stack([own_block, *came])
    fields_first, fields_last = swap_sides(mine, mine)
    return pl.pallas_call(
        functools.partial(image_products, 1.0 / shots),
        out_shape=(
            struct(1, levels, extent, across),
            struct(1, levels, extent, across),
            struct(OFFS, share, extent, across),
        ),
        in_specs=[VMEM] * 6,
        out_specs=[HBM] * 3,
        scratch_shapes=[
            scratch(shots, 2, share, 3 * extent, across),
            scratch(OFFS, share, extent, across),
            pltpu.SemaphoreType.DMA((2,)),
            pltpu.SemaphoreType.DMA((3,)),
        ],
        compiler_params=params,
        name="image_products",
    )(up_first, inside, final, mine, fields_last, fields_first)


def solution(mesh):
    field = P(("groups", "shot"), None, "tile", None)
    return jax.shard_map(
        per_device,
        mesh=mesh,
        in_specs=(
            field,
            field,
            field,
            field,
            P("groups"),
            P(None, ("groups", "tile"), None),
            P(("groups", "shot")),
            P(("groups", "shot"), None),
            P(("groups", "shot"), "tile"),
            P(("groups", "shot"), None, "tile"),
        ),
        out_specs=(field, field, P(None, "shot", ("groups", "tile"), None)),
        check_vma=False,
    )
```

```python
import functools

import jax
import jax.numpy as jnp
from jax import lax
from jax.experimental import pallas as pl
from jax.experimental.pallas import tpu as pltpu
from jax.sharding import PartitionSpec as P

OFFS = 33
REACH = OFFS // 2
HALO = 4
LEAD = 8

COEFS = (-205.0 / 72.0, 8.0 / 5.0, -1.0 / 5.0, 8.0 / 315.0, -1.0 / 560.0)

VMEM = pl.BlockSpec(memory_space=pltpu.VMEM)
HBM = pl.BlockSpec(memory_space=pltpu.HBM)
SMEM = pl.BlockSpec(memory_space=pltpu.SMEM)
LIMIT = 16 * 1024 * 1024


def lane_weights(shape):
    lane = lax.broadcasted_iota(jnp.int32, shape, 1)
    across = shape[1]
    after = [jnp.where(lane < across - k, COEFS[k], 0.0) for k in range(1, HALO + 1)]
    before = [jnp.where(lane >= k, COEFS[k], 0.0) for k in range(1, HALO + 1)]
    return after, before


def laplace_level(wide, field, level, levels, extent, weights):
    after, before = weights
    centre = wide[field, level, LEAD : LEAD + extent, :]
    across = centre.shape[1]
    total = 3.0 * COEFS[0] * centre
    for k in range(1, HALO + 1):
        beside = (
            wide[field, level, LEAD + k : LEAD + k + extent, :]
            + wide[field, level, LEAD - k : LEAD - k + extent, :]
        )
        if level + k < levels:
            beside = beside + wide[field, level + k, LEAD : LEAD + extent, :]
        if level - k >= 0:
            beside = beside + wide[field, level - k, LEAD : LEAD + extent, :]
        total = total + COEFS[k] * beside
        total = total + after[k - 1] * pltpu.roll(centre, across - k, 1)
        total = total + before[k - 1] * pltpu.roll(centre, k, 1)
    return total


def goes_up_first():
    return lax.rem(lax.axis_index("tile"), 2) == 0


def source_and_order(
    width, cell_ref, amps_ref, later_ref, source_ref, source_later_ref, up_first_ref, inside_ref, bits_ref
):
    levels, extent, across = source_later_ref.shape
    cell = cell_ref[0]
    deep = lax.div(cell, width * across)
    row = lax.rem(lax.div(cell, across), width) - lax.axis_index("tile") * extent + LEAD
    shape = (extent + 2 * LEAD, across)
    rows = lax.broadcasted_iota(jnp.int32, shape, 0)
    lanes = lax.broadcasted_iota(jnp.int32, shape, 1)
    hit = jnp.where((rows == row) & (lanes == lax.rem(cell, across)), 1.0, 0.0)
    for level in range(levels):
        here = hit * jnp.where(deep == level, 1.0, 0.0)
        source_ref[level] = here * amps_ref[0:1, 0:1]
        source_later_ref[level] = (
            later_ref[0, level] + here[LEAD : LEAD + extent, :] * amps_ref[0:1, 1:2]
        )
    up_first_ref[...] = jnp.full(
        up_first_ref.shape, jnp.where(goes_up_first(), 1, 0), dtype=jnp.int32
    )
    tile = lax.axis_index("tile")
    inside = (tile > 0) & (tile < lax.axis_size("tile") - 1)
    inside_ref[...] = jnp.full(inside_ref.shape, jnp.where(inside, 1, 0), dtype=jnp.int32)
    shot = jnp.full(bits_ref.shape[1:], lax.axis_index("shot"), dtype=jnp.int32)
    for bit in range(bits_ref.shape[0]):
        bits_ref[bit] = shot & (1 << bit)


def own_part(
    table_hbm,
    spots_hbm,
    traces_hbm,
    amps_hbm,
    ids_hbm,
    src_now,
    rec_now,
    src_prev,
    rec_prev,
    amps_ref,
    wide,
    part_ref,
    later_ref,
    coef_ref,
    sent_first_ref,
    sent_last_ref,
    table,
    spots_ref,
    traces_ref,
    ids_ref,
    prev_ref,
    sems,
):
    levels, extent, across = ids_ref.shape
    shape = (extent, across)
    regions = table_hbm.shape[1]
    end = LEAD + extent
    moves = (
        (table_hbm, table),
        (ids_hbm, ids_ref),
        (spots_hbm, spots_ref),
        (traces_hbm, traces_ref),
        (src_now.at[0], wide.at[0, :, pl.ds(LEAD, extent), :]),
        (src_prev.at[0], prev_ref.at[0]),
        (rec_now.at[0], wide.at[1, :, pl.ds(LEAD, extent), :]),
        (rec_prev.at[0], prev_ref.at[1]),
        (amps_hbm, amps_ref),
    )
    copies = [
        pltpu.make_async_copy(here, there, sems.at[i]) for i, (here, there) in enumerate(moves)
    ]
    for copy in copies:
        copy.start()
    zeros = jnp.zeros((LEAD, across), jnp.float32)
    for field in range(2):
        for level in range(levels):
            wide[field, level, 0:LEAD, :] = zeros
            wide[field, level, end : end + LEAD, :] = zeros
    weights = lane_weights(shape)

    for copy in copies[2:4]:
        copy.wait()
    spots = spots_ref[...]
    column = lax.broadcasted_iota(jnp.int32, (extent, spots.shape[1]), 0) * across
    in_column = (spots >= column) & (spots < column + across)
    lane = lax.broadcasted_iota(jnp.int32, (across, spots.shape[1]), 0)
    in_row = jnp.where(lax.rem(spots, across) == lane, 1.0, 0.0)
    traces = jnp.concatenate(
        [jnp.where(in_column, traces_ref[0, t : t + 1, :], 0.0) for t in range(2)], axis=0
    )
    planes = lax.dot_general(
        traces,
        in_row,
        (((1,), (1,)), ((), ())),
        precision=lax.Precision.HIGHEST,
        preferred_element_type=jnp.float32,
    )

    up_first = goes_up_first()

    def send(place, rows, value):
        low = value[0:HALO, :]
        high = value[extent - HALO : extent, :]
        sent_first_ref[place, rows, :] = jnp.where(up_first, high, low)
        sent_last_ref[place, rows, :] = jnp.where(up_first, low, high)

    copies[0].wait()
    copies[1].wait()
    speeds = jnp.concatenate(
        [table[...], jnp.zeros((1, across - regions), jnp.float32)], axis=1
    )
    speeds = jnp.broadcast_to(speeds, (8, across))
    for level in range(levels):
        for row in range(0, extent, 8):
            ids = ids_ref[level, row : row + 8, :]
            coef_ref[level, row : row + 8, :] = jnp.take_along_axis(
                speeds, ids, axis=1, mode="promise_in_bounds"
            )
        send(2 * levels + level // 2, pl.ds(level % 2 * HALO, HALO), coef_ref[level])

    for field in range(2):
        copies[4 + 2 * field].wait()
        copies[5 + 2 * field].wait()
        for level in range(levels):
            total = laplace_level(wide, field, level, levels, extent, weights)
            now = wide[field, level, LEAD:end, :]
            value = 2.0 * now - prev_ref[field, level] + coef_ref[level] * total
            later = -now
            if field == 1 and level == 0:
                value = value + planes[:extent, :]
                later = later + planes[extent:, :]
            part_ref[field, level] = value
            later_ref[field, level] = later
            place = field * levels + level
            send(place, pl.ds(0, HALO), now)
            send(place, pl.ds(HALO, HALO), value)
    copies[8].wait()


def both_steps(
    up_first_ref,
    inside_ref,
    bits_ref,
    own,
    part_ref,
    later_ref,
    source_ref,
    source_later_ref,
    coef_ref,
    came_first_ref,
    came_last_ref,
    final_ref,
    mine_ref,
    *rest,
):
    *theirs, other, middle = rest
    blocks = [mine_ref, *theirs]
    levels, extent, across = coef_ref.shape
    shape = (extent, across)
    share = mine_ref.shape[1]
    end = LEAD + extent
    up_first = up_first_ref[0:HALO, :] != 0
    inside = inside_ref[0:HALO, :] != 0

    def received(place, rows):
        first = came_first_ref[place, rows, :]
        last = jnp.where(inside, came_last_ref[place, rows, :], 0.0)
        return jnp.where(up_first, last, first), jnp.where(up_first, first, last)

    for field in range(2):
        for level in range(levels):
            low, high = received(field * levels + level, pl.ds(0, HALO))
            other[field, level, LEAD:end, :] = jnp.zeros(shape, jnp.float32)
            other[field, level, LEAD - HALO : LEAD, :] = low
            other[field, level, end : end + HALO, :] = high
    for field in range(2):
        for level in range(levels):
            below = jnp.zeros((HALO, across), jnp.float32)
            above = jnp.zeros((HALO, across), jnp.float32)
            left = jnp.zeros((8, across), jnp.float32)
            right = jnp.zeros((8, across), jnp.float32)
            for k in range(1, HALO + 1):
                begin = LEAD - HALO + k
                below = below + COEFS[k] * own[field, level, begin : begin + HALO, :]
                above = above + COEFS[k] * own[field, level, end - k : end - k + HALO, :]
                left = left + COEFS[k] * other[field, level, LEAD - k : LEAD - k + 8, :]
                right = right + COEFS[k] * other[field, level, end - 8 + k : end + k, :]
            low, high = received(field * levels + level, pl.ds(HALO, HALO))
            low_coef, high_coef = received(
                2 * levels + level // 2, pl.ds(level % 2 * HALO, HALO)
            )
            low = low + low_coef * below
            high = high + high_coef * above
            left = part_ref[field, level, 0:8, :] + coef_ref[level, 0:8, :] * left
            right = (
                part_ref[field, level, extent - 8 : extent, :]
                + coef_ref[level, extent - 8 : extent, :] * right
            )
            if field == 0:
                low = low + source_ref[level, LEAD - HALO : LEAD, :]
                left = left + source_ref[level, LEAD : LEAD + 8, :]
                right = right + source_ref[level, end - 8 : end, :]
                high = high + source_ref[level, end : end + HALO, :]
            middle[field, level, LEAD - HALO : LEAD, :] = low
            middle[field, level, LEAD : LEAD + 8, :] = left
            middle[field, level, end - 8 : end, :] = right
            middle[field, level, end : end + HALO, :] = high
    weights = lane_weights(shape)
    for field in range(2):
        for level in range(levels):
            total = laplace_level(middle, field, level, levels, extent, weights)
            later = source_later_ref[level] if field == 0 else later_ref[field, level]
            value = 2.0 * middle[field, level, LEAD:end, :] + later
            final_ref[field, level] = value + coef_ref[level] * total
    masks = [
        jnp.concatenate([bits_ref[bit]] * (extent // 8), axis=0) != 0
        for bit in range(bits_ref.shape[0])
    ]
    for field in range(2):
        for level in range(share):
            parts = [final_ref[field, place * share + level] for place in range(len(blocks))]
            for bit, mask in enumerate(masks):
                parts = [
                    jnp.where(mask, parts[place ^ (1 << bit)], parts[place])
                    for place in range(len(blocks))
                ]
            for block, part in zip(blocks, parts):
                block[field, level] = part


def image_products(
    weight,
    up_first_ref,
    inside_ref,
    final_ref,
    mine_ref,
    came_last_ref,
    came_first_ref,
    src_hbm,
    rec_hbm,
    image_hbm,
    wide,
    image_ref,
    field_sems,
    image_sems,
):
    shots, _, share, extent, across = mine_ref.shape
    copies = []
    for field, out in enumerate((src_hbm, rec_hbm)):
        copies.append(
            pltpu.make_async_copy(final_ref.at[field], out.at[0], field_sems.at[field])
        )
    for copy in copies:
        copy.start()
    up_first = jnp.concatenate([up_first_ref[...]] * (extent // 8), axis=0) != 0
    inside = jnp.concatenate([inside_ref[...]] * (extent // 8), axis=0) != 0
    for shot in range(shots):
        for field in range(2):
            for level in range(share):
                scale = weight if field == 0 else 1.0
                first = scale * came_first_ref[shot, field, level]
                last = jnp.where(inside, scale * came_last_ref[shot, field, level], 0.0)
                wide[shot, field, level, 0:extent, :] = jnp.where(up_first, last, first)
                wide[shot, field, level, extent : 2 * extent, :] = (
                    scale * mine_ref[shot, field, level]
                )
                wide[shot, field, level, 2 * extent : 3 * extent, :] = jnp.where(
                    up_first, first, last
                )
    parts = image_sems.shape[0]
    for piece in range(parts):
        offsets = range(piece * OFFS // parts, (piece + 1) * OFFS // parts)
        for offset in offsets:
            for level in range(share):
                total = jnp.zeros((extent, across), jnp.float32)
                for shot in range(shots):
                    lower = extent + REACH - offset
                    upper = extent - REACH + offset
                    total = total + (
                        wide[shot, 0, level, lower : lower + extent, :]
                        * wide[shot, 1, level, upper : upper + extent, :]
                    )
                image_ref[offset, level] = total
        rows = pl.ds(offsets[0], len(offsets))
        copy = pltpu.make_async_copy(image_ref.at[rows], image_hbm.at[rows], image_sems.at[piece])
        copy.start()
        copies.append(copy)
    for copy in copies:
        copy.wait()


def swap_sides(first, last):
    tiles, shots = lax.axis_size("tile"), lax.axis_size("shot")

    def swap(value, begin):
        pairs = []
        for tile in range(tiles):
            partner = tile + 1 if (tile - begin) % 2 == 0 else tile - 1
            inside = 0 <= partner < tiles
            for shot in range(shots):
                target = partner * shots + shot if inside else tile * shots + (shot ^ 1)
                pairs.append((tile * shots + shot, target))
        return lax.ppermute(value, ("tile", "shot"), pairs)

    came_last = swap(last, 1)
    return swap(first, 0), came_last


def per_device(
    src_prev,
    src_now,
    rec_prev,
    rec_now,
    speed_table,
    region_ids,
    source_cell,
    wavelet,
    receiver_cell,
    receiver_data,
):
    _, levels, extent, across = src_now.shape
    tiles = lax.axis_size("tile")
    width = extent * tiles
    shots = lax.axis_size("shot")
    share = levels // shots
    params = pltpu.CompilerParams(vmem_limit_bytes=LIMIT)

    def struct(*shape):
        return jax.ShapeDtypeStruct(shape, jnp.float32)

    def scratch(*shape, dtype=jnp.float32):
        return pltpu.VMEM(shape, dtype)

    wide_shape = (2, levels, extent + 2 * LEAD, across)
    message = struct(2 * levels + levels // 2, 2 * HALO, across)
    amps, own, part, later, coef, first, last = pl.pallas_call(
        own_part,
        out_shape=(
            struct(*wavelet.shape),
            struct(*wide_shape),
            struct(2, levels, extent, across),
            struct(2, levels, extent, across),
            struct(levels, extent, across),
            message,
            message,
        ),
        in_specs=[HBM] * 9,
        out_specs=[VMEM] * 7,
        scratch_shapes=[
            scratch(1, speed_table.shape[0]),
            scratch(*receiver_cell.shape, dtype=jnp.int32),
            scratch(*receiver_data.shape),
            scratch(levels, extent, across, dtype=jnp.int32),
            scratch(2, levels, extent, across),
            pltpu.SemaphoreType.DMA((9,)),
        ],
        compiler_params=params,
        name="own_part",
    )(
        *(
            pltpu.with_memory_space_constraint(array, pltpu.HBM)
            for array in (
                speed_table.reshape(1, -1),
                receiver_cell,
                receiver_data,
                wavelet,
                region_ids,
                src_now,
                rec_now,
                src_prev,
                rec_prev,
            )
        )
    )
    came_first, came_last = swap_sides(first, last)
    source, source_later, up_first, inside, bits = pl.pallas_call(
        functools.partial(source_and_order, width),
        out_shape=(
            struct(levels, extent + 2 * LEAD, across),
            struct(levels, extent, across),
            jax.ShapeDtypeStruct((8, across), jnp.int32),
            jax.ShapeDtypeStruct((8, across), jnp.int32),
            jax.ShapeDtypeStruct((shots.bit_length() - 1, 8, across), jnp.int32),
        ),
        in_specs=[SMEM] + [VMEM] * 2,
        out_specs=[VMEM] * 5,
        compiler_params=params,
        name="source_and_order",
    )(source_cell, amps, later)
    block = struct(2, share, extent, across)
    final, own_block, *blocks = pl.pallas_call(
        both_steps,
        out_shape=(struct(2, levels, extent, across), *([block] * shots)),
        in_specs=[VMEM] * 11,
        out_specs=[VMEM] * (1 + shots),
        scratch_shapes=[scratch(*wide_shape), scratch(*wide_shape)],
        compiler_params=params,
        name="both_steps",
    )(up_first, inside, bits, own, part, later, source, source_later, coef, came_first, came_last)
    came = [
        lax.ppermute(sent, "shot", [(shot, shot ^ (1 + i)) for shot in range(shots)])
        for i, sent in enumerate(blocks)
    ]
    mine = jnp.stack([own_block, *came])
    fields_first, fields_last = swap_sides(mine, mine)
    return pl.pallas_call(
        functools.partial(image_products, 1.0 / shots),
        out_shape=(
            struct(1, levels, extent, across),
            struct(1, levels, extent, across),
            struct(OFFS, share, extent, across),
        ),
        in_specs=[VMEM] * 6,
        out_specs=[HBM] * 3,
        scratch_shapes=[
            scratch(shots, 2, share, 3 * extent, across),
            scratch(OFFS, share, extent, across),
            pltpu.SemaphoreType.DMA((2,)),
            pltpu.SemaphoreType.DMA((3,)),
        ],
        compiler_params=params,
        name="image_products",
    )(up_first, inside, final, mine, fields_last, fields_first)


def solution(mesh):
    field = P(("groups", "shot"), None, "tile", None)
    return jax.shard_map(
        per_device,
        mesh=mesh,
        in_specs=(
            field,
            field,
            field,
            field,
            P("groups"),
            P(None, ("groups", "tile"), None),
            P(("groups", "shot")),
            P(("groups", "shot"), None),
            P(("groups", "shot"), "tile"),
            P(("groups", "shot"), None, "tile"),
        ),
        out_specs=(field, field, P(None, "shot", ("groups", "tile"), None)),
        check_vma=False,
    )
```

```python
import functools

import jax
import jax.numpy as jnp
from jax import lax
from jax.experimental import pallas as pl
from jax.experimental.pallas import tpu as pltpu
from jax.sharding import PartitionSpec as P

OFFS = 33
REACH = OFFS // 2
HALO = 4
LEAD = 8

COEFS = (-205.0 / 72.0, 8.0 / 5.0, -1.0 / 5.0, 8.0 / 315.0, -1.0 / 560.0)

VMEM = pl.BlockSpec(memory_space=pltpu.VMEM)
HBM = pl.BlockSpec(memory_space=pltpu.HBM)
SMEM = pl.BlockSpec(memory_space=pltpu.SMEM)
LIMIT = 16 * 1024 * 1024


def lane_weights(shape):
    lane = lax.broadcasted_iota(jnp.int32, shape, 1)
    across = shape[1]
    after = [jnp.where(lane < across - k, COEFS[k], 0.0) for k in range(1, HALO + 1)]
    before = [jnp.where(lane >= k, COEFS[k], 0.0) for k in range(1, HALO + 1)]
    return after, before


def laplace_level(wide, field, level, levels, extent, weights):
    after, before = weights
    centre = wide[field, level, LEAD : LEAD + extent, :]
    across = centre.shape[1]
    total = 3.0 * COEFS[0] * centre
    for k in range(1, HALO + 1):
        beside = (
            wide[field, level, LEAD + k : LEAD + k + extent, :]
            + wide[field, level, LEAD - k : LEAD - k + extent, :]
        )
        if level + k < levels:
            beside = beside + wide[field, level + k, LEAD : LEAD + extent, :]
        if level - k >= 0:
            beside = beside + wide[field, level - k, LEAD : LEAD + extent, :]
        total = total + COEFS[k] * beside
        total = total + after[k - 1] * pltpu.roll(centre, across - k, 1)
        total = total + before[k - 1] * pltpu.roll(centre, k, 1)
    return total


def goes_up_first():
    return lax.rem(lax.axis_index("tile"), 2) == 0


def source_and_order(
    width, cell_ref, amps_ref, later_ref, source_ref, source_later_ref, up_first_ref, inside_ref, bits_ref
):
    levels, extent, across = source_later_ref.shape
    cell = cell_ref[0]
    deep = lax.div(cell, width * across)
    row = lax.rem(lax.div(cell, across), width) - lax.axis_index("tile") * extent + LEAD
    shape = (extent + 2 * LEAD, across)
    rows = lax.broadcasted_iota(jnp.int32, shape, 0)
    lanes = lax.broadcasted_iota(jnp.int32, shape, 1)
    hit = jnp.where((rows == row) & (lanes == lax.rem(cell, across)), 1.0, 0.0)
    for level in range(levels):
        here = hit * jnp.where(deep == level, 1.0, 0.0)
        source_ref[level] = here * amps_ref[0:1, 0:1]
        source_later_ref[level] = (
            later_ref[0, level] + here[LEAD : LEAD + extent, :] * amps_ref[0:1, 1:2]
        )
    up_first_ref[...] = jnp.full(
        up_first_ref.shape, jnp.where(goes_up_first(), 1, 0), dtype=jnp.int32
    )
    tile = lax.axis_index("tile")
    inside = (tile > 0) & (tile < lax.axis_size("tile") - 1)
    inside_ref[...] = jnp.full(inside_ref.shape, jnp.where(inside, 1, 0), dtype=jnp.int32)
    shot = jnp.full(bits_ref.shape[1:], lax.axis_index("shot"), dtype=jnp.int32)
    for bit in range(bits_ref.shape[0]):
        bits_ref[bit] = shot & (1 << bit)


def own_part(
    table_hbm,
    spots_hbm,
    traces_hbm,
    amps_hbm,
    ids_hbm,
    src_now,
    rec_now,
    src_prev,
    rec_prev,
    amps_ref,
    wide,
    part_ref,
    later_ref,
    coef_ref,
    sent_first_ref,
    sent_last_ref,
    table,
    spots_ref,
    traces_ref,
    ids_ref,
    prev_ref,
    sems,
):
    levels, extent, across = ids_ref.shape
    shape = (extent, across)
    regions = table_hbm.shape[1]
    end = LEAD + extent
    moves = (
        (table_hbm, table),
        (ids_hbm, ids_ref),
        (spots_hbm, spots_ref),
        (traces_hbm, traces_ref),
        (src_now.at[0], wide.at[0, :, pl.ds(LEAD, extent), :]),
        (src_prev.at[0], prev_ref.at[0]),
        (rec_now.at[0], wide.at[1, :, pl.ds(LEAD, extent), :]),
        (rec_prev.at[0], prev_ref.at[1]),
        (amps_hbm, amps_ref),
    )
    copies = [
        pltpu.make_async_copy(here, there, sems.at[i]) for i, (here, there) in enumerate(moves)
    ]
    for copy in copies:
        copy.start()
    zeros = jnp.zeros((LEAD, across), jnp.float32)
    for field in range(2):
        for level in range(levels):
            wide[field, level, 0:LEAD, :] = zeros
            wide[field, level, end : end + LEAD, :] = zeros
    weights = lane_weights(shape)

    for copy in copies[2:4]:
        copy.wait()
    spots = spots_ref[...]
    column = lax.broadcasted_iota(jnp.int32, (extent, spots.shape[1]), 0) * across
    in_column = (spots >= column) & (spots < column + across)
    lane = lax.broadcasted_iota(jnp.int32, (across, spots.shape[1]), 0)
    in_row = jnp.where(lax.rem(spots, across) == lane, 1.0, 0.0)
    traces = jnp.concatenate(
        [jnp.where(in_column, traces_ref[0, t : t + 1, :], 0.0) for t in range(2)], axis=0
    )
    planes = lax.dot_general(
        traces,
        in_row,
        (((1,), (1,)), ((), ())),
        precision=lax.Precision.HIGHEST,
        preferred_element_type=jnp.float32,
    )

    up_first = goes_up_first()

    def send(place, rows, value):
        low = value[0:HALO, :]
        high = value[extent - HALO : extent, :]
        sent_first_ref[place, rows, :] = jnp.where(up_first, high, low)
        sent_last_ref[place, rows, :] = jnp.where(up_first, low, high)

    copies[0].wait()
    copies[1].wait()
    speeds = jnp.concatenate(
        [table[...], jnp.zeros((1, across - regions), jnp.float32)], axis=1
    )
    speeds = jnp.broadcast_to(speeds, (8, across))
    for level in range(levels):
        for row in range(0, extent, 8):
            ids = ids_ref[level, row : row + 8, :]
            coef_ref[level, row : row + 8, :] = jnp.take_along_axis(
                speeds, ids, axis=1, mode="promise_in_bounds"
            )
        send(2 * levels + level // 2, pl.ds(level % 2 * HALO, HALO), coef_ref[level])

    for field in range(2):
        copies[4 + 2 * field].wait()
        copies[5 + 2 * field].wait()
        for level in range(levels):
            total = laplace_level(wide, field, level, levels, extent, weights)
            now = wide[field, level, LEAD:end, :]
            value = 2.0 * now - prev_ref[field, level] + coef_ref[level] * total
            later = -now
            if field == 1 and level == 0:
                value = value + planes[:extent, :]
                later = later + planes[extent:, :]
            part_ref[field, level] = value
            later_ref[field, level] = later
            place = field * levels + level
            send(place, pl.ds(0, HALO), now)
            send(place, pl.ds(HALO, HALO), value)
    copies[8].wait()


def both_steps(
    up_first_ref,
    inside_ref,
    bits_ref,
    own,
    part_ref,
    later_ref,
    source_ref,
    source_later_ref,
    coef_ref,
    came_first_ref,
    came_last_ref,
    final_ref,
    mine_ref,
    *rest,
):
    *theirs, other, middle = rest
    blocks = [mine_ref, *theirs]
    levels, extent, across = coef_ref.shape
    shape = (extent, across)
    share = mine_ref.shape[1]
    end = LEAD + extent
    up_first = up_first_ref[0:HALO, :] != 0
    inside = inside_ref[0:HALO, :] != 0

    def received(place, rows):
        first = came_first_ref[place, rows, :]
        last = jnp.where(inside, came_last_ref[place, rows, :], 0.0)
        return jnp.where(up_first, last, first), jnp.where(up_first, first, last)

    for field in range(2):
        for level in range(levels):
            low, high = received(field * levels + level, pl.ds(0, HALO))
            other[field, level, LEAD:end, :] = jnp.zeros(shape, jnp.float32)
            other[field, level, LEAD - HALO : LEAD, :] = low
            other[field, level, end : end + HALO, :] = high
    for field in range(2):
        for level in range(levels):
            below = jnp.zeros((HALO, across), jnp.float32)
            above = jnp.zeros((HALO, across), jnp.float32)
            left = jnp.zeros((8, across), jnp.float32)
            right = jnp.zeros((8, across), jnp.float32)
            for k in range(1, HALO + 1):
                begin = LEAD - HALO + k
                below = below + COEFS[k] * own[field, level, begin : begin + HALO, :]
                above = above + COEFS[k] * own[field, level, end - k : end - k + HALO, :]
                left = left + COEFS[k] * other[field, level, LEAD - k : LEAD - k + 8, :]
                right = right + COEFS[k] * other[field, level, end - 8 + k : end + k, :]
            low, high = received(field * levels + level, pl.ds(HALO, HALO))
            low_coef, high_coef = received(
                2 * levels + level // 2, pl.ds(level % 2 * HALO, HALO)
            )
            low = low + low_coef * below
            high = high + high_coef * above
            left = part_ref[field, level, 0:8, :] + coef_ref[level, 0:8, :] * left
            right = (
                part_ref[field, level, extent - 8 : extent, :]
                + coef_ref[level, extent - 8 : extent, :] * right
            )
            if field == 0:
                low = low + source_ref[level, LEAD - HALO : LEAD, :]
                left = left + source_ref[level, LEAD : LEAD + 8, :]
                right = right + source_ref[level, end - 8 : end, :]
                high = high + source_ref[level, end : end + HALO, :]
            middle[field, level, LEAD - HALO : LEAD, :] = low
            middle[field, level, LEAD : LEAD + 8, :] = left
            middle[field, level, end - 8 : end, :] = right
            middle[field, level, end : end + HALO, :] = high
    weights = lane_weights(shape)
    for field in range(2):
        for level in range(levels):
            total = laplace_level(middle, field, level, levels, extent, weights)
            later = source_later_ref[level] if field == 0 else later_ref[field, level]
            value = 2.0 * middle[field, level, LEAD:end, :] + later
            final_ref[field, level] = value + coef_ref[level] * total
    masks = [
        jnp.concatenate([bits_ref[bit]] * (extent // 8), axis=0) != 0
        for bit in range(bits_ref.shape[0])
    ]
    for field in range(2):
        for level in range(share):
            parts = [final_ref[field, place * share + level] for place in range(len(blocks))]
            for bit, mask in enumerate(masks):
                parts = [
                    jnp.where(mask, parts[place ^ (1 << bit)], parts[place])
                    for place in range(len(blocks))
                ]
            for block, part in zip(blocks, parts):
                block[field, level] = part


def widen(weight, masks, blocks, wide):
    mine_ref, came_last_ref, came_first_ref = blocks
    shots, _, share, extent, _ = mine_ref.shape
    up_first, inside = (
        jnp.concatenate([mask[...]] * (extent // 8), axis=0) != 0 for mask in masks
    )
    for shot in range(shots):
        for field in range(2):
            for level in range(share):
                scale = weight if field == 0 else 1.0
                first = scale * came_first_ref[shot, field, level]
                last = jnp.where(inside, scale * came_last_ref[shot, field, level], 0.0)
                wide[shot, field, level, 0:extent, :] = jnp.where(up_first, last, first)
                wide[shot, field, level, extent : 2 * extent, :] = (
                    scale * mine_ref[shot, field, level]
                )
                wide[shot, field, level, 2 * extent : 3 * extent, :] = jnp.where(
                    up_first, first, last
                )


def offset_product(wide, offset, level, total):
    extent = wide.shape[3] // 3
    lower = extent + REACH - offset
    upper = extent - REACH + offset
    for shot in range(wide.shape[0]):
        product = (
            wide[shot, 0, level, lower : lower + extent, :]
            * wide[shot, 1, level, upper : upper + extent, :]
        )
        total = product if total is None else total + product
    return total


def stack(count, *refs):
    for place in range(count):
        refs[-1][place] = refs[place][...]


def own_products(
    weight, up_first_ref, inside_ref, mine_ref, came_last_ref, came_first_ref, image_ref, wide
):
    widen(
        weight, (up_first_ref, inside_ref), (mine_ref, came_last_ref, came_first_ref), wide
    )
    for offset in range(OFFS):
        for level in range(wide.shape[2]):
            image_ref[offset, level] = offset_product(wide, offset, level, None)


def image_products(
    weight,
    up_first_ref,
    inside_ref,
    mine_ref,
    came_last_ref,
    came_first_ref,
    before_ref,
    final_ref,
    src_hbm,
    rec_hbm,
    image_hbm,
    wide,
    image_ref,
    field_sems,
    image_sems,
):
    copies = []
    for field, out in enumerate((src_hbm, rec_hbm)):
        copies.append(
            pltpu.make_async_copy(final_ref.at[field], out.at[0], field_sems.at[field])
        )
    for copy in copies:
        copy.start()
    widen(
        weight, (up_first_ref, inside_ref), (mine_ref, came_last_ref, came_first_ref), wide
    )
    parts = image_sems.shape[0]
    for piece in range(parts):
        offsets = range(piece * OFFS // parts, (piece + 1) * OFFS // parts)
        for offset in offsets:
            for level in range(wide.shape[2]):
                image_ref[offset, level] = offset_product(
                    wide, offset, level, before_ref[offset, level]
                )
        rows = pl.ds(offsets[0], len(offsets))
        copy = pltpu.make_async_copy(image_ref.at[rows], image_hbm.at[rows], image_sems.at[piece])
        copy.start()
        copies.append(copy)
    for copy in copies:
        copy.wait()


def swap_sides(first, last):
    tiles, shots = lax.axis_size("tile"), lax.axis_size("shot")

    def swap(value, begin):
        pairs = []
        for tile in range(tiles):
            partner = tile + 1 if (tile - begin) % 2 == 0 else tile - 1
            inside = 0 <= partner < tiles
            for shot in range(shots):
                target = partner * shots + shot if inside else tile * shots + (shot ^ 1)
                pairs.append((tile * shots + shot, target))
        return lax.ppermute(value, ("tile", "shot"), pairs)

    came_last = swap(last, 1)
    return swap(first, 0), came_last


def per_device(
    src_prev,
    src_now,
    rec_prev,
    rec_now,
    speed_table,
    region_ids,
    source_cell,
    wavelet,
    receiver_cell,
    receiver_data,
):
    _, levels, extent, across = src_now.shape
    tiles = lax.axis_size("tile")
    width = extent * tiles
    shots = lax.axis_size("shot")
    share = levels // shots
    params = pltpu.CompilerParams(vmem_limit_bytes=LIMIT)

    def struct(*shape):
        return jax.ShapeDtypeStruct(shape, jnp.float32)

    def scratch(*shape, dtype=jnp.float32):
        return pltpu.VMEM(shape, dtype)

    wide_shape = (2, levels, extent + 2 * LEAD, across)
    message = struct(2 * levels + levels // 2, 2 * HALO, across)
    amps, own, part, later, coef, first, last = pl.pallas_call(
        own_part,
        out_shape=(
            struct(*wavelet.shape),
            struct(*wide_shape),
            struct(2, levels, extent, across),
            struct(2, levels, extent, across),
            struct(levels, extent, across),
            message,
            message,
        ),
        in_specs=[HBM] * 9,
        out_specs=[VMEM] * 7,
        scratch_shapes=[
            scratch(1, speed_table.shape[0]),
            scratch(*receiver_cell.shape, dtype=jnp.int32),
            scratch(*receiver_data.shape),
            scratch(levels, extent, across, dtype=jnp.int32),
            scratch(2, levels, extent, across),
            pltpu.SemaphoreType.DMA((9,)),
        ],
        compiler_params=params,
        name="own_part",
    )(
        *(
            pltpu.with_memory_space_constraint(array, pltpu.HBM)
            for array in (
                speed_table.reshape(1, -1),
                receiver_cell,
                receiver_data,
                wavelet,
                region_ids,
                src_now,
                rec_now,
                src_prev,
                rec_prev,
            )
        )
    )
    came_first, came_last = swap_sides(first, last)
    source, source_later, up_first, inside, bits = pl.pallas_call(
        functools.partial(source_and_order, width),
        out_shape=(
            struct(levels, extent + 2 * LEAD, across),
            struct(levels, extent, across),
            jax.ShapeDtypeStruct((8, across), jnp.int32),
            jax.ShapeDtypeStruct((8, across), jnp.int32),
            jax.ShapeDtypeStruct((shots.bit_length() - 1, 8, across), jnp.int32),
        ),
        in_specs=[SMEM] + [VMEM] * 2,
        out_specs=[VMEM] * 5,
        compiler_params=params,
        name="source_and_order",
    )(source_cell, amps, later)
    block = struct(2, share, extent, across)
    final, own_block, *blocks = pl.pallas_call(
        both_steps,
        out_shape=(struct(2, levels, extent, across), *([block] * shots)),
        in_specs=[VMEM] * 11,
        out_specs=[VMEM] * (1 + shots),
        scratch_shapes=[scratch(*wide_shape), scratch(*wide_shape)],
        compiler_params=params,
        name="both_steps",
    )(up_first, inside, bits, own, part, later, source, source_later, coef, came_first, came_last)
    came = [
        lax.ppermute(sent, "shot", [(shot, shot ^ (1 + i)) for shot in range(shots)])
        for i, sent in enumerate(blocks)
    ]
    weight = 1.0 / shots
    image_shape = (OFFS, share, extent, across)

    def wide_scratch(blocks):
        return scratch(blocks.shape[0], 2, share, 3 * extent, across)

    mine = own_block[None]
    fields_first, fields_last = swap_sides(mine, mine)
    others = pl.pallas_call(
        functools.partial(stack, len(came)),
        out_shape=struct(len(came), *own_block.shape),
        in_specs=[VMEM] * (len(came) + 2),
        out_specs=VMEM,
        compiler_params=params,
        name="stack",
    )(*came, fields_last, fields_first)
    products = OFFS * share * extent * across
    before = pl.pallas_call(
        functools.partial(own_products, weight),
        out_shape=struct(*image_shape),
        in_specs=[VMEM] * 5,
        out_specs=VMEM,
        scratch_shapes=[wide_scratch(mine)],
        compiler_params=params,
        cost_estimate=pl.CostEstimate(
            flops=2 * products, bytes_accessed=8 * products, transcendentals=0
        ),
        name="own_products",
    )(up_first, inside, mine, fields_last, fields_first)
    fields_first, fields_last = swap_sides(others, others)
    return pl.pallas_call(
        functools.partial(image_products, weight),
        out_shape=(
            struct(1, levels, extent, across),
            struct(1, levels, extent, across),
            struct(*image_shape),
        ),
        in_specs=[VMEM] * 7,
        out_specs=[HBM] * 3,
        scratch_shapes=[
            wide_scratch(others),
            scratch(*image_shape),
            pltpu.SemaphoreType.DMA((2,)),
            pltpu.SemaphoreType.DMA((3,)),
        ],
        compiler_params=params,
        name="image_products",
    )(up_first, inside, others, fields_last, fields_first, before, final)


def solution(mesh):
    field = P(("groups", "shot"), None, "tile", None)
    return jax.shard_map(
        per_device,
        mesh=mesh,
        in_specs=(
            field,
            field,
            field,
            field,
            P("groups"),
            P(None, ("groups", "tile"), None),
            P(("groups", "shot")),
            P(("groups", "shot"), None),
            P(("groups", "shot"), "tile"),
            P(("groups", "shot"), None, "tile"),
        ),
        out_specs=(field, field, P(None, "shot", ("groups", "tile"), None)),
        check_vma=False,
    )
```

```python
import functools

import jax
import jax.numpy as jnp
from jax import lax
from jax.experimental import pallas as pl
from jax.experimental.pallas import tpu as pltpu
from jax.sharding import PartitionSpec as P

OFFS = 33
REACH = OFFS // 2
HALO = 4
LEAD = 8

COEFS = (-205.0 / 72.0, 8.0 / 5.0, -1.0 / 5.0, 8.0 / 315.0, -1.0 / 560.0)

VMEM = pl.BlockSpec(memory_space=pltpu.VMEM)
HBM = pl.BlockSpec(memory_space=pltpu.HBM)
SMEM = pl.BlockSpec(memory_space=pltpu.SMEM)
LIMIT = 16 * 1024 * 1024


def lane_weights(shape):
    lane = lax.broadcasted_iota(jnp.int32, shape, 1)
    across = shape[1]
    after = [jnp.where(lane < across - k, COEFS[k], 0.0) for k in range(1, HALO + 1)]
    before = [jnp.where(lane >= k, COEFS[k], 0.0) for k in range(1, HALO + 1)]
    return after, before


def laplace_level(wide, field, level, levels, extent, weights):
    after, before = weights
    centre = wide[field, level, LEAD : LEAD + extent, :]
    across = centre.shape[1]
    total = 3.0 * COEFS[0] * centre
    for k in range(1, HALO + 1):
        beside = (
            wide[field, level, LEAD + k : LEAD + k + extent, :]
            + wide[field, level, LEAD - k : LEAD - k + extent, :]
        )
        if level + k < levels:
            beside = beside + wide[field, level + k, LEAD : LEAD + extent, :]
        if level - k >= 0:
            beside = beside + wide[field, level - k, LEAD : LEAD + extent, :]
        total = total + COEFS[k] * beside
        total = total + after[k - 1] * pltpu.roll(centre, across - k, 1)
        total = total + before[k - 1] * pltpu.roll(centre, k, 1)
    return total


def goes_up_first():
    return lax.rem(lax.axis_index("tile"), 2) == 0


def source_and_order(
    width, cell_ref, amps_ref, later_ref, source_ref, source_later_ref, up_first_ref, inside_ref, bits_ref
):
    levels, extent, across = source_later_ref.shape
    cell = cell_ref[0]
    deep = lax.div(cell, width * across)
    row = lax.rem(lax.div(cell, across), width) - lax.axis_index("tile") * extent + LEAD
    shape = (extent + 2 * LEAD, across)
    rows = lax.broadcasted_iota(jnp.int32, shape, 0)
    lanes = lax.broadcasted_iota(jnp.int32, shape, 1)
    hit = jnp.where((rows == row) & (lanes == lax.rem(cell, across)), 1.0, 0.0)
    for level in range(levels):
        here = hit * jnp.where(deep == level, 1.0, 0.0)
        source_ref[level] = here * amps_ref[0:1, 0:1]
        source_later_ref[level] = (
            later_ref[0, level] + here[LEAD : LEAD + extent, :] * amps_ref[0:1, 1:2]
        )
    up_first_ref[...] = jnp.full(
        up_first_ref.shape, jnp.where(goes_up_first(), 1, 0), dtype=jnp.int32
    )
    tile = lax.axis_index("tile")
    inside = (tile > 0) & (tile < lax.axis_size("tile") - 1)
    inside_ref[...] = jnp.full(inside_ref.shape, jnp.where(inside, 1, 0), dtype=jnp.int32)
    shot = jnp.full(bits_ref.shape[1:], lax.axis_index("shot"), dtype=jnp.int32)
    for bit in range(bits_ref.shape[0]):
        bits_ref[bit] = shot & (1 << bit)


def own_part(
    table_hbm,
    spots_hbm,
    traces_hbm,
    amps_hbm,
    ids_hbm,
    src_now,
    rec_now,
    src_prev,
    rec_prev,
    amps_ref,
    wide,
    part_ref,
    later_ref,
    coef_ref,
    sent_first_ref,
    sent_last_ref,
    table,
    spots_ref,
    traces_ref,
    ids_ref,
    prev_ref,
    sems,
):
    levels, extent, across = ids_ref.shape
    shape = (extent, across)
    regions = table_hbm.shape[1]
    end = LEAD + extent
    rows = pl.ds(LEAD, extent)
    moves = [(table_hbm, table), (spots_hbm, spots_ref), (traces_hbm, traces_ref)]
    for begin in range(0, levels, levels // 2):
        part = pl.ds(begin, levels // 2)
        moves += [
            (src_now.at[0, part], wide.at[0, part, rows, :]),
            (rec_now.at[0, part], wide.at[1, part, rows, :]),
            (ids_hbm.at[part], ids_ref.at[part]),
            (src_prev.at[0, part], prev_ref.at[0, part]),
            (rec_prev.at[0, part], prev_ref.at[1, part]),
        ]
    moves.append((amps_hbm, amps_ref))
    copies = [
        pltpu.make_async_copy(here, there, sems.at[i]) for i, (here, there) in enumerate(moves)
    ]
    for copy in copies:
        copy.start()
    zeros = jnp.zeros((LEAD, across), jnp.float32)
    for field in range(2):
        for level in range(levels):
            wide[field, level, 0:LEAD, :] = zeros
            wide[field, level, end : end + LEAD, :] = zeros
    weights = lane_weights(shape)
    up_first = goes_up_first()
    for copy in copies:
        copy.wait()

    def send(place, rows, value):
        low = value[0:HALO, :]
        high = value[extent - HALO : extent, :]
        sent_first_ref[place, rows, :] = jnp.where(up_first, high, low)
        sent_last_ref[place, rows, :] = jnp.where(up_first, low, high)

    spots = spots_ref[...]
    column = lax.broadcasted_iota(jnp.int32, (extent, spots.shape[1]), 0) * across
    in_column = (spots >= column) & (spots < column + across)
    lane = lax.broadcasted_iota(jnp.int32, (across, spots.shape[1]), 0)
    in_row = jnp.where(lax.rem(spots, across) == lane, 1.0, 0.0)
    traces = jnp.concatenate(
        [jnp.where(in_column, traces_ref[0, t : t + 1, :], 0.0) for t in range(2)], axis=0
    )
    planes = lax.dot_general(
        traces,
        in_row,
        (((1,), (1,)), ((), ())),
        precision=lax.Precision.HIGHEST,
        preferred_element_type=jnp.float32,
    )

    speeds = jnp.concatenate(
        [table[...], jnp.zeros((1, across - regions), jnp.float32)], axis=1
    )
    speeds = jnp.broadcast_to(speeds, (8, across))
    for level in range(levels):
        for row in range(0, extent, 8):
            ids = ids_ref[level, row : row + 8, :]
            coef_ref[level, row : row + 8, :] = jnp.take_along_axis(
                speeds, ids, axis=1, mode="promise_in_bounds"
            )
        send(2 * levels + level // 2, pl.ds(level % 2 * HALO, HALO), coef_ref[level])

    for field in range(2):
        for level in range(levels):
            total = laplace_level(wide, field, level, levels, extent, weights)
            now = wide[field, level, LEAD:end, :]
            value = 2.0 * now - prev_ref[field, level] + coef_ref[level] * total
            later = -now
            if field == 1 and level == 0:
                value = value + planes[:extent, :]
                later = later + planes[extent:, :]
            part_ref[field, level] = value
            later_ref[field, level] = later
            place = field * levels + level
            send(place, pl.ds(0, HALO), now)
            send(place, pl.ds(HALO, HALO), value)


def both_steps(
    up_first_ref,
    inside_ref,
    bits_ref,
    own,
    part_ref,
    later_ref,
    source_ref,
    source_later_ref,
    coef_ref,
    came_last_ref,
    came_first_ref,
    final_ref,
    mine_ref,
    *rest,
):
    *theirs, other, middle = rest
    blocks = [mine_ref, *theirs]
    levels, extent, across = coef_ref.shape
    shape = (extent, across)
    share = mine_ref.shape[1]
    end = LEAD + extent
    up_first = up_first_ref[0:HALO, :] != 0
    inside = inside_ref[0:HALO, :] != 0

    def received(place, rows):
        first = came_first_ref[place, rows, :]
        last = jnp.where(inside, came_last_ref[place, rows, :], 0.0)
        return jnp.where(up_first, last, first), jnp.where(up_first, first, last)

    for field in range(2):
        for level in range(levels):
            low, high = received(field * levels + level, pl.ds(0, HALO))
            other[field, level, LEAD:end, :] = jnp.zeros(shape, jnp.float32)
            other[field, level, LEAD - HALO : LEAD, :] = low
            other[field, level, end : end + HALO, :] = high
    for field in range(2):
        for level in range(levels):
            below = jnp.zeros((HALO, across), jnp.float32)
            above = jnp.zeros((HALO, across), jnp.float32)
            left = jnp.zeros((8, across), jnp.float32)
            right = jnp.zeros((8, across), jnp.float32)
            for k in range(1, HALO + 1):
                begin = LEAD - HALO + k
                below = below + COEFS[k] * own[field, level, begin : begin + HALO, :]
                above = above + COEFS[k] * own[field, level, end - k : end - k + HALO, :]
                left = left + COEFS[k] * other[field, level, LEAD - k : LEAD - k + 8, :]
                right = right + COEFS[k] * other[field, level, end - 8 + k : end + k, :]
            low, high = received(field * levels + level, pl.ds(HALO, HALO))
            low_coef, high_coef = received(
                2 * levels + level // 2, pl.ds(level % 2 * HALO, HALO)
            )
            low = low + low_coef * below
            high = high + high_coef * above
            left = part_ref[field, level, 0:8, :] + coef_ref[level, 0:8, :] * left
            right = (
                part_ref[field, level, extent - 8 : extent, :]
                + coef_ref[level, extent - 8 : extent, :] * right
            )
            if field == 0:
                low = low + source_ref[level, LEAD - HALO : LEAD, :]
                left = left + source_ref[level, LEAD : LEAD + 8, :]
                right = right + source_ref[level, end - 8 : end, :]
                high = high + source_ref[level, end : end + HALO, :]
            middle[field, level, LEAD - HALO : LEAD, :] = low
            middle[field, level, LEAD : LEAD + 8, :] = left
            middle[field, level, end - 8 : end, :] = right
            middle[field, level, end : end + HALO, :] = high
    weights = lane_weights(shape)
    for field in range(2):
        for level in range(levels):
            total = laplace_level(middle, field, level, levels, extent, weights)
            later = source_later_ref[level] if field == 0 else later_ref[field, level]
            value = 2.0 * middle[field, level, LEAD:end, :] + later
            final_ref[field, level] = value + coef_ref[level] * total
    masks = [
        jnp.concatenate([bits_ref[bit]] * (extent // 8), axis=0) != 0
        for bit in range(bits_ref.shape[0])
    ]
    for field in range(2):
        for level in range(share):
            parts = [final_ref[field, place * share + level] for place in range(len(blocks))]
            for bit, mask in enumerate(masks):
                parts = [
                    jnp.where(mask, parts[place ^ (1 << bit)], parts[place])
                    for place in range(len(blocks))
                ]
            for block, part in zip(blocks, parts):
                block[field, level] = part


def widen(weight, masks, blocks, wide):
    mine_ref, came_last_ref, came_first_ref = blocks
    shots, _, share, extent, _ = mine_ref.shape
    up_first, inside = (
        jnp.concatenate([mask[...]] * (extent // 8), axis=0) != 0 for mask in masks
    )
    for shot in range(shots):
        for field in range(2):
            for level in range(share):
                scale = weight if field == 0 else 1.0
                first = scale * came_first_ref[shot, field, level]
                last = jnp.where(inside, scale * came_last_ref[shot, field, level], 0.0)
                wide[shot, field, level, 0:extent, :] = jnp.where(up_first, last, first)
                wide[shot, field, level, extent : 2 * extent, :] = (
                    scale * mine_ref[shot, field, level]
                )
                wide[shot, field, level, 2 * extent : 3 * extent, :] = jnp.where(
                    up_first, first, last
                )


def offset_product(wide, offset, level, total):
    extent = wide.shape[3] // 3
    lower = extent + REACH - offset
    upper = extent - REACH + offset
    for shot in range(wide.shape[0]):
        product = (
            wide[shot, 0, level, lower : lower + extent, :]
            * wide[shot, 1, level, upper : upper + extent, :]
        )
        total = product if total is None else total + product
    return total


def stack(count, *refs):
    for place in range(count):
        refs[-1][place] = refs[place][...]


def own_products(
    weight,
    up_first_ref,
    inside_ref,
    mine_ref,
    came_last_ref,
    came_first_ref,
    final_ref,
    src_hbm,
    rec_hbm,
    image_ref,
    wide,
    sems,
):
    copies = [
        pltpu.make_async_copy(final_ref.at[field], out.at[0], sems.at[field])
        for field, out in enumerate((src_hbm, rec_hbm))
    ]
    for copy in copies:
        copy.start()
    widen(
        weight, (up_first_ref, inside_ref), (mine_ref, came_last_ref, came_first_ref), wide
    )
    for offset in range(OFFS):
        for level in range(wide.shape[2]):
            image_ref[offset, level] = offset_product(wide, offset, level, None)
    for copy in copies:
        copy.wait()


def image_products(
    weight,
    up_first_ref,
    inside_ref,
    mine_ref,
    came_last_ref,
    came_first_ref,
    before_ref,
    image_hbm,
    wide,
    image_ref,
    sems,
):
    widen(
        weight, (up_first_ref, inside_ref), (mine_ref, came_last_ref, came_first_ref), wide
    )
    parts = sems.shape[0]
    copies = []
    for piece in range(parts):
        offsets = range(piece * OFFS // parts, (piece + 1) * OFFS // parts)
        for offset in offsets:
            for level in range(wide.shape[2]):
                image_ref[offset, level] = offset_product(
                    wide, offset, level, before_ref[offset, level]
                )
        rows = pl.ds(offsets[0], len(offsets))
        copy = pltpu.make_async_copy(image_ref.at[rows], image_hbm.at[rows], sems.at[piece])
        copy.start()
        copies.append(copy)
    for copy in copies:
        copy.wait()


def swap_sides(first, last):
    tiles, shots = lax.axis_size("tile"), lax.axis_size("shot")

    def swap(value, begin):
        pairs = []
        for tile in range(tiles):
            partner = tile + 1 if (tile - begin) % 2 == 0 else tile - 1
            inside = 0 <= partner < tiles
            for shot in range(shots):
                target = partner * shots + shot if inside else tile * shots + (shot ^ 1)
                pairs.append((tile * shots + shot, target))
        return lax.ppermute(value, ("tile", "shot"), pairs)

    came_last = swap(last, 1)
    return swap(first, 0), came_last


def per_device(
    src_prev,
    src_now,
    rec_prev,
    rec_now,
    speed_table,
    region_ids,
    source_cell,
    wavelet,
    receiver_cell,
    receiver_data,
):
    _, levels, extent, across = src_now.shape
    tiles = lax.axis_size("tile")
    width = extent * tiles
    shots = lax.axis_size("shot")
    share = levels // shots
    params = pltpu.CompilerParams(vmem_limit_bytes=LIMIT)

    def struct(*shape):
        return jax.ShapeDtypeStruct(shape, jnp.float32)

    def scratch(*shape, dtype=jnp.float32):
        return pltpu.VMEM(shape, dtype)

    wide_shape = (2, levels, extent + 2 * LEAD, across)
    message = struct(2 * levels + levels // 2, 2 * HALO, across)
    amps, own, part, later, coef, first, last = pl.pallas_call(
        own_part,
        out_shape=(
            struct(*wavelet.shape),
            struct(*wide_shape),
            struct(2, levels, extent, across),
            struct(2, levels, extent, across),
            struct(levels, extent, across),
            message,
            message,
        ),
        in_specs=[HBM] * 9,
        out_specs=[VMEM] * 7,
        scratch_shapes=[
            scratch(1, speed_table.shape[0]),
            scratch(*receiver_cell.shape, dtype=jnp.int32),
            scratch(*receiver_data.shape),
            scratch(levels, extent, across, dtype=jnp.int32),
            scratch(2, levels, extent, across),
            pltpu.SemaphoreType.DMA((14,)),
        ],
        compiler_params=params,
        name="own_part",
    )(
        *(
            pltpu.with_memory_space_constraint(array, pltpu.HBM)
            for array in (
                speed_table.reshape(1, -1),
                receiver_cell,
                receiver_data,
                wavelet,
                region_ids,
                src_now,
                rec_now,
                src_prev,
                rec_prev,
            )
        )
    )
    came_first, came_last = swap_sides(first, last)
    source, source_later, up_first, inside, bits = pl.pallas_call(
        functools.partial(source_and_order, width),
        out_shape=(
            struct(levels, extent + 2 * LEAD, across),
            struct(levels, extent, across),
            jax.ShapeDtypeStruct((8, across), jnp.int32),
            jax.ShapeDtypeStruct((8, across), jnp.int32),
            jax.ShapeDtypeStruct((shots.bit_length() - 1, 8, across), jnp.int32),
        ),
        in_specs=[SMEM] + [VMEM] * 2,
        out_specs=[VMEM] * 5,
        compiler_params=params,
        name="source_and_order",
    )(source_cell, amps, later)
    block = struct(2, share, extent, across)
    final, own_block, *blocks = pl.pallas_call(
        both_steps,
        out_shape=(struct(2, levels, extent, across), *([block] * shots)),
        in_specs=[VMEM] * 11,
        out_specs=[VMEM] * (1 + shots),
        scratch_shapes=[scratch(*wide_shape), scratch(*wide_shape)],
        compiler_params=params,
        name="both_steps",
    )(up_first, inside, bits, own, part, later, source, source_later, coef, came_last, came_first)
    came = [
        lax.ppermute(sent, "shot", [(shot, shot ^ (1 + i)) for shot in range(shots)])
        for i, sent in enumerate(blocks)
    ]
    weight = 1.0 / shots
    image_shape = (OFFS, share, extent, across)

    def wide_scratch(blocks):
        return scratch(blocks.shape[0], 2, share, 3 * extent, across)

    mine = own_block[None]
    fields_first, fields_last = swap_sides(mine, mine)
    others = pl.pallas_call(
        functools.partial(stack, len(came)),
        out_shape=struct(len(came), *own_block.shape),
        in_specs=[VMEM] * (len(came) + 2),
        out_specs=VMEM,
        compiler_params=params,
        name="stack",
    )(*came, fields_last, fields_first)
    products = OFFS * share * extent * across
    src_next, rec_next, before = pl.pallas_call(
        functools.partial(own_products, weight),
        out_shape=(
            struct(1, levels, extent, across),
            struct(1, levels, extent, across),
            struct(*image_shape),
        ),
        in_specs=[VMEM] * 6,
        out_specs=[HBM, HBM, VMEM],
        scratch_shapes=[wide_scratch(mine), pltpu.SemaphoreType.DMA((2,))],
        compiler_params=params,
        cost_estimate=pl.CostEstimate(
            flops=2 * products, bytes_accessed=8 * products, transcendentals=0
        ),
        name="own_products",
    )(up_first, inside, mine, fields_last, fields_first, final)
    fields_first, fields_last = swap_sides(others, others)
    image = pl.pallas_call(
        functools.partial(image_products, weight),
        out_shape=struct(*image_shape),
        in_specs=[VMEM] * 6,
        out_specs=HBM,
        scratch_shapes=[
            wide_scratch(others),
            scratch(*image_shape),
            pltpu.SemaphoreType.DMA((11,)),
        ],
        compiler_params=params,
        name="image_products",
    )(up_first, inside, others, fields_last, fields_first, before)
    return src_next, rec_next, image


def solution(mesh):
    field = P(("groups", "shot"), None, "tile", None)
    return jax.shard_map(
        per_device,
        mesh=mesh,
        in_specs=(
            field,
            field,
            field,
            field,
            P("groups"),
            P(None, ("groups", "tile"), None),
            P(("groups", "shot")),
            P(("groups", "shot"), None),
            P(("groups", "shot"), "tile"),
            P(("groups", "shot"), None, "tile"),
        ),
        out_specs=(field, field, P(None, "shot", ("groups", "tile"), None)),
        check_vma=False,
    )
```

```python
import functools

import jax
import jax.numpy as jnp
from jax import lax
from jax.experimental import pallas as pl
from jax.experimental.pallas import tpu as pltpu
from jax.sharding import PartitionSpec as P

OFFS = 33
REACH = OFFS // 2
HALO = 4
LEAD = 8

COEFS = (-205.0 / 72.0, 8.0 / 5.0, -1.0 / 5.0, 8.0 / 315.0, -1.0 / 560.0)

VMEM = pl.BlockSpec(memory_space=pltpu.VMEM)
HBM = pl.BlockSpec(memory_space=pltpu.HBM)
SMEM = pl.BlockSpec(memory_space=pltpu.SMEM)
LIMIT = 16 * 1024 * 1024


def lane_weights(shape):
    lane = lax.broadcasted_iota(jnp.int32, shape, 1)
    across = shape[1]
    after = [jnp.where(lane < across - k, COEFS[k], 0.0) for k in range(1, HALO + 1)]
    before = [jnp.where(lane >= k, COEFS[k], 0.0) for k in range(1, HALO + 1)]
    return after, before


def laplace_level(wide, field, level, levels, extent, weights):
    after, before = weights
    centre = wide[field, level, LEAD : LEAD + extent, :]
    across = centre.shape[1]
    total = 3.0 * COEFS[0] * centre
    for k in range(1, HALO + 1):
        beside = (
            wide[field, level, LEAD + k : LEAD + k + extent, :]
            + wide[field, level, LEAD - k : LEAD - k + extent, :]
        )
        if level + k < levels:
            beside = beside + wide[field, level + k, LEAD : LEAD + extent, :]
        if level - k >= 0:
            beside = beside + wide[field, level - k, LEAD : LEAD + extent, :]
        total = total + COEFS[k] * beside
        total = total + after[k - 1] * pltpu.roll(centre, across - k, 1)
        total = total + before[k - 1] * pltpu.roll(centre, k, 1)
    return total


def goes_up_first():
    return lax.rem(lax.axis_index("tile"), 2) == 0


def source_and_order(
    width, cell_ref, amps_ref, later_ref, source_ref, source_later_ref, up_first_ref, inside_ref, bits_ref
):
    levels, extent, across = source_later_ref.shape
    cell = cell_ref[0]
    deep = lax.div(cell, width * across)
    row = lax.rem(lax.div(cell, across), width) - lax.axis_index("tile") * extent + LEAD
    shape = (extent + 2 * LEAD, across)
    rows = lax.broadcasted_iota(jnp.int32, shape, 0)
    lanes = lax.broadcasted_iota(jnp.int32, shape, 1)
    hit = jnp.where((rows == row) & (lanes == lax.rem(cell, across)), 1.0, 0.0)
    for level in range(levels):
        here = hit * jnp.where(deep == level, 1.0, 0.0)
        source_ref[level] = here * amps_ref[0:1, 0:1]
        source_later_ref[level] = (
            later_ref[0, level] + here[LEAD : LEAD + extent, :] * amps_ref[0:1, 1:2]
        )
    up_first_ref[...] = jnp.full(
        up_first_ref.shape, jnp.where(goes_up_first(), 1, 0), dtype=jnp.int32
    )
    tile = lax.axis_index("tile")
    inside = (tile > 0) & (tile < lax.axis_size("tile") - 1)
    inside_ref[...] = jnp.full(inside_ref.shape, jnp.where(inside, 1, 0), dtype=jnp.int32)
    shot = jnp.full(bits_ref.shape[1:], lax.axis_index("shot"), dtype=jnp.int32)
    for bit in range(bits_ref.shape[0]):
        bits_ref[bit] = shot & (1 << bit)


def own_part(
    table_hbm,
    spots_hbm,
    traces_hbm,
    amps_hbm,
    ids_hbm,
    src_now,
    rec_now,
    src_prev,
    rec_prev,
    amps_ref,
    wide,
    part_ref,
    later_ref,
    coef_ref,
    sent_first_ref,
    sent_last_ref,
    table,
    spots_ref,
    traces_ref,
    ids_ref,
    prev_ref,
    sems,
):
    levels, extent, across = ids_ref.shape
    shape = (extent, across)
    regions = table_hbm.shape[1]
    end = LEAD + extent
    rows = pl.ds(LEAD, extent)
    moves = [(table_hbm, table), (spots_hbm, spots_ref), (traces_hbm, traces_ref)]
    for begin in range(0, levels, levels // 2):
        part = pl.ds(begin, levels // 2)
        moves += [
            (src_now.at[0, part], wide.at[0, part, rows, :]),
            (rec_now.at[0, part], wide.at[1, part, rows, :]),
            (ids_hbm.at[part], ids_ref.at[part]),
            (src_prev.at[0, part], prev_ref.at[0, part]),
            (rec_prev.at[0, part], prev_ref.at[1, part]),
        ]
    moves.append((amps_hbm, amps_ref))
    copies = [
        pltpu.make_async_copy(here, there, sems.at[i]) for i, (here, there) in enumerate(moves)
    ]
    for copy in copies:
        copy.start()
    zeros = jnp.zeros((LEAD, across), jnp.float32)
    for field in range(2):
        for level in range(levels):
            wide[field, level, 0:LEAD, :] = zeros
            wide[field, level, end : end + LEAD, :] = zeros
    weights = lane_weights(shape)
    up_first = goes_up_first()
    for copy in copies:
        copy.wait()

    def send(place, rows, value):
        low = value[0:HALO, :]
        high = value[extent - HALO : extent, :]
        sent_first_ref[place, rows, :] = jnp.where(up_first, high, low)
        sent_last_ref[place, rows, :] = jnp.where(up_first, low, high)

    spots = spots_ref[...]
    column = lax.broadcasted_iota(jnp.int32, (extent, spots.shape[1]), 0) * across
    in_column = (spots >= column) & (spots < column + across)
    lane = lax.broadcasted_iota(jnp.int32, (across, spots.shape[1]), 0)
    in_row = jnp.where(lax.rem(spots, across) == lane, 1.0, 0.0)
    traces = jnp.concatenate(
        [jnp.where(in_column, traces_ref[0, t : t + 1, :], 0.0) for t in range(2)], axis=0
    )
    planes = lax.dot_general(
        traces,
        in_row,
        (((1,), (1,)), ((), ())),
        precision=lax.Precision.HIGHEST,
        preferred_element_type=jnp.float32,
    )

    speeds = jnp.concatenate(
        [table[...], jnp.zeros((1, across - regions), jnp.float32)], axis=1
    )
    speeds = jnp.broadcast_to(speeds, (8, across))
    for level in range(levels):
        for row in range(0, extent, 8):
            ids = ids_ref[level, row : row + 8, :]
            coef_ref[level, row : row + 8, :] = jnp.take_along_axis(
                speeds, ids, axis=1, mode="promise_in_bounds"
            )
        send(2 * levels + level // 2, pl.ds(level % 2 * HALO, HALO), coef_ref[level])

    for field in range(2):
        for level in range(levels):
            total = laplace_level(wide, field, level, levels, extent, weights)
            now = wide[field, level, LEAD:end, :]
            value = 2.0 * now - prev_ref[field, level] + coef_ref[level] * total
            later = -now
            if field == 1 and level == 0:
                value = value + planes[:extent, :]
                later = later + planes[extent:, :]
            part_ref[field, level] = value
            later_ref[field, level] = later
            place = field * levels + level
            send(place, pl.ds(0, HALO), now)
            send(place, pl.ds(HALO, HALO), value)


def both_steps(
    up_first_ref,
    inside_ref,
    bits_ref,
    own,
    part_ref,
    later_ref,
    source_ref,
    source_later_ref,
    coef_ref,
    came_last_ref,
    came_first_ref,
    final_ref,
    mine_ref,
    *rest,
):
    *theirs, other, middle = rest
    blocks = [mine_ref, *theirs]
    levels, extent, across = coef_ref.shape
    shape = (extent, across)
    share = mine_ref.shape[1]
    end = LEAD + extent
    up_first = up_first_ref[0:HALO, :] != 0
    inside = inside_ref[0:HALO, :] != 0

    def received(place, rows):
        first = came_first_ref[place, rows, :]
        last = jnp.where(inside, came_last_ref[place, rows, :], 0.0)
        return jnp.where(up_first, last, first), jnp.where(up_first, first, last)

    for field in range(2):
        for level in range(levels):
            low, high = received(field * levels + level, pl.ds(0, HALO))
            other[field, level, LEAD:end, :] = jnp.zeros(shape, jnp.float32)
            other[field, level, LEAD - HALO : LEAD, :] = low
            other[field, level, end : end + HALO, :] = high
    for field in range(2):
        for level in range(levels):
            below = jnp.zeros((HALO, across), jnp.float32)
            above = jnp.zeros((HALO, across), jnp.float32)
            left = jnp.zeros((8, across), jnp.float32)
            right = jnp.zeros((8, across), jnp.float32)
            for k in range(1, HALO + 1):
                begin = LEAD - HALO + k
                below = below + COEFS[k] * own[field, level, begin : begin + HALO, :]
                above = above + COEFS[k] * own[field, level, end - k : end - k + HALO, :]
                left = left + COEFS[k] * other[field, level, LEAD - k : LEAD - k + 8, :]
                right = right + COEFS[k] * other[field, level, end - 8 + k : end + k, :]
            low, high = received(field * levels + level, pl.ds(HALO, HALO))
            low_coef, high_coef = received(
                2 * levels + level // 2, pl.ds(level % 2 * HALO, HALO)
            )
            low = low + low_coef * below
            high = high + high_coef * above
            left = part_ref[field, level, 0:8, :] + coef_ref[level, 0:8, :] * left
            right = (
                part_ref[field, level, extent - 8 : extent, :]
                + coef_ref[level, extent - 8 : extent, :] * right
            )
            if field == 0:
                low = low + source_ref[level, LEAD - HALO : LEAD, :]
                left = left + source_ref[level, LEAD : LEAD + 8, :]
                right = right + source_ref[level, end - 8 : end, :]
                high = high + source_ref[level, end : end + HALO, :]
            middle[field, level, LEAD - HALO : LEAD, :] = low
            middle[field, level, LEAD : LEAD + 8, :] = left
            middle[field, level, end - 8 : end, :] = right
            middle[field, level, end : end + HALO, :] = high
    weights = lane_weights(shape)
    for field in range(2):
        for level in range(levels):
            total = laplace_level(middle, field, level, levels, extent, weights)
            later = source_later_ref[level] if field == 0 else later_ref[field, level]
            value = 2.0 * middle[field, level, LEAD:end, :] + later
            final_ref[field, level] = value + coef_ref[level] * total
    masks = [
        jnp.concatenate([bits_ref[bit]] * (extent // 8), axis=0) != 0
        for bit in range(bits_ref.shape[0])
    ]
    for field in range(2):
        for level in range(share):
            parts = [final_ref[field, place * share + level] for place in range(len(blocks))]
            for bit, mask in enumerate(masks):
                parts = [
                    jnp.where(mask, parts[place ^ (1 << bit)], parts[place])
                    for place in range(len(blocks))
                ]
            for block, part in zip(blocks, parts):
                block[field, level] = part


def widen(weight, masks, blocks, wide):
    mine_ref, came_last_ref, came_first_ref = blocks
    shots, _, share, extent, _ = mine_ref.shape
    up_first, inside = (
        jnp.concatenate([mask[...]] * (extent // 8), axis=0) != 0 for mask in masks
    )
    for shot in range(shots):
        for field in range(2):
            for level in range(share):
                scale = weight if field == 0 else 1.0
                first = scale * came_first_ref[shot, field, level]
                last = jnp.where(inside, scale * came_last_ref[shot, field, level], 0.0)
                wide[shot, field, level, 0:extent, :] = jnp.where(up_first, last, first)
                wide[shot, field, level, extent : 2 * extent, :] = (
                    scale * mine_ref[shot, field, level]
                )
                wide[shot, field, level, 2 * extent : 3 * extent, :] = jnp.where(
                    up_first, first, last
                )


def offset_product(wide, offset, level, total):
    extent = wide.shape[3] // 3
    lower = extent + REACH - offset
    upper = extent - REACH + offset
    for shot in range(wide.shape[0]):
        product = (
            wide[shot, 0, level, lower : lower + extent, :]
            * wide[shot, 1, level, upper : upper + extent, :]
        )
        total = product if total is None else total + product
    return total


def stack(*refs):
    for place in range(len(refs) - 1):
        refs[-1][place] = refs[place][...]


def write_fields(final_ref, src_hbm, rec_hbm, sems):
    copies = [
        pltpu.make_async_copy(final_ref.at[field], out.at[0], sems.at[field])
        for field, out in enumerate((src_hbm, rec_hbm))
    ]
    for copy in copies:
        copy.start()
    for copy in copies:
        copy.wait()


def image_products(weight, up_first_ref, inside_ref, *rest):
    groups, (image_hbm, *wides, image_ref, sems) = (rest[0:3], rest[3:6]), rest[6:]
    for blocks, wide in zip(groups, wides):
        widen(weight, (up_first_ref, inside_ref), blocks, wide)
    parts = sems.shape[0]
    copies = []
    for piece in range(parts):
        offsets = range(piece * OFFS // parts, (piece + 1) * OFFS // parts)
        for offset in offsets:
            for level in range(image_ref.shape[1]):
                total = None
                for wide in wides:
                    total = offset_product(wide, offset, level, total)
                image_ref[offset, level] = total
        rows = pl.ds(offsets[0], len(offsets))
        copy = pltpu.make_async_copy(image_ref.at[rows], image_hbm.at[rows], sems.at[piece])
        copy.start()
        copies.append(copy)
    for copy in copies:
        copy.wait()


def swap_sides(first, last):
    tiles, shots = lax.axis_size("tile"), lax.axis_size("shot")

    def swap(value, begin):
        pairs = []
        for tile in range(tiles):
            partner = tile + 1 if (tile - begin) % 2 == 0 else tile - 1
            inside = 0 <= partner < tiles
            for shot in range(shots):
                target = partner * shots + shot if inside else tile * shots + (shot ^ 1)
                pairs.append((tile * shots + shot, target))
        return lax.ppermute(value, ("tile", "shot"), pairs)

    came_last = swap(last, 1)
    return swap(first, 0), came_last


def per_device(
    src_prev,
    src_now,
    rec_prev,
    rec_now,
    speed_table,
    region_ids,
    source_cell,
    wavelet,
    receiver_cell,
    receiver_data,
):
    _, levels, extent, across = src_now.shape
    tiles = lax.axis_size("tile")
    width = extent * tiles
    shots = lax.axis_size("shot")
    share = levels // shots
    params = pltpu.CompilerParams(vmem_limit_bytes=LIMIT)

    def struct(*shape):
        return jax.ShapeDtypeStruct(shape, jnp.float32)

    def scratch(*shape, dtype=jnp.float32):
        return pltpu.VMEM(shape, dtype)

    wide_shape = (2, levels, extent + 2 * LEAD, across)
    message = struct(2 * levels + levels // 2, 2 * HALO, across)
    amps, own, part, later, coef, first, last = pl.pallas_call(
        own_part,
        out_shape=(
            struct(*wavelet.shape),
            struct(*wide_shape),
            struct(2, levels, extent, across),
            struct(2, levels, extent, across),
            struct(levels, extent, across),
            message,
            message,
        ),
        in_specs=[HBM] * 9,
        out_specs=[VMEM] * 7,
        scratch_shapes=[
            scratch(1, speed_table.shape[0]),
            scratch(*receiver_cell.shape, dtype=jnp.int32),
            scratch(*receiver_data.shape),
            scratch(levels, extent, across, dtype=jnp.int32),
            scratch(2, levels, extent, across),
            pltpu.SemaphoreType.DMA((14,)),
        ],
        compiler_params=params,
        name="own_part",
    )(
        *(
            pltpu.with_memory_space_constraint(array, pltpu.HBM)
            for array in (
                speed_table.reshape(1, -1),
                receiver_cell,
                receiver_data,
                wavelet,
                region_ids,
                src_now,
                rec_now,
                src_prev,
                rec_prev,
            )
        )
    )
    came_first, came_last = swap_sides(first, last)
    source, source_later, up_first, inside, bits = pl.pallas_call(
        functools.partial(source_and_order, width),
        out_shape=(
            struct(levels, extent + 2 * LEAD, across),
            struct(levels, extent, across),
            jax.ShapeDtypeStruct((8, across), jnp.int32),
            jax.ShapeDtypeStruct((8, across), jnp.int32),
            jax.ShapeDtypeStruct((shots.bit_length() - 1, 8, across), jnp.int32),
        ),
        in_specs=[SMEM] + [VMEM] * 2,
        out_specs=[VMEM] * 5,
        compiler_params=params,
        name="source_and_order",
    )(source_cell, amps, later)
    block = struct(2, share, extent, across)
    final, own_block, *blocks = pl.pallas_call(
        both_steps,
        out_shape=(struct(2, levels, extent, across), *([block] * shots)),
        in_specs=[VMEM] * 11,
        out_specs=[VMEM] * (1 + shots),
        scratch_shapes=[scratch(*wide_shape), scratch(*wide_shape)],
        compiler_params=params,
        name="both_steps",
    )(up_first, inside, bits, own, part, later, source, source_later, coef, came_last, came_first)
    came = [
        lax.ppermute(sent, "shot", [(shot, shot ^ (1 + i)) for shot in range(shots)])
        for i, sent in enumerate(blocks)
    ]
    weight = 1.0 / shots
    image_shape = (OFFS, share, extent, across)

    def wide_scratch(blocks):
        return scratch(blocks.shape[0], 2, share, 3 * extent, across)

    src_next, rec_next = pl.pallas_call(
        write_fields,
        out_shape=(struct(1, levels, extent, across), struct(1, levels, extent, across)),
        in_specs=[VMEM],
        out_specs=[HBM, HBM],
        scratch_shapes=[pltpu.SemaphoreType.DMA((2,))],
        compiler_params=params,
        name="write_fields",
    )(final)
    operands, wides = [], []
    for blocks in ([own_block, came[0]], came[1:]):
        group = pl.pallas_call(
            stack,
            out_shape=struct(len(blocks), *own_block.shape),
            in_specs=[VMEM] * len(blocks),
            out_specs=VMEM,
            compiler_params=params,
            name="stack",
        )(*blocks)
        fields_first, fields_last = swap_sides(group, group)
        operands = [group, fields_last, fields_first, *operands]
        wides.insert(0, wide_scratch(group))
    image = pl.pallas_call(
        functools.partial(image_products, weight),
        out_shape=struct(*image_shape),
        in_specs=[VMEM] * (2 + len(operands)),
        out_specs=HBM,
        scratch_shapes=[*wides, scratch(*image_shape), pltpu.SemaphoreType.DMA((11,))],
        compiler_params=params,
        name="image_products",
    )(up_first, inside, *operands)
    return src_next, rec_next, image


def solution(mesh):
    field = P(("groups", "shot"), None, "tile", None)
    return jax.shard_map(
        per_device,
        mesh=mesh,
        in_specs=(
            field,
            field,
            field,
            field,
            P("groups"),
            P(None, ("groups", "tile"), None),
            P(("groups", "shot")),
            P(("groups", "shot"), None),
            P(("groups", "shot"), "tile"),
            P(("groups", "shot"), None, "tile"),
        ),
        out_specs=(field, field, P(None, "shot", ("groups", "tile"), None)),
        check_vma=False,
    )
```

```python
import functools

import jax
import jax.numpy as jnp
from jax import lax
from jax.experimental import pallas as pl
from jax.experimental.pallas import tpu as pltpu
from jax.sharding import PartitionSpec as P

OFFS = 33
REACH = OFFS // 2
HALO = 4
LEAD = 8
ROUNDS = 3

COEFS = (-205.0 / 72.0, 8.0 / 5.0, -1.0 / 5.0, 8.0 / 315.0, -1.0 / 560.0)

VMEM = pl.BlockSpec(memory_space=pltpu.VMEM)
HBM = pl.BlockSpec(memory_space=pltpu.HBM)
SMEM = pl.BlockSpec(memory_space=pltpu.SMEM)
LIMIT = 16 * 1024 * 1024


def lane_weights(shape):
    lane = lax.broadcasted_iota(jnp.int32, shape, 1)
    across = shape[1]
    after = [jnp.where(lane < across - k, COEFS[k], 0.0) for k in range(1, HALO + 1)]
    before = [jnp.where(lane >= k, COEFS[k], 0.0) for k in range(1, HALO + 1)]
    return after, before


def laplace_level(wide, field, level, levels, extent, weights):
    after, before = weights
    centre = wide[field, level, LEAD : LEAD + extent, :]
    across = centre.shape[1]
    total = 3.0 * COEFS[0] * centre
    for k in range(1, HALO + 1):
        beside = (
            wide[field, level, LEAD + k : LEAD + k + extent, :]
            + wide[field, level, LEAD - k : LEAD - k + extent, :]
        )
        if level + k < levels:
            beside = beside + wide[field, level + k, LEAD : LEAD + extent, :]
        if level - k >= 0:
            beside = beside + wide[field, level - k, LEAD : LEAD + extent, :]
        total = total + COEFS[k] * beside
        total = total + after[k - 1] * pltpu.roll(centre, across - k, 1)
        total = total + before[k - 1] * pltpu.roll(centre, k, 1)
    return total


def goes_up_first():
    return lax.rem(lax.axis_index("tile"), 2) == 0


def source_and_order(
    width, cell_ref, amps_ref, later_ref, source_ref, source_later_ref, up_first_ref, inside_ref, sides_ref, bits_ref
):
    levels, extent, across = source_later_ref.shape
    cell = cell_ref[0]
    deep = lax.div(cell, width * across)
    row = lax.rem(lax.div(cell, across), width) - lax.axis_index("tile") * extent + LEAD
    shape = (extent + 2 * LEAD, across)
    rows = lax.broadcasted_iota(jnp.int32, shape, 0)
    lanes = lax.broadcasted_iota(jnp.int32, shape, 1)
    hit = jnp.where((rows == row) & (lanes == lax.rem(cell, across)), 1.0, 0.0)
    for level in range(levels):
        here = hit * jnp.where(deep == level, 1.0, 0.0)
        source_ref[level] = here * amps_ref[0:1, 0:1]
        source_later_ref[level] = (
            later_ref[0, level] + here[LEAD : LEAD + extent, :] * amps_ref[0:1, 1:2]
        )
    up_first_ref[...] = jnp.full(
        up_first_ref.shape, jnp.where(goes_up_first(), 1, 0), dtype=jnp.int32
    )
    tile, tiles = lax.axis_index("tile"), lax.axis_size("tile")
    inside = (tile > 0) & (tile < tiles - 1)
    inside_ref[...] = jnp.full(inside_ref.shape, jnp.where(inside, 1, 0), dtype=jnp.int32)
    rounds = (tile % ROUNDS, jnp.where(tile > 0, 1, 0), jnp.where(tile < tiles - 1, 1, 0))
    for place, value in enumerate(rounds):
        sides_ref[place] = jnp.full(sides_ref.shape[1:], value, dtype=jnp.int32)
    shot = jnp.full(bits_ref.shape[1:], lax.axis_index("shot"), dtype=jnp.int32)
    for bit in range(bits_ref.shape[0]):
        bits_ref[bit] = shot & (1 << bit)


def own_part(
    table_hbm,
    spots_hbm,
    traces_hbm,
    amps_hbm,
    ids_hbm,
    src_now,
    rec_now,
    src_prev,
    rec_prev,
    amps_ref,
    wide,
    part_ref,
    later_ref,
    coef_ref,
    *rest,
):
    sent_refs, rest = rest[:ROUNDS], rest[ROUNDS:]
    table, spots_ref, traces_ref, ids_ref, prev_ref, sems = rest

    levels, extent, across = ids_ref.shape
    shape = (extent, across)
    regions = table_hbm.shape[1]
    end = LEAD + extent
    rows = pl.ds(LEAD, extent)
    moves = [(table_hbm, table), (spots_hbm, spots_ref), (traces_hbm, traces_ref)]
    for begin in range(0, levels, levels // 2):
        part = pl.ds(begin, levels // 2)
        moves += [
            (src_now.at[0, part], wide.at[0, part, rows, :]),
            (rec_now.at[0, part], wide.at[1, part, rows, :]),
            (ids_hbm.at[part], ids_ref.at[part]),
            (src_prev.at[0, part], prev_ref.at[0, part]),
            (rec_prev.at[0, part], prev_ref.at[1, part]),
        ]
    moves.append((amps_hbm, amps_ref))
    copies = [
        pltpu.make_async_copy(here, there, sems.at[i]) for i, (here, there) in enumerate(moves)
    ]
    for copy in copies:
        copy.start()
    zeros = jnp.zeros((LEAD, across), jnp.float32)
    for field in range(2):
        for level in range(levels):
            wide[field, level, 0:LEAD, :] = zeros
            wide[field, level, end : end + LEAD, :] = zeros
    weights = lane_weights(shape)
    my_round = lax.rem(lax.axis_index("tile"), ROUNDS)
    for copy in copies:
        copy.wait()

    def send(place, rows, value):
        low = value[0:HALO, :]
        high = value[extent - HALO : extent, :]
        for number, sent_ref in enumerate(sent_refs):
            sent_ref[place, rows, :] = jnp.where(my_round == number, high, low)

    spots = spots_ref[...]
    column = lax.broadcasted_iota(jnp.int32, (extent, spots.shape[1]), 0) * across
    in_column = (spots >= column) & (spots < column + across)
    lane = lax.broadcasted_iota(jnp.int32, (across, spots.shape[1]), 0)
    in_row = jnp.where(lax.rem(spots, across) == lane, 1.0, 0.0)
    traces = jnp.concatenate(
        [jnp.where(in_column, traces_ref[0, t : t + 1, :], 0.0) for t in range(2)], axis=0
    )
    planes = lax.dot_general(
        traces,
        in_row,
        (((1,), (1,)), ((), ())),
        precision=lax.Precision.HIGHEST,
        preferred_element_type=jnp.float32,
    )

    speeds = jnp.concatenate(
        [table[...], jnp.zeros((1, across - regions), jnp.float32)], axis=1
    )
    speeds = jnp.broadcast_to(speeds, (8, across))
    for level in range(levels):
        for row in range(0, extent, 8):
            ids = ids_ref[level, row : row + 8, :]
            coef_ref[level, row : row + 8, :] = jnp.take_along_axis(
                speeds, ids, axis=1, mode="promise_in_bounds"
            )
        send(2 * levels + level // 2, pl.ds(level % 2 * HALO, HALO), coef_ref[level])

    for field in range(2):
        for level in range(levels):
            total = laplace_level(wide, field, level, levels, extent, weights)
            now = wide[field, level, LEAD:end, :]
            value = 2.0 * now - prev_ref[field, level] + coef_ref[level] * total
            later = -now
            if field == 1 and level == 0:
                value = value + planes[:extent, :]
                later = later + planes[extent:, :]
            part_ref[field, level] = value
            later_ref[field, level] = later
            place = field * levels + level
            send(place, pl.ds(0, HALO), now)
            send(place, pl.ds(HALO, HALO), value)


def both_steps(
    sides_ref,
    bits_ref,
    own,
    part_ref,
    later_ref,
    source_ref,
    source_later_ref,
    coef_ref,
    *rest,
):
    came_refs, (final_ref, *blocks, other, middle) = rest[:ROUNDS], rest[ROUNDS:]
    levels, extent, across = coef_ref.shape
    shape = (extent, across)
    share = blocks[0].shape[1]
    end = LEAD + extent
    my_round = sides_ref[0, 0:HALO, :]
    has_low = sides_ref[1, 0:HALO, :] != 0
    has_high = sides_ref[2, 0:HALO, :] != 0

    def received(place, rows):
        came = [ref[place, rows, :] for ref in came_refs]
        low, high = came[-1], came[0]
        for number in range(1, ROUNDS):
            low = jnp.where(my_round == number, came[number - 1], low)
            high = jnp.where(my_round == number, came[number], high)
        return jnp.where(has_low, low, 0.0), jnp.where(has_high, high, 0.0)

    for field in range(2):
        for level in range(levels):
            low, high = received(field * levels + level, pl.ds(0, HALO))
            other[field, level, LEAD:end, :] = jnp.zeros(shape, jnp.float32)
            other[field, level, LEAD - HALO : LEAD, :] = low
            other[field, level, end : end + HALO, :] = high
    for field in range(2):
        for level in range(levels):
            below = jnp.zeros((HALO, across), jnp.float32)
            above = jnp.zeros((HALO, across), jnp.float32)
            left = jnp.zeros((8, across), jnp.float32)
            right = jnp.zeros((8, across), jnp.float32)
            for k in range(1, HALO + 1):
                begin = LEAD - HALO + k
                below = below + COEFS[k] * own[field, level, begin : begin + HALO, :]
                above = above + COEFS[k] * own[field, level, end - k : end - k + HALO, :]
                left = left + COEFS[k] * other[field, level, LEAD - k : LEAD - k + 8, :]
                right = right + COEFS[k] * other[field, level, end - 8 + k : end + k, :]
            low, high = received(field * levels + level, pl.ds(HALO, HALO))
            low_coef, high_coef = received(
                2 * levels + level // 2, pl.ds(level % 2 * HALO, HALO)
            )
            low = low + low_coef * below
            high = high + high_coef * above
            left = part_ref[field, level, 0:8, :] + coef_ref[level, 0:8, :] * left
            right = (
                part_ref[field, level, extent - 8 : extent, :]
                + coef_ref[level, extent - 8 : extent, :] * right
            )
            if field == 0:
                low = low + source_ref[level, LEAD - HALO : LEAD, :]
                left = left + source_ref[level, LEAD : LEAD + 8, :]
                right = right + source_ref[level, end - 8 : end, :]
                high = high + source_ref[level, end : end + HALO, :]
            middle[field, level, LEAD - HALO : LEAD, :] = low
            middle[field, level, LEAD : LEAD + 8, :] = left
            middle[field, level, end - 8 : end, :] = right
            middle[field, level, end : end + HALO, :] = high
    weights = lane_weights(shape)
    for field in range(2):
        for level in range(levels):
            total = laplace_level(middle, field, level, levels, extent, weights)
            later = source_later_ref[level] if field == 0 else later_ref[field, level]
            value = 2.0 * middle[field, level, LEAD:end, :] + later
            final_ref[field, level] = value + coef_ref[level] * total
    masks = [
        jnp.concatenate([bits_ref[bit]] * (extent // 8), axis=0) != 0
        for bit in range(bits_ref.shape[0])
    ]
    for field in range(2):
        for level in range(share):
            parts = [final_ref[field, place * share + level] for place in range(len(blocks))]
            for bit, mask in enumerate(masks):
                parts = [
                    jnp.where(mask, parts[place ^ (1 << bit)], parts[place])
                    for place in range(len(blocks))
                ]
            for block, part in zip(blocks, parts):
                block[field, level] = part


def widen(weight, masks, blocks, wide):
    mine_ref, came_last_ref, came_first_ref = blocks
    shots, _, share, extent, _ = mine_ref.shape
    up_first, inside = (
        jnp.concatenate([mask[...]] * (extent // 8), axis=0) != 0 for mask in masks
    )
    for shot in range(shots):
        for field in range(2):
            for level in range(share):
                scale = weight if field == 0 else 1.0
                first = scale * came_first_ref[shot, field, level]
                last = jnp.where(inside, scale * came_last_ref[shot, field, level], 0.0)
                wide[shot, field, level, 0:extent, :] = jnp.where(up_first, last, first)
                wide[shot, field, level, extent : 2 * extent, :] = (
                    scale * mine_ref[shot, field, level]
                )
                wide[shot, field, level, 2 * extent : 3 * extent, :] = jnp.where(
                    up_first, first, last
                )


def offset_product(wide, offset, level, total):
    extent = wide.shape[3] // 3
    lower = extent + REACH - offset
    upper = extent - REACH + offset
    for shot in range(wide.shape[0]):
        product = (
            wide[shot, 0, level, lower : lower + extent, :]
            * wide[shot, 1, level, upper : upper + extent, :]
        )
        total = product if total is None else total + product
    return total


def stack(*refs):
    for place in range(len(refs) - 1):
        refs[-1][place] = refs[place][...]


def write_fields(final_ref, src_hbm, rec_hbm, sems):
    copies = [
        pltpu.make_async_copy(final_ref.at[field], out.at[0], sems.at[field])
        for field, out in enumerate((src_hbm, rec_hbm))
    ]
    for copy in copies:
        copy.start()
    for copy in copies:
        copy.wait()


def image_products(weight, up_first_ref, inside_ref, *rest):
    groups, (image_hbm, *wides, image_ref, sems) = (rest[0:3], rest[3:6]), rest[6:]
    for blocks, wide in zip(groups, wides):
        widen(weight, (up_first_ref, inside_ref), blocks, wide)
    parts = sems.shape[0]
    copies = []
    for piece in range(parts):
        offsets = range(piece * OFFS // parts, (piece + 1) * OFFS // parts)
        for offset in offsets:
            for level in range(image_ref.shape[1]):
                total = None
                for wide in wides:
                    total = offset_product(wide, offset, level, total)
                image_ref[offset, level] = total
        rows = pl.ds(offsets[0], len(offsets))
        copy = pltpu.make_async_copy(image_ref.at[rows], image_hbm.at[rows], sems.at[piece])
        copy.start()
        copies.append(copy)
    for copy in copies:
        copy.wait()


def swap_tiles(value, lower):
    tiles, shots = lax.axis_size("tile"), lax.axis_size("shot")
    partner = {}
    for tile in lower:
        partner[tile], partner[tile + 1] = tile + 1, tile
    pairs = []
    for tile in range(tiles):
        for shot in range(shots):
            here = tile * shots + shot
            there = partner[tile] * shots + shot if tile in partner else here ^ 1
            pairs.append((here, there))
    return lax.ppermute(value, ("tile", "shot"), pairs)


def swap_sides(value):
    tiles = lax.axis_size("tile")
    came_last = swap_tiles(value, range(1, tiles - 1, 2))
    return swap_tiles(value, range(0, tiles - 1, 2)), came_last


def per_device(
    src_prev,
    src_now,
    rec_prev,
    rec_now,
    speed_table,
    region_ids,
    source_cell,
    wavelet,
    receiver_cell,
    receiver_data,
):
    _, levels, extent, across = src_now.shape
    tiles = lax.axis_size("tile")
    width = extent * tiles
    shots = lax.axis_size("shot")
    share = levels // shots
    params = pltpu.CompilerParams(vmem_limit_bytes=LIMIT)

    def struct(*shape):
        return jax.ShapeDtypeStruct(shape, jnp.float32)

    def scratch(*shape, dtype=jnp.float32):
        return pltpu.VMEM(shape, dtype)

    wide_shape = (2, levels, extent + 2 * LEAD, across)
    message = struct(2 * levels + levels // 2, 2 * HALO, across)
    amps, own, part, later, coef, *sent = pl.pallas_call(
        own_part,
        out_shape=(
            struct(*wavelet.shape),
            struct(*wide_shape),
            struct(2, levels, extent, across),
            struct(2, levels, extent, across),
            struct(levels, extent, across),
            *([message] * ROUNDS),
        ),
        in_specs=[HBM] * 9,
        out_specs=[VMEM] * (5 + ROUNDS),
        scratch_shapes=[
            scratch(1, speed_table.shape[0]),
            scratch(*receiver_cell.shape, dtype=jnp.int32),
            scratch(*receiver_data.shape),
            scratch(levels, extent, across, dtype=jnp.int32),
            scratch(2, levels, extent, across),
            pltpu.SemaphoreType.DMA((14,)),
        ],
        compiler_params=params,
        name="own_part",
    )(
        *(
            pltpu.with_memory_space_constraint(array, pltpu.HBM)
            for array in (
                speed_table.reshape(1, -1),
                receiver_cell,
                receiver_data,
                wavelet,
                region_ids,
                src_now,
                rec_now,
                src_prev,
                rec_prev,
            )
        )
    )
    sides = [
        swap_tiles(message, range(number, tiles - 1, ROUNDS)) for number, message in enumerate(sent)
    ]
    source, source_later, up_first, inside, edges, bits = pl.pallas_call(
        functools.partial(source_and_order, width),
        out_shape=(
            struct(levels, extent + 2 * LEAD, across),
            struct(levels, extent, across),
            jax.ShapeDtypeStruct((8, across), jnp.int32),
            jax.ShapeDtypeStruct((8, across), jnp.int32),
            jax.ShapeDtypeStruct((3, 8, across), jnp.int32),
            jax.ShapeDtypeStruct((shots.bit_length() - 1, 8, across), jnp.int32),
        ),
        in_specs=[SMEM] + [VMEM] * 2,
        out_specs=[VMEM] * 6,
        compiler_params=params,
        name="source_and_order",
    )(source_cell, amps, later)
    block = struct(2, share, extent, across)
    final, own_block, *blocks = pl.pallas_call(
        both_steps,
        out_shape=(struct(2, levels, extent, across), *([block] * shots)),
        in_specs=[VMEM] * (8 + ROUNDS),
        out_specs=[VMEM] * (1 + shots),
        scratch_shapes=[scratch(*wide_shape), scratch(*wide_shape)],
        compiler_params=params,
        name="both_steps",
    )(edges, bits, own, part, later, source, source_later, coef, *sides)
    came = [
        lax.ppermute(sent, "shot", [(shot, shot ^ (1 + i)) for shot in range(shots)])
        for i, sent in enumerate(blocks)
    ]
    weight = 1.0 / shots
    image_shape = (OFFS, share, extent, across)

    def wide_scratch(blocks):
        return scratch(blocks.shape[0], 2, share, 3 * extent, across)

    src_next, rec_next = pl.pallas_call(
        write_fields,
        out_shape=(struct(1, levels, extent, across), struct(1, levels, extent, across)),
        in_specs=[VMEM],
        out_specs=[HBM, HBM],
        scratch_shapes=[pltpu.SemaphoreType.DMA((2,))],
        compiler_params=params,
        name="write_fields",
    )(final)
    operands, wides = [], []
    for blocks in ([own_block, came[0]], came[:0:-1]):
        group = pl.pallas_call(
            stack,
            out_shape=struct(len(blocks), *own_block.shape),
            in_specs=[VMEM] * len(blocks),
            out_specs=VMEM,
            compiler_params=params,
            name="stack",
        )(*blocks)
        fields_first, fields_last = swap_sides(group)
        operands = [group, fields_last, fields_first, *operands]
        wides.insert(0, wide_scratch(group))
    image = pl.pallas_call(
        functools.partial(image_products, weight),
        out_shape=struct(*image_shape),
        in_specs=[VMEM] * (2 + len(operands)),
        out_specs=HBM,
        scratch_shapes=[*wides, scratch(*image_shape), pltpu.SemaphoreType.DMA((11,))],
        compiler_params=params,
        name="image_products",
    )(up_first, inside, *operands)
    return src_next, rec_next, image


def solution(mesh):
    field = P(("groups", "shot"), None, "tile", None)
    return jax.shard_map(
        per_device,
        mesh=mesh,
        in_specs=(
            field,
            field,
            field,
            field,
            P("groups"),
            P(None, ("groups", "tile"), None),
            P(("groups", "shot")),
            P(("groups", "shot"), None),
            P(("groups", "shot"), "tile"),
            P(("groups", "shot"), None, "tile"),
        ),
        out_specs=(field, field, P(None, "shot", ("groups", "tile"), None)),
        check_vma=False,
    )
```

```python
import functools

import jax
import jax.numpy as jnp
from jax import lax
from jax.experimental import pallas as pl
from jax.experimental.pallas import tpu as pltpu
from jax.sharding import PartitionSpec as P

OFFS = 33
REACH = OFFS // 2
HALO = 4
LEAD = 8
ROUNDS = 3
SHIFTS = {2: 1, 3: 0}

COEFS = (-205.0 / 72.0, 8.0 / 5.0, -1.0 / 5.0, 8.0 / 315.0, -1.0 / 560.0)

VMEM = pl.BlockSpec(memory_space=pltpu.VMEM)
HBM = pl.BlockSpec(memory_space=pltpu.HBM)
SMEM = pl.BlockSpec(memory_space=pltpu.SMEM)
LIMIT = 16 * 1024 * 1024


def lane_weights(shape):
    lane = lax.broadcasted_iota(jnp.int32, shape, 1)
    across = shape[1]
    after = [jnp.where(lane < across - k, COEFS[k], 0.0) for k in range(1, HALO + 1)]
    before = [jnp.where(lane >= k, COEFS[k], 0.0) for k in range(1, HALO + 1)]
    return after, before


def laplace_level(wide, field, level, levels, extent, weights):
    after, before = weights
    centre = wide[field, level, LEAD : LEAD + extent, :]
    across = centre.shape[1]
    total = 3.0 * COEFS[0] * centre
    for k in range(1, HALO + 1):
        beside = (
            wide[field, level, LEAD + k : LEAD + k + extent, :]
            + wide[field, level, LEAD - k : LEAD - k + extent, :]
        )
        if level + k < levels:
            beside = beside + wide[field, level + k, LEAD : LEAD + extent, :]
        if level - k >= 0:
            beside = beside + wide[field, level - k, LEAD : LEAD + extent, :]
        total = total + COEFS[k] * beside
        total = total + after[k - 1] * pltpu.roll(centre, across - k, 1)
        total = total + before[k - 1] * pltpu.roll(centre, k, 1)
    return total


def source_and_order(
    width, cell_ref, amps_ref, later_ref, source_ref, source_later_ref, sides_ref, bits_ref
):
    levels, extent, across = source_later_ref.shape
    cell = cell_ref[0]
    deep = lax.div(cell, width * across)
    row = lax.rem(lax.div(cell, across), width) - lax.axis_index("tile") * extent + LEAD
    shape = (extent + 2 * LEAD, across)
    rows = lax.broadcasted_iota(jnp.int32, shape, 0)
    lanes = lax.broadcasted_iota(jnp.int32, shape, 1)
    hit = jnp.where((rows == row) & (lanes == lax.rem(cell, across)), 1.0, 0.0)
    for level in range(levels):
        here = hit * jnp.where(deep == level, 1.0, 0.0)
        source_ref[level] = here * amps_ref[0:1, 0:1]
        source_later_ref[level] = (
            later_ref[0, level] + here[LEAD : LEAD + extent, :] * amps_ref[0:1, 1:2]
        )
    tile, tiles = lax.axis_index("tile"), lax.axis_size("tile")
    places = (jnp.where(tile > 0, 1, 0), jnp.where(tile < tiles - 1, 1, 0))
    places += tuple((tile + SHIFTS[rounds]) % rounds for rounds in (2, 3))
    for place, value in enumerate(places):
        sides_ref[place] = jnp.full(sides_ref.shape[1:], value, dtype=jnp.int32)
    shot = jnp.full(bits_ref.shape[1:], lax.axis_index("shot"), dtype=jnp.int32)
    for bit in range(bits_ref.shape[0]):
        bits_ref[bit] = shot & (1 << bit)


def own_part(
    table_hbm,
    spots_hbm,
    traces_hbm,
    amps_hbm,
    ids_hbm,
    src_now,
    rec_now,
    src_prev,
    rec_prev,
    amps_ref,
    wide,
    part_ref,
    later_ref,
    coef_ref,
    *rest,
):
    sent_refs, rest = rest[:ROUNDS], rest[ROUNDS:]
    table, spots_ref, traces_ref, ids_ref, prev_ref, sems = rest

    levels, extent, across = ids_ref.shape
    shape = (extent, across)
    regions = table_hbm.shape[1]
    end = LEAD + extent
    rows = pl.ds(LEAD, extent)
    moves = [(table_hbm, table), (spots_hbm, spots_ref), (traces_hbm, traces_ref)]
    for begin in range(0, levels, levels // 2):
        part = pl.ds(begin, levels // 2)
        moves += [
            (src_now.at[0, part], wide.at[0, part, rows, :]),
            (rec_now.at[0, part], wide.at[1, part, rows, :]),
            (ids_hbm.at[part], ids_ref.at[part]),
            (src_prev.at[0, part], prev_ref.at[0, part]),
            (rec_prev.at[0, part], prev_ref.at[1, part]),
        ]
    moves.append((amps_hbm, amps_ref))
    copies = [
        pltpu.make_async_copy(here, there, sems.at[i]) for i, (here, there) in enumerate(moves)
    ]
    for copy in copies:
        copy.start()
    zeros = jnp.zeros((LEAD, across), jnp.float32)
    for field in range(2):
        for level in range(levels):
            wide[field, level, 0:LEAD, :] = zeros
            wide[field, level, end : end + LEAD, :] = zeros
    weights = lane_weights(shape)
    my_round = lax.rem(lax.axis_index("tile"), ROUNDS)
    for copy in copies:
        copy.wait()

    def send(place, rows, value):
        low = value[0:HALO, :]
        high = value[extent - HALO : extent, :]
        for number, sent_ref in enumerate(sent_refs):
            sent_ref[place, rows, :] = jnp.where(my_round == number, high, low)

    spots = spots_ref[...]
    column = lax.broadcasted_iota(jnp.int32, (extent, spots.shape[1]), 0) * across
    in_column = (spots >= column) & (spots < column + across)
    lane = lax.broadcasted_iota(jnp.int32, (across, spots.shape[1]), 0)
    in_row = jnp.where(lax.rem(spots, across) == lane, 1.0, 0.0)
    traces = jnp.concatenate(
        [jnp.where(in_column, traces_ref[0, t : t + 1, :], 0.0) for t in range(2)], axis=0
    )
    planes = lax.dot_general(
        traces,
        in_row,
        (((1,), (1,)), ((), ())),
        precision=lax.Precision.HIGHEST,
        preferred_element_type=jnp.float32,
    )

    speeds = jnp.concatenate(
        [table[...], jnp.zeros((1, across - regions), jnp.float32)], axis=1
    )
    speeds = jnp.broadcast_to(speeds, (8, across))
    for level in range(levels):
        for row in range(0, extent, 8):
            ids = ids_ref[level, row : row + 8, :]
            coef_ref[level, row : row + 8, :] = jnp.take_along_axis(
                speeds, ids, axis=1, mode="promise_in_bounds"
            )
        send(2 * levels + level // 2, pl.ds(level % 2 * HALO, HALO), coef_ref[level])

    for field in range(2):
        for level in range(levels):
            total = laplace_level(wide, field, level, levels, extent, weights)
            now = wide[field, level, LEAD:end, :]
            value = 2.0 * now - prev_ref[field, level] + coef_ref[level] * total
            later = -now
            if field == 1 and level == 0:
                value = value + planes[:extent, :]
                later = later + planes[extent:, :]
            part_ref[field, level] = value
            later_ref[field, level] = later
            place = field * levels + level
            send(place, pl.ds(0, HALO), now)
            send(place, pl.ds(HALO, HALO), value)


def both_sides(sides, came):
    has_low, has_high, my_round = sides[0], sides[1], sides[len(came)]
    low, high = came[-1], came[0]
    for number in range(1, len(came)):
        low = jnp.where(my_round == number, came[number - 1], low)
        high = jnp.where(my_round == number, came[number], high)
    return jnp.where(has_low != 0, low, 0.0), jnp.where(has_high != 0, high, 0.0)


def both_steps(
    sides_ref,
    bits_ref,
    own,
    part_ref,
    later_ref,
    source_ref,
    source_later_ref,
    coef_ref,
    *rest,
):
    came_refs, (final_ref, *blocks, other, middle) = rest[:ROUNDS], rest[ROUNDS:]
    levels, extent, across = coef_ref.shape
    shape = (extent, across)
    share = blocks[0].shape[1]
    end = LEAD + extent
    sides = [sides_ref[place, 0:HALO, :] for place in range(4)]

    def received(place, rows):
        return both_sides(sides, [ref[place, rows, :] for ref in came_refs])

    for field in range(2):
        for level in range(levels):
            low, high = received(field * levels + level, pl.ds(0, HALO))
            other[field, level, LEAD:end, :] = jnp.zeros(shape, jnp.float32)
            other[field, level, LEAD - HALO : LEAD, :] = low
            other[field, level, end : end + HALO, :] = high
    for field in range(2):
        for level in range(levels):
            below = jnp.zeros((HALO, across), jnp.float32)
            above = jnp.zeros((HALO, across), jnp.float32)
            left = jnp.zeros((8, across), jnp.float32)
            right = jnp.zeros((8, across), jnp.float32)
            for k in range(1, HALO + 1):
                begin = LEAD - HALO + k
                below = below + COEFS[k] * own[field, level, begin : begin + HALO, :]
                above = above + COEFS[k] * own[field, level, end - k : end - k + HALO, :]
                left = left + COEFS[k] * other[field, level, LEAD - k : LEAD - k + 8, :]
                right = right + COEFS[k] * other[field, level, end - 8 + k : end + k, :]
            low, high = received(field * levels + level, pl.ds(HALO, HALO))
            low_coef, high_coef = received(
                2 * levels + level // 2, pl.ds(level % 2 * HALO, HALO)
            )
            low = low + low_coef * below
            high = high + high_coef * above
            left = part_ref[field, level, 0:8, :] + coef_ref[level, 0:8, :] * left
            right = (
                part_ref[field, level, extent - 8 : extent, :]
                + coef_ref[level, extent - 8 : extent, :] * right
            )
            if field == 0:
                low = low + source_ref[level, LEAD - HALO : LEAD, :]
                left = left + source_ref[level, LEAD : LEAD + 8, :]
                right = right + source_ref[level, end - 8 : end, :]
                high = high + source_ref[level, end : end + HALO, :]
            middle[field, level, LEAD - HALO : LEAD, :] = low
            middle[field, level, LEAD : LEAD + 8, :] = left
            middle[field, level, end - 8 : end, :] = right
            middle[field, level, end : end + HALO, :] = high
    weights = lane_weights(shape)
    for field in range(2):
        for level in range(levels):
            total = laplace_level(middle, field, level, levels, extent, weights)
            later = source_later_ref[level] if field == 0 else later_ref[field, level]
            value = 2.0 * middle[field, level, LEAD:end, :] + later
            final_ref[field, level] = value + coef_ref[level] * total
    masks = [
        jnp.concatenate([bits_ref[bit]] * (extent // 8), axis=0) != 0
        for bit in range(bits_ref.shape[0])
    ]
    for field in range(2):
        for level in range(share):
            parts = [final_ref[field, place * share + level] for place in range(len(blocks))]
            for bit, mask in enumerate(masks):
                parts = [
                    jnp.where(mask, parts[place ^ (1 << bit)], parts[place])
                    for place in range(len(blocks))
                ]
            for block, part in zip(blocks, parts):
                block[field, level] = part


def widen(weight, sides_ref, blocks, wide):
    mine_ref, *came_refs = blocks
    shots, _, share, extent, _ = mine_ref.shape
    sides = [
        jnp.concatenate([sides_ref[place]] * (extent // 8), axis=0) for place in range(4)
    ]
    for shot in range(shots):
        for field in range(2):
            for level in range(share):
                scale = weight if field == 0 else 1.0
                low, high = both_sides(sides, [ref[shot, field, level] for ref in came_refs])
                wide[shot, field, level, 0:extent, :] = scale * low
                wide[shot, field, level, extent : 2 * extent, :] = (
                    scale * mine_ref[shot, field, level]
                )
                wide[shot, field, level, 2 * extent : 3 * extent, :] = scale * high


def offset_product(wide, offset, level, total):
    extent = wide.shape[3] // 3
    lower = extent + REACH - offset
    upper = extent - REACH + offset
    for shot in range(wide.shape[0]):
        product = (
            wide[shot, 0, level, lower : lower + extent, :]
            * wide[shot, 1, level, upper : upper + extent, :]
        )
        total = product if total is None else total + product
    return total


def stack(*refs):
    for place in range(len(refs) - 1):
        refs[-1][place] = refs[place][...]


def write_fields(final_ref, src_hbm, rec_hbm, sems):
    copies = [
        pltpu.make_async_copy(final_ref.at[field], out.at[0], sems.at[field])
        for field, out in enumerate((src_hbm, rec_hbm))
    ]
    for copy in copies:
        copy.start()
    for copy in copies:
        copy.wait()


def image_products(weight, rounds, sides_ref, *rest):
    groups, begin = [], 0
    for count in rounds:
        mine_ref, *came_refs = rest[begin : begin + 1 + count]
        groups.append((mine_ref, *came_refs[::-1]))
        begin += 1 + count
    image_hbm, *wides, image_ref, sems = rest[begin:]
    for blocks, wide in zip(groups, wides):
        widen(weight, sides_ref, blocks, wide)
    parts = sems.shape[0]
    copies = []
    for piece in range(parts):
        offsets = range(piece * OFFS // parts, (piece + 1) * OFFS // parts)
        for offset in offsets:
            for level in range(image_ref.shape[1]):
                total = None
                for wide in wides:
                    total = offset_product(wide, offset, level, total)
                image_ref[offset, level] = total
        rows = pl.ds(offsets[0], len(offsets))
        copy = pltpu.make_async_copy(image_ref.at[rows], image_hbm.at[rows], sems.at[piece])
        copy.start()
        copies.append(copy)
    for copy in copies:
        copy.wait()


def swap_tiles(value, lower):
    tiles, shots = lax.axis_size("tile"), lax.axis_size("shot")
    partner = {}
    for tile in lower:
        partner[tile], partner[tile + 1] = tile + 1, tile
    pairs = []
    for tile in range(tiles):
        for shot in range(shots):
            here = tile * shots + shot
            there = partner[tile] * shots + shot if tile in partner else here ^ 1
            pairs.append((here, there))
    return lax.ppermute(value, ("tile", "shot"), pairs)


def swap_rounds(values):
    tiles, rounds = lax.axis_size("tile"), len(values)
    return [
        swap_tiles(value, range((number - SHIFTS[rounds]) % rounds, tiles - 1, rounds))
        for number, value in enumerate(values)
    ]


def per_device(
    src_prev,
    src_now,
    rec_prev,
    rec_now,
    speed_table,
    region_ids,
    source_cell,
    wavelet,
    receiver_cell,
    receiver_data,
):
    _, levels, extent, across = src_now.shape
    tiles = lax.axis_size("tile")
    width = extent * tiles
    shots = lax.axis_size("shot")
    share = levels // shots
    params = pltpu.CompilerParams(vmem_limit_bytes=LIMIT)

    def struct(*shape):
        return jax.ShapeDtypeStruct(shape, jnp.float32)

    def scratch(*shape, dtype=jnp.float32):
        return pltpu.VMEM(shape, dtype)

    wide_shape = (2, levels, extent + 2 * LEAD, across)
    message = struct(2 * levels + levels // 2, 2 * HALO, across)
    amps, own, part, later, coef, *sent = pl.pallas_call(
        own_part,
        out_shape=(
            struct(*wavelet.shape),
            struct(*wide_shape),
            struct(2, levels, extent, across),
            struct(2, levels, extent, across),
            struct(levels, extent, across),
            *([message] * ROUNDS),
        ),
        in_specs=[HBM] * 9,
        out_specs=[VMEM] * (5 + ROUNDS),
        scratch_shapes=[
            scratch(1, speed_table.shape[0]),
            scratch(*receiver_cell.shape, dtype=jnp.int32),
            scratch(*receiver_data.shape),
            scratch(levels, extent, across, dtype=jnp.int32),
            scratch(2, levels, extent, across),
            pltpu.SemaphoreType.DMA((14,)),
        ],
        compiler_params=params,
        name="own_part",
    )(
        *(
            pltpu.with_memory_space_constraint(array, pltpu.HBM)
            for array in (
                speed_table.reshape(1, -1),
                receiver_cell,
                receiver_data,
                wavelet,
                region_ids,
                src_now,
                rec_now,
                src_prev,
                rec_prev,
            )
        )
    )
    came_sides = swap_rounds(sent)
    source, source_later, sides, bits = pl.pallas_call(
        functools.partial(source_and_order, width),
        out_shape=(
            struct(levels, extent + 2 * LEAD, across),
            struct(levels, extent, across),
            jax.ShapeDtypeStruct((4, 8, across), jnp.int32),
            jax.ShapeDtypeStruct((shots.bit_length() - 1, 8, across), jnp.int32),
        ),
        in_specs=[SMEM] + [VMEM] * 2,
        out_specs=[VMEM] * 4,
        compiler_params=params,
        name="source_and_order",
    )(source_cell, amps, later)
    block = struct(2, share, extent, across)
    final, own_block, *blocks = pl.pallas_call(
        both_steps,
        out_shape=(struct(2, levels, extent, across), *([block] * shots)),
        in_specs=[VMEM] * (8 + ROUNDS),
        out_specs=[VMEM] * (1 + shots),
        scratch_shapes=[scratch(*wide_shape), scratch(*wide_shape)],
        compiler_params=params,
        name="both_steps",
    )(sides, bits, own, part, later, source, source_later, coef, *came_sides)
    came = [
        lax.ppermute(sent, "shot", [(shot, shot ^ (1 + i)) for shot in range(shots)])
        for i, sent in enumerate(blocks)
    ]
    weight = 1.0 / shots
    image_shape = (OFFS, share, extent, across)

    def wide_scratch(blocks):
        return scratch(blocks.shape[0], 2, share, 3 * extent, across)

    src_next, rec_next = pl.pallas_call(
        write_fields,
        out_shape=(struct(1, levels, extent, across), struct(1, levels, extent, across)),
        in_specs=[VMEM],
        out_specs=[HBM, HBM],
        scratch_shapes=[pltpu.SemaphoreType.DMA((2,))],
        compiler_params=params,
        name="write_fields",
    )(final)
    operands, wides, rounds = [], [], []
    for blocks, count in (([own_block, came[0]], 2), (came[1:], 3)):
        group = pl.pallas_call(
            stack,
            out_shape=struct(len(blocks), *own_block.shape),
            in_specs=[VMEM] * len(blocks),
            out_specs=VMEM,
            compiler_params=params,
            name="stack",
        )(*blocks)
        operands = [group, *swap_rounds([group] * count)[::-1], *operands]
        wides.insert(0, wide_scratch(group))
        rounds.insert(0, count)
    image = pl.pallas_call(
        functools.partial(image_products, weight, rounds),
        out_shape=struct(*image_shape),
        in_specs=[VMEM] * (1 + len(operands)),
        out_specs=HBM,
        scratch_shapes=[*wides, scratch(*image_shape), pltpu.SemaphoreType.DMA((11,))],
        compiler_params=params,
        name="image_products",
    )(sides, *operands)
    return src_next, rec_next, image


def solution(mesh):
    field = P(("groups", "shot"), None, "tile", None)
    return jax.shard_map(
        per_device,
        mesh=mesh,
        in_specs=(
            field,
            field,
            field,
            field,
            P("groups"),
            P(None, ("groups", "tile"), None),
            P(("groups", "shot")),
            P(("groups", "shot"), None),
            P(("groups", "shot"), "tile"),
            P(("groups", "shot"), None, "tile"),
        ),
        out_specs=(field, field, P(None, "shot", ("groups", "tile"), None)),
        check_vma=False,
    )
```

```python
import functools

import jax
import jax.numpy as jnp
from jax import lax
from jax.experimental import pallas as pl
from jax.experimental.pallas import tpu as pltpu
from jax.sharding import PartitionSpec as P

OFFS = 33
REACH = OFFS // 2
HALO = 4
LEAD = 8
ROUNDS = 3
SHIFTS = {2: 0, 3: 0}

COEFS = (-205.0 / 72.0, 8.0 / 5.0, -1.0 / 5.0, 8.0 / 315.0, -1.0 / 560.0)

VMEM = pl.BlockSpec(memory_space=pltpu.VMEM)
HBM = pl.BlockSpec(memory_space=pltpu.HBM)
SMEM = pl.BlockSpec(memory_space=pltpu.SMEM)
LIMIT = 16 * 1024 * 1024


def lane_weights(shape):
    lane = lax.broadcasted_iota(jnp.int32, shape, 1)
    across = shape[1]
    after = [jnp.where(lane < across - k, COEFS[k], 0.0) for k in range(1, HALO + 1)]
    before = [jnp.where(lane >= k, COEFS[k], 0.0) for k in range(1, HALO + 1)]
    return after, before


def laplace_level(wide, field, level, levels, extent, weights):
    after, before = weights
    centre = wide[field, level, LEAD : LEAD + extent, :]
    across = centre.shape[1]
    total = 3.0 * COEFS[0] * centre
    for k in range(1, HALO + 1):
        beside = (
            wide[field, level, LEAD + k : LEAD + k + extent, :]
            + wide[field, level, LEAD - k : LEAD - k + extent, :]
        )
        if level + k < levels:
            beside = beside + wide[field, level + k, LEAD : LEAD + extent, :]
        if level - k >= 0:
            beside = beside + wide[field, level - k, LEAD : LEAD + extent, :]
        total = total + COEFS[k] * beside
        total = total + after[k - 1] * pltpu.roll(centre, across - k, 1)
        total = total + before[k - 1] * pltpu.roll(centre, k, 1)
    return total


def source_and_order(
    width, cell_ref, amps_ref, later_ref, source_ref, source_later_ref, sides_ref, bits_ref
):
    levels, extent, across = source_later_ref.shape
    cell = cell_ref[0]
    deep = lax.div(cell, width * across)
    row = lax.rem(lax.div(cell, across), width) - lax.axis_index("tile") * extent + LEAD
    shape = (extent + 2 * LEAD, across)
    rows = lax.broadcasted_iota(jnp.int32, shape, 0)
    lanes = lax.broadcasted_iota(jnp.int32, shape, 1)
    hit = jnp.where((rows == row) & (lanes == lax.rem(cell, across)), 1.0, 0.0)
    for level in range(levels):
        here = hit * jnp.where(deep == level, 1.0, 0.0)
        source_ref[level] = here * amps_ref[0:1, 0:1]
        source_later_ref[level] = (
            later_ref[0, level] + here[LEAD : LEAD + extent, :] * amps_ref[0:1, 1:2]
        )
    tile, tiles = lax.axis_index("tile"), lax.axis_size("tile")
    places = (jnp.where(tile > 0, 1, 0), jnp.where(tile < tiles - 1, 1, 0))
    places += tuple((tile + SHIFTS[rounds]) % rounds for rounds in (2, 3))
    for place, value in enumerate(places):
        sides_ref[place] = jnp.full(sides_ref.shape[1:], value, dtype=jnp.int32)
    shot = jnp.full(bits_ref.shape[1:], lax.axis_index("shot"), dtype=jnp.int32)
    for bit in range(bits_ref.shape[0]):
        bits_ref[bit] = shot & (1 << bit)


def own_part(
    table_hbm,
    spots_hbm,
    traces_hbm,
    amps_hbm,
    ids_hbm,
    src_now,
    rec_now,
    src_prev,
    rec_prev,
    amps_ref,
    wide,
    part_ref,
    later_ref,
    coef_ref,
    *rest,
):
    sent_refs, rest = rest[:ROUNDS], rest[ROUNDS:]
    table, spots_ref, traces_ref, ids_ref, prev_ref, sems = rest

    levels, extent, across = ids_ref.shape
    shape = (extent, across)
    regions = table_hbm.shape[1]
    end = LEAD + extent
    rows = pl.ds(LEAD, extent)
    moves = [(table_hbm, table), (spots_hbm, spots_ref), (traces_hbm, traces_ref)]
    for begin in range(0, levels, levels // 2):
        part = pl.ds(begin, levels // 2)
        moves += [
            (src_now.at[0, part], wide.at[0, part, rows, :]),
            (rec_now.at[0, part], wide.at[1, part, rows, :]),
            (ids_hbm.at[part], ids_ref.at[part]),
            (src_prev.at[0, part], prev_ref.at[0, part]),
            (rec_prev.at[0, part], prev_ref.at[1, part]),
        ]
    moves.append((amps_hbm, amps_ref))
    copies = [
        pltpu.make_async_copy(here, there, sems.at[i]) for i, (here, there) in enumerate(moves)
    ]
    for copy in copies:
        copy.start()
    zeros = jnp.zeros((LEAD, across), jnp.float32)
    for field in range(2):
        for level in range(levels):
            wide[field, level, 0:LEAD, :] = zeros
            wide[field, level, end : end + LEAD, :] = zeros
    weights = lane_weights(shape)
    my_round = lax.rem(lax.axis_index("tile"), ROUNDS)
    for copy in copies:
        copy.wait()

    def send(place, rows, value):
        low = value[0:HALO, :]
        high = value[extent - HALO : extent, :]
        for number, sent_ref in enumerate(sent_refs):
            sent_ref[place, rows, :] = jnp.where(my_round == number, high, low)

    spots = spots_ref[...]
    column = lax.broadcasted_iota(jnp.int32, (extent, spots.shape[1]), 0) * across
    in_column = (spots >= column) & (spots < column + across)
    lane = lax.broadcasted_iota(jnp.int32, (across, spots.shape[1]), 0)
    in_row = jnp.where(lax.rem(spots, across) == lane, 1.0, 0.0)
    traces = jnp.concatenate(
        [jnp.where(in_column, traces_ref[0, t : t + 1, :], 0.0) for t in range(2)], axis=0
    )
    planes = lax.dot_general(
        traces,
        in_row,
        (((1,), (1,)), ((), ())),
        precision=lax.Precision.HIGHEST,
        preferred_element_type=jnp.float32,
    )

    speeds = jnp.concatenate(
        [table[...], jnp.zeros((1, across - regions), jnp.float32)], axis=1
    )
    speeds = jnp.broadcast_to(speeds, (8, across))
    for level in range(levels):
        for row in range(0, extent, 8):
            ids = ids_ref[level, row : row + 8, :]
            coef_ref[level, row : row + 8, :] = jnp.take_along_axis(
                speeds, ids, axis=1, mode="promise_in_bounds"
            )
        send(2 * levels + level // 2, pl.ds(level % 2 * HALO, HALO), coef_ref[level])

    for field in range(2):
        for level in range(levels):
            total = laplace_level(wide, field, level, levels, extent, weights)
            now = wide[field, level, LEAD:end, :]
            value = 2.0 * now - prev_ref[field, level] + coef_ref[level] * total
            later = -now
            if field == 1 and level == 0:
                value = value + planes[:extent, :]
                later = later + planes[extent:, :]
            part_ref[field, level] = value
            later_ref[field, level] = later
            place = field * levels + level
            send(place, pl.ds(0, HALO), now)
            send(place, pl.ds(HALO, HALO), value)


def both_sides(sides, came):
    has_low, has_high, my_round = sides[0], sides[1], sides[len(came)]
    low, high = came[-1], came[0]
    for number in range(1, len(came)):
        low = jnp.where(my_round == number, came[number - 1], low)
        high = jnp.where(my_round == number, came[number], high)
    return jnp.where(has_low != 0, low, 0.0), jnp.where(has_high != 0, high, 0.0)


def both_steps(
    sides_ref,
    bits_ref,
    own,
    part_ref,
    later_ref,
    source_ref,
    source_later_ref,
    coef_ref,
    *rest,
):
    came_refs, (final_ref, *blocks, other, middle) = rest[:ROUNDS], rest[ROUNDS:]
    levels, extent, across = coef_ref.shape
    shape = (extent, across)
    share = blocks[0].shape[1]
    end = LEAD + extent
    sides = [sides_ref[place, 0:HALO, :] for place in range(4)]

    def received(place, rows):
        return both_sides(sides, [ref[place, rows, :] for ref in came_refs])

    for field in range(2):
        for level in range(levels):
            low, high = received(field * levels + level, pl.ds(0, HALO))
            other[field, level, LEAD:end, :] = jnp.zeros(shape, jnp.float32)
            other[field, level, LEAD - HALO : LEAD, :] = low
            other[field, level, end : end + HALO, :] = high
    for field in range(2):
        for level in range(levels):
            below = jnp.zeros((HALO, across), jnp.float32)
            above = jnp.zeros((HALO, across), jnp.float32)
            left = jnp.zeros((8, across), jnp.float32)
            right = jnp.zeros((8, across), jnp.float32)
            for k in range(1, HALO + 1):
                begin = LEAD - HALO + k
                below = below + COEFS[k] * own[field, level, begin : begin + HALO, :]
                above = above + COEFS[k] * own[field, level, end - k : end - k + HALO, :]
                left = left + COEFS[k] * other[field, level, LEAD - k : LEAD - k + 8, :]
                right = right + COEFS[k] * other[field, level, end - 8 + k : end + k, :]
            low, high = received(field * levels + level, pl.ds(HALO, HALO))
            low_coef, high_coef = received(
                2 * levels + level // 2, pl.ds(level % 2 * HALO, HALO)
            )
            low = low + low_coef * below
            high = high + high_coef * above
            left = part_ref[field, level, 0:8, :] + coef_ref[level, 0:8, :] * left
            right = (
                part_ref[field, level, extent - 8 : extent, :]
                + coef_ref[level, extent - 8 : extent, :] * right
            )
            if field == 0:
                low = low + source_ref[level, LEAD - HALO : LEAD, :]
                left = left + source_ref[level, LEAD : LEAD + 8, :]
                right = right + source_ref[level, end - 8 : end, :]
                high = high + source_ref[level, end : end + HALO, :]
            middle[field, level, LEAD - HALO : LEAD, :] = low
            middle[field, level, LEAD : LEAD + 8, :] = left
            middle[field, level, end - 8 : end, :] = right
            middle[field, level, end : end + HALO, :] = high
    weights = lane_weights(shape)
    for field in range(2):
        for level in range(levels):
            total = laplace_level(middle, field, level, levels, extent, weights)
            later = source_later_ref[level] if field == 0 else later_ref[field, level]
            value = 2.0 * middle[field, level, LEAD:end, :] + later
            final_ref[field, level] = value + coef_ref[level] * total
    masks = [
        jnp.concatenate([bits_ref[bit]] * (extent // 8), axis=0) != 0
        for bit in range(bits_ref.shape[0])
    ]
    for field in range(2):
        for level in range(share):
            parts = [final_ref[field, place * share + level] for place in range(len(blocks))]
            for bit, mask in enumerate(masks):
                parts = [
                    jnp.where(mask, parts[place ^ (1 << bit)], parts[place])
                    for place in range(len(blocks))
                ]
            for block, part in zip(blocks, parts):
                block[field, level] = part


def widen(weight, sides_ref, blocks, wide):
    mine_ref, *came_refs = blocks
    shots, _, share, extent, _ = mine_ref.shape
    sides = [
        jnp.concatenate([sides_ref[place]] * (extent // 8), axis=0) for place in range(4)
    ]
    for shot in range(shots):
        for field in range(2):
            for level in range(share):
                scale = weight if field == 0 else 1.0
                low, high = both_sides(sides, [ref[shot, field, level] for ref in came_refs])
                wide[shot, field, level, 0:extent, :] = scale * low
                wide[shot, field, level, extent : 2 * extent, :] = (
                    scale * mine_ref[shot, field, level]
                )
                wide[shot, field, level, 2 * extent : 3 * extent, :] = scale * high


def offset_product(wide, offset, level, total):
    extent = wide.shape[3] // 3
    lower = extent + REACH - offset
    upper = extent - REACH + offset
    for shot in range(wide.shape[0]):
        product = (
            wide[shot, 0, level, lower : lower + extent, :]
            * wide[shot, 1, level, upper : upper + extent, :]
        )
        total = product if total is None else total + product
    return total


def stack(*refs):
    for place in range(len(refs) - 1):
        refs[-1][place] = refs[place][...]


def write_fields(final_ref, src_hbm, rec_hbm, sems):
    copies = [
        pltpu.make_async_copy(final_ref.at[field], out.at[0], sems.at[field])
        for field, out in enumerate((src_hbm, rec_hbm))
    ]
    for copy in copies:
        copy.start()
    for copy in copies:
        copy.wait()


def image_products(weight, rounds, sides_ref, *rest):
    groups, begin = [], 0
    for count in rounds:
        mine_ref, *came_refs = rest[begin : begin + 1 + count]
        groups.append((mine_ref, *came_refs[::-1]))
        begin += 1 + count
    image_hbm, *wides, image_ref, sems = rest[begin:]
    for blocks, wide in zip(groups, wides):
        widen(weight, sides_ref, blocks, wide)
    parts = sems.shape[0]
    copies = []
    for piece in range(parts):
        offsets = range(piece * OFFS // parts, (piece + 1) * OFFS // parts)
        for offset in offsets:
            for level in range(image_ref.shape[1]):
                total = None
                for wide in wides:
                    total = offset_product(wide, offset, level, total)
                image_ref[offset, level] = total
        rows = pl.ds(offsets[0], len(offsets))
        copy = pltpu.make_async_copy(image_ref.at[rows], image_hbm.at[rows], sems.at[piece])
        copy.start()
        copies.append(copy)
    for copy in copies:
        copy.wait()


def swap_tiles(value, lower):
    tiles, shots = lax.axis_size("tile"), lax.axis_size("shot")
    partner = {}
    for tile in lower:
        partner[tile], partner[tile + 1] = tile + 1, tile
    pairs = []
    for tile in range(tiles):
        for shot in range(shots):
            here = tile * shots + shot
            there = partner[tile] * shots + shot if tile in partner else here ^ 1
            pairs.append((here, there))
    return lax.ppermute(value, ("tile", "shot"), pairs)


def swap_rounds(values):
    tiles, rounds = lax.axis_size("tile"), len(values)
    return [
        swap_tiles(value, range((number - SHIFTS[rounds]) % rounds, tiles - 1, rounds))
        for number, value in enumerate(values)
    ]


def per_device(
    src_prev,
    src_now,
    rec_prev,
    rec_now,
    speed_table,
    region_ids,
    source_cell,
    wavelet,
    receiver_cell,
    receiver_data,
):
    _, levels, extent, across = src_now.shape
    tiles = lax.axis_size("tile")
    width = extent * tiles
    shots = lax.axis_size("shot")
    share = levels // shots
    params = pltpu.CompilerParams(vmem_limit_bytes=LIMIT)

    def struct(*shape):
        return jax.ShapeDtypeStruct(shape, jnp.float32)

    def scratch(*shape, dtype=jnp.float32):
        return pltpu.VMEM(shape, dtype)

    wide_shape = (2, levels, extent + 2 * LEAD, across)
    message = struct(2 * levels + levels // 2, 2 * HALO, across)
    amps, own, part, later, coef, *sent = pl.pallas_call(
        own_part,
        out_shape=(
            struct(*wavelet.shape),
            struct(*wide_shape),
            struct(2, levels, extent, across),
            struct(2, levels, extent, across),
            struct(levels, extent, across),
            *([message] * ROUNDS),
        ),
        in_specs=[HBM] * 9,
        out_specs=[VMEM] * (5 + ROUNDS),
        scratch_shapes=[
            scratch(1, speed_table.shape[0]),
            scratch(*receiver_cell.shape, dtype=jnp.int32),
            scratch(*receiver_data.shape),
            scratch(levels, extent, across, dtype=jnp.int32),
            scratch(2, levels, extent, across),
            pltpu.SemaphoreType.DMA((14,)),
        ],
        compiler_params=params,
        name="own_part",
    )(
        *(
            pltpu.with_memory_space_constraint(array, pltpu.HBM)
            for array in (
                speed_table.reshape(1, -1),
                receiver_cell,
                receiver_data,
                wavelet,
                region_ids,
                src_now,
                rec_now,
                src_prev,
                rec_prev,
            )
        )
    )
    came_sides = swap_rounds(sent)
    source, source_later, sides, bits = pl.pallas_call(
        functools.partial(source_and_order, width),
        out_shape=(
            struct(levels, extent + 2 * LEAD, across),
            struct(levels, extent, across),
            jax.ShapeDtypeStruct((4, 8, across), jnp.int32),
            jax.ShapeDtypeStruct((shots.bit_length() - 1, 8, across), jnp.int32),
        ),
        in_specs=[SMEM] + [VMEM] * 2,
        out_specs=[VMEM] * 4,
        compiler_params=params,
        name="source_and_order",
    )(source_cell, amps, later)
    block = struct(2, share, extent, across)
    final, own_block, *blocks = pl.pallas_call(
        both_steps,
        out_shape=(struct(2, levels, extent, across), *([block] * shots)),
        in_specs=[VMEM] * (8 + ROUNDS),
        out_specs=[VMEM] * (1 + shots),
        scratch_shapes=[scratch(*wide_shape), scratch(*wide_shape)],
        compiler_params=params,
        name="both_steps",
    )(sides, bits, own, part, later, source, source_later, coef, *came_sides)
    came = [
        lax.ppermute(sent, "shot", [(shot, shot ^ (1 + i)) for shot in range(shots)])
        for i, sent in enumerate(blocks)
    ]
    weight = 1.0 / shots
    image_shape = (OFFS, share, extent, across)

    def wide_scratch(blocks):
        return scratch(blocks.shape[0], 2, share, 3 * extent, across)

    src_next, rec_next = pl.pallas_call(
        write_fields,
        out_shape=(struct(1, levels, extent, across), struct(1, levels, extent, across)),
        in_specs=[VMEM],
        out_specs=[HBM, HBM],
        scratch_shapes=[pltpu.SemaphoreType.DMA((2,))],
        compiler_params=params,
        name="write_fields",
    )(final)
    operands, wides, rounds = [], [], []
    for blocks, count in (([own_block, came[0]], 2), (came[1:], 3)):
        group = pl.pallas_call(
            stack,
            out_shape=struct(len(blocks), *own_block.shape),
            in_specs=[VMEM] * len(blocks),
            out_specs=VMEM,
            compiler_params=params,
            name="stack",
        )(*blocks)
        operands = [group, *swap_rounds([group] * count)[::-1], *operands]
        wides.insert(0, wide_scratch(group))
        rounds.insert(0, count)
    image = pl.pallas_call(
        functools.partial(image_products, weight, rounds),
        out_shape=struct(*image_shape),
        in_specs=[VMEM] * (1 + len(operands)),
        out_specs=HBM,
        scratch_shapes=[*wides, scratch(*image_shape), pltpu.SemaphoreType.DMA((11,))],
        compiler_params=params,
        name="image_products",
    )(sides, *operands)
    return src_next, rec_next, image


def solution(mesh):
    field = P(("groups", "shot"), None, "tile", None)
    return jax.shard_map(
        per_device,
        mesh=mesh,
        in_specs=(
            field,
            field,
            field,
            field,
            P("groups"),
            P(None, ("groups", "tile"), None),
            P(("groups", "shot")),
            P(("groups", "shot"), None),
            P(("groups", "shot"), "tile"),
            P(("groups", "shot"), None, "tile"),
        ),
        out_specs=(field, field, P(None, "shot", ("groups", "tile"), None)),
        check_vma=False,
    )
```

```python
import functools

import jax
import jax.numpy as jnp
from jax import lax
from jax.experimental import pallas as pl
from jax.experimental.pallas import tpu as pltpu
from jax.sharding import PartitionSpec as P

OFFS = 33
REACH = OFFS // 2
HALO = 4
LEAD = 8
ROUNDS = 3
SHIFTS = {2: 0, 3: 0}

COEFS = (-205.0 / 72.0, 8.0 / 5.0, -1.0 / 5.0, 8.0 / 315.0, -1.0 / 560.0)

VMEM = pl.BlockSpec(memory_space=pltpu.VMEM)
HBM = pl.BlockSpec(memory_space=pltpu.HBM)
SMEM = pl.BlockSpec(memory_space=pltpu.SMEM)
LIMIT = 16 * 1024 * 1024


def lane_weights(shape):
    lane = lax.broadcasted_iota(jnp.int32, shape, 1)
    across = shape[1]
    after = [jnp.where(lane < across - k, COEFS[k], 0.0) for k in range(1, HALO + 1)]
    before = [jnp.where(lane >= k, COEFS[k], 0.0) for k in range(1, HALO + 1)]
    return after, before


def lane_sum(centre, weights):
    after, before = weights
    across = centre.shape[1]
    total = 3.0 * COEFS[0] * centre
    for k in range(1, HALO + 1):
        total = total + after[k - 1] * pltpu.roll(centre, across - k, 1)
        total = total + before[k - 1] * pltpu.roll(centre, k, 1)
    return total


def beside_sum(wide, field, level, begin, count):
    total = None
    for k in range(1, HALO + 1):
        pair = (
            wide[field, level, begin + k : begin + k + count, :]
            + wide[field, level, begin - k : begin - k + count, :]
        )
        total = COEFS[k] * pair if total is None else total + COEFS[k] * pair
    return total


def depth_sum(rows_of, level, levels, total):
    for k in range(1, HALO + 1):
        for near in (level - k, level + k):
            if 0 <= near < levels:
                total = total + COEFS[k] * rows_of(near)
    return total


def laplace_level(wide, field, level, levels, extent, weights):
    def rows_of(near):
        return wide[field, near, LEAD : LEAD + extent, :]

    total = lane_sum(rows_of(level), weights) + beside_sum(wide, field, level, LEAD, extent)
    return depth_sum(rows_of, level, levels, total)


def is_low(across):
    return lax.broadcasted_iota(jnp.int32, (8, across), 0) < HALO


def own_edges(
    table_hbm,
    spots_hbm,
    traces_hbm,
    amps_hbm,
    ids_hbm,
    src_now,
    rec_now,
    src_prev,
    rec_prev,
    amps_ref,
    wide,
    prev_ref,
    ids_ref,
    speeds_ref,
    planes_ref,
    *rest,
):
    sent_refs, rest = rest[:ROUNDS], rest[ROUNDS:]
    table, spots_ref, traces_ref, edges, sems = rest
    levels, extent, across = ids_ref.shape
    regions = table_hbm.shape[1]
    end = LEAD + extent
    rows = pl.ds(LEAD, extent)
    moves = [(table_hbm, table), (spots_hbm, spots_ref), (traces_hbm, traces_ref)]
    for begin in range(0, levels, levels // 2):
        part = pl.ds(begin, levels // 2)
        moves += [
            (src_now.at[0, part], wide.at[0, part, rows, :]),
            (rec_now.at[0, part], wide.at[1, part, rows, :]),
            (ids_hbm.at[part], ids_ref.at[part]),
            (src_prev.at[0, part], prev_ref.at[0, part]),
            (rec_prev.at[0, part], prev_ref.at[1, part]),
        ]
    moves.append((amps_hbm, amps_ref))
    copies = [
        pltpu.make_async_copy(here, there, sems.at[i]) for i, (here, there) in enumerate(moves)
    ]
    for copy in copies:
        copy.start()
    zeros = jnp.zeros((LEAD, across), jnp.float32)
    for field in range(2):
        for level in range(levels):
            wide[field, level, 0:LEAD, :] = zeros
            wide[field, level, end : end + LEAD, :] = zeros
    weights = lane_weights((8, across))
    low_half = is_low(across)
    my_round = lax.rem(lax.axis_index("tile"), ROUNDS)
    for copy in copies:
        copy.wait()

    spots = spots_ref[...]
    column = lax.broadcasted_iota(jnp.int32, (extent, spots.shape[1]), 0) * across
    in_column = (spots >= column) & (spots < column + across)
    lane = lax.broadcasted_iota(jnp.int32, (across, spots.shape[1]), 0)
    in_row = jnp.where(lax.rem(spots, across) == lane, 1.0, 0.0)
    traces = jnp.concatenate(
        [jnp.where(in_column, traces_ref[0, t : t + 1, :], 0.0) for t in range(2)], axis=0
    )
    planes = lax.dot_general(
        traces,
        in_row,
        (((1,), (1,)), ((), ())),
        precision=lax.Precision.HIGHEST,
        preferred_element_type=jnp.float32,
    )
    planes_ref[...] = planes

    def send(place, low, high):
        for number, sent_ref in enumerate(sent_refs):
            sent_ref[place] = jnp.where(my_round == number, high, low)

    def halves(ref, *place):
        return jnp.where(
            low_half, ref[(*place, pl.ds(0, 8))], ref[(*place, pl.ds(extent - 8, 8))]
        )

    speeds = jnp.concatenate(
        [table[...], jnp.zeros((1, across - regions), jnp.float32)], axis=1
    )
    speeds = jnp.broadcast_to(speeds, (8, across))
    speeds_ref[...] = speeds
    coefs = [
        jnp.take_along_axis(speeds, halves(ids_ref, level), axis=1, mode="promise_in_bounds")
        for level in range(levels)
    ]
    for level in range(0, levels, 2):
        here, after = coefs[level], coefs[level + 1]
        send(
            2 * levels + level // 2,
            jnp.where(low_half, here, pltpu.roll(after, HALO, 0)),
            jnp.where(low_half, pltpu.roll(here, HALO, 0), after),
        )

    for field in range(2):
        for level in range(levels):
            edges[field, level] = jnp.where(
                low_half, wide[field, level, LEAD : LEAD + 8, :], wide[field, level, end - 8 : end, :]
            )
    for field in range(2):
        for level in range(levels):
            now = edges[field, level]
            total = lane_sum(now, weights) + jnp.where(
                low_half,
                beside_sum(wide, field, level, LEAD, 8),
                beside_sum(wide, field, level, end - 8, 8),
            )
            total = depth_sum(lambda near: edges[field, near], level, levels, total)
            value = 2.0 * now - halves(prev_ref, field, level) + coefs[level] * total
            if field == 1 and level == 0:
                value = value + jnp.where(low_half, planes[0:8, :], planes[extent - 8 : extent, :])
            send(
                field * levels + level,
                jnp.where(low_half, now, pltpu.roll(value, HALO, 0)),
                jnp.where(low_half, pltpu.roll(now, HALO, 0), value),
            )


def own_steps(
    width,
    cell_ref,
    amps_ref,
    own,
    prev_ref,
    ids_ref,
    speeds_ref,
    planes_ref,
    coef_ref,
    steps_ref,
    outside_ref,
    source_ref,
    sides_ref,
    bits_ref,
    middle,
):
    levels, extent, across = ids_ref.shape
    end = LEAD + extent
    cell = cell_ref[0]
    deep = lax.div(cell, width * across)
    row = lax.rem(lax.div(cell, across), width) - lax.axis_index("tile") * extent + LEAD
    shape = (extent + 2 * LEAD, across)
    rows = lax.broadcasted_iota(jnp.int32, shape, 0)
    lanes = lax.broadcasted_iota(jnp.int32, shape, 1)
    hit = jnp.where((rows == row) & (lanes == lax.rem(cell, across)), 1.0, 0.0)
    weights = lane_weights((extent, across))
    speeds = speeds_ref[...]
    zeros = jnp.zeros((LEAD, across), jnp.float32)
    for level in range(levels):
        here = hit * jnp.where(deep == level, 1.0, 0.0)
        source_ref[level] = here * amps_ref[0:1, 0:1]
        steps_ref[0, level] = here[LEAD:end, :] * amps_ref[0:1, 1:2] - own[0, level, LEAD:end, :]
        steps_ref[1, level] = -own[1, level, LEAD:end, :]
        for begin in range(0, extent, 8):
            coef_ref[level, begin : begin + 8, :] = jnp.take_along_axis(
                speeds, ids_ref[level, begin : begin + 8, :], axis=1, mode="promise_in_bounds"
            )
    steps_ref[1, 0] += planes_ref[extent:, :]
    for field in range(2):
        for level in range(levels):
            total = laplace_level(own, field, level, levels, extent, weights)
            value = 2.0 * own[field, level, LEAD:end, :] - prev_ref[field, level]
            value = value + coef_ref[level] * total
            if field == 0:
                value = value + source_ref[level, LEAD:end, :]
            elif level == 0:
                value = value + planes_ref[:extent, :]
            middle[field, level, 0:LEAD, :] = zeros
            middle[field, level, LEAD:end, :] = value
            middle[field, level, end : end + LEAD, :] = zeros
            below = above = jnp.zeros((HALO, across), jnp.float32)
            for k in range(1, HALO + 1):
                begin = LEAD - HALO + k
                below = below + COEFS[k] * own[field, level, begin : begin + HALO, :]
                above = above + COEFS[k] * own[field, level, end - k : end - k + HALO, :]
            outside_ref[field, level, 0:HALO, :] = below
            outside_ref[field, level, HALO : 2 * HALO, :] = above
    for field in range(2):
        for level in range(levels):
            total = laplace_level(middle, field, level, levels, extent, weights)
            steps_ref[field, level] += (
                2.0 * middle[field, level, LEAD:end, :] + coef_ref[level] * total
            )
    tile, tiles = lax.axis_index("tile"), lax.axis_size("tile")
    places = (jnp.where(tile > 0, 1, 0), jnp.where(tile < tiles - 1, 1, 0))
    places += tuple((tile + SHIFTS[rounds]) % rounds for rounds in (2, 3))
    for place, value in enumerate(places):
        sides_ref[place] = jnp.full(sides_ref.shape[1:], value, dtype=jnp.int32)
    shot = jnp.full(bits_ref.shape[1:], lax.axis_index("shot"), dtype=jnp.int32)
    for bit in range(bits_ref.shape[0]):
        bits_ref[bit] = shot & (1 << bit)


def both_sides(sides, came):
    has_low, has_high, my_round = sides[0], sides[1], sides[len(came)]
    low, high = came[-1], came[0]
    for number in range(1, len(came)):
        low = jnp.where(my_round == number, came[number - 1], low)
        high = jnp.where(my_round == number, came[number], high)
    return jnp.where(has_low != 0, low, 0.0), jnp.where(has_high != 0, high, 0.0)


def neighbours_part(
    sides_ref, bits_ref, steps_ref, outside_ref, source_ref, coef_ref, *rest
):
    came_refs, (final_ref, *blocks, other, change, edges) = rest[:ROUNDS], rest[ROUNDS:]
    levels, extent, across = coef_ref.shape
    share = blocks[0].shape[1]
    end = LEAD + extent
    low_half = is_low(across)
    weights = lane_weights((8, across))
    sides = [sides_ref[place] for place in range(4)]
    zeros = jnp.zeros((8, across), jnp.float32)

    def received(place):
        return both_sides(sides, [ref[place] for ref in came_refs])

    coefs = [received(2 * levels + pair) for pair in range(levels // 2)]
    for field in range(2):
        for level in range(levels):
            low, high = received(field * levels + level)
            other[field, level, LEAD : LEAD + 8, :] = zeros
            other[field, level, end - 8 : end, :] = zeros
            other[field, level, LEAD - HALO : LEAD, :] = low[0:HALO, :]
            other[field, level, end : end + HALO, :] = high[0:HALO, :]
            half = slice(level % 2 * HALO, level % 2 * HALO + HALO)
            low_coef, high_coef = (coef[half, :] for coef in coefs[level // 2])
            low = low[HALO:, :] + low_coef * outside_ref[field, level, 0:HALO, :]
            high = high[HALO:, :] + high_coef * outside_ref[field, level, HALO : 2 * HALO, :]
            if field == 0:
                low = low + source_ref[level, LEAD - HALO : LEAD, :]
                high = high + source_ref[level, end : end + HALO, :]
            change[field, level, LEAD - HALO : LEAD, :] = low
            change[field, level, end : end + HALO, :] = high
    for field in range(2):
        for level in range(levels):
            left = right = zeros
            for k in range(1, HALO + 1):
                left = left + COEFS[k] * other[field, level, LEAD - k : LEAD - k + 8, :]
                right = right + COEFS[k] * other[field, level, end - 8 + k : end + k, :]
            left = coef_ref[level, 0:8, :] * left
            right = coef_ref[level, extent - 8 : extent, :] * right
            change[field, level, LEAD : LEAD + 8, :] = left
            change[field, level, end - 8 : end, :] = right
            edges[field, level] = left + right
    for field in range(2):
        for level in range(levels):
            total = depth_sum(
                lambda near: edges[field, near],
                level,
                levels,
                lane_sum(edges[field, level], weights),
            )
            for begin, mine in ((0, low_half), (extent - 8, ~low_half)):
                part = beside_sum(change, field, level, LEAD + begin, 8)
                part = part + jnp.where(mine, total, 0.0)
                final_ref[field, level, begin : begin + 8, :] = (
                    steps_ref[field, level, begin : begin + 8, :]
                    + 2.0 * change[field, level, LEAD + begin : LEAD + begin + 8, :]
                    + coef_ref[level, begin : begin + 8, :] * part
                )
    masks = [
        jnp.concatenate([bits_ref[bit]] * (extent // 8), axis=0) != 0
        for bit in range(bits_ref.shape[0])
    ]
    for field in range(2):
        for level in range(share):
            parts = [final_ref[field, place * share + level] for place in range(len(blocks))]
            for bit, mask in enumerate(masks):
                parts = [
                    jnp.where(mask, parts[place ^ (1 << bit)], parts[place])
                    for place in range(len(blocks))
                ]
            for block, part in zip(blocks, parts):
                block[field, level] = part


def widen(weight, sides_ref, blocks, wide):
    mine_ref, *came_refs = blocks
    shots, _, share, extent, _ = mine_ref.shape
    sides = [
        jnp.concatenate([sides_ref[place]] * (extent // 8), axis=0) for place in range(4)
    ]
    for shot in range(shots):
        for field in range(2):
            for level in range(share):
                scale = weight if field == 0 else 1.0
                low, high = both_sides(sides, [ref[shot, field, level] for ref in came_refs])
                wide[shot, field, level, 0:extent, :] = scale * low
                wide[shot, field, level, extent : 2 * extent, :] = (
                    scale * mine_ref[shot, field, level]
                )
                wide[shot, field, level, 2 * extent : 3 * extent, :] = scale * high


def offset_product(wide, offset, level, total):
    extent = wide.shape[3] // 3
    lower = extent + REACH - offset
    upper = extent - REACH + offset
    for shot in range(wide.shape[0]):
        product = (
            wide[shot, 0, level, lower : lower + extent, :]
            * wide[shot, 1, level, upper : upper + extent, :]
        )
        total = product if total is None else total + product
    return total


def stack(*refs):
    for place in range(len(refs) - 1):
        refs[-1][place] = refs[place][...]


def write_fields(final_ref, src_hbm, rec_hbm, sems):
    copies = [
        pltpu.make_async_copy(final_ref.at[field], out.at[0], sems.at[field])
        for field, out in enumerate((src_hbm, rec_hbm))
    ]
    for copy in copies:
        copy.start()
    for copy in copies:
        copy.wait()


def image_products(weight, rounds, sides_ref, *rest):
    groups, begin = [], 0
    for count in rounds:
        mine_ref, *came_refs = rest[begin : begin + 1 + count]
        groups.append((mine_ref, *came_refs[::-1]))
        begin += 1 + count
    image_hbm, *wides, image_ref, sems = rest[begin:]
    for blocks, wide in zip(groups, wides):
        widen(weight, sides_ref, blocks, wide)
    parts = sems.shape[0]
    copies = []
    for piece in range(parts):
        offsets = range(piece * OFFS // parts, (piece + 1) * OFFS // parts)
        for offset in offsets:
            for level in range(image_ref.shape[1]):
                total = None
                for wide in wides:
                    total = offset_product(wide, offset, level, total)
                image_ref[offset, level] = total
        rows = pl.ds(offsets[0], len(offsets))
        copy = pltpu.make_async_copy(image_ref.at[rows], image_hbm.at[rows], sems.at[piece])
        copy.start()
        copies.append(copy)
    for copy in copies:
        copy.wait()


def swap_tiles(value, lower):
    tiles, shots = lax.axis_size("tile"), lax.axis_size("shot")
    partner = {}
    for tile in lower:
        partner[tile], partner[tile + 1] = tile + 1, tile
    pairs = []
    for tile in range(tiles):
        for shot in range(shots):
            here = tile * shots + shot
            there = partner[tile] * shots + shot if tile in partner else here ^ 1
            pairs.append((here, there))
    return lax.ppermute(value, ("tile", "shot"), pairs)


def swap_rounds(values):
    tiles, rounds = lax.axis_size("tile"), len(values)
    return [
        swap_tiles(value, range((number - SHIFTS[rounds]) % rounds, tiles - 1, rounds))
        for number, value in enumerate(values)
    ]


def per_device(
    src_prev,
    src_now,
    rec_prev,
    rec_now,
    speed_table,
    region_ids,
    source_cell,
    wavelet,
    receiver_cell,
    receiver_data,
):
    _, levels, extent, across = src_now.shape
    tiles = lax.axis_size("tile")
    width = extent * tiles
    shots = lax.axis_size("shot")
    share = levels // shots
    params = pltpu.CompilerParams(vmem_limit_bytes=LIMIT)

    def struct(*shape):
        return jax.ShapeDtypeStruct(shape, jnp.float32)

    def scratch(*shape, dtype=jnp.float32):
        return pltpu.VMEM(shape, dtype)

    wide_shape = (2, levels, extent + 2 * LEAD, across)
    message = struct(2 * levels + levels // 2, 2 * HALO, across)
    fields_shape = (2, levels, extent, across)
    amps, own, prev, ids, speeds, planes, *sent = pl.pallas_call(
        own_edges,
        out_shape=(
            struct(*wavelet.shape),
            struct(*wide_shape),
            struct(*fields_shape),
            jax.ShapeDtypeStruct(region_ids.shape, jnp.int32),
            struct(8, across),
            struct(2 * extent, across),
            *([message] * ROUNDS),
        ),
        in_specs=[HBM] * 9,
        out_specs=[VMEM] * (6 + ROUNDS),
        scratch_shapes=[
            scratch(1, speed_table.shape[0]),
            scratch(*receiver_cell.shape, dtype=jnp.int32),
            scratch(*receiver_data.shape),
            scratch(2, levels, 8, across),
            pltpu.SemaphoreType.DMA((14,)),
        ],
        compiler_params=params,
        name="own_edges",
    )(
        *(
            pltpu.with_memory_space_constraint(array, pltpu.HBM)
            for array in (
                speed_table.reshape(1, -1),
                receiver_cell,
                receiver_data,
                wavelet,
                region_ids,
                src_now,
                rec_now,
                src_prev,
                rec_prev,
            )
        )
    )
    came_sides = swap_rounds(sent)
    coef, steps, outside, source, sides, bits = pl.pallas_call(
        functools.partial(own_steps, width),
        out_shape=(
            struct(levels, extent, across),
            struct(*fields_shape),
            struct(2, levels, 2 * HALO, across),
            struct(levels, extent + 2 * LEAD, across),
            jax.ShapeDtypeStruct((4, 8, across), jnp.int32),
            jax.ShapeDtypeStruct((shots.bit_length() - 1, 8, across), jnp.int32),
        ),
        in_specs=[SMEM] + [VMEM] * 6,
        out_specs=[VMEM] * 6,
        scratch_shapes=[scratch(*wide_shape)],
        compiler_params=params,
        name="own_steps",
    )(source_cell, amps, own, prev, ids, speeds, planes)
    block = struct(2, share, extent, across)
    final, own_block, *blocks = pl.pallas_call(
        neighbours_part,
        out_shape=(struct(*fields_shape), *([block] * shots)),
        in_specs=[VMEM] * (6 + ROUNDS),
        out_specs=[VMEM] * (1 + shots),
        scratch_shapes=[
            scratch(*wide_shape),
            scratch(*wide_shape),
            scratch(2, levels, 8, across),
        ],
        compiler_params=params,
        name="neighbours_part",
    )(sides, bits, steps, outside, source, coef, *came_sides)
    came = [
        lax.ppermute(sent, "shot", [(shot, shot ^ (1 + i)) for shot in range(shots)])
        for i, sent in enumerate(blocks)
    ]
    weight = 1.0 / shots
    image_shape = (OFFS, share, extent, across)

    def wide_scratch(blocks):
        return scratch(blocks.shape[0], 2, share, 3 * extent, across)

    src_next, rec_next = pl.pallas_call(
        write_fields,
        out_shape=(struct(1, levels, extent, across), struct(1, levels, extent, across)),
        in_specs=[VMEM],
        out_specs=[HBM, HBM],
        scratch_shapes=[pltpu.SemaphoreType.DMA((2,))],
        compiler_params=params,
        name="write_fields",
    )(final)
    operands, wides, rounds = [], [], []
    for blocks, count in (([own_block, came[0]], 2), (came[1:], 3)):
        group = pl.pallas_call(
            stack,
            out_shape=struct(len(blocks), *own_block.shape),
            in_specs=[VMEM] * len(blocks),
            out_specs=VMEM,
            compiler_params=params,
            name="stack",
        )(*blocks)
        operands = [group, *swap_rounds([group] * count)[::-1], *operands]
        wides.insert(0, wide_scratch(group))
        rounds.insert(0, count)
    image = pl.pallas_call(
        functools.partial(image_products, weight, rounds),
        out_shape=struct(*image_shape),
        in_specs=[VMEM] * (1 + len(operands)),
        out_specs=HBM,
        scratch_shapes=[*wides, scratch(*image_shape), pltpu.SemaphoreType.DMA((11,))],
        compiler_params=params,
        name="image_products",
    )(sides, *operands)
    return src_next, rec_next, image


def solution(mesh):
    field = P(("groups", "shot"), None, "tile", None)
    return jax.shard_map(
        per_device,
        mesh=mesh,
        in_specs=(
            field,
            field,
            field,
            field,
            P("groups"),
            P(None, ("groups", "tile"), None),
            P(("groups", "shot")),
            P(("groups", "shot"), None),
            P(("groups", "shot"), "tile"),
            P(("groups", "shot"), None, "tile"),
        ),
        out_specs=(field, field, P(None, "shot", ("groups", "tile"), None)),
        check_vma=False,
    )
```

```python
import functools

import jax
import jax.numpy as jnp
from jax import lax
from jax.experimental import pallas as pl
from jax.experimental.pallas import tpu as pltpu
from jax.sharding import PartitionSpec as P

OFFS = 33
REACH = OFFS // 2
HALO = 4
LEAD = 8
ROUNDS = 3
SHIFTS = {2: 0, 3: 0}

COEFS = (-205.0 / 72.0, 8.0 / 5.0, -1.0 / 5.0, 8.0 / 315.0, -1.0 / 560.0)

VMEM = pl.BlockSpec(memory_space=pltpu.VMEM)
HBM = pl.BlockSpec(memory_space=pltpu.HBM)
SMEM = pl.BlockSpec(memory_space=pltpu.SMEM)
LIMIT = 16 * 1024 * 1024


def lane_weights(shape):
    lane = lax.broadcasted_iota(jnp.int32, shape, 1)
    across = shape[1]
    after = [jnp.where(lane < across - k, COEFS[k], 0.0) for k in range(1, HALO + 1)]
    before = [jnp.where(lane >= k, COEFS[k], 0.0) for k in range(1, HALO + 1)]
    return after, before


def lane_sum(centre, weights):
    after, before = weights
    across = centre.shape[1]
    total = 3.0 * COEFS[0] * centre
    for k in range(1, HALO + 1):
        total = total + after[k - 1] * pltpu.roll(centre, across - k, 1)
        total = total + before[k - 1] * pltpu.roll(centre, k, 1)
    return total


def beside_sum(wide, field, level, begin, count):
    total = None
    for k in range(1, HALO + 1):
        pair = (
            wide[field, level, begin + k : begin + k + count, :]
            + wide[field, level, begin - k : begin - k + count, :]
        )
        total = COEFS[k] * pair if total is None else total + COEFS[k] * pair
    return total


def depth_sum(rows_of, level, levels, total):
    for k in range(1, HALO + 1):
        for near in (level - k, level + k):
            if 0 <= near < levels:
                total = total + COEFS[k] * rows_of(near)
    return total


def laplace_level(wide, field, level, levels, extent, weights):
    def rows_of(near):
        return wide[field, near, LEAD : LEAD + extent, :]

    total = lane_sum(rows_of(level), weights) + beside_sum(wide, field, level, LEAD, extent)
    return depth_sum(rows_of, level, levels, total)


def is_low(across):
    return lax.broadcasted_iota(jnp.int32, (8, across), 0) < HALO


def own_edges(
    table_hbm,
    spots_hbm,
    traces_hbm,
    amps_hbm,
    ids_hbm,
    src_now,
    rec_now,
    src_prev,
    rec_prev,
    amps_ref,
    wide,
    prev_ref,
    ids_ref,
    speeds_ref,
    planes_ref,
    *rest,
):
    sent_refs, rest = rest[:ROUNDS], rest[ROUNDS:]
    table, spots_ref, traces_ref, edges, sems = rest
    levels, extent, across = ids_ref.shape
    regions = table_hbm.shape[1]
    end = LEAD + extent
    rows = pl.ds(LEAD, extent)
    moves = [(table_hbm, table), (spots_hbm, spots_ref), (traces_hbm, traces_ref)]
    for begin in range(0, levels, levels // 2):
        part = pl.ds(begin, levels // 2)
        moves += [
            (src_now.at[0, part], wide.at[0, part, rows, :]),
            (rec_now.at[0, part], wide.at[1, part, rows, :]),
            (ids_hbm.at[part], ids_ref.at[part]),
            (src_prev.at[0, part], prev_ref.at[0, part]),
            (rec_prev.at[0, part], prev_ref.at[1, part]),
        ]
    moves.append((amps_hbm, amps_ref))
    copies = [
        pltpu.make_async_copy(here, there, sems.at[i]) for i, (here, there) in enumerate(moves)
    ]
    for copy in copies:
        copy.start()
    zeros = jnp.zeros((LEAD, across), jnp.float32)
    for field in range(2):
        for level in range(levels):
            wide[field, level, 0:LEAD, :] = zeros
            wide[field, level, end : end + LEAD, :] = zeros
    weights = lane_weights((8, across))
    low_half = is_low(across)
    my_round = lax.rem(lax.axis_index("tile"), ROUNDS)
    for copy in copies:
        copy.wait()

    spots = spots_ref[...]
    column = lax.broadcasted_iota(jnp.int32, (extent, spots.shape[1]), 0) * across
    in_column = (spots >= column) & (spots < column + across)
    lane = lax.broadcasted_iota(jnp.int32, (across, spots.shape[1]), 0)
    in_row = jnp.where(lax.rem(spots, across) == lane, 1.0, 0.0)
    traces = jnp.concatenate(
        [jnp.where(in_column, traces_ref[0, t : t + 1, :], 0.0) for t in range(2)], axis=0
    )
    planes = lax.dot_general(
        traces,
        in_row,
        (((1,), (1,)), ((), ())),
        precision=lax.Precision.HIGHEST,
        preferred_element_type=jnp.float32,
    )
    planes_ref[...] = planes

    def send(place, low, high):
        for number, sent_ref in enumerate(sent_refs):
            sent_ref[place] = jnp.where(my_round == number, high, low)

    def halves(ref, *place):
        return jnp.where(
            low_half, ref[(*place, pl.ds(0, 8))], ref[(*place, pl.ds(extent - 8, 8))]
        )

    speeds = jnp.concatenate(
        [table[...], jnp.zeros((1, across - regions), jnp.float32)], axis=1
    )
    speeds = jnp.broadcast_to(speeds, (8, across))
    speeds_ref[...] = speeds
    coefs = [
        jnp.take_along_axis(speeds, halves(ids_ref, level), axis=1, mode="promise_in_bounds")
        for level in range(levels)
    ]
    for level in range(0, levels, 2):
        here, after = coefs[level], coefs[level + 1]
        send(
            2 * levels + level // 2,
            jnp.where(low_half, here, pltpu.roll(after, HALO, 0)),
            jnp.where(low_half, pltpu.roll(here, HALO, 0), after),
        )

    for field in range(2):
        for level in range(levels):
            edges[field, level] = jnp.where(
                low_half, wide[field, level, LEAD : LEAD + 8, :], wide[field, level, end - 8 : end, :]
            )
    for field in range(2):
        for level in range(levels):
            now = edges[field, level]
            total = lane_sum(now, weights) + jnp.where(
                low_half,
                beside_sum(wide, field, level, LEAD, 8),
                beside_sum(wide, field, level, end - 8, 8),
            )
            total = depth_sum(lambda near: edges[field, near], level, levels, total)
            value = 2.0 * now - halves(prev_ref, field, level) + coefs[level] * total
            if field == 1 and level == 0:
                value = value + jnp.where(low_half, planes[0:8, :], planes[extent - 8 : extent, :])
            send(
                field * levels + level,
                jnp.where(low_half, now, pltpu.roll(value, HALO, 0)),
                jnp.where(low_half, pltpu.roll(now, HALO, 0), value),
            )


def own_steps(
    width,
    cell_ref,
    amps_ref,
    own,
    prev_ref,
    ids_ref,
    speeds_ref,
    planes_ref,
    coef_ref,
    steps_ref,
    outside_ref,
    source_ref,
    sides_ref,
    bits_ref,
    middle,
):
    levels, extent, across = ids_ref.shape
    end = LEAD + extent
    cell = cell_ref[0]
    deep = lax.div(cell, width * across)
    row = lax.rem(lax.div(cell, across), width) - lax.axis_index("tile") * extent + LEAD
    shape = (extent + 2 * LEAD, across)
    rows = lax.broadcasted_iota(jnp.int32, shape, 0)
    lanes = lax.broadcasted_iota(jnp.int32, shape, 1)
    hit = jnp.where((rows == row) & (lanes == lax.rem(cell, across)), 1.0, 0.0)
    weights = lane_weights((extent, across))
    speeds = speeds_ref[...]
    zeros = jnp.zeros((LEAD, across), jnp.float32)
    for level in range(levels):
        here = hit * jnp.where(deep == level, 1.0, 0.0)
        source_ref[level] = here * amps_ref[0:1, 0:1]
        steps_ref[0, level] = here[LEAD:end, :] * amps_ref[0:1, 1:2] - own[0, level, LEAD:end, :]
        steps_ref[1, level] = -own[1, level, LEAD:end, :]
        for begin in range(0, extent, 8):
            coef_ref[level, begin : begin + 8, :] = jnp.take_along_axis(
                speeds, ids_ref[level, begin : begin + 8, :], axis=1, mode="promise_in_bounds"
            )
    steps_ref[1, 0] += planes_ref[extent:, :]
    for field in range(2):
        for level in range(levels):
            total = laplace_level(own, field, level, levels, extent, weights)
            value = 2.0 * own[field, level, LEAD:end, :] - prev_ref[field, level]
            value = value + coef_ref[level] * total
            if field == 0:
                value = value + source_ref[level, LEAD:end, :]
            elif level == 0:
                value = value + planes_ref[:extent, :]
            middle[field, level, 0:LEAD, :] = zeros
            middle[field, level, LEAD:end, :] = value
            middle[field, level, end : end + LEAD, :] = zeros
            below = above = jnp.zeros((HALO, across), jnp.float32)
            for k in range(1, HALO + 1):
                begin = LEAD - HALO + k
                below = below + COEFS[k] * own[field, level, begin : begin + HALO, :]
                above = above + COEFS[k] * own[field, level, end - k : end - k + HALO, :]
            outside_ref[field, level, 0:HALO, :] = below
            outside_ref[field, level, HALO : 2 * HALO, :] = above
    for field in range(2):
        for level in range(levels):
            total = laplace_level(middle, field, level, levels, extent, weights)
            steps_ref[field, level] += (
                2.0 * middle[field, level, LEAD:end, :] + coef_ref[level] * total
            )
    tile, tiles = lax.axis_index("tile"), lax.axis_size("tile")
    places = (jnp.where(tile > 0, 1, 0), jnp.where(tile < tiles - 1, 1, 0))
    places += tuple((tile + SHIFTS[rounds]) % rounds for rounds in (2, 3))
    for place, value in enumerate(places):
        sides_ref[place] = jnp.full(sides_ref.shape[1:], value, dtype=jnp.int32)
    shot = jnp.full(bits_ref.shape[1:], lax.axis_index("shot"), dtype=jnp.int32)
    for bit in range(bits_ref.shape[0]):
        bits_ref[bit] = shot & (1 << bit)


def both_sides(sides, came):
    has_low, has_high, my_round = sides[0], sides[1], sides[len(came)]
    low, high = came[-1], came[0]
    for number in range(1, len(came)):
        low = jnp.where(my_round == number, came[number - 1], low)
        high = jnp.where(my_round == number, came[number], high)
    return jnp.where(has_low != 0, low, 0.0), jnp.where(has_high != 0, high, 0.0)


def neighbours_part(
    sides_ref, bits_ref, steps_ref, outside_ref, source_ref, coef_ref, *rest
):
    came_refs, (final_ref, mine_ref, *blocks, other, change, edges) = rest[:ROUNDS], rest[ROUNDS:]
    blocks = [mine_ref.at[0], mine_ref.at[1], *blocks]
    levels, extent, across = coef_ref.shape
    share = mine_ref.shape[2]
    end = LEAD + extent
    low_half = is_low(across)
    weights = lane_weights((8, across))
    sides = [sides_ref[place] for place in range(4)]
    zeros = jnp.zeros((8, across), jnp.float32)

    def received(place):
        return both_sides(sides, [ref[place] for ref in came_refs])

    coefs = [received(2 * levels + pair) for pair in range(levels // 2)]
    for field in range(2):
        for level in range(levels):
            low, high = received(field * levels + level)
            other[field, level, LEAD : LEAD + 8, :] = zeros
            other[field, level, end - 8 : end, :] = zeros
            other[field, level, LEAD - HALO : LEAD, :] = low[0:HALO, :]
            other[field, level, end : end + HALO, :] = high[0:HALO, :]
            half = slice(level % 2 * HALO, level % 2 * HALO + HALO)
            low_coef, high_coef = (coef[half, :] for coef in coefs[level // 2])
            low = low[HALO:, :] + low_coef * outside_ref[field, level, 0:HALO, :]
            high = high[HALO:, :] + high_coef * outside_ref[field, level, HALO : 2 * HALO, :]
            if field == 0:
                low = low + source_ref[level, LEAD - HALO : LEAD, :]
                high = high + source_ref[level, end : end + HALO, :]
            change[field, level, LEAD - HALO : LEAD, :] = low
            change[field, level, end : end + HALO, :] = high
    for field in range(2):
        for level in range(levels):
            left = right = zeros
            for k in range(1, HALO + 1):
                left = left + COEFS[k] * other[field, level, LEAD - k : LEAD - k + 8, :]
                right = right + COEFS[k] * other[field, level, end - 8 + k : end + k, :]
            left = coef_ref[level, 0:8, :] * left
            right = coef_ref[level, extent - 8 : extent, :] * right
            change[field, level, LEAD : LEAD + 8, :] = left
            change[field, level, end - 8 : end, :] = right
            edges[field, level] = left + right
    for field in range(2):
        for level in range(levels):
            total = depth_sum(
                lambda near: edges[field, near],
                level,
                levels,
                lane_sum(edges[field, level], weights),
            )
            for begin, mine in ((0, low_half), (extent - 8, ~low_half)):
                part = beside_sum(change, field, level, LEAD + begin, 8)
                part = part + jnp.where(mine, total, 0.0)
                final_ref[field, level, begin : begin + 8, :] = (
                    steps_ref[field, level, begin : begin + 8, :]
                    + 2.0 * change[field, level, LEAD + begin : LEAD + begin + 8, :]
                    + coef_ref[level, begin : begin + 8, :] * part
                )
    masks = [
        jnp.concatenate([bits_ref[bit]] * (extent // 8), axis=0) != 0
        for bit in range(bits_ref.shape[0])
    ]
    for field in range(2):
        for level in range(share):
            parts = [final_ref[field, place * share + level] for place in range(len(blocks))]
            for bit, mask in enumerate(masks):
                parts = [
                    jnp.where(mask, parts[place ^ (1 << bit)], parts[place])
                    for place in range(len(blocks))
                ]
            for block, part in zip(blocks, parts):
                block[field, level] = part


def widen(weight, sides_ref, shot, mine_ref, came_refs, wide):
    _, share, extent, _ = mine_ref.shape
    sides = [
        jnp.concatenate([sides_ref[place]] * (extent // 8), axis=0) for place in range(4)
    ]
    for field in range(2):
        for level in range(share):
            scale = weight if field == 0 else 1.0
            low, high = both_sides(sides, [ref[field, level] for ref in came_refs])
            wide[shot, field, level, 0:extent, :] = scale * low
            wide[shot, field, level, extent : 2 * extent, :] = scale * mine_ref[field, level]
            wide[shot, field, level, 2 * extent : 3 * extent, :] = scale * high


def offset_product(wide, offset, level):
    extent = wide.shape[3] // 3
    lower = extent + REACH - offset
    upper = extent - REACH + offset
    total = None
    for shot in range(wide.shape[0]):
        product = (
            wide[shot, 0, level, lower : lower + extent, :]
            * wide[shot, 1, level, upper : upper + extent, :]
        )
        total = product if total is None else total + product
    return total


def stack(*refs):
    for place in range(len(refs) - 1):
        refs[-1][place] = refs[place][...]


def write_fields(final_ref, src_hbm, rec_hbm, sems):
    copies = [
        pltpu.make_async_copy(final_ref.at[field], out.at[0], sems.at[field])
        for field, out in enumerate((src_hbm, rec_hbm))
    ]
    for copy in copies:
        copy.start()
    for copy in copies:
        copy.wait()


def image_products(weight, sides_ref, others_ref, *rest):
    others_sides, rest = rest[ROUNDS - 1 :: -1], rest[ROUNDS:]
    mine_ref, last_ref, first_ref, *partner_refs, image_hbm, wide, image_ref, sems = rest
    places = [
        (mine_ref.at[0], (first_ref.at[0], last_ref.at[0])),
        (partner_refs[0], partner_refs[1:]),
    ]
    for place in range(others_ref.shape[0]):
        places.append((others_ref.at[place], [ref.at[place] for ref in others_sides]))
    for shot, (own_ref, came_refs) in enumerate(places):
        widen(weight, sides_ref, shot, own_ref, came_refs, wide)
    parts = sems.shape[0]
    copies = []
    for piece in range(parts):
        offsets = range(piece * OFFS // parts, (piece + 1) * OFFS // parts)
        for offset in offsets:
            for level in range(image_ref.shape[1]):
                image_ref[offset, level] = offset_product(wide, offset, level)
        rows = pl.ds(offsets[0], len(offsets))
        copy = pltpu.make_async_copy(image_ref.at[rows], image_hbm.at[rows], sems.at[piece])
        copy.start()
        copies.append(copy)
    for copy in copies:
        copy.wait()


def swap_tiles(value, lower):
    tiles, shots = lax.axis_size("tile"), lax.axis_size("shot")
    partner = {}
    for tile in lower:
        partner[tile], partner[tile + 1] = tile + 1, tile
    pairs = []
    for tile in range(tiles):
        for shot in range(shots):
            here = tile * shots + shot
            there = partner[tile] * shots + shot if tile in partner else here ^ 1
            pairs.append((here, there))
    return lax.ppermute(value, ("tile", "shot"), pairs)


def swap_rounds(values):
    tiles, rounds = lax.axis_size("tile"), len(values)
    return [
        swap_tiles(value, range((number - SHIFTS[rounds]) % rounds, tiles - 1, rounds))
        for number, value in enumerate(values)
    ]


def per_device(
    src_prev,
    src_now,
    rec_prev,
    rec_now,
    speed_table,
    region_ids,
    source_cell,
    wavelet,
    receiver_cell,
    receiver_data,
):
    _, levels, extent, across = src_now.shape
    tiles = lax.axis_size("tile")
    width = extent * tiles
    shots = lax.axis_size("shot")
    share = levels // shots
    params = pltpu.CompilerParams(vmem_limit_bytes=LIMIT)

    def struct(*shape):
        return jax.ShapeDtypeStruct(shape, jnp.float32)

    def scratch(*shape, dtype=jnp.float32):
        return pltpu.VMEM(shape, dtype)

    wide_shape = (2, levels, extent + 2 * LEAD, across)
    message = struct(2 * levels + levels // 2, 2 * HALO, across)
    fields_shape = (2, levels, extent, across)
    amps, own, prev, ids, speeds, planes, *sent = pl.pallas_call(
        own_edges,
        out_shape=(
            struct(*wavelet.shape),
            struct(*wide_shape),
            struct(*fields_shape),
            jax.ShapeDtypeStruct(region_ids.shape, jnp.int32),
            struct(8, across),
            struct(2 * extent, across),
            *([message] * ROUNDS),
        ),
        in_specs=[HBM] * 9,
        out_specs=[VMEM] * (6 + ROUNDS),
        scratch_shapes=[
            scratch(1, speed_table.shape[0]),
            scratch(*receiver_cell.shape, dtype=jnp.int32),
            scratch(*receiver_data.shape),
            scratch(2, levels, 8, across),
            pltpu.SemaphoreType.DMA((14,)),
        ],
        compiler_params=params,
        name="own_edges",
    )(
        *(
            pltpu.with_memory_space_constraint(array, pltpu.HBM)
            for array in (
                speed_table.reshape(1, -1),
                receiver_cell,
                receiver_data,
                wavelet,
                region_ids,
                src_now,
                rec_now,
                src_prev,
                rec_prev,
            )
        )
    )
    came_sides = swap_rounds(sent)
    coef, steps, outside, source, sides, bits = pl.pallas_call(
        functools.partial(own_steps, width),
        out_shape=(
            struct(levels, extent, across),
            struct(*fields_shape),
            struct(2, levels, 2 * HALO, across),
            struct(levels, extent + 2 * LEAD, across),
            jax.ShapeDtypeStruct((4, 8, across), jnp.int32),
            jax.ShapeDtypeStruct((shots.bit_length() - 1, 8, across), jnp.int32),
        ),
        in_specs=[SMEM] + [VMEM] * 6,
        out_specs=[VMEM] * 6,
        scratch_shapes=[scratch(*wide_shape)],
        compiler_params=params,
        name="own_steps",
    )(source_cell, amps, own, prev, ids, speeds, planes)
    block = struct(2, share, extent, across)
    final, mine, *blocks = pl.pallas_call(
        neighbours_part,
        out_shape=(struct(*fields_shape), struct(2, *block.shape), *([block] * (shots - 2))),
        in_specs=[VMEM] * (6 + ROUNDS),
        out_specs=[VMEM] * shots,
        scratch_shapes=[
            scratch(*wide_shape),
            scratch(*wide_shape),
            scratch(2, levels, 8, across),
        ],
        compiler_params=params,
        name="neighbours_part",
    )(sides, bits, steps, outside, source, coef, *came_sides)
    def swap_shots(value, number):
        return lax.ppermute(value, "shot", [(shot, shot ^ number) for shot in range(shots)])

    came = [swap_shots(sent, 2 + i) for i, sent in enumerate(blocks)]
    weight = 1.0 / shots
    image_shape = (OFFS, share, extent, across)

    src_next, rec_next = pl.pallas_call(
        write_fields,
        out_shape=(struct(1, levels, extent, across), struct(1, levels, extent, across)),
        in_specs=[VMEM],
        out_specs=[HBM, HBM],
        scratch_shapes=[pltpu.SemaphoreType.DMA((2,))],
        compiler_params=params,
        name="write_fields",
    )(final)
    others = pl.pallas_call(
        stack,
        out_shape=struct(len(came), *block.shape),
        in_specs=[VMEM] * len(came),
        out_specs=VMEM,
        compiler_params=params,
        name="stack",
    )(*came[::-1])
    mine_sides = swap_rounds([mine] * 2)
    others_sides = swap_rounds([others] * ROUNDS)
    partner = [swap_shots(value[1], 1) for value in (mine, *mine_sides)]
    operands = [others, *others_sides[::-1], mine, *mine_sides[::-1], *partner]
    image = pl.pallas_call(
        functools.partial(image_products, weight),
        out_shape=struct(*image_shape),
        in_specs=[VMEM] * (1 + len(operands)),
        out_specs=HBM,
        scratch_shapes=[
            scratch(shots, 2, share, 3 * extent, across),
            scratch(*image_shape),
            pltpu.SemaphoreType.DMA((11,)),
        ],
        compiler_params=params,
        name="image_products",
    )(sides, *operands)
    return src_next, rec_next, image


def solution(mesh):
    field = P(("groups", "shot"), None, "tile", None)
    return jax.shard_map(
        per_device,
        mesh=mesh,
        in_specs=(
            field,
            field,
            field,
            field,
            P("groups"),
            P(None, ("groups", "tile"), None),
            P(("groups", "shot")),
            P(("groups", "shot"), None),
            P(("groups", "shot"), "tile"),
            P(("groups", "shot"), None, "tile"),
        ),
        out_specs=(field, field, P(None, "shot", ("groups", "tile"), None)),
        check_vma=False,
    )
```

```python
import functools

import jax
import jax.numpy as jnp
from jax import lax
from jax.experimental import pallas as pl
from jax.experimental.pallas import tpu as pltpu
from jax.sharding import PartitionSpec as P

OFFS = 33
REACH = OFFS // 2
HALO = 4
LEAD = 8
ROUNDS = 3
SHIFTS = {2: 0, 3: 0}

COEFS = (-205.0 / 72.0, 8.0 / 5.0, -1.0 / 5.0, 8.0 / 315.0, -1.0 / 560.0)

VMEM = pl.BlockSpec(memory_space=pltpu.VMEM)
HBM = pl.BlockSpec(memory_space=pltpu.HBM)
SMEM = pl.BlockSpec(memory_space=pltpu.SMEM)
LIMIT = 16 * 1024 * 1024


def lane_weights(shape):
    lane = lax.broadcasted_iota(jnp.int32, shape, 1)
    across = shape[1]
    after = [jnp.where(lane < across - k, COEFS[k], 0.0) for k in range(1, HALO + 1)]
    before = [jnp.where(lane >= k, COEFS[k], 0.0) for k in range(1, HALO + 1)]
    return after, before


def lane_sum(centre, weights):
    after, before = weights
    across = centre.shape[1]
    total = 3.0 * COEFS[0] * centre
    for k in range(1, HALO + 1):
        total = total + after[k - 1] * pltpu.roll(centre, across - k, 1)
        total = total + before[k - 1] * pltpu.roll(centre, k, 1)
    return total


def beside_sum(wide, field, level, begin, count):
    total = None
    for k in range(1, HALO + 1):
        pair = (
            wide[field, level, begin + k : begin + k + count, :]
            + wide[field, level, begin - k : begin - k + count, :]
        )
        total = COEFS[k] * pair if total is None else total + COEFS[k] * pair
    return total


def depth_sum(rows_of, level, levels, total):
    for k in range(1, HALO + 1):
        for near in (level - k, level + k):
            if 0 <= near < levels:
                total = total + COEFS[k] * rows_of(near)
    return total


def laplace_level(wide, field, level, levels, extent, weights):
    def rows_of(near):
        return wide[field, near, LEAD : LEAD + extent, :]

    total = lane_sum(rows_of(level), weights) + beside_sum(wide, field, level, LEAD, extent)
    return depth_sum(rows_of, level, levels, total)


def is_low(across):
    return lax.broadcasted_iota(jnp.int32, (8, across), 0) < HALO


def own_edges(
    table_hbm,
    spots_hbm,
    traces_hbm,
    amps_hbm,
    ids_hbm,
    src_now,
    rec_now,
    src_prev,
    rec_prev,
    amps_ref,
    wide,
    prev_ref,
    ids_ref,
    speeds_ref,
    planes_ref,
    *rest,
):
    sent_refs, rest = rest[:ROUNDS], rest[ROUNDS:]
    table, spots_ref, traces_ref, edges, sems = rest
    levels, extent, across = ids_ref.shape
    regions = table_hbm.shape[1]
    end = LEAD + extent
    rows = pl.ds(LEAD, extent)
    moves = [(table_hbm, table), (spots_hbm, spots_ref), (traces_hbm, traces_ref)]
    moves += [
        (src_now.at[0], wide.at[0, :, rows, :]),
        (rec_now.at[0], wide.at[1, :, rows, :]),
        (ids_hbm, ids_ref),
        (src_prev.at[0], prev_ref.at[0]),
        (rec_prev.at[0], prev_ref.at[1]),
    ]
    moves.append((amps_hbm, amps_ref))
    copies = [
        pltpu.make_async_copy(here, there, sems.at[i]) for i, (here, there) in enumerate(moves)
    ]
    for copy in copies:
        copy.start()
    zeros = jnp.zeros((LEAD, across), jnp.float32)
    for field in range(2):
        for level in range(levels):
            wide[field, level, 0:LEAD, :] = zeros
            wide[field, level, end : end + LEAD, :] = zeros
    weights = lane_weights((8, across))
    low_half = is_low(across)
    my_round = lax.rem(lax.axis_index("tile"), ROUNDS)
    for copy in copies:
        copy.wait()

    spots = spots_ref[...]
    column = lax.broadcasted_iota(jnp.int32, (extent, spots.shape[1]), 0) * across
    in_column = (spots >= column) & (spots < column + across)
    lane = lax.broadcasted_iota(jnp.int32, (across, spots.shape[1]), 0)
    in_row = jnp.where(lax.rem(spots, across) == lane, 1.0, 0.0)
    traces = jnp.concatenate(
        [jnp.where(in_column, traces_ref[0, t : t + 1, :], 0.0) for t in range(2)], axis=0
    )
    planes = lax.dot_general(
        traces,
        in_row,
        (((1,), (1,)), ((), ())),
        precision=lax.Precision.HIGHEST,
        preferred_element_type=jnp.float32,
    )
    planes_ref[...] = planes

    def send(place, low, high):
        for number, sent_ref in enumerate(sent_refs):
            sent_ref[place] = jnp.where(my_round == number, high, low)

    def halves(ref, *place):
        return jnp.where(
            low_half, ref[(*place, pl.ds(0, 8))], ref[(*place, pl.ds(extent - 8, 8))]
        )

    speeds = jnp.concatenate(
        [table[...], jnp.zeros((1, across - regions), jnp.float32)], axis=1
    )
    speeds = jnp.broadcast_to(speeds, (8, across))
    speeds_ref[...] = speeds
    coefs = [
        jnp.take_along_axis(speeds, halves(ids_ref, level), axis=1, mode="promise_in_bounds")
        for level in range(levels)
    ]
    for level in range(0, levels, 2):
        here, after = coefs[level], coefs[level + 1]
        send(
            2 * levels + level // 2,
            jnp.where(low_half, here, pltpu.roll(after, HALO, 0)),
            jnp.where(low_half, pltpu.roll(here, HALO, 0), after),
        )

    for field in range(2):
        for level in range(levels):
            edges[field, level] = jnp.where(
                low_half, wide[field, level, LEAD : LEAD + 8, :], wide[field, level, end - 8 : end, :]
            )
    for field in range(2):
        for level in range(levels):
            now = edges[field, level]
            total = lane_sum(now, weights) + jnp.where(
                low_half,
                beside_sum(wide, field, level, LEAD, 8),
                beside_sum(wide, field, level, end - 8, 8),
            )
            total = depth_sum(lambda near: edges[field, near], level, levels, total)
            value = 2.0 * now - halves(prev_ref, field, level) + coefs[level] * total
            if field == 1 and level == 0:
                value = value + jnp.where(low_half, planes[0:8, :], planes[extent - 8 : extent, :])
            send(
                field * levels + level,
                jnp.where(low_half, now, pltpu.roll(value, HALO, 0)),
                jnp.where(low_half, pltpu.roll(now, HALO, 0), value),
            )


def own_steps(
    width,
    cell_ref,
    amps_ref,
    own,
    prev_ref,
    ids_ref,
    speeds_ref,
    planes_ref,
    coef_ref,
    steps_ref,
    outside_ref,
    source_ref,
    sides_ref,
    bits_ref,
    middle,
):
    levels, extent, across = ids_ref.shape
    end = LEAD + extent
    cell = cell_ref[0]
    deep = lax.div(cell, width * across)
    row = lax.rem(lax.div(cell, across), width) - lax.axis_index("tile") * extent + LEAD
    shape = (extent + 2 * LEAD, across)
    rows = lax.broadcasted_iota(jnp.int32, shape, 0)
    lanes = lax.broadcasted_iota(jnp.int32, shape, 1)
    hit = jnp.where((rows == row) & (lanes == lax.rem(cell, across)), 1.0, 0.0)
    weights = lane_weights((extent, across))
    speeds = speeds_ref[...]
    zeros = jnp.zeros((LEAD, across), jnp.float32)
    for level in range(levels):
        here = hit * jnp.where(deep == level, 1.0, 0.0)
        source_ref[level] = here * amps_ref[0:1, 0:1]
        steps_ref[0, level] = here[LEAD:end, :] * amps_ref[0:1, 1:2] - own[0, level, LEAD:end, :]
        steps_ref[1, level] = -own[1, level, LEAD:end, :]
        for begin in range(0, extent, 8):
            coef_ref[level, begin : begin + 8, :] = jnp.take_along_axis(
                speeds, ids_ref[level, begin : begin + 8, :], axis=1, mode="promise_in_bounds"
            )
    steps_ref[1, 0] += planes_ref[extent:, :]
    for field in range(2):
        for level in range(levels):
            total = laplace_level(own, field, level, levels, extent, weights)
            value = 2.0 * own[field, level, LEAD:end, :] - prev_ref[field, level]
            value = value + coef_ref[level] * total
            if field == 0:
                value = value + source_ref[level, LEAD:end, :]
            elif level == 0:
                value = value + planes_ref[:extent, :]
            middle[field, level, 0:LEAD, :] = zeros
            middle[field, level, LEAD:end, :] = value
            middle[field, level, end : end + LEAD, :] = zeros
            below = above = jnp.zeros((HALO, across), jnp.float32)
            for k in range(1, HALO + 1):
                begin = LEAD - HALO + k
                below = below + COEFS[k] * own[field, level, begin : begin + HALO, :]
                above = above + COEFS[k] * own[field, level, end - k : end - k + HALO, :]
            outside_ref[field, level, 0:HALO, :] = below
            outside_ref[field, level, HALO : 2 * HALO, :] = above
    for field in range(2):
        for level in range(levels):
            total = laplace_level(middle, field, level, levels, extent, weights)
            steps_ref[field, level] += (
                2.0 * middle[field, level, LEAD:end, :] + coef_ref[level] * total
            )
    tile, tiles = lax.axis_index("tile"), lax.axis_size("tile")
    places = (jnp.where(tile > 0, 1, 0), jnp.where(tile < tiles - 1, 1, 0))
    places += tuple((tile + SHIFTS[rounds]) % rounds for rounds in (2, 3))
    for place, value in enumerate(places):
        sides_ref[place] = jnp.full(sides_ref.shape[1:], value, dtype=jnp.int32)
    shot = jnp.full(bits_ref.shape[1:], lax.axis_index("shot"), dtype=jnp.int32)
    for bit in range(bits_ref.shape[0]):
        bits_ref[bit] = shot & (1 << bit)


def both_sides(sides, came):
    has_low, has_high, my_round = sides[0], sides[1], sides[len(came)]
    low, high = came[-1], came[0]
    for number in range(1, len(came)):
        low = jnp.where(my_round == number, came[number - 1], low)
        high = jnp.where(my_round == number, came[number], high)
    return jnp.where(has_low != 0, low, 0.0), jnp.where(has_high != 0, high, 0.0)


def neighbours_part(
    sides_ref, bits_ref, steps_ref, outside_ref, source_ref, coef_ref, *rest
):
    came_refs, (final_ref, *blocks, other, change, edges) = rest[:ROUNDS], rest[ROUNDS:]
    levels, extent, across = coef_ref.shape
    share = blocks[0].shape[1]
    end = LEAD + extent
    low_half = is_low(across)
    weights = lane_weights((8, across))
    sides = [sides_ref[place] for place in range(4)]
    zeros = jnp.zeros((8, across), jnp.float32)

    def received(place):
        return both_sides(sides, [ref[place] for ref in came_refs])

    coefs = [received(2 * levels + pair) for pair in range(levels // 2)]
    for field in range(2):
        for level in range(levels):
            low, high = received(field * levels + level)
            other[field, level, LEAD : LEAD + 8, :] = zeros
            other[field, level, end - 8 : end, :] = zeros
            other[field, level, LEAD - HALO : LEAD, :] = low[0:HALO, :]
            other[field, level, end : end + HALO, :] = high[0:HALO, :]
            half = slice(level % 2 * HALO, level % 2 * HALO + HALO)
            low_coef, high_coef = (coef[half, :] for coef in coefs[level // 2])
            low = low[HALO:, :] + low_coef * outside_ref[field, level, 0:HALO, :]
            high = high[HALO:, :] + high_coef * outside_ref[field, level, HALO : 2 * HALO, :]
            if field == 0:
                low = low + source_ref[level, LEAD - HALO : LEAD, :]
                high = high + source_ref[level, end : end + HALO, :]
            change[field, level, LEAD - HALO : LEAD, :] = low
            change[field, level, end : end + HALO, :] = high
    for field in range(2):
        for level in range(levels):
            left = right = zeros
            for k in range(1, HALO + 1):
                left = left + COEFS[k] * other[field, level, LEAD - k : LEAD - k + 8, :]
                right = right + COEFS[k] * other[field, level, end - 8 + k : end + k, :]
            left = coef_ref[level, 0:8, :] * left
            right = coef_ref[level, extent - 8 : extent, :] * right
            change[field, level, LEAD : LEAD + 8, :] = left
            change[field, level, end - 8 : end, :] = right
            edges[field, level] = left + right
    for field in range(2):
        for level in range(levels):
            total = depth_sum(
                lambda near: edges[field, near],
                level,
                levels,
                lane_sum(edges[field, level], weights),
            )
            for begin, mine in ((0, low_half), (extent - 8, ~low_half)):
                part = beside_sum(change, field, level, LEAD + begin, 8)
                part = part + jnp.where(mine, total, 0.0)
                final_ref[field, level, begin : begin + 8, :] = (
                    steps_ref[field, level, begin : begin + 8, :]
                    + 2.0 * change[field, level, LEAD + begin : LEAD + begin + 8, :]
                    + coef_ref[level, begin : begin + 8, :] * part
                )
    masks = [
        jnp.concatenate([bits_ref[bit]] * (extent // 8), axis=0) != 0
        for bit in range(bits_ref.shape[0])
    ]
    for field in range(2):
        for level in range(share):
            parts = [final_ref[field, place * share + level] for place in range(len(blocks))]
            for bit, mask in enumerate(masks):
                parts = [
                    jnp.where(mask, parts[place ^ (1 << bit)], parts[place])
                    for place in range(len(blocks))
                ]
            for block, part in zip(blocks, parts):
                block[field, level] = part


def widen(weight, sides_ref, blocks, wide):
    mine_ref, *came_refs = blocks
    shots, _, share, extent, _ = mine_ref.shape
    sides = [
        jnp.concatenate([sides_ref[place]] * (extent // 8), axis=0) for place in range(4)
    ]
    for shot in range(shots):
        for field in range(2):
            for level in range(share):
                scale = weight if field == 0 else 1.0
                low, high = both_sides(sides, [ref[shot, field, level] for ref in came_refs])
                wide[shot, field, level, 0:extent, :] = scale * low
                wide[shot, field, level, extent : 2 * extent, :] = (
                    scale * mine_ref[shot, field, level]
                )
                wide[shot, field, level, 2 * extent : 3 * extent, :] = scale * high


def offset_product(wide, offset, level, total):
    extent = wide.shape[3] // 3
    lower = extent + REACH - offset
    upper = extent - REACH + offset
    for shot in range(wide.shape[0]):
        product = (
            wide[shot, 0, level, lower : lower + extent, :]
            * wide[shot, 1, level, upper : upper + extent, :]
        )
        total = product if total is None else total + product
    return total


def stack(*refs):
    for place in range(len(refs) - 1):
        refs[-1][place] = refs[place][...]


def write_fields(final_ref, src_hbm, rec_hbm, sems):
    copies = [
        pltpu.make_async_copy(final_ref.at[field], out.at[0], sems.at[field])
        for field, out in enumerate((src_hbm, rec_hbm))
    ]
    for copy in copies:
        copy.start()
    for copy in copies:
        copy.wait()


def early_products(weight, sides_ref, mine_ref, last_ref, first_ref, image_ref, wide):
    widen(weight, sides_ref, (mine_ref, first_ref, last_ref), wide)
    for offset in range(OFFS):
        for level in range(wide.shape[2]):
            image_ref[offset, level] = offset_product(wide, offset, level, None)


def image_products(weight, sides_ref, mine_ref, *rest):
    came_refs, (early_ref, image_hbm, wide, image_ref, sems) = rest[ROUNDS - 1 :: -1], rest[ROUNDS:]
    widen(weight, sides_ref, (mine_ref, *came_refs), wide)
    parts = sems.shape[0]
    copies = []
    for piece in range(parts):
        offsets = range(piece * OFFS // parts, (piece + 1) * OFFS // parts)
        for offset in offsets:
            for level in range(image_ref.shape[1]):
                image_ref[offset, level] = offset_product(
                    wide, offset, level, early_ref[offset, level]
                )
        rows = pl.ds(offsets[0], len(offsets))
        copy = pltpu.make_async_copy(image_ref.at[rows], image_hbm.at[rows], sems.at[piece])
        copy.start()
        copies.append(copy)
    for copy in copies:
        copy.wait()


def swap_tiles(value, lower):
    tiles, shots = lax.axis_size("tile"), lax.axis_size("shot")
    partner = {}
    for tile in lower:
        partner[tile], partner[tile + 1] = tile + 1, tile
    pairs = []
    for tile in range(tiles):
        for shot in range(shots):
            here = tile * shots + shot
            there = partner[tile] * shots + shot if tile in partner else here ^ 1
            pairs.append((here, there))
    return lax.ppermute(value, ("tile", "shot"), pairs)


def swap_rounds(values):
    tiles, rounds = lax.axis_size("tile"), len(values)
    return [
        swap_tiles(value, range((number - SHIFTS[rounds]) % rounds, tiles - 1, rounds))
        for number, value in enumerate(values)
    ]


def per_device(
    src_prev,
    src_now,
    rec_prev,
    rec_now,
    speed_table,
    region_ids,
    source_cell,
    wavelet,
    receiver_cell,
    receiver_data,
):
    _, levels, extent, across = src_now.shape
    tiles = lax.axis_size("tile")
    width = extent * tiles
    shots = lax.axis_size("shot")
    share = levels // shots
    params = pltpu.CompilerParams(vmem_limit_bytes=LIMIT)

    def struct(*shape):
        return jax.ShapeDtypeStruct(shape, jnp.float32)

    def scratch(*shape, dtype=jnp.float32):
        return pltpu.VMEM(shape, dtype)

    wide_shape = (2, levels, extent + 2 * LEAD, across)
    message = struct(2 * levels + levels // 2, 2 * HALO, across)
    fields_shape = (2, levels, extent, across)
    amps, own, prev, ids, speeds, planes, *sent = pl.pallas_call(
        own_edges,
        out_shape=(
            struct(*wavelet.shape),
            struct(*wide_shape),
            struct(*fields_shape),
            jax.ShapeDtypeStruct(region_ids.shape, jnp.int32),
            struct(8, across),
            struct(2 * extent, across),
            *([message] * ROUNDS),
        ),
        in_specs=[HBM] * 9,
        out_specs=[VMEM] * (6 + ROUNDS),
        scratch_shapes=[
            scratch(1, speed_table.shape[0]),
            scratch(*receiver_cell.shape, dtype=jnp.int32),
            scratch(*receiver_data.shape),
            scratch(2, levels, 8, across),
            pltpu.SemaphoreType.DMA((9,)),
        ],
        compiler_params=params,
        name="own_edges",
    )(
        *(
            pltpu.with_memory_space_constraint(array, pltpu.HBM)
            for array in (
                speed_table.reshape(1, -1),
                receiver_cell,
                receiver_data,
                wavelet,
                region_ids,
                src_now,
                rec_now,
                src_prev,
                rec_prev,
            )
        )
    )
    came_sides = swap_rounds(sent)
    coef, steps, outside, source, sides, bits = pl.pallas_call(
        functools.partial(own_steps, width),
        out_shape=(
            struct(levels, extent, across),
            struct(*fields_shape),
            struct(2, levels, 2 * HALO, across),
            struct(levels, extent + 2 * LEAD, across),
            jax.ShapeDtypeStruct((4, 8, across), jnp.int32),
            jax.ShapeDtypeStruct((shots.bit_length() - 1, 8, across), jnp.int32),
        ),
        in_specs=[SMEM] + [VMEM] * 6,
        out_specs=[VMEM] * 6,
        scratch_shapes=[scratch(*wide_shape)],
        compiler_params=params,
        name="own_steps",
    )(source_cell, amps, own, prev, ids, speeds, planes)
    block = struct(2, share, extent, across)
    final, own_block, *blocks = pl.pallas_call(
        neighbours_part,
        out_shape=(struct(*fields_shape), *([block] * shots)),
        in_specs=[VMEM] * (6 + ROUNDS),
        out_specs=[VMEM] * (1 + shots),
        scratch_shapes=[
            scratch(*wide_shape),
            scratch(*wide_shape),
            scratch(2, levels, 8, across),
        ],
        compiler_params=params,
        name="neighbours_part",
    )(sides, bits, steps, outside, source, coef, *came_sides)
    came = [
        lax.ppermute(sent, "shot", [(shot, shot ^ (1 + i)) for shot in range(shots)])
        for i, sent in enumerate(blocks)
    ]
    weight = 1.0 / shots
    image_shape = (OFFS, share, extent, across)

    def wide_scratch(blocks):
        return scratch(blocks.shape[0], 2, share, 3 * extent, across)

    src_next, rec_next = pl.pallas_call(
        write_fields,
        out_shape=(struct(1, levels, extent, across), struct(1, levels, extent, across)),
        in_specs=[VMEM],
        out_specs=[HBM, HBM],
        scratch_shapes=[pltpu.SemaphoreType.DMA((2,))],
        compiler_params=params,
        name="write_fields",
    )(final)
    groups = []
    for blocks in ([own_block, came[0]], came[1:]):
        group = pl.pallas_call(
            stack,
            out_shape=struct(len(blocks), *own_block.shape),
            in_specs=[VMEM] * len(blocks),
            out_specs=VMEM,
            compiler_params=params,
            name="stack",
        )(*blocks)
        groups.append(group)
    early = pl.pallas_call(
        functools.partial(early_products, weight),
        out_shape=struct(*image_shape),
        in_specs=[VMEM] * 4,
        out_specs=VMEM,
        scratch_shapes=[wide_scratch(groups[0])],
        compiler_params=params,
        name="early_products",
    )(sides, groups[0], *swap_rounds([groups[0]] * 2)[::-1])
    image = pl.pallas_call(
        functools.partial(image_products, weight),
        out_shape=struct(*image_shape),
        in_specs=[VMEM] * (3 + ROUNDS),
        out_specs=HBM,
        scratch_shapes=[
            wide_scratch(groups[1]),
            scratch(*image_shape),
            pltpu.SemaphoreType.DMA((11,)),
        ],
        compiler_params=params,
        name="image_products",
    )(sides, groups[1], *swap_rounds([groups[1]] * ROUNDS)[::-1], early)
    return src_next, rec_next, image


def solution(mesh):
    field = P(("groups", "shot"), None, "tile", None)
    return jax.shard_map(
        per_device,
        mesh=mesh,
        in_specs=(
            field,
            field,
            field,
            field,
            P("groups"),
            P(None, ("groups", "tile"), None),
            P(("groups", "shot")),
            P(("groups", "shot"), None),
            P(("groups", "shot"), "tile"),
            P(("groups", "shot"), None, "tile"),
        ),
        out_specs=(field, field, P(None, "shot", ("groups", "tile"), None)),
        check_vma=False,
    )
```

```python
import functools

import jax
import jax.numpy as jnp
from jax import lax
from jax.experimental import pallas as pl
from jax.experimental.pallas import tpu as pltpu
from jax.sharding import PartitionSpec as P

OFFS = 33
REACH = OFFS // 2
HALO = 4
LEAD = 8
ROUNDS = 3
SHIFTS = {2: 0, 3: 0}

COEFS = (-205.0 / 72.0, 8.0 / 5.0, -1.0 / 5.0, 8.0 / 315.0, -1.0 / 560.0)

VMEM = pl.BlockSpec(memory_space=pltpu.VMEM)
HBM = pl.BlockSpec(memory_space=pltpu.HBM)
SMEM = pl.BlockSpec(memory_space=pltpu.SMEM)
LIMIT = 16 * 1024 * 1024


def lane_weights(shape):
    lane = lax.broadcasted_iota(jnp.int32, shape, 1)
    across = shape[1]
    after = [jnp.where(lane < across - k, COEFS[k], 0.0) for k in range(1, HALO + 1)]
    before = [jnp.where(lane >= k, COEFS[k], 0.0) for k in range(1, HALO + 1)]
    return after, before


def lane_sum(centre, weights):
    after, before = weights
    across = centre.shape[1]
    total = 3.0 * COEFS[0] * centre
    for k in range(1, HALO + 1):
        total = total + after[k - 1] * pltpu.roll(centre, across - k, 1)
        total = total + before[k - 1] * pltpu.roll(centre, k, 1)
    return total


def beside_sum(wide, field, level, begin, count):
    total = None
    for k in range(1, HALO + 1):
        pair = (
            wide[field, level, begin + k : begin + k + count, :]
            + wide[field, level, begin - k : begin - k + count, :]
        )
        total = COEFS[k] * pair if total is None else total + COEFS[k] * pair
    return total


def depth_sum(rows_of, level, levels, total):
    for k in range(1, HALO + 1):
        for near in (level - k, level + k):
            if 0 <= near < levels:
                total = total + COEFS[k] * rows_of(near)
    return total


def laplace_level(wide, field, level, levels, extent, weights):
    def rows_of(near):
        return wide[field, near, LEAD : LEAD + extent, :]

    total = lane_sum(rows_of(level), weights) + beside_sum(wide, field, level, LEAD, extent)
    return depth_sum(rows_of, level, levels, total)


def receiver_rows(spots, across):
    lane = lax.broadcasted_iota(jnp.int32, (across, spots.shape[1]), 0)
    return jnp.where(lax.rem(spots, across) == lane, 1.0, 0.0)


def receiver_values(spots, trace, columns, across):
    begin = columns * across
    return jnp.where((spots >= begin) & (spots < begin + across), trace, 0.0)


def receiver_product(values, rows, precision=None):
    return lax.dot_general(
        values,
        rows,
        (((1,), (1,)), ((), ())),
        precision=precision,
        preferred_element_type=jnp.float32,
    )


def is_low(across):
    return lax.broadcasted_iota(jnp.int32, (8, across), 0) < HALO


def own_edges(
    table_hbm,
    spots_hbm,
    traces_hbm,
    amps_hbm,
    ids_hbm,
    src_now,
    rec_now,
    src_prev,
    rec_prev,
    amps_ref,
    wide,
    prev_ref,
    ids_ref,
    speeds_ref,
    spots_ref,
    traces_ref,
    *rest,
):
    sent_refs, rest = rest[:ROUNDS], rest[ROUNDS:]
    table, edges, sems = rest
    levels, extent, across = ids_ref.shape
    regions = table_hbm.shape[1]
    end = LEAD + extent
    rows = pl.ds(LEAD, extent)
    moves = [(table_hbm, table), (spots_hbm, spots_ref), (traces_hbm, traces_ref)]
    moves += [
        (src_now.at[0], wide.at[0, :, rows, :]),
        (rec_now.at[0], wide.at[1, :, rows, :]),
        (ids_hbm, ids_ref),
        (src_prev.at[0], prev_ref.at[0]),
        (rec_prev.at[0], prev_ref.at[1]),
    ]
    moves.append((amps_hbm, amps_ref))
    copies = [
        pltpu.make_async_copy(here, there, sems.at[i]) for i, (here, there) in enumerate(moves)
    ]
    for copy in copies:
        copy.start()
    zeros = jnp.zeros((LEAD, across), jnp.float32)
    for field in range(2):
        for level in range(levels):
            wide[field, level, 0:LEAD, :] = zeros
            wide[field, level, end : end + LEAD, :] = zeros
    weights = lane_weights((8, across))
    low_half = is_low(across)
    my_round = lax.rem(lax.axis_index("tile"), ROUNDS)
    for copy in copies:
        copy.wait()

    spots = spots_ref[...]
    row = lax.broadcasted_iota(jnp.int32, (8, spots.shape[1]), 0)
    columns = jnp.where(row < HALO, row, row + extent - 8)
    values = receiver_values(spots, traces_ref[0, 0:1, :], columns, across)
    parts = []
    for _ in range(3):
        parts.append(values.astype(jnp.bfloat16).astype(jnp.float32))
        values = values - parts[-1]
    parts = jnp.concatenate([*parts, jnp.zeros_like(values)], axis=0).astype(jnp.bfloat16)
    planes = receiver_product(parts, receiver_rows(spots, across).astype(jnp.bfloat16))
    injected = planes[0:8, :] + planes[8:16, :] + planes[16:24, :]

    def send(place, low, high):
        for number, sent_ref in enumerate(sent_refs):
            sent_ref[place] = jnp.where(my_round == number, high, low)

    def halves(ref, *place):
        return jnp.where(
            low_half, ref[(*place, pl.ds(0, 8))], ref[(*place, pl.ds(extent - 8, 8))]
        )

    speeds = jnp.concatenate(
        [table[...], jnp.zeros((1, across - regions), jnp.float32)], axis=1
    )
    speeds = jnp.broadcast_to(speeds, (8, across))
    speeds_ref[...] = speeds
    coefs = [
        jnp.take_along_axis(speeds, halves(ids_ref, level), axis=1, mode="promise_in_bounds")
        for level in range(levels)
    ]
    for level in range(0, levels, 2):
        here, after = coefs[level], coefs[level + 1]
        send(
            2 * levels + level // 2,
            jnp.where(low_half, here, pltpu.roll(after, HALO, 0)),
            jnp.where(low_half, pltpu.roll(here, HALO, 0), after),
        )

    for field in range(2):
        for level in range(levels):
            edges[field, level] = jnp.where(
                low_half, wide[field, level, LEAD : LEAD + 8, :], wide[field, level, end - 8 : end, :]
            )
    for field in range(2):
        for level in range(levels):
            now = edges[field, level]
            total = lane_sum(now, weights) + jnp.where(
                low_half,
                beside_sum(wide, field, level, LEAD, 8),
                beside_sum(wide, field, level, end - 8, 8),
            )
            total = depth_sum(lambda near: edges[field, near], level, levels, total)
            value = 2.0 * now - halves(prev_ref, field, level) + coefs[level] * total
            if field == 1 and level == 0:
                value = value + injected
            send(
                field * levels + level,
                jnp.where(low_half, now, pltpu.roll(value, HALO, 0)),
                jnp.where(low_half, pltpu.roll(now, HALO, 0), value),
            )


def own_steps(
    width,
    cell_ref,
    amps_ref,
    own,
    prev_ref,
    ids_ref,
    speeds_ref,
    spots_ref,
    traces_ref,
    coef_ref,
    steps_ref,
    outside_ref,
    source_ref,
    sides_ref,
    bits_ref,
    middle,
):
    levels, extent, across = ids_ref.shape
    end = LEAD + extent
    cell = cell_ref[0]
    deep = lax.div(cell, width * across)
    row = lax.rem(lax.div(cell, across), width) - lax.axis_index("tile") * extent + LEAD
    shape = (extent + 2 * LEAD, across)
    rows = lax.broadcasted_iota(jnp.int32, shape, 0)
    lanes = lax.broadcasted_iota(jnp.int32, shape, 1)
    hit = jnp.where((rows == row) & (lanes == lax.rem(cell, across)), 1.0, 0.0)
    weights = lane_weights((extent, across))
    speeds = speeds_ref[...]
    zeros = jnp.zeros((LEAD, across), jnp.float32)
    for level in range(levels):
        here = hit * jnp.where(deep == level, 1.0, 0.0)
        source_ref[level] = here * amps_ref[0:1, 0:1]
        steps_ref[0, level] = here[LEAD:end, :] * amps_ref[0:1, 1:2] - own[0, level, LEAD:end, :]
        steps_ref[1, level] = -own[1, level, LEAD:end, :]
        for begin in range(0, extent, 8):
            coef_ref[level, begin : begin + 8, :] = jnp.take_along_axis(
                speeds, ids_ref[level, begin : begin + 8, :], axis=1, mode="promise_in_bounds"
            )
    spots = spots_ref[...]
    columns = lax.broadcasted_iota(jnp.int32, (extent, spots.shape[1]), 0)
    planes = receiver_product(
        jnp.concatenate(
            [
                receiver_values(spots, traces_ref[0, t : t + 1, :], columns, across)
                for t in range(2)
            ],
            axis=0,
        ),
        receiver_rows(spots, across),
        lax.Precision.HIGHEST,
    )
    steps_ref[1, 0] += planes[extent:, :]
    for field in range(2):
        for level in range(levels):
            total = laplace_level(own, field, level, levels, extent, weights)
            value = 2.0 * own[field, level, LEAD:end, :] - prev_ref[field, level]
            value = value + coef_ref[level] * total
            if field == 0:
                value = value + source_ref[level, LEAD:end, :]
            elif level == 0:
                value = value + planes[:extent, :]
            middle[field, level, 0:LEAD, :] = zeros
            middle[field, level, LEAD:end, :] = value
            middle[field, level, end : end + LEAD, :] = zeros
            below = above = jnp.zeros((HALO, across), jnp.float32)
            for k in range(1, HALO + 1):
                begin = LEAD - HALO + k
                below = below + COEFS[k] * own[field, level, begin : begin + HALO, :]
                above = above + COEFS[k] * own[field, level, end - k : end - k + HALO, :]
            outside_ref[field, level, 0:HALO, :] = below
            outside_ref[field, level, HALO : 2 * HALO, :] = above
    for field in range(2):
        for level in range(levels):
            total = laplace_level(middle, field, level, levels, extent, weights)
            steps_ref[field, level] += (
                2.0 * middle[field, level, LEAD:end, :] + coef_ref[level] * total
            )
    tile, tiles = lax.axis_index("tile"), lax.axis_size("tile")
    places = (jnp.where(tile > 0, 1, 0), jnp.where(tile < tiles - 1, 1, 0))
    places += tuple((tile + SHIFTS[rounds]) % rounds for rounds in (2, 3))
    for place, value in enumerate(places):
        sides_ref[place] = jnp.full(sides_ref.shape[1:], value, dtype=jnp.int32)
    shot = jnp.full(bits_ref.shape[1:], lax.axis_index("shot"), dtype=jnp.int32)
    for bit in range(bits_ref.shape[0]):
        bits_ref[bit] = shot & (1 << bit)


def both_sides(sides, came):
    has_low, has_high, my_round = sides[0], sides[1], sides[len(came)]
    low, high = came[-1], came[0]
    for number in range(1, len(came)):
        low = jnp.where(my_round == number, came[number - 1], low)
        high = jnp.where(my_round == number, came[number], high)
    return jnp.where(has_low != 0, low, 0.0), jnp.where(has_high != 0, high, 0.0)


def neighbours_part(
    sides_ref, bits_ref, steps_ref, outside_ref, source_ref, coef_ref, *rest
):
    came_refs, (final_ref, *blocks, other, change, edges) = rest[:ROUNDS], rest[ROUNDS:]
    levels, extent, across = coef_ref.shape
    share = blocks[0].shape[1]
    end = LEAD + extent
    low_half = is_low(across)
    weights = lane_weights((8, across))
    sides = [sides_ref[place] for place in range(4)]
    zeros = jnp.zeros((8, across), jnp.float32)

    def received(place):
        return both_sides(sides, [ref[place] for ref in came_refs])

    coefs = [received(2 * levels + pair) for pair in range(levels // 2)]
    for field in range(2):
        for level in range(levels):
            low, high = received(field * levels + level)
            other[field, level, LEAD : LEAD + 8, :] = zeros
            other[field, level, end - 8 : end, :] = zeros
            other[field, level, LEAD - HALO : LEAD, :] = low[0:HALO, :]
            other[field, level, end : end + HALO, :] = high[0:HALO, :]
            half = slice(level % 2 * HALO, level % 2 * HALO + HALO)
            low_coef, high_coef = (coef[half, :] for coef in coefs[level // 2])
            low = low[HALO:, :] + low_coef * outside_ref[field, level, 0:HALO, :]
            high = high[HALO:, :] + high_coef * outside_ref[field, level, HALO : 2 * HALO, :]
            if field == 0:
                low = low + source_ref[level, LEAD - HALO : LEAD, :]
                high = high + source_ref[level, end : end + HALO, :]
            change[field, level, LEAD - HALO : LEAD, :] = low
            change[field, level, end : end + HALO, :] = high
    for field in range(2):
        for level in range(levels):
            left = right = zeros
            for k in range(1, HALO + 1):
                left = left + COEFS[k] * other[field, level, LEAD - k : LEAD - k + 8, :]
                right = right + COEFS[k] * other[field, level, end - 8 + k : end + k, :]
            left = coef_ref[level, 0:8, :] * left
            right = coef_ref[level, extent - 8 : extent, :] * right
            change[field, level, LEAD : LEAD + 8, :] = left
            change[field, level, end - 8 : end, :] = right
            edges[field, level] = left + right
    for field in range(2):
        for level in range(levels):
            total = depth_sum(
                lambda near: edges[field, near],
                level,
                levels,
                lane_sum(edges[field, level], weights),
            )
            for begin, mine in ((0, low_half), (extent - 8, ~low_half)):
                part = beside_sum(change, field, level, LEAD + begin, 8)
                part = part + jnp.where(mine, total, 0.0)
                final_ref[field, level, begin : begin + 8, :] = (
                    steps_ref[field, level, begin : begin + 8, :]
                    + 2.0 * change[field, level, LEAD + begin : LEAD + begin + 8, :]
                    + coef_ref[level, begin : begin + 8, :] * part
                )
    masks = [
        jnp.concatenate([bits_ref[bit]] * (extent // 8), axis=0) != 0
        for bit in range(bits_ref.shape[0])
    ]
    for field in range(2):
        for level in range(share):
            parts = [final_ref[field, place * share + level] for place in range(len(blocks))]
            for bit, mask in enumerate(masks):
                parts = [
                    jnp.where(mask, parts[place ^ (1 << bit)], parts[place])
                    for place in range(len(blocks))
                ]
            for block, part in zip(blocks, parts):
                block[field, level] = part


def widen(weight, sides_ref, blocks, wide):
    mine_ref, *came_refs = blocks
    shots, _, share, extent, _ = mine_ref.shape
    sides = [
        jnp.concatenate([sides_ref[place]] * (extent // 8), axis=0) for place in range(4)
    ]
    for shot in range(shots):
        for field in range(2):
            for level in range(share):
                scale = weight if field == 0 else 1.0
                low, high = both_sides(sides, [ref[shot, field, level] for ref in came_refs])
                wide[shot, field, level, 0:extent, :] = scale * low
                wide[shot, field, level, extent : 2 * extent, :] = (
                    scale * mine_ref[shot, field, level]
                )
                wide[shot, field, level, 2 * extent : 3 * extent, :] = scale * high


def offset_product(wide, offset, level, total):
    extent = wide.shape[3] // 3
    lower = extent + REACH - offset
    upper = extent - REACH + offset
    for shot in range(wide.shape[0]):
        product = (
            wide[shot, 0, level, lower : lower + extent, :]
            * wide[shot, 1, level, upper : upper + extent, :]
        )
        total = product if total is None else total + product
    return total


def stack(*refs):
    for place in range(len(refs) - 1):
        refs[-1][place] = refs[place][...]


def write_fields(final_ref, src_hbm, rec_hbm, sems):
    copies = [
        pltpu.make_async_copy(final_ref.at[field], out.at[0], sems.at[field])
        for field, out in enumerate((src_hbm, rec_hbm))
    ]
    for copy in copies:
        copy.start()
    for copy in copies:
        copy.wait()


def early_products(weight, sides_ref, mine_ref, last_ref, first_ref, image_ref, wide):
    widen(weight, sides_ref, (mine_ref, first_ref, last_ref), wide)
    for offset in range(OFFS):
        for level in range(wide.shape[2]):
            image_ref[offset, level] = offset_product(wide, offset, level, None)


def image_products(weight, sides_ref, mine_ref, *rest):
    came_refs, (early_ref, image_hbm, wide, image_ref, sems) = rest[ROUNDS - 1 :: -1], rest[ROUNDS:]
    widen(weight, sides_ref, (mine_ref, *came_refs), wide)
    parts = sems.shape[0]
    copies = []
    for piece in range(parts):
        offsets = range(piece * OFFS // parts, (piece + 1) * OFFS // parts)
        for offset in offsets:
            for level in range(image_ref.shape[1]):
                image_ref[offset, level] = offset_product(
                    wide, offset, level, early_ref[offset, level]
                )
        rows = pl.ds(offsets[0], len(offsets))
        copy = pltpu.make_async_copy(image_ref.at[rows], image_hbm.at[rows], sems.at[piece])
        copy.start()
        copies.append(copy)
    for copy in copies:
        copy.wait()


def swap_tiles(value, lower):
    tiles, shots = lax.axis_size("tile"), lax.axis_size("shot")
    partner = {}
    for tile in lower:
        partner[tile], partner[tile + 1] = tile + 1, tile
    pairs = []
    for tile in range(tiles):
        for shot in range(shots):
            here = tile * shots + shot
            there = partner[tile] * shots + shot if tile in partner else here ^ 1
            pairs.append((here, there))
    return lax.ppermute(value, ("tile", "shot"), pairs)


def swap_rounds(values):
    tiles, rounds = lax.axis_size("tile"), len(values)
    return [
        swap_tiles(value, range((number - SHIFTS[rounds]) % rounds, tiles - 1, rounds))
        for number, value in enumerate(values)
    ]


def per_device(
    src_prev,
    src_now,
    rec_prev,
    rec_now,
    speed_table,
    region_ids,
    source_cell,
    wavelet,
    receiver_cell,
    receiver_data,
):
    _, levels, extent, across = src_now.shape
    tiles = lax.axis_size("tile")
    width = extent * tiles
    shots = lax.axis_size("shot")
    share = levels // shots
    params = pltpu.CompilerParams(vmem_limit_bytes=LIMIT)

    def struct(*shape):
        return jax.ShapeDtypeStruct(shape, jnp.float32)

    def scratch(*shape, dtype=jnp.float32):
        return pltpu.VMEM(shape, dtype)

    wide_shape = (2, levels, extent + 2 * LEAD, across)
    message = struct(2 * levels + levels // 2, 2 * HALO, across)
    fields_shape = (2, levels, extent, across)
    amps, own, prev, ids, speeds, spots, traces, *sent = pl.pallas_call(
        own_edges,
        out_shape=(
            struct(*wavelet.shape),
            struct(*wide_shape),
            struct(*fields_shape),
            jax.ShapeDtypeStruct(region_ids.shape, jnp.int32),
            struct(8, across),
            jax.ShapeDtypeStruct(receiver_cell.shape, jnp.int32),
            struct(*receiver_data.shape),
            *([message] * ROUNDS),
        ),
        in_specs=[HBM] * 9,
        out_specs=[VMEM] * (7 + ROUNDS),
        scratch_shapes=[
            scratch(1, speed_table.shape[0]),
            scratch(2, levels, 8, across),
            pltpu.SemaphoreType.DMA((9,)),
        ],
        compiler_params=params,
        name="own_edges",
    )(
        *(
            pltpu.with_memory_space_constraint(array, pltpu.HBM)
            for array in (
                speed_table.reshape(1, -1),
                receiver_cell,
                receiver_data,
                wavelet,
                region_ids,
                src_now,
                rec_now,
                src_prev,
                rec_prev,
            )
        )
    )
    came_sides = swap_rounds(sent)
    coef, steps, outside, source, sides, bits = pl.pallas_call(
        functools.partial(own_steps, width),
        out_shape=(
            struct(levels, extent, across),
            struct(*fields_shape),
            struct(2, levels, 2 * HALO, across),
            struct(levels, extent + 2 * LEAD, across),
            jax.ShapeDtypeStruct((4, 8, across), jnp.int32),
            jax.ShapeDtypeStruct((shots.bit_length() - 1, 8, across), jnp.int32),
        ),
        in_specs=[SMEM] + [VMEM] * 7,
        out_specs=[VMEM] * 6,
        scratch_shapes=[scratch(*wide_shape)],
        compiler_params=params,
        name="own_steps",
    )(source_cell, amps, own, prev, ids, speeds, spots, traces)
    block = struct(2, share, extent, across)
    final, own_block, *blocks = pl.pallas_call(
        neighbours_part,
        out_shape=(struct(*fields_shape), *([block] * shots)),
        in_specs=[VMEM] * (6 + ROUNDS),
        out_specs=[VMEM] * (1 + shots),
        scratch_shapes=[
            scratch(*wide_shape),
            scratch(*wide_shape),
            scratch(2, levels, 8, across),
        ],
        compiler_params=params,
        name="neighbours_part",
    )(sides, bits, steps, outside, source, coef, *came_sides)
    came = [
        lax.ppermute(sent, "shot", [(shot, shot ^ (1 + i)) for shot in range(shots)])
        for i, sent in enumerate(blocks)
    ]
    weight = 1.0 / shots
    image_shape = (OFFS, share, extent, across)

    def wide_scratch(blocks):
        return scratch(blocks.shape[0], 2, share, 3 * extent, across)

    src_next, rec_next = pl.pallas_call(
        write_fields,
        out_shape=(struct(1, levels, extent, across), struct(1, levels, extent, across)),
        in_specs=[VMEM],
        out_specs=[HBM, HBM],
        scratch_shapes=[pltpu.SemaphoreType.DMA((2,))],
        compiler_params=params,
        name="write_fields",
    )(final)
    groups = []
    for blocks in ([own_block, came[0]], came[1:]):
        group = pl.pallas_call(
            stack,
            out_shape=struct(len(blocks), *own_block.shape),
            in_specs=[VMEM] * len(blocks),
            out_specs=VMEM,
            compiler_params=params,
            name="stack",
        )(*blocks)
        groups.append(group)
    early = pl.pallas_call(
        functools.partial(early_products, weight),
        out_shape=struct(*image_shape),
        in_specs=[VMEM] * 4,
        out_specs=VMEM,
        scratch_shapes=[wide_scratch(groups[0])],
        compiler_params=params,
        name="early_products",
    )(sides, groups[0], *swap_rounds([groups[0]] * 2)[::-1])
    image = pl.pallas_call(
        functools.partial(image_products, weight),
        out_shape=struct(*image_shape),
        in_specs=[VMEM] * (3 + ROUNDS),
        out_specs=HBM,
        scratch_shapes=[
            wide_scratch(groups[1]),
            scratch(*image_shape),
            pltpu.SemaphoreType.DMA((11,)),
        ],
        compiler_params=params,
        name="image_products",
    )(sides, groups[1], *swap_rounds([groups[1]] * ROUNDS)[::-1], early)
    return src_next, rec_next, image


def solution(mesh):
    field = P(("groups", "shot"), None, "tile", None)
    return jax.shard_map(
        per_device,
        mesh=mesh,
        in_specs=(
            field,
            field,
            field,
            field,
            P("groups"),
            P(None, ("groups", "tile"), None),
            P(("groups", "shot")),
            P(("groups", "shot"), None),
            P(("groups", "shot"), "tile"),
            P(("groups", "shot"), None, "tile"),
        ),
        out_specs=(field, field, P(None, "shot", ("groups", "tile"), None)),
        check_vma=False,
    )
```

```python
import functools

import jax
import jax.numpy as jnp
from jax import lax
from jax.experimental import pallas as pl
from jax.experimental.pallas import tpu as pltpu
from jax.sharding import PartitionSpec as P

OFFS = 33
REACH = OFFS // 2
HALO = 4
LEAD = 8
ROUNDS = 3
SHIFTS = {2: 0, 3: 0}

COEFS = (-205.0 / 72.0, 8.0 / 5.0, -1.0 / 5.0, 8.0 / 315.0, -1.0 / 560.0)

VMEM = pl.BlockSpec(memory_space=pltpu.VMEM)
HBM = pl.BlockSpec(memory_space=pltpu.HBM)
SMEM = pl.BlockSpec(memory_space=pltpu.SMEM)
LIMIT = 16 * 1024 * 1024


def lane_weights(shape):
    lane = lax.broadcasted_iota(jnp.int32, shape, 1)
    across = shape[1]
    after = [jnp.where(lane < across - k, COEFS[k], 0.0) for k in range(1, HALO + 1)]
    before = [jnp.where(lane >= k, COEFS[k], 0.0) for k in range(1, HALO + 1)]
    return after, before


def lane_sum(centre, weights):
    after, before = weights
    across = centre.shape[1]
    total = 3.0 * COEFS[0] * centre
    for k in range(1, HALO + 1):
        total = total + after[k - 1] * pltpu.roll(centre, across - k, 1)
        total = total + before[k - 1] * pltpu.roll(centre, k, 1)
    return total


def beside_sum(wide, field, level, begin, count):
    total = None
    for k in range(1, HALO + 1):
        pair = (
            wide[field, level, begin + k : begin + k + count, :]
            + wide[field, level, begin - k : begin - k + count, :]
        )
        total = COEFS[k] * pair if total is None else total + COEFS[k] * pair
    return total


def depth_sum(rows_of, level, levels, total):
    for k in range(1, HALO + 1):
        for near in (level - k, level + k):
            if 0 <= near < levels:
                total = total + COEFS[k] * rows_of(near)
    return total


def laplace_level(wide, field, level, levels, extent, weights):
    def rows_of(near):
        return wide[field, near, LEAD : LEAD + extent, :]

    total = lane_sum(rows_of(level), weights) + beside_sum(wide, field, level, LEAD, extent)
    return depth_sum(rows_of, level, levels, total)


def is_low(across):
    return lax.broadcasted_iota(jnp.int32, (8, across), 0) < HALO


def own_edges(
    table_hbm,
    spots_hbm,
    traces_hbm,
    amps_hbm,
    ids_hbm,
    src_now,
    rec_now,
    src_prev,
    rec_prev,
    amps_ref,
    wide,
    prev_ref,
    ids_ref,
    speeds_ref,
    planes_ref,
    *rest,
):
    sent_refs, rest = rest[:ROUNDS], rest[ROUNDS:]
    table, spots_ref, traces_ref, edges, sems = rest
    levels, extent, across = ids_ref.shape
    regions = table_hbm.shape[1]
    end = LEAD + extent
    rows = pl.ds(LEAD, extent)
    moves = [(table_hbm, table), (spots_hbm, spots_ref), (traces_hbm, traces_ref)]
    for begin in range(0, levels, levels // 2):
        part = pl.ds(begin, levels // 2)
        moves += [
            (src_now.at[0, part], wide.at[0, part, rows, :]),
            (rec_now.at[0, part], wide.at[1, part, rows, :]),
            (ids_hbm.at[part], ids_ref.at[part]),
            (src_prev.at[0, part], prev_ref.at[0, part]),
            (rec_prev.at[0, part], prev_ref.at[1, part]),
        ]
    moves.append((amps_hbm, amps_ref))
    copies = [
        pltpu.make_async_copy(here, there, sems.at[i]) for i, (here, there) in enumerate(moves)
    ]
    for copy in copies:
        copy.start()
    zeros = jnp.zeros((LEAD, across), jnp.float32)
    for field in range(2):
        for level in range(levels):
            wide[field, level, 0:LEAD, :] = zeros
            wide[field, level, end : end + LEAD, :] = zeros
    weights = lane_weights((8, across))
    low_half = is_low(across)
    my_round = lax.rem(lax.axis_index("tile"), ROUNDS)
    for copy in copies:
        copy.wait()

    spots = spots_ref[...]
    column = lax.broadcasted_iota(jnp.int32, (extent, spots.shape[1]), 0) * across
    in_column = (spots >= column) & (spots < column + across)
    lane = lax.broadcasted_iota(jnp.int32, (across, spots.shape[1]), 0)
    in_row = jnp.where(lax.rem(spots, across) == lane, 1.0, 0.0)
    traces = jnp.concatenate(
        [jnp.where(in_column, traces_ref[0, t : t + 1, :], 0.0) for t in range(2)], axis=0
    )
    planes = lax.dot_general(
        traces,
        in_row,
        (((1,), (1,)), ((), ())),
        precision=lax.Precision.HIGHEST,
        preferred_element_type=jnp.float32,
    )
    planes_ref[...] = planes

    def send(place, low, high):
        for number, sent_ref in enumerate(sent_refs):
            sent_ref[place] = jnp.where(my_round == number, high, low)

    def halves(ref, *place):
        return jnp.where(
            low_half, ref[(*place, pl.ds(0, 8))], ref[(*place, pl.ds(extent - 8, 8))]
        )

    speeds = jnp.concatenate(
        [table[...], jnp.zeros((1, across - regions), jnp.float32)], axis=1
    )
    speeds = jnp.broadcast_to(speeds, (8, across))
    speeds_ref[...] = speeds
    coefs = [
        jnp.take_along_axis(speeds, halves(ids_ref, level), axis=1, mode="promise_in_bounds")
        for level in range(levels)
    ]
    for level in range(0, levels, 2):
        here, after = coefs[level], coefs[level + 1]
        send(
            2 * levels + level // 2,
            jnp.where(low_half, here, pltpu.roll(after, HALO, 0)),
            jnp.where(low_half, pltpu.roll(here, HALO, 0), after),
        )

    for field in range(2):
        for level in range(levels):
            edges[field, level] = jnp.where(
                low_half, wide[field, level, LEAD : LEAD + 8, :], wide[field, level, end - 8 : end, :]
            )
    for field in range(2):
        for level in range(levels):
            now = edges[field, level]
            total = lane_sum(now, weights) + jnp.where(
                low_half,
                beside_sum(wide, field, level, LEAD, 8),
                beside_sum(wide, field, level, end - 8, 8),
            )
            total = depth_sum(lambda near: edges[field, near], level, levels, total)
            value = 2.0 * now - halves(prev_ref, field, level) + coefs[level] * total
            if field == 1 and level == 0:
                value = value + jnp.where(low_half, planes[0:8, :], planes[extent - 8 : extent, :])
            send(
                field * levels + level,
                jnp.where(low_half, now, pltpu.roll(value, HALO, 0)),
                jnp.where(low_half, pltpu.roll(now, HALO, 0), value),
            )


def own_steps(
    width,
    cell_ref,
    amps_ref,
    own,
    prev_ref,
    ids_ref,
    speeds_ref,
    planes_ref,
    coef_ref,
    steps_ref,
    outside_ref,
    source_ref,
    sides_ref,
    bits_ref,
    middle,
):
    levels, extent, across = ids_ref.shape
    end = LEAD + extent
    cell = cell_ref[0]
    deep = lax.div(cell, width * across)
    row = lax.rem(lax.div(cell, across), width) - lax.axis_index("tile") * extent + LEAD
    shape = (extent + 2 * LEAD, across)
    rows = lax.broadcasted_iota(jnp.int32, shape, 0)
    lanes = lax.broadcasted_iota(jnp.int32, shape, 1)
    hit = jnp.where((rows == row) & (lanes == lax.rem(cell, across)), 1.0, 0.0)
    weights = lane_weights((extent, across))
    speeds = speeds_ref[...]
    zeros = jnp.zeros((LEAD, across), jnp.float32)
    for level in range(levels):
        here = hit * jnp.where(deep == level, 1.0, 0.0)
        source_ref[level] = here * amps_ref[0:1, 0:1]
        steps_ref[0, level] = here[LEAD:end, :] * amps_ref[0:1, 1:2] - own[0, level, LEAD:end, :]
        steps_ref[1, level] = -own[1, level, LEAD:end, :]
        for begin in range(0, extent, 8):
            coef_ref[level, begin : begin + 8, :] = jnp.take_along_axis(
                speeds, ids_ref[level, begin : begin + 8, :], axis=1, mode="promise_in_bounds"
            )
    steps_ref[1, 0] += planes_ref[extent:, :]
    for field in range(2):
        for level in range(levels):
            total = laplace_level(own, field, level, levels, extent, weights)
            value = 2.0 * own[field, level, LEAD:end, :] - prev_ref[field, level]
            value = value + coef_ref[level] * total
            if field == 0:
                value = value + source_ref[level, LEAD:end, :]
            elif level == 0:
                value = value + planes_ref[:extent, :]
            middle[field, level, 0:LEAD, :] = zeros
            middle[field, level, LEAD:end, :] = value
            middle[field, level, end : end + LEAD, :] = zeros
            below = above = jnp.zeros((HALO, across), jnp.float32)
            for k in range(1, HALO + 1):
                begin = LEAD - HALO + k
                below = below + COEFS[k] * own[field, level, begin : begin + HALO, :]
                above = above + COEFS[k] * own[field, level, end - k : end - k + HALO, :]
            outside_ref[field, level, 0:HALO, :] = below
            outside_ref[field, level, HALO : 2 * HALO, :] = above
    for field in range(2):
        for level in range(levels):
            total = laplace_level(middle, field, level, levels, extent, weights)
            steps_ref[field, level] += (
                2.0 * middle[field, level, LEAD:end, :] + coef_ref[level] * total
            )
    tile, tiles = lax.axis_index("tile"), lax.axis_size("tile")
    places = (jnp.where(tile > 0, 1, 0), jnp.where(tile < tiles - 1, 1, 0))
    places += tuple((tile + SHIFTS[rounds]) % rounds for rounds in (2, 3))
    for place, value in enumerate(places):
        sides_ref[place] = jnp.full(sides_ref.shape[1:], value, dtype=jnp.int32)
    shot = jnp.full(bits_ref.shape[1:], lax.axis_index("shot"), dtype=jnp.int32)
    for bit in range(bits_ref.shape[0]):
        bits_ref[bit] = shot & (1 << bit)


def both_sides(sides, came):
    has_low, has_high, my_round = sides[0], sides[1], sides[len(came)]
    low, high = came[-1], came[0]
    for number in range(1, len(came)):
        low = jnp.where(my_round == number, came[number - 1], low)
        high = jnp.where(my_round == number, came[number], high)
    return jnp.where(has_low != 0, low, 0.0), jnp.where(has_high != 0, high, 0.0)


def neighbours_part(
    sides_ref, bits_ref, steps_ref, outside_ref, source_ref, coef_ref, *rest
):
    came_refs, (final_ref, mine_ref, *blocks, other, change, edges) = rest[:ROUNDS], rest[ROUNDS:]
    blocks = [mine_ref.at[0], mine_ref.at[1], *blocks]
    levels, extent, across = coef_ref.shape
    share = mine_ref.shape[2]
    end = LEAD + extent
    low_half = is_low(across)
    weights = lane_weights((8, across))
    sides = [sides_ref[place] for place in range(4)]
    zeros = jnp.zeros((8, across), jnp.float32)

    def received(place):
        return both_sides(sides, [ref[place] for ref in came_refs])

    coefs = [received(2 * levels + pair) for pair in range(levels // 2)]
    for field in range(2):
        for level in range(levels):
            low, high = received(field * levels + level)
            other[field, level, LEAD : LEAD + 8, :] = zeros
            other[field, level, end - 8 : end, :] = zeros
            other[field, level, LEAD - HALO : LEAD, :] = low[0:HALO, :]
            other[field, level, end : end + HALO, :] = high[0:HALO, :]
            half = slice(level % 2 * HALO, level % 2 * HALO + HALO)
            low_coef, high_coef = (coef[half, :] for coef in coefs[level // 2])
            low = low[HALO:, :] + low_coef * outside_ref[field, level, 0:HALO, :]
            high = high[HALO:, :] + high_coef * outside_ref[field, level, HALO : 2 * HALO, :]
            if field == 0:
                low = low + source_ref[level, LEAD - HALO : LEAD, :]
                high = high + source_ref[level, end : end + HALO, :]
            change[field, level, LEAD - HALO : LEAD, :] = low
            change[field, level, end : end + HALO, :] = high
    for field in range(2):
        for level in range(levels):
            left = right = zeros
            for k in range(1, HALO + 1):
                left = left + COEFS[k] * other[field, level, LEAD - k : LEAD - k + 8, :]
                right = right + COEFS[k] * other[field, level, end - 8 + k : end + k, :]
            left = coef_ref[level, 0:8, :] * left
            right = coef_ref[level, extent - 8 : extent, :] * right
            change[field, level, LEAD : LEAD + 8, :] = left
            change[field, level, end - 8 : end, :] = right
            edges[field, level] = left + right
    for field in range(2):
        for level in range(levels):
            total = depth_sum(
                lambda near: edges[field, near],
                level,
                levels,
                lane_sum(edges[field, level], weights),
            )
            for begin, mine in ((0, low_half), (extent - 8, ~low_half)):
                part = beside_sum(change, field, level, LEAD + begin, 8)
                part = part + jnp.where(mine, total, 0.0)
                final_ref[field, level, begin : begin + 8, :] = (
                    steps_ref[field, level, begin : begin + 8, :]
                    + 2.0 * change[field, level, LEAD + begin : LEAD + begin + 8, :]
                    + coef_ref[level, begin : begin + 8, :] * part
                )
    masks = [
        jnp.concatenate([bits_ref[bit]] * (extent // 8), axis=0) != 0
        for bit in range(bits_ref.shape[0])
    ]
    for field in range(2):
        for level in range(share):
            parts = [final_ref[field, place * share + level] for place in range(len(blocks))]
            for bit, mask in enumerate(masks):
                parts = [
                    jnp.where(mask, parts[place ^ (1 << bit)], parts[place])
                    for place in range(len(blocks))
                ]
            for block, part in zip(blocks, parts):
                block[field, level] = part


def widen(weight, sides_ref, shot, mine_ref, came_refs, wide):
    _, share, extent, _ = mine_ref.shape
    sides = [
        jnp.concatenate([sides_ref[place]] * (extent // 8), axis=0) for place in range(4)
    ]
    for field in range(2):
        for level in range(share):
            scale = weight if field == 0 else 1.0
            low, high = both_sides(sides, [ref[field, level] for ref in came_refs])
            wide[shot, field, level, 0:extent, :] = scale * low
            wide[shot, field, level, extent : 2 * extent, :] = scale * mine_ref[field, level]
            wide[shot, field, level, 2 * extent : 3 * extent, :] = scale * high


def offset_product(wide, offset, level):
    extent = wide.shape[3] // 3
    lower = extent + REACH - offset
    upper = extent - REACH + offset
    total = None
    for shot in range(wide.shape[0]):
        product = (
            wide[shot, 0, level, lower : lower + extent, :]
            * wide[shot, 1, level, upper : upper + extent, :]
        )
        total = product if total is None else total + product
    return total


def stack(*refs):
    for place in range(len(refs) - 1):
        refs[-1][place] = refs[place][...]


def write_fields(final_ref, src_hbm, rec_hbm, sems):
    copies = [
        pltpu.make_async_copy(final_ref.at[field], out.at[0], sems.at[field])
        for field, out in enumerate((src_hbm, rec_hbm))
    ]
    for copy in copies:
        copy.start()
    for copy in copies:
        copy.wait()


def image_products(weight, sides_ref, others_ref, *rest):
    others_sides, rest = rest[1::-1], rest[2:]
    mine_ref, last_ref, first_ref, *partner_refs, image_hbm, wide, image_ref, sems = rest
    places = [
        (mine_ref.at[0], (first_ref.at[0], last_ref.at[0])),
        (partner_refs[0], partner_refs[1:]),
    ]
    for place in range(others_ref.shape[0]):
        places.append((others_ref.at[place], [ref.at[place] for ref in others_sides]))
    for shot, (own_ref, came_refs) in enumerate(places):
        widen(weight, sides_ref, shot, own_ref, came_refs, wide)
    parts = sems.shape[0]
    copies = []
    for piece in range(parts):
        offsets = range(piece * OFFS // parts, (piece + 1) * OFFS // parts)
        for offset in offsets:
            for level in range(image_ref.shape[1]):
                image_ref[offset, level] = offset_product(wide, offset, level)
        rows = pl.ds(offsets[0], len(offsets))
        copy = pltpu.make_async_copy(image_ref.at[rows], image_hbm.at[rows], sems.at[piece])
        copy.start()
        copies.append(copy)
    for copy in copies:
        copy.wait()


def swap_tiles(value, lower):
    tiles, shots = lax.axis_size("tile"), lax.axis_size("shot")
    partner = {}
    for tile in lower:
        partner[tile], partner[tile + 1] = tile + 1, tile
    pairs = []
    for tile in range(tiles):
        for shot in range(shots):
            here = tile * shots + shot
            there = partner[tile] * shots + shot if tile in partner else here ^ 1
            pairs.append((here, there))
    return lax.ppermute(value, ("tile", "shot"), pairs)


def swap_rounds(values):
    tiles, rounds = lax.axis_size("tile"), len(values)
    return [
        swap_tiles(value, range((number - SHIFTS[rounds]) % rounds, tiles - 1, rounds))
        for number, value in enumerate(values)
    ]


def per_device(
    src_prev,
    src_now,
    rec_prev,
    rec_now,
    speed_table,
    region_ids,
    source_cell,
    wavelet,
    receiver_cell,
    receiver_data,
):
    _, levels, extent, across = src_now.shape
    tiles = lax.axis_size("tile")
    width = extent * tiles
    shots = lax.axis_size("shot")
    share = levels // shots
    params = pltpu.CompilerParams(vmem_limit_bytes=LIMIT)

    def struct(*shape):
        return jax.ShapeDtypeStruct(shape, jnp.float32)

    def scratch(*shape, dtype=jnp.float32):
        return pltpu.VMEM(shape, dtype)

    wide_shape = (2, levels, extent + 2 * LEAD, across)
    message = struct(2 * levels + levels // 2, 2 * HALO, across)
    fields_shape = (2, levels, extent, across)
    amps, own, prev, ids, speeds, planes, *sent = pl.pallas_call(
        own_edges,
        out_shape=(
            struct(*wavelet.shape),
            struct(*wide_shape),
            struct(*fields_shape),
            jax.ShapeDtypeStruct(region_ids.shape, jnp.int32),
            struct(8, across),
            struct(2 * extent, across),
            *([message] * ROUNDS),
        ),
        in_specs=[HBM] * 9,
        out_specs=[VMEM] * (6 + ROUNDS),
        scratch_shapes=[
            scratch(1, speed_table.shape[0]),
            scratch(*receiver_cell.shape, dtype=jnp.int32),
            scratch(*receiver_data.shape),
            scratch(2, levels, 8, across),
            pltpu.SemaphoreType.DMA((14,)),
        ],
        compiler_params=params,
        name="own_edges",
    )(
        *(
            pltpu.with_memory_space_constraint(array, pltpu.HBM)
            for array in (
                speed_table.reshape(1, -1),
                receiver_cell,
                receiver_data,
                wavelet,
                region_ids,
                src_now,
                rec_now,
                src_prev,
                rec_prev,
            )
        )
    )
    came_sides = swap_rounds(sent)
    coef, steps, outside, source, sides, bits = pl.pallas_call(
        functools.partial(own_steps, width),
        out_shape=(
            struct(levels, extent, across),
            struct(*fields_shape),
            struct(2, levels, 2 * HALO, across),
            struct(levels, extent + 2 * LEAD, across),
            jax.ShapeDtypeStruct((4, 8, across), jnp.int32),
            jax.ShapeDtypeStruct((shots.bit_length() - 1, 8, across), jnp.int32),
        ),
        in_specs=[SMEM] + [VMEM] * 6,
        out_specs=[VMEM] * 6,
        scratch_shapes=[scratch(*wide_shape)],
        compiler_params=params,
        name="own_steps",
    )(source_cell, amps, own, prev, ids, speeds, planes)
    block = struct(2, share, extent, across)
    final, mine, *blocks = pl.pallas_call(
        neighbours_part,
        out_shape=(struct(*fields_shape), struct(2, *block.shape), *([block] * (shots - 2))),
        in_specs=[VMEM] * (6 + ROUNDS),
        out_specs=[VMEM] * shots,
        scratch_shapes=[
            scratch(*wide_shape),
            scratch(*wide_shape),
            scratch(2, levels, 8, across),
        ],
        compiler_params=params,
        name="neighbours_part",
    )(sides, bits, steps, outside, source, coef, *came_sides)
    def swap_shots(value, number):
        return lax.ppermute(value, "shot", [(shot, shot ^ number) for shot in range(shots)])

    came = [swap_shots(sent, 2 + i) for i, sent in enumerate(blocks)]
    weight = 1.0 / shots
    image_shape = (OFFS, share, extent, across)

    src_next, rec_next = pl.pallas_call(
        write_fields,
        out_shape=(struct(1, levels, extent, across), struct(1, levels, extent, across)),
        in_specs=[VMEM],
        out_specs=[HBM, HBM],
        scratch_shapes=[pltpu.SemaphoreType.DMA((2,))],
        compiler_params=params,
        name="write_fields",
    )(final)
    others = pl.pallas_call(
        stack,
        out_shape=struct(len(came), *block.shape),
        in_specs=[VMEM] * len(came),
        out_specs=VMEM,
        compiler_params=params,
        name="stack",
    )(*came[::-1])
    mine_sides = swap_rounds([mine] * 2)
    others_sides = swap_rounds([others] * 2)
    partner = [swap_shots(value[1], 1) for value in (mine, *mine_sides)]
    operands = [others, *others_sides[::-1], mine, *mine_sides[::-1], *partner]
    image = pl.pallas_call(
        functools.partial(image_products, weight),
        out_shape=struct(*image_shape),
        in_specs=[VMEM] * (1 + len(operands)),
        out_specs=HBM,
        scratch_shapes=[
            scratch(shots, 2, share, 3 * extent, across),
            scratch(*image_shape),
            pltpu.SemaphoreType.DMA((11,)),
        ],
        compiler_params=params,
        name="image_products",
    )(sides, *operands)
    return src_next, rec_next, image


def solution(mesh):
    field = P(("groups", "shot"), None, "tile", None)
    return jax.shard_map(
        per_device,
        mesh=mesh,
        in_specs=(
            field,
            field,
            field,
            field,
            P("groups"),
            P(None, ("groups", "tile"), None),
            P(("groups", "shot")),
            P(("groups", "shot"), None),
            P(("groups", "shot"), "tile"),
            P(("groups", "shot"), None, "tile"),
        ),
        out_specs=(field, field, P(None, "shot", ("groups", "tile"), None)),
        check_vma=False,
    )
```

```python
import functools

import jax
import jax.numpy as jnp
from jax import lax
from jax.experimental import pallas as pl
from jax.experimental.pallas import tpu as pltpu
from jax.sharding import PartitionSpec as P

OFFS = 33
REACH = OFFS // 2
HALO = 4
LEAD = 8
ROUNDS = 3
SHIFTS = {2: 0, 3: 0}

COEFS = (-205.0 / 72.0, 8.0 / 5.0, -1.0 / 5.0, 8.0 / 315.0, -1.0 / 560.0)

VMEM = pl.BlockSpec(memory_space=pltpu.VMEM)
HBM = pl.BlockSpec(memory_space=pltpu.HBM)
SMEM = pl.BlockSpec(memory_space=pltpu.SMEM)
LIMIT = 16 * 1024 * 1024


def lane_weights(shape):
    lane = lax.broadcasted_iota(jnp.int32, shape, 1)
    across = shape[1]
    after = [jnp.where(lane < across - k, COEFS[k], 0.0) for k in range(1, HALO + 1)]
    before = [jnp.where(lane >= k, COEFS[k], 0.0) for k in range(1, HALO + 1)]
    return after, before


def lane_sum(centre, weights):
    after, before = weights
    across = centre.shape[1]
    total = 3.0 * COEFS[0] * centre
    for k in range(1, HALO + 1):
        total = total + after[k - 1] * pltpu.roll(centre, across - k, 1)
        total = total + before[k - 1] * pltpu.roll(centre, k, 1)
    return total


def beside_sum(wide, field, level, begin, count):
    total = None
    for k in range(1, HALO + 1):
        pair = (
            wide[field, level, begin + k : begin + k + count, :]
            + wide[field, level, begin - k : begin - k + count, :]
        )
        total = COEFS[k] * pair if total is None else total + COEFS[k] * pair
    return total


def depth_sum(rows_of, level, levels, total):
    for k in range(1, HALO + 1):
        for near in (level - k, level + k):
            if 0 <= near < levels:
                total = total + COEFS[k] * rows_of(near)
    return total


def laplace_level(wide, field, level, levels, extent, weights):
    def rows_of(near):
        return wide[field, near, LEAD : LEAD + extent, :]

    total = lane_sum(rows_of(level), weights) + beside_sum(wide, field, level, LEAD, extent)
    return depth_sum(rows_of, level, levels, total)


def is_low(across):
    return lax.broadcasted_iota(jnp.int32, (8, across), 0) < HALO


def own_edges(
    table_hbm,
    spots_hbm,
    traces_hbm,
    amps_hbm,
    ids_hbm,
    src_now,
    rec_now,
    src_prev,
    rec_prev,
    amps_ref,
    wide,
    prev_ref,
    ids_ref,
    speeds_ref,
    planes_ref,
    *rest,
):
    sent_refs, rest = rest[:ROUNDS], rest[ROUNDS:]
    table, spots_ref, traces_ref, edges, sems = rest
    levels, extent, across = ids_ref.shape
    regions = table_hbm.shape[1]
    end = LEAD + extent
    rows = pl.ds(LEAD, extent)
    moves = [(table_hbm, table), (spots_hbm, spots_ref), (traces_hbm, traces_ref)]
    for begin in range(0, levels, levels // 2):
        part = pl.ds(begin, levels // 2)
        moves += [
            (src_now.at[0, part], wide.at[0, part, rows, :]),
            (rec_now.at[0, part], wide.at[1, part, rows, :]),
            (ids_hbm.at[part], ids_ref.at[part]),
            (src_prev.at[0, part], prev_ref.at[0, part]),
            (rec_prev.at[0, part], prev_ref.at[1, part]),
        ]
    moves.append((amps_hbm, amps_ref))
    copies = [
        pltpu.make_async_copy(here, there, sems.at[i]) for i, (here, there) in enumerate(moves)
    ]
    for copy in copies:
        copy.start()
    zeros = jnp.zeros((LEAD, across), jnp.float32)
    for field in range(2):
        for level in range(levels):
            wide[field, level, 0:LEAD, :] = zeros
            wide[field, level, end : end + LEAD, :] = zeros
    weights = lane_weights((8, across))
    low_half = is_low(across)
    my_round = lax.rem(lax.axis_index("tile"), ROUNDS)
    for copy in copies:
        copy.wait()

    spots = spots_ref[...]
    column = lax.broadcasted_iota(jnp.int32, (extent, spots.shape[1]), 0) * across
    in_column = (spots >= column) & (spots < column + across)
    lane = lax.broadcasted_iota(jnp.int32, (across, spots.shape[1]), 0)
    in_row = jnp.where(lax.rem(spots, across) == lane, 1.0, 0.0)
    traces = jnp.concatenate(
        [jnp.where(in_column, traces_ref[0, t : t + 1, :], 0.0) for t in range(2)], axis=0
    )
    planes = lax.dot_general(
        traces,
        in_row,
        (((1,), (1,)), ((), ())),
        precision=lax.Precision.HIGHEST,
        preferred_element_type=jnp.float32,
    )
    planes_ref[...] = planes

    def send(place, low, high):
        for number, sent_ref in enumerate(sent_refs):
            sent_ref[place] = jnp.where(my_round == number, high, low)

    def halves(ref, *place):
        return jnp.where(
            low_half, ref[(*place, pl.ds(0, 8))], ref[(*place, pl.ds(extent - 8, 8))]
        )

    speeds = jnp.concatenate(
        [table[...], jnp.zeros((1, across - regions), jnp.float32)], axis=1
    )
    speeds = jnp.broadcast_to(speeds, (8, across))
    speeds_ref[...] = speeds
    coefs = [
        jnp.take_along_axis(speeds, halves(ids_ref, level), axis=1, mode="promise_in_bounds")
        for level in range(levels)
    ]
    for level in range(0, levels, 2):
        here, after = coefs[level], coefs[level + 1]
        send(
            2 * levels + level // 2,
            jnp.where(low_half, here, pltpu.roll(after, HALO, 0)),
            jnp.where(low_half, pltpu.roll(here, HALO, 0), after),
        )

    for field in range(2):
        for level in range(levels):
            edges[field, level] = jnp.where(
                low_half, wide[field, level, LEAD : LEAD + 8, :], wide[field, level, end - 8 : end, :]
            )
    for field in range(2):
        for level in range(levels):
            now = edges[field, level]
            total = lane_sum(now, weights) + jnp.where(
                low_half,
                beside_sum(wide, field, level, LEAD, 8),
                beside_sum(wide, field, level, end - 8, 8),
            )
            total = depth_sum(lambda near: edges[field, near], level, levels, total)
            value = 2.0 * now - halves(prev_ref, field, level) + coefs[level] * total
            if field == 1 and level == 0:
                value = value + jnp.where(low_half, planes[0:8, :], planes[extent - 8 : extent, :])
            send(
                field * levels + level,
                jnp.where(low_half, now, pltpu.roll(value, HALO, 0)),
                jnp.where(low_half, pltpu.roll(now, HALO, 0), value),
            )


def own_steps(
    width,
    cell_ref,
    amps_ref,
    own,
    prev_ref,
    ids_ref,
    speeds_ref,
    planes_ref,
    coef_ref,
    steps_ref,
    outside_ref,
    source_ref,
    sides_ref,
    bits_ref,
    middle,
):
    levels, extent, across = ids_ref.shape
    end = LEAD + extent
    cell = cell_ref[0]
    deep = lax.div(cell, width * across)
    row = lax.rem(lax.div(cell, across), width) - lax.axis_index("tile") * extent + LEAD
    shape = (extent + 2 * LEAD, across)
    rows = lax.broadcasted_iota(jnp.int32, shape, 0)
    lanes = lax.broadcasted_iota(jnp.int32, shape, 1)
    hit = jnp.where((rows == row) & (lanes == lax.rem(cell, across)), 1.0, 0.0)
    weights = lane_weights((extent, across))
    speeds = speeds_ref[...]
    zeros = jnp.zeros((LEAD, across), jnp.float32)
    for level in range(levels):
        here = hit * jnp.where(deep == level, 1.0, 0.0)
        source_ref[level] = here * amps_ref[0:1, 0:1]
        steps_ref[0, level] = here[LEAD:end, :] * amps_ref[0:1, 1:2] - own[0, level, LEAD:end, :]
        steps_ref[1, level] = -own[1, level, LEAD:end, :]
        for begin in range(0, extent, 8):
            coef_ref[level, begin : begin + 8, :] = jnp.take_along_axis(
                speeds, ids_ref[level, begin : begin + 8, :], axis=1, mode="promise_in_bounds"
            )
    steps_ref[1, 0] += planes_ref[extent:, :]
    for field in range(2):
        for level in range(levels):
            total = laplace_level(own, field, level, levels, extent, weights)
            value = 2.0 * own[field, level, LEAD:end, :] - prev_ref[field, level]
            value = value + coef_ref[level] * total
            if field == 0:
                value = value + source_ref[level, LEAD:end, :]
            elif level == 0:
                value = value + planes_ref[:extent, :]
            middle[field, level, 0:LEAD, :] = zeros
            middle[field, level, LEAD:end, :] = value
            middle[field, level, end : end + LEAD, :] = zeros
            below = above = jnp.zeros((HALO, across), jnp.float32)
            for k in range(1, HALO + 1):
                begin = LEAD - HALO + k
                below = below + COEFS[k] * own[field, level, begin : begin + HALO, :]
                above = above + COEFS[k] * own[field, level, end - k : end - k + HALO, :]
            outside_ref[field, level, 0:HALO, :] = below
            outside_ref[field, level, HALO : 2 * HALO, :] = above
    for field in range(2):
        for level in range(levels):
            total = laplace_level(middle, field, level, levels, extent, weights)
            steps_ref[field, level] += (
                2.0 * middle[field, level, LEAD:end, :] + coef_ref[level] * total
            )
    tile, tiles = lax.axis_index("tile"), lax.axis_size("tile")
    places = (jnp.where(tile > 0, 1, 0), jnp.where(tile < tiles - 1, 1, 0))
    places += tuple((tile + SHIFTS[rounds]) % rounds for rounds in (2, 3))
    for place, value in enumerate(places):
        sides_ref[place] = jnp.full(sides_ref.shape[1:], value, dtype=jnp.int32)
    shot = jnp.full(bits_ref.shape[1:], lax.axis_index("shot"), dtype=jnp.int32)
    for bit in range(bits_ref.shape[0]):
        bits_ref[bit] = shot & (1 << bit)


def both_sides(sides, came):
    has_low, has_high, my_round = sides[0], sides[1], sides[len(came)]
    low, high = came[-1], came[0]
    for number in range(1, len(came)):
        low = jnp.where(my_round == number, came[number - 1], low)
        high = jnp.where(my_round == number, came[number], high)
    return jnp.where(has_low != 0, low, 0.0), jnp.where(has_high != 0, high, 0.0)


def neighbours_part(
    sides_ref, bits_ref, steps_ref, outside_ref, source_ref, coef_ref, *rest
):
    came_refs, (final_ref, mine_ref, *blocks, other, change, edges) = rest[:ROUNDS], rest[ROUNDS:]
    blocks = [mine_ref.at[0], mine_ref.at[1], *blocks]
    levels, extent, across = coef_ref.shape
    share = mine_ref.shape[2]
    end = LEAD + extent
    low_half = is_low(across)
    weights = lane_weights((8, across))
    sides = [sides_ref[place] for place in range(4)]
    zeros = jnp.zeros((8, across), jnp.float32)

    def received(place):
        return both_sides(sides, [ref[place] for ref in came_refs])

    coefs = [received(2 * levels + pair) for pair in range(levels // 2)]
    for field in range(2):
        for level in range(levels):
            low, high = received(field * levels + level)
            other[field, level, LEAD : LEAD + 8, :] = zeros
            other[field, level, end - 8 : end, :] = zeros
            other[field, level, LEAD - HALO : LEAD, :] = low[0:HALO, :]
            other[field, level, end : end + HALO, :] = high[0:HALO, :]
            half = slice(level % 2 * HALO, level % 2 * HALO + HALO)
            low_coef, high_coef = (coef[half, :] for coef in coefs[level // 2])
            low = low[HALO:, :] + low_coef * outside_ref[field, level, 0:HALO, :]
            high = high[HALO:, :] + high_coef * outside_ref[field, level, HALO : 2 * HALO, :]
            if field == 0:
                low = low + source_ref[level, LEAD - HALO : LEAD, :]
                high = high + source_ref[level, end : end + HALO, :]
            change[field, level, LEAD - HALO : LEAD, :] = low
            change[field, level, end : end + HALO, :] = high
    for field in range(2):
        for level in range(levels):
            left = right = zeros
            for k in range(1, HALO + 1):
                left = left + COEFS[k] * other[field, level, LEAD - k : LEAD - k + 8, :]
                right = right + COEFS[k] * other[field, level, end - 8 + k : end + k, :]
            left = coef_ref[level, 0:8, :] * left
            right = coef_ref[level, extent - 8 : extent, :] * right
            change[field, level, LEAD : LEAD + 8, :] = left
            change[field, level, end - 8 : end, :] = right
            edges[field, level] = left + right
    for field in range(2):
        for level in range(levels):
            total = depth_sum(
                lambda near: edges[field, near],
                level,
                levels,
                lane_sum(edges[field, level], weights),
            )
            for begin, mine in ((0, low_half), (extent - 8, ~low_half)):
                part = beside_sum(change, field, level, LEAD + begin, 8)
                part = part + jnp.where(mine, total, 0.0)
                final_ref[field, level, begin : begin + 8, :] = (
                    steps_ref[field, level, begin : begin + 8, :]
                    + 2.0 * change[field, level, LEAD + begin : LEAD + begin + 8, :]
                    + coef_ref[level, begin : begin + 8, :] * part
                )
    masks = [
        jnp.concatenate([bits_ref[bit]] * (extent // 8), axis=0) != 0
        for bit in range(bits_ref.shape[0])
    ]
    for field in range(2):
        for level in range(share):
            parts = [final_ref[field, place * share + level] for place in range(len(blocks))]
            for bit, mask in enumerate(masks):
                parts = [
                    jnp.where(mask, parts[place ^ (1 << bit)], parts[place])
                    for place in range(len(blocks))
                ]
            for block, part in zip(blocks, parts):
                block[field, level] = part


def widen(weight, sides_ref, shot, mine_ref, came_refs, wide):
    _, share, extent, _ = mine_ref.shape
    sides = [
        jnp.concatenate([sides_ref[place]] * (extent // 8), axis=0) for place in range(4)
    ]
    for field in range(2):
        for level in range(share):
            scale = weight if field == 0 else 1.0
            low, high = both_sides(sides, [ref[field, level] for ref in came_refs])
            wide[shot, field, level, 0:extent, :] = scale * low
            wide[shot, field, level, extent : 2 * extent, :] = scale * mine_ref[field, level]
            wide[shot, field, level, 2 * extent : 3 * extent, :] = scale * high


def offset_product(wide, offset, level):
    extent = wide.shape[3] // 3
    lower = extent + REACH - offset
    upper = extent - REACH + offset
    total = None
    for shot in range(wide.shape[0]):
        product = (
            wide[shot, 0, level, lower : lower + extent, :]
            * wide[shot, 1, level, upper : upper + extent, :]
        )
        total = product if total is None else total + product
    return total


def stack(*refs):
    for place in range(len(refs) - 1):
        refs[-1][place] = refs[place][...]


def write_fields(final_ref, src_hbm, rec_hbm, sems):
    copies = [
        pltpu.make_async_copy(final_ref.at[field], out.at[0], sems.at[field])
        for field, out in enumerate((src_hbm, rec_hbm))
    ]
    for copy in copies:
        copy.start()
    for copy in copies:
        copy.wait()


def image_products(weight, sides_ref, others_ref, *rest):
    others_sides, rest = rest[1::-1], rest[2:]
    mine_ref, first_ref, last_ref, *partner_refs, image_hbm, wide, image_ref, sems = rest
    places = [
        (mine_ref.at[0], (first_ref.at[0], last_ref.at[0])),
        (partner_refs[0], partner_refs[1:]),
    ]
    for place in range(others_ref.shape[0]):
        places.append((others_ref.at[place], [ref.at[place] for ref in others_sides]))
    for shot, (own_ref, came_refs) in enumerate(places):
        widen(weight, sides_ref, shot, own_ref, came_refs, wide)
    parts = sems.shape[0]
    copies = []
    for piece in range(parts):
        offsets = range(piece * OFFS // parts, (piece + 1) * OFFS // parts)
        for offset in offsets:
            for level in range(image_ref.shape[1]):
                image_ref[offset, level] = offset_product(wide, offset, level)
        rows = pl.ds(offsets[0], len(offsets))
        copy = pltpu.make_async_copy(image_ref.at[rows], image_hbm.at[rows], sems.at[piece])
        copy.start()
        copies.append(copy)
    for copy in copies:
        copy.wait()


def swap_tiles(value, lower):
    tiles, shots = lax.axis_size("tile"), lax.axis_size("shot")
    partner = {}
    for tile in lower:
        partner[tile], partner[tile + 1] = tile + 1, tile
    pairs = []
    for tile in range(tiles):
        for shot in range(shots):
            here = tile * shots + shot
            there = partner[tile] * shots + shot if tile in partner else here ^ 1
            pairs.append((here, there))
    return lax.ppermute(value, ("tile", "shot"), pairs)


def swap_rounds(values):
    tiles, rounds = lax.axis_size("tile"), len(values)
    return [
        swap_tiles(value, range((number - SHIFTS[rounds]) % rounds, tiles - 1, rounds))
        for number, value in enumerate(values)
    ]


def per_device(
    src_prev,
    src_now,
    rec_prev,
    rec_now,
    speed_table,
    region_ids,
    source_cell,
    wavelet,
    receiver_cell,
    receiver_data,
):
    _, levels, extent, across = src_now.shape
    tiles = lax.axis_size("tile")
    width = extent * tiles
    shots = lax.axis_size("shot")
    share = levels // shots
    params = pltpu.CompilerParams(vmem_limit_bytes=LIMIT)

    def struct(*shape):
        return jax.ShapeDtypeStruct(shape, jnp.float32)

    def scratch(*shape, dtype=jnp.float32):
        return pltpu.VMEM(shape, dtype)

    wide_shape = (2, levels, extent + 2 * LEAD, across)
    message = struct(2 * levels + levels // 2, 2 * HALO, across)
    fields_shape = (2, levels, extent, across)
    amps, own, prev, ids, speeds, planes, *sent = pl.pallas_call(
        own_edges,
        out_shape=(
            struct(*wavelet.shape),
            struct(*wide_shape),
            struct(*fields_shape),
            jax.ShapeDtypeStruct(region_ids.shape, jnp.int32),
            struct(8, across),
            struct(2 * extent, across),
            *([message] * ROUNDS),
        ),
        in_specs=[HBM] * 9,
        out_specs=[VMEM] * (6 + ROUNDS),
        scratch_shapes=[
            scratch(1, speed_table.shape[0]),
            scratch(*receiver_cell.shape, dtype=jnp.int32),
            scratch(*receiver_data.shape),
            scratch(2, levels, 8, across),
            pltpu.SemaphoreType.DMA((14,)),
        ],
        compiler_params=params,
        name="own_edges",
    )(
        *(
            pltpu.with_memory_space_constraint(array, pltpu.HBM)
            for array in (
                speed_table.reshape(1, -1),
                receiver_cell,
                receiver_data,
                wavelet,
                region_ids,
                src_now,
                rec_now,
                src_prev,
                rec_prev,
            )
        )
    )
    came_sides = swap_rounds(sent)
    coef, steps, outside, source, sides, bits = pl.pallas_call(
        functools.partial(own_steps, width),
        out_shape=(
            struct(levels, extent, across),
            struct(*fields_shape),
            struct(2, levels, 2 * HALO, across),
            struct(levels, extent + 2 * LEAD, across),
            jax.ShapeDtypeStruct((4, 8, across), jnp.int32),
            jax.ShapeDtypeStruct((shots.bit_length() - 1, 8, across), jnp.int32),
        ),
        in_specs=[SMEM] + [VMEM] * 6,
        out_specs=[VMEM] * 6,
        scratch_shapes=[scratch(*wide_shape)],
        compiler_params=params,
        name="own_steps",
    )(source_cell, amps, own, prev, ids, speeds, planes)
    block = struct(2, share, extent, across)
    final, mine, *blocks = pl.pallas_call(
        neighbours_part,
        out_shape=(struct(*fields_shape), struct(2, *block.shape), *([block] * (shots - 2))),
        in_specs=[VMEM] * (6 + ROUNDS),
        out_specs=[VMEM] * shots,
        scratch_shapes=[
            scratch(*wide_shape),
            scratch(*wide_shape),
            scratch(2, levels, 8, across),
        ],
        compiler_params=params,
        name="neighbours_part",
    )(sides, bits, steps, outside, source, coef, *came_sides)
    def swap_shots(value, number):
        return lax.ppermute(value, "shot", [(shot, shot ^ number) for shot in range(shots)])

    came = [swap_shots(sent, 2 + i) for i, sent in enumerate(blocks)]
    weight = 1.0 / shots
    image_shape = (OFFS, share, extent, across)

    src_next, rec_next = pl.pallas_call(
        write_fields,
        out_shape=(struct(1, levels, extent, across), struct(1, levels, extent, across)),
        in_specs=[VMEM],
        out_specs=[HBM, HBM],
        scratch_shapes=[pltpu.SemaphoreType.DMA((2,))],
        compiler_params=params,
        name="write_fields",
    )(final)
    others = pl.pallas_call(
        stack,
        out_shape=struct(len(came), *block.shape),
        in_specs=[VMEM] * len(came),
        out_specs=VMEM,
        compiler_params=params,
        name="stack",
    )(*came[::-1])
    mine_sides = swap_rounds([mine] * 2)
    others_sides = swap_rounds([others] * 2)
    partner = [swap_shots(value[1], 1) for value in (mine, *mine_sides)]
    operands = [others, *others_sides[::-1], mine, *mine_sides, *partner]
    image = pl.pallas_call(
        functools.partial(image_products, weight),
        out_shape=struct(*image_shape),
        in_specs=[VMEM] * (1 + len(operands)),
        out_specs=HBM,
        scratch_shapes=[
            scratch(shots, 2, share, 3 * extent, across),
            scratch(*image_shape),
            pltpu.SemaphoreType.DMA((11,)),
        ],
        compiler_params=params,
        name="image_products",
    )(sides, *operands)
    return src_next, rec_next, image


def solution(mesh):
    field = P(("groups", "shot"), None, "tile", None)
    return jax.shard_map(
        per_device,
        mesh=mesh,
        in_specs=(
            field,
            field,
            field,
            field,
            P("groups"),
            P(None, ("groups", "tile"), None),
            P(("groups", "shot")),
            P(("groups", "shot"), None),
            P(("groups", "shot"), "tile"),
            P(("groups", "shot"), None, "tile"),
        ),
        out_specs=(field, field, P(None, "shot", ("groups", "tile"), None)),
        check_vma=False,
    )
```

```python
import functools

import jax
import jax.numpy as jnp
from jax import lax
from jax.experimental import pallas as pl
from jax.experimental.pallas import tpu as pltpu
from jax.sharding import PartitionSpec as P

OFFS = 33
REACH = OFFS // 2
HALO = 4
LEAD = 8
ROUNDS = 3
SHIFTS = {2: 0, 3: 0}

COEFS = (-205.0 / 72.0, 8.0 / 5.0, -1.0 / 5.0, 8.0 / 315.0, -1.0 / 560.0)

VMEM = pl.BlockSpec(memory_space=pltpu.VMEM)
HBM = pl.BlockSpec(memory_space=pltpu.HBM)
SMEM = pl.BlockSpec(memory_space=pltpu.SMEM)
LIMIT = 16 * 1024 * 1024


def lane_weights(shape):
    lane = lax.broadcasted_iota(jnp.int32, shape, 1)
    across = shape[1]
    after = [jnp.where(lane < across - k, COEFS[k], 0.0) for k in range(1, HALO + 1)]
    before = [jnp.where(lane >= k, COEFS[k], 0.0) for k in range(1, HALO + 1)]
    return after, before


def lane_sum(centre, weights):
    after, before = weights
    across = centre.shape[1]
    total = 3.0 * COEFS[0] * centre
    for k in range(1, HALO + 1):
        total = total + after[k - 1] * pltpu.roll(centre, across - k, 1)
        total = total + before[k - 1] * pltpu.roll(centre, k, 1)
    return total


def beside_sum(wide, field, level, begin, count):
    total = None
    for k in range(1, HALO + 1):
        pair = (
            wide[field, level, begin + k : begin + k + count, :]
            + wide[field, level, begin - k : begin - k + count, :]
        )
        total = COEFS[k] * pair if total is None else total + COEFS[k] * pair
    return total


def depth_sum(rows_of, level, levels, total):
    for k in range(1, HALO + 1):
        for near in (level - k, level + k):
            if 0 <= near < levels:
                total = total + COEFS[k] * rows_of(near)
    return total


def laplace_level(wide, field, level, levels, extent, weights):
    def rows_of(near):
        return wide[field, near, LEAD : LEAD + extent, :]

    total = lane_sum(rows_of(level), weights) + beside_sum(wide, field, level, LEAD, extent)
    return depth_sum(rows_of, level, levels, total)


def is_low(across):
    return lax.broadcasted_iota(jnp.int32, (8, across), 0) < HALO


def own_edges(
    table_hbm,
    spots_hbm,
    traces_hbm,
    amps_hbm,
    ids_hbm,
    src_now,
    rec_now,
    src_prev,
    rec_prev,
    amps_ref,
    wide,
    prev_ref,
    ids_ref,
    speeds_ref,
    planes_ref,
    *rest,
):
    sent_refs, rest = rest[:ROUNDS], rest[ROUNDS:]
    table, spots_ref, traces_ref, edges, sems = rest
    levels, extent, across = ids_ref.shape
    regions = table_hbm.shape[1]
    end = LEAD + extent
    rows = pl.ds(LEAD, extent)
    moves = [(table_hbm, table), (spots_hbm, spots_ref), (traces_hbm, traces_ref)]
    for begin in range(0, levels, levels // 2):
        part = pl.ds(begin, levels // 2)
        moves += [
            (src_now.at[0, part], wide.at[0, part, rows, :]),
            (rec_now.at[0, part], wide.at[1, part, rows, :]),
            (ids_hbm.at[part], ids_ref.at[part]),
            (src_prev.at[0, part], prev_ref.at[0, part]),
            (rec_prev.at[0, part], prev_ref.at[1, part]),
        ]
    moves.append((amps_hbm, amps_ref))
    copies = [
        pltpu.make_async_copy(here, there, sems.at[i]) for i, (here, there) in enumerate(moves)
    ]
    for copy in copies:
        copy.start()
    zeros = jnp.zeros((LEAD, across), jnp.float32)
    for field in range(2):
        for level in range(levels):
            wide[field, level, 0:LEAD, :] = zeros
            wide[field, level, end : end + LEAD, :] = zeros
    weights = lane_weights((8, across))
    low_half = is_low(across)
    my_round = lax.rem(lax.axis_index("tile"), ROUNDS)
    for copy in copies:
        copy.wait()

    spots = spots_ref[...]
    column = lax.broadcasted_iota(jnp.int32, (extent, spots.shape[1]), 0) * across
    in_column = (spots >= column) & (spots < column + across)
    lane = lax.broadcasted_iota(jnp.int32, (across, spots.shape[1]), 0)
    in_row = jnp.where(lax.rem(spots, across) == lane, 1.0, 0.0)
    traces = jnp.concatenate(
        [jnp.where(in_column, traces_ref[0, t : t + 1, :], 0.0) for t in range(2)], axis=0
    )
    planes = lax.dot_general(
        traces,
        in_row,
        (((1,), (1,)), ((), ())),
        precision=lax.Precision.HIGHEST,
        preferred_element_type=jnp.float32,
    )
    planes_ref[...] = planes

    def send(place, low, high):
        for number, sent_ref in enumerate(sent_refs):
            sent_ref[place] = jnp.where(my_round == number, high, low)

    def halves(ref, *place):
        return jnp.where(
            low_half, ref[(*place, pl.ds(0, 8))], ref[(*place, pl.ds(extent - 8, 8))]
        )

    speeds = jnp.concatenate(
        [table[...], jnp.zeros((1, across - regions), jnp.float32)], axis=1
    )
    speeds = jnp.broadcast_to(speeds, (8, across))
    speeds_ref[...] = speeds
    coefs = [
        jnp.take_along_axis(speeds, halves(ids_ref, level), axis=1, mode="promise_in_bounds")
        for level in range(levels)
    ]
    for level in range(0, levels, 2):
        here, after = coefs[level], coefs[level + 1]
        send(
            2 * levels + level // 2,
            jnp.where(low_half, here, pltpu.roll(after, HALO, 0)),
            jnp.where(low_half, pltpu.roll(here, HALO, 0), after),
        )

    for field in range(2):
        for level in range(levels):
            edges[field, level] = jnp.where(
                low_half, wide[field, level, LEAD : LEAD + 8, :], wide[field, level, end - 8 : end, :]
            )
    for field in range(2):
        for level in range(levels):
            now = edges[field, level]
            total = lane_sum(now, weights) + jnp.where(
                low_half,
                beside_sum(wide, field, level, LEAD, 8),
                beside_sum(wide, field, level, end - 8, 8),
            )
            total = depth_sum(lambda near: edges[field, near], level, levels, total)
            value = 2.0 * now - halves(prev_ref, field, level) + coefs[level] * total
            if field == 1 and level == 0:
                value = value + jnp.where(low_half, planes[0:8, :], planes[extent - 8 : extent, :])
            send(
                field * levels + level,
                jnp.where(low_half, now, pltpu.roll(value, HALO, 0)),
                jnp.where(low_half, pltpu.roll(now, HALO, 0), value),
            )


def own_steps(
    width,
    cell_ref,
    amps_ref,
    own,
    prev_ref,
    ids_ref,
    speeds_ref,
    planes_ref,
    coef_ref,
    steps_ref,
    outside_ref,
    source_ref,
    sides_ref,
    bits_ref,
    middle,
):
    levels, extent, across = ids_ref.shape
    end = LEAD + extent
    cell = cell_ref[0]
    deep = lax.div(cell, width * across)
    row = lax.rem(lax.div(cell, across), width) - lax.axis_index("tile") * extent + LEAD
    shape = (extent + 2 * LEAD, across)
    rows = lax.broadcasted_iota(jnp.int32, shape, 0)
    lanes = lax.broadcasted_iota(jnp.int32, shape, 1)
    hit = jnp.where((rows == row) & (lanes == lax.rem(cell, across)), 1.0, 0.0)
    weights = lane_weights((extent, across))
    speeds = speeds_ref[...]
    zeros = jnp.zeros((LEAD, across), jnp.float32)
    for level in range(levels):
        here = hit * jnp.where(deep == level, 1.0, 0.0)
        source_ref[level] = here * amps_ref[0:1, 0:1]
        steps_ref[0, level] = here[LEAD:end, :] * amps_ref[0:1, 1:2] - own[0, level, LEAD:end, :]
        steps_ref[1, level] = -own[1, level, LEAD:end, :]
        for begin in range(0, extent, 8):
            coef_ref[level, begin : begin + 8, :] = jnp.take_along_axis(
                speeds, ids_ref[level, begin : begin + 8, :], axis=1, mode="promise_in_bounds"
            )
    steps_ref[1, 0] += planes_ref[extent:, :]
    for field in range(2):
        for level in range(levels):
            total = laplace_level(own, field, level, levels, extent, weights)
            value = 2.0 * own[field, level, LEAD:end, :] - prev_ref[field, level]
            value = value + coef_ref[level] * total
            if field == 0:
                value = value + source_ref[level, LEAD:end, :]
            elif level == 0:
                value = value + planes_ref[:extent, :]
            middle[field, level, 0:LEAD, :] = zeros
            middle[field, level, LEAD:end, :] = value
            middle[field, level, end : end + LEAD, :] = zeros
            below = above = jnp.zeros((HALO, across), jnp.float32)
            for k in range(1, HALO + 1):
                begin = LEAD - HALO + k
                below = below + COEFS[k] * own[field, level, begin : begin + HALO, :]
                above = above + COEFS[k] * own[field, level, end - k : end - k + HALO, :]
            outside_ref[field, level, 0:HALO, :] = below
            outside_ref[field, level, HALO : 2 * HALO, :] = above
    for field in range(2):
        for level in range(levels):
            total = laplace_level(middle, field, level, levels, extent, weights)
            steps_ref[field, level] += (
                2.0 * middle[field, level, LEAD:end, :] + coef_ref[level] * total
            )
    tile, tiles = lax.axis_index("tile"), lax.axis_size("tile")
    places = (jnp.where(tile > 0, 1, 0), jnp.where(tile < tiles - 1, 1, 0))
    places += tuple((tile + SHIFTS[rounds]) % rounds for rounds in (2, 3))
    for place, value in enumerate(places):
        sides_ref[place] = jnp.full(sides_ref.shape[1:], value, dtype=jnp.int32)
    shot = jnp.full(bits_ref.shape[1:], lax.axis_index("shot"), dtype=jnp.int32)
    for bit in range(bits_ref.shape[0]):
        bits_ref[bit] = shot & (1 << bit)


def both_sides(sides, came):
    has_low, has_high, my_round = sides[0], sides[1], sides[len(came)]
    low, high = came[-1], came[0]
    for number in range(1, len(came)):
        low = jnp.where(my_round == number, came[number - 1], low)
        high = jnp.where(my_round == number, came[number], high)
    return jnp.where(has_low != 0, low, 0.0), jnp.where(has_high != 0, high, 0.0)


def neighbours_part(
    sides_ref, bits_ref, steps_ref, outside_ref, source_ref, coef_ref, *rest
):
    came_refs, (final_ref, mine_ref, *blocks, other, change, edges) = rest[:ROUNDS], rest[ROUNDS:]
    blocks = [mine_ref.at[0], mine_ref.at[1], *blocks]
    levels, extent, across = coef_ref.shape
    share = mine_ref.shape[2]
    end = LEAD + extent
    low_half = is_low(across)
    weights = lane_weights((8, across))
    sides = [sides_ref[place] for place in range(4)]
    zeros = jnp.zeros((8, across), jnp.float32)

    def received(place):
        return both_sides(sides, [ref[place] for ref in came_refs])

    coefs = [received(2 * levels + pair) for pair in range(levels // 2)]
    for field in range(2):
        for level in range(levels):
            low, high = received(field * levels + level)
            other[field, level, LEAD : LEAD + 8, :] = zeros
            other[field, level, end - 8 : end, :] = zeros
            other[field, level, LEAD - HALO : LEAD, :] = low[0:HALO, :]
            other[field, level, end : end + HALO, :] = high[0:HALO, :]
            half = slice(level % 2 * HALO, level % 2 * HALO + HALO)
            low_coef, high_coef = (coef[half, :] for coef in coefs[level // 2])
            low = low[HALO:, :] + low_coef * outside_ref[field, level, 0:HALO, :]
            high = high[HALO:, :] + high_coef * outside_ref[field, level, HALO : 2 * HALO, :]
            if field == 0:
                low = low + source_ref[level, LEAD - HALO : LEAD, :]
                high = high + source_ref[level, end : end + HALO, :]
            change[field, level, LEAD - HALO : LEAD, :] = low
            change[field, level, end : end + HALO, :] = high
    for field in range(2):
        for level in range(levels):
            left = right = zeros
            for k in range(1, HALO + 1):
                left = left + COEFS[k] * other[field, level, LEAD - k : LEAD - k + 8, :]
                right = right + COEFS[k] * other[field, level, end - 8 + k : end + k, :]
            left = coef_ref[level, 0:8, :] * left
            right = coef_ref[level, extent - 8 : extent, :] * right
            change[field, level, LEAD : LEAD + 8, :] = left
            change[field, level, end - 8 : end, :] = right
            edges[field, level] = left + right
    for field in range(2):
        for level in range(levels):
            total = depth_sum(
                lambda near: edges[field, near],
                level,
                levels,
                lane_sum(edges[field, level], weights),
            )
            for begin, mine in ((0, low_half), (extent - 8, ~low_half)):
                part = beside_sum(change, field, level, LEAD + begin, 8)
                part = part + jnp.where(mine, total, 0.0)
                final_ref[field, level, begin : begin + 8, :] = (
                    steps_ref[field, level, begin : begin + 8, :]
                    + 2.0 * change[field, level, LEAD + begin : LEAD + begin + 8, :]
                    + coef_ref[level, begin : begin + 8, :] * part
                )
    masks = [
        jnp.concatenate([bits_ref[bit]] * (extent // 8), axis=0) != 0
        for bit in range(bits_ref.shape[0])
    ]
    for field in range(2):
        for level in range(share):
            parts = [final_ref[field, place * share + level] for place in range(len(blocks))]
            for bit, mask in enumerate(masks):
                parts = [
                    jnp.where(mask, parts[place ^ (1 << bit)], parts[place])
                    for place in range(len(blocks))
                ]
            for block, part in zip(blocks, parts):
                block[field, level] = part


def widen(weight, sides_ref, shot, mine_ref, came_refs, wide):
    _, share, extent, _ = mine_ref.shape
    sides = [
        jnp.concatenate([sides_ref[place]] * (extent // 8), axis=0) for place in range(4)
    ]
    for field in range(2):
        for level in range(share):
            scale = weight if field == 0 else 1.0
            low, high = both_sides(sides, [ref[field, level] for ref in came_refs])
            wide[shot, field, level, 0:extent, :] = scale * low
            wide[shot, field, level, extent : 2 * extent, :] = scale * mine_ref[field, level]
            wide[shot, field, level, 2 * extent : 3 * extent, :] = scale * high


def offset_product(wide, offset, level):
    extent = wide.shape[3] // 3
    lower = extent + REACH - offset
    upper = extent - REACH + offset
    total = None
    for shot in range(wide.shape[0]):
        product = (
            wide[shot, 0, level, lower : lower + extent, :]
            * wide[shot, 1, level, upper : upper + extent, :]
        )
        total = product if total is None else total + product
    return total


def stack(*refs):
    for place in range(len(refs) - 1):
        refs[-1][place] = refs[place][...]


def write_fields(final_ref, src_hbm, rec_hbm, sems):
    copies = [
        pltpu.make_async_copy(final_ref.at[field], out.at[0], sems.at[field])
        for field, out in enumerate((src_hbm, rec_hbm))
    ]
    for copy in copies:
        copy.start()
    for copy in copies:
        copy.wait()


def image_products(weight, sides_ref, others_ref, *rest):
    others_sides, rest = rest[1::-1], rest[2:]
    mine_ref, rest = rest[0], rest[1:]
    mine_sides, rest = rest[ROUNDS - 1 :: -1], rest[ROUNDS:]
    partner_refs, rest = rest[: 1 + ROUNDS], rest[1 + ROUNDS :]
    image_hbm, wide, image_ref, sems = rest
    places = [
        (mine_ref.at[0], [ref.at[0] for ref in mine_sides]),
        (partner_refs[0], partner_refs[1:]),
    ]
    for place in range(others_ref.shape[0]):
        places.append((others_ref.at[place], [ref.at[place] for ref in others_sides]))
    for shot, (own_ref, came_refs) in enumerate(places):
        widen(weight, sides_ref, shot, own_ref, came_refs, wide)
    parts = sems.shape[0]
    copies = []
    for piece in range(parts):
        offsets = range(piece * OFFS // parts, (piece + 1) * OFFS // parts)
        for offset in offsets:
            for level in range(image_ref.shape[1]):
                image_ref[offset, level] = offset_product(wide, offset, level)
        rows = pl.ds(offsets[0], len(offsets))
        copy = pltpu.make_async_copy(image_ref.at[rows], image_hbm.at[rows], sems.at[piece])
        copy.start()
        copies.append(copy)
    for copy in copies:
        copy.wait()


def swap_tiles(value, lower):
    tiles, shots = lax.axis_size("tile"), lax.axis_size("shot")
    partner = {}
    for tile in lower:
        partner[tile], partner[tile + 1] = tile + 1, tile
    pairs = []
    for tile in range(tiles):
        for shot in range(shots):
            here = tile * shots + shot
            there = partner[tile] * shots + shot if tile in partner else here ^ 1
            pairs.append((here, there))
    return lax.ppermute(value, ("tile", "shot"), pairs)


def swap_rounds(values):
    tiles, rounds = lax.axis_size("tile"), len(values)
    return [
        swap_tiles(value, range((number - SHIFTS[rounds]) % rounds, tiles - 1, rounds))
        for number, value in enumerate(values)
    ]


def per_device(
    src_prev,
    src_now,
    rec_prev,
    rec_now,
    speed_table,
    region_ids,
    source_cell,
    wavelet,
    receiver_cell,
    receiver_data,
):
    _, levels, extent, across = src_now.shape
    tiles = lax.axis_size("tile")
    width = extent * tiles
    shots = lax.axis_size("shot")
    share = levels // shots
    params = pltpu.CompilerParams(vmem_limit_bytes=LIMIT)

    def struct(*shape):
        return jax.ShapeDtypeStruct(shape, jnp.float32)

    def scratch(*shape, dtype=jnp.float32):
        return pltpu.VMEM(shape, dtype)

    wide_shape = (2, levels, extent + 2 * LEAD, across)
    message = struct(2 * levels + levels // 2, 2 * HALO, across)
    fields_shape = (2, levels, extent, across)
    amps, own, prev, ids, speeds, planes, *sent = pl.pallas_call(
        own_edges,
        out_shape=(
            struct(*wavelet.shape),
            struct(*wide_shape),
            struct(*fields_shape),
            jax.ShapeDtypeStruct(region_ids.shape, jnp.int32),
            struct(8, across),
            struct(2 * extent, across),
            *([message] * ROUNDS),
        ),
        in_specs=[HBM] * 9,
        out_specs=[VMEM] * (6 + ROUNDS),
        scratch_shapes=[
            scratch(1, speed_table.shape[0]),
            scratch(*receiver_cell.shape, dtype=jnp.int32),
            scratch(*receiver_data.shape),
            scratch(2, levels, 8, across),
            pltpu.SemaphoreType.DMA((14,)),
        ],
        compiler_params=params,
        name="own_edges",
    )(
        *(
            pltpu.with_memory_space_constraint(array, pltpu.HBM)
            for array in (
                speed_table.reshape(1, -1),
                receiver_cell,
                receiver_data,
                wavelet,
                region_ids,
                src_now,
                rec_now,
                src_prev,
                rec_prev,
            )
        )
    )
    came_sides = swap_rounds(sent)
    coef, steps, outside, source, sides, bits = pl.pallas_call(
        functools.partial(own_steps, width),
        out_shape=(
            struct(levels, extent, across),
            struct(*fields_shape),
            struct(2, levels, 2 * HALO, across),
            struct(levels, extent + 2 * LEAD, across),
            jax.ShapeDtypeStruct((4, 8, across), jnp.int32),
            jax.ShapeDtypeStruct((shots.bit_length() - 1, 8, across), jnp.int32),
        ),
        in_specs=[SMEM] + [VMEM] * 6,
        out_specs=[VMEM] * 6,
        scratch_shapes=[scratch(*wide_shape)],
        compiler_params=params,
        name="own_steps",
    )(source_cell, amps, own, prev, ids, speeds, planes)
    block = struct(2, share, extent, across)
    final, mine, *blocks = pl.pallas_call(
        neighbours_part,
        out_shape=(struct(*fields_shape), struct(2, *block.shape), *([block] * (shots - 2))),
        in_specs=[VMEM] * (6 + ROUNDS),
        out_specs=[VMEM] * shots,
        scratch_shapes=[
            scratch(*wide_shape),
            scratch(*wide_shape),
            scratch(2, levels, 8, across),
        ],
        compiler_params=params,
        name="neighbours_part",
    )(sides, bits, steps, outside, source, coef, *came_sides)
    def swap_shots(value, number):
        return lax.ppermute(value, "shot", [(shot, shot ^ number) for shot in range(shots)])

    came = [swap_shots(sent, 2 + i) for i, sent in enumerate(blocks)]
    weight = 1.0 / shots
    image_shape = (OFFS, share, extent, across)

    src_next, rec_next = pl.pallas_call(
        write_fields,
        out_shape=(struct(1, levels, extent, across), struct(1, levels, extent, across)),
        in_specs=[VMEM],
        out_specs=[HBM, HBM],
        scratch_shapes=[pltpu.SemaphoreType.DMA((2,))],
        compiler_params=params,
        name="write_fields",
    )(final)
    others = pl.pallas_call(
        stack,
        out_shape=struct(len(came), *block.shape),
        in_specs=[VMEM] * len(came),
        out_specs=VMEM,
        compiler_params=params,
        name="stack",
    )(*came[::-1])
    mine_sides = swap_rounds([mine] * ROUNDS)
    others_sides = swap_rounds([others] * 2)
    partner = [swap_shots(value[1], 1) for value in (mine, *mine_sides)]
    operands = [others, *others_sides[::-1], mine, *mine_sides[::-1], *partner]
    image = pl.pallas_call(
        functools.partial(image_products, weight),
        out_shape=struct(*image_shape),
        in_specs=[VMEM] * (1 + len(operands)),
        out_specs=HBM,
        scratch_shapes=[
            scratch(shots, 2, share, 3 * extent, across),
            scratch(*image_shape),
            pltpu.SemaphoreType.DMA((11,)),
        ],
        compiler_params=params,
        name="image_products",
    )(sides, *operands)
    return src_next, rec_next, image


def solution(mesh):
    field = P(("groups", "shot"), None, "tile", None)
    return jax.shard_map(
        per_device,
        mesh=mesh,
        in_specs=(
            field,
            field,
            field,
            field,
            P("groups"),
            P(None, ("groups", "tile"), None),
            P(("groups", "shot")),
            P(("groups", "shot"), None),
            P(("groups", "shot"), "tile"),
            P(("groups", "shot"), None, "tile"),
        ),
        out_specs=(field, field, P(None, "shot", ("groups", "tile"), None)),
        check_vma=False,
    )
```

```python
import functools

import jax
import jax.numpy as jnp
from jax import lax
from jax.experimental import pallas as pl
from jax.experimental.pallas import tpu as pltpu
from jax.sharding import PartitionSpec as P

OFFS = 33
REACH = OFFS // 2
HALO = 4
LEAD = 8
ROUNDS = 3
SHIFTS = {2: 0, 3: 0}

COEFS = (-205.0 / 72.0, 8.0 / 5.0, -1.0 / 5.0, 8.0 / 315.0, -1.0 / 560.0)

VMEM = pl.BlockSpec(memory_space=pltpu.VMEM)
HBM = pl.BlockSpec(memory_space=pltpu.HBM)
SMEM = pl.BlockSpec(memory_space=pltpu.SMEM)
LIMIT = 16 * 1024 * 1024


def lane_weights(shape):
    lane = lax.broadcasted_iota(jnp.int32, shape, 1)
    across = shape[1]
    after = [jnp.where(lane < across - k, COEFS[k], 0.0) for k in range(1, HALO + 1)]
    before = [jnp.where(lane >= k, COEFS[k], 0.0) for k in range(1, HALO + 1)]
    return after, before


def lane_sum(centre, weights):
    after, before = weights
    across = centre.shape[1]
    total = 3.0 * COEFS[0] * centre
    for k in range(1, HALO + 1):
        total = total + after[k - 1] * pltpu.roll(centre, across - k, 1)
        total = total + before[k - 1] * pltpu.roll(centre, k, 1)
    return total


def beside_sum(wide, field, level, begin, count):
    total = None
    for k in range(1, HALO + 1):
        pair = (
            wide[field, level, begin + k : begin + k + count, :]
            + wide[field, level, begin - k : begin - k + count, :]
        )
        total = COEFS[k] * pair if total is None else total + COEFS[k] * pair
    return total


def depth_sum(rows_of, level, levels, total):
    for k in range(1, HALO + 1):
        for near in (level - k, level + k):
            if 0 <= near < levels:
                total = total + COEFS[k] * rows_of(near)
    return total


def laplace_level(wide, field, level, levels, extent, weights):
    def rows_of(near):
        return wide[field, near, LEAD : LEAD + extent, :]

    total = lane_sum(rows_of(level), weights) + beside_sum(wide, field, level, LEAD, extent)
    return depth_sum(rows_of, level, levels, total)


def is_low(across):
    return lax.broadcasted_iota(jnp.int32, (8, across), 0) < HALO


def own_edges(
    table_hbm,
    spots_hbm,
    traces_hbm,
    amps_hbm,
    ids_hbm,
    src_now,
    rec_now,
    src_prev,
    rec_prev,
    amps_ref,
    wide,
    prev_ref,
    ids_ref,
    speeds_ref,
    planes_ref,
    *rest,
):
    sent_refs, rest = rest[:ROUNDS], rest[ROUNDS:]
    table, spots_ref, traces_ref, edges, sems = rest
    levels, extent, across = ids_ref.shape
    regions = table_hbm.shape[1]
    end = LEAD + extent
    rows = pl.ds(LEAD, extent)
    moves = [(table_hbm, table), (spots_hbm, spots_ref), (traces_hbm, traces_ref)]
    for begin in range(0, levels, levels // 2):
        part = pl.ds(begin, levels // 2)
        moves += [
            (src_now.at[0, part], wide.at[0, part, rows, :]),
            (rec_now.at[0, part], wide.at[1, part, rows, :]),
            (ids_hbm.at[part], ids_ref.at[part]),
            (src_prev.at[0, part], prev_ref.at[0, part]),
            (rec_prev.at[0, part], prev_ref.at[1, part]),
        ]
    moves.append((amps_hbm, amps_ref))
    copies = [
        pltpu.make_async_copy(here, there, sems.at[i]) for i, (here, there) in enumerate(moves)
    ]
    for copy in copies:
        copy.start()
    zeros = jnp.zeros((LEAD, across), jnp.float32)
    for field in range(2):
        for level in range(levels):
            wide[field, level, 0:LEAD, :] = zeros
            wide[field, level, end : end + LEAD, :] = zeros
    weights = lane_weights((8, across))
    low_half = is_low(across)
    my_round = lax.rem(lax.axis_index("tile"), ROUNDS)
    for copy in copies:
        copy.wait()

    spots = spots_ref[...]
    column = lax.broadcasted_iota(jnp.int32, (extent, spots.shape[1]), 0) * across
    in_column = (spots >= column) & (spots < column + across)
    lane = lax.broadcasted_iota(jnp.int32, (across, spots.shape[1]), 0)
    in_row = jnp.where(lax.rem(spots, across) == lane, 1.0, 0.0)
    traces = jnp.concatenate(
        [jnp.where(in_column, traces_ref[0, t : t + 1, :], 0.0) for t in range(2)], axis=0
    )
    planes = lax.dot_general(
        traces,
        in_row,
        (((1,), (1,)), ((), ())),
        precision=lax.Precision.HIGHEST,
        preferred_element_type=jnp.float32,
    )
    planes_ref[...] = planes

    def send(place, low, high):
        for number, sent_ref in enumerate(sent_refs):
            sent_ref[place] = jnp.where(my_round == number, high, low)

    def halves(ref, *place):
        return jnp.where(
            low_half, ref[(*place, pl.ds(0, 8))], ref[(*place, pl.ds(extent - 8, 8))]
        )

    speeds = jnp.concatenate(
        [table[...], jnp.zeros((1, across - regions), jnp.float32)], axis=1
    )
    speeds = jnp.broadcast_to(speeds, (8, across))
    speeds_ref[...] = speeds
    coefs = [
        jnp.take_along_axis(speeds, halves(ids_ref, level), axis=1, mode="promise_in_bounds")
        for level in range(levels)
    ]
    for level in range(0, levels, 2):
        here, after = coefs[level], coefs[level + 1]
        send(
            2 * levels + level // 2,
            jnp.where(low_half, here, pltpu.roll(after, HALO, 0)),
            jnp.where(low_half, pltpu.roll(here, HALO, 0), after),
        )

    for field in range(2):
        for level in range(levels):
            edges[field, level] = jnp.where(
                low_half, wide[field, level, LEAD : LEAD + 8, :], wide[field, level, end - 8 : end, :]
            )
    for field in range(2):
        for level in range(levels):
            now = edges[field, level]
            total = lane_sum(now, weights) + jnp.where(
                low_half,
                beside_sum(wide, field, level, LEAD, 8),
                beside_sum(wide, field, level, end - 8, 8),
            )
            total = depth_sum(lambda near: edges[field, near], level, levels, total)
            value = 2.0 * now - halves(prev_ref, field, level) + coefs[level] * total
            if field == 1 and level == 0:
                value = value + jnp.where(low_half, planes[0:8, :], planes[extent - 8 : extent, :])
            send(
                field * levels + level,
                jnp.where(low_half, now, pltpu.roll(value, HALO, 0)),
                jnp.where(low_half, pltpu.roll(now, HALO, 0), value),
            )


def own_steps(
    width,
    cell_ref,
    amps_ref,
    own,
    prev_ref,
    ids_ref,
    speeds_ref,
    planes_ref,
    coef_ref,
    steps_ref,
    outside_ref,
    source_ref,
    sides_ref,
    bits_ref,
    middle,
):
    levels, extent, across = ids_ref.shape
    end = LEAD + extent
    cell = cell_ref[0]
    deep = lax.div(cell, width * across)
    row = lax.rem(lax.div(cell, across), width) - lax.axis_index("tile") * extent + LEAD
    shape = (extent + 2 * LEAD, across)
    rows = lax.broadcasted_iota(jnp.int32, shape, 0)
    lanes = lax.broadcasted_iota(jnp.int32, shape, 1)
    hit = jnp.where((rows == row) & (lanes == lax.rem(cell, across)), 1.0, 0.0)
    weights = lane_weights((extent, across))
    speeds = speeds_ref[...]
    zeros = jnp.zeros((LEAD, across), jnp.float32)
    for level in range(levels):
        here = hit * jnp.where(deep == level, 1.0, 0.0)
        source_ref[level] = here * amps_ref[0:1, 0:1]
        steps_ref[0, level] = here[LEAD:end, :] * amps_ref[0:1, 1:2] - own[0, level, LEAD:end, :]
        steps_ref[1, level] = -own[1, level, LEAD:end, :]
        for begin in range(0, extent, 8):
            coef_ref[level, begin : begin + 8, :] = jnp.take_along_axis(
                speeds, ids_ref[level, begin : begin + 8, :], axis=1, mode="promise_in_bounds"
            )
    steps_ref[1, 0] += planes_ref[extent:, :]
    for field in range(2):
        for level in range(levels):
            total = laplace_level(own, field, level, levels, extent, weights)
            value = 2.0 * own[field, level, LEAD:end, :] - prev_ref[field, level]
            value = value + coef_ref[level] * total
            if field == 0:
                value = value + source_ref[level, LEAD:end, :]
            elif level == 0:
                value = value + planes_ref[:extent, :]
            middle[field, level, 0:LEAD, :] = zeros
            middle[field, level, LEAD:end, :] = value
            middle[field, level, end : end + LEAD, :] = zeros
            below = above = jnp.zeros((HALO, across), jnp.float32)
            for k in range(1, HALO + 1):
                begin = LEAD - HALO + k
                below = below + COEFS[k] * own[field, level, begin : begin + HALO, :]
                above = above + COEFS[k] * own[field, level, end - k : end - k + HALO, :]
            outside_ref[field, level, 0:HALO, :] = below
            outside_ref[field, level, HALO : 2 * HALO, :] = above
    for field in range(2):
        for level in range(levels):
            total = laplace_level(middle, field, level, levels, extent, weights)
            steps_ref[field, level] += (
                2.0 * middle[field, level, LEAD:end, :] + coef_ref[level] * total
            )
    tile, tiles = lax.axis_index("tile"), lax.axis_size("tile")
    places = (jnp.where(tile > 0, 1, 0), jnp.where(tile < tiles - 1, 1, 0))
    places += tuple((tile + SHIFTS[rounds]) % rounds for rounds in (2, 3))
    for place, value in enumerate(places):
        sides_ref[place] = jnp.full(sides_ref.shape[1:], value, dtype=jnp.int32)
    shot = jnp.full(bits_ref.shape[1:], lax.axis_index("shot"), dtype=jnp.int32)
    for bit in range(bits_ref.shape[0]):
        bits_ref[bit] = shot & (1 << bit)


def both_sides(sides, came):
    has_low, has_high, my_round = sides[0], sides[1], sides[len(came)]
    low, high = came[-1], came[0]
    for number in range(1, len(came)):
        low = jnp.where(my_round == number, came[number - 1], low)
        high = jnp.where(my_round == number, came[number], high)
    return jnp.where(has_low != 0, low, 0.0), jnp.where(has_high != 0, high, 0.0)


def neighbours_part(
    sides_ref, bits_ref, steps_ref, outside_ref, source_ref, coef_ref, *rest
):
    came_refs, (final_ref, mine_ref, *blocks, other, change, edges) = rest[:ROUNDS], rest[ROUNDS:]
    blocks = [mine_ref.at[0], mine_ref.at[1], *blocks]
    levels, extent, across = coef_ref.shape
    share = mine_ref.shape[2]
    end = LEAD + extent
    low_half = is_low(across)
    weights = lane_weights((8, across))
    sides = [sides_ref[place] for place in range(4)]
    zeros = jnp.zeros((8, across), jnp.float32)

    def received(place):
        return both_sides(sides, [ref[place] for ref in came_refs])

    coefs = [received(2 * levels + pair) for pair in range(levels // 2)]
    for field in range(2):
        for level in range(levels):
            low, high = received(field * levels + level)
            other[field, level, LEAD : LEAD + 8, :] = zeros
            other[field, level, end - 8 : end, :] = zeros
            other[field, level, LEAD - HALO : LEAD, :] = low[0:HALO, :]
            other[field, level, end : end + HALO, :] = high[0:HALO, :]
            half = slice(level % 2 * HALO, level % 2 * HALO + HALO)
            low_coef, high_coef = (coef[half, :] for coef in coefs[level // 2])
            low = low[HALO:, :] + low_coef * outside_ref[field, level, 0:HALO, :]
            high = high[HALO:, :] + high_coef * outside_ref[field, level, HALO : 2 * HALO, :]
            if field == 0:
                low = low + source_ref[level, LEAD - HALO : LEAD, :]
                high = high + source_ref[level, end : end + HALO, :]
            change[field, level, LEAD - HALO : LEAD, :] = low
            change[field, level, end : end + HALO, :] = high
    for field in range(2):
        for level in range(levels):
            left = right = zeros
            for k in range(1, HALO + 1):
                left = left + COEFS[k] * other[field, level, LEAD - k : LEAD - k + 8, :]
                right = right + COEFS[k] * other[field, level, end - 8 + k : end + k, :]
            left = coef_ref[level, 0:8, :] * left
            right = coef_ref[level, extent - 8 : extent, :] * right
            change[field, level, LEAD : LEAD + 8, :] = left
            change[field, level, end - 8 : end, :] = right
            edges[field, level] = left + right
    for field in range(2):
        for level in range(levels):
            total = depth_sum(
                lambda near: edges[field, near],
                level,
                levels,
                lane_sum(edges[field, level], weights),
            )
            for begin, mine in ((0, low_half), (extent - 8, ~low_half)):
                part = beside_sum(change, field, level, LEAD + begin, 8)
                part = part + jnp.where(mine, total, 0.0)
                final_ref[field, level, begin : begin + 8, :] = (
                    steps_ref[field, level, begin : begin + 8, :]
                    + 2.0 * change[field, level, LEAD + begin : LEAD + begin + 8, :]
                    + coef_ref[level, begin : begin + 8, :] * part
                )
    masks = [
        jnp.concatenate([bits_ref[bit]] * (extent // 8), axis=0) != 0
        for bit in range(bits_ref.shape[0])
    ]
    for field in range(2):
        for level in range(share):
            parts = [final_ref[field, place * share + level] for place in range(len(blocks))]
            for bit, mask in enumerate(masks):
                parts = [
                    jnp.where(mask, parts[place ^ (1 << bit)], parts[place])
                    for place in range(len(blocks))
                ]
            for block, part in zip(blocks, parts):
                block[field, level] = part


def widen(weight, sides_ref, shot, mine_ref, came_refs, wide):
    _, share, extent, _ = mine_ref.shape
    sides = [
        jnp.concatenate([sides_ref[place]] * (extent // 8), axis=0) for place in range(4)
    ]
    for field in range(2):
        for level in range(share):
            scale = weight if field == 0 else 1.0
            low, high = both_sides(sides, [ref[field, level] for ref in came_refs])
            wide[shot, field, level, 0:extent, :] = scale * low
            wide[shot, field, level, extent : 2 * extent, :] = scale * mine_ref[field, level]
            wide[shot, field, level, 2 * extent : 3 * extent, :] = scale * high


def offset_product(wide, offset, level):
    extent = wide.shape[3] // 3
    lower = extent + REACH - offset
    upper = extent - REACH + offset
    total = None
    for shot in range(wide.shape[0]):
        product = (
            wide[shot, 0, level, lower : lower + extent, :]
            * wide[shot, 1, level, upper : upper + extent, :]
        )
        total = product if total is None else total + product
    return total


def stack(*refs):
    for place in range(len(refs) - 1):
        refs[-1][place] = refs[place][...]


def hold(mine_ref, _others_ref, held_ref):
    held_ref[...] = mine_ref[...]


def write_fields(final_ref, src_hbm, rec_hbm, sems):
    copies = [
        pltpu.make_async_copy(final_ref.at[field], out.at[0], sems.at[field])
        for field, out in enumerate((src_hbm, rec_hbm))
    ]
    for copy in copies:
        copy.start()
    for copy in copies:
        copy.wait()


def image_products(weight, sides_ref, others_ref, *rest):
    others_sides, rest = rest[ROUNDS - 1 :: -1], rest[ROUNDS:]
    mine_ref, rest = rest[0], rest[1:]
    mine_sides, rest = rest[ROUNDS - 1 :: -1], rest[ROUNDS:]
    partner_refs, rest = rest[: 1 + ROUNDS], rest[1 + ROUNDS :]
    image_hbm, wide, image_ref, sems = rest
    places = [
        (mine_ref.at[0], [ref.at[0] for ref in mine_sides]),
        (partner_refs[0], partner_refs[1:]),
    ]
    for place in range(others_ref.shape[0]):
        places.append((others_ref.at[place], [ref.at[place] for ref in others_sides]))
    for shot, (own_ref, came_refs) in enumerate(places):
        widen(weight, sides_ref, shot, own_ref, came_refs, wide)
    parts = sems.shape[0]
    copies = []
    for piece in range(parts):
        offsets = range(piece * OFFS // parts, (piece + 1) * OFFS // parts)
        for offset in offsets:
            for level in range(image_ref.shape[1]):
                image_ref[offset, level] = offset_product(wide, offset, level)
        rows = pl.ds(offsets[0], len(offsets))
        copy = pltpu.make_async_copy(image_ref.at[rows], image_hbm.at[rows], sems.at[piece])
        copy.start()
        copies.append(copy)
    for copy in copies:
        copy.wait()


def swap_tiles(value, lower):
    tiles, shots = lax.axis_size("tile"), lax.axis_size("shot")
    partner = {}
    for tile in lower:
        partner[tile], partner[tile + 1] = tile + 1, tile
    pairs = []
    for tile in range(tiles):
        for shot in range(shots):
            here = tile * shots + shot
            there = partner[tile] * shots + shot if tile in partner else here ^ 1
            pairs.append((here, there))
    return lax.ppermute(value, ("tile", "shot"), pairs)


def swap_rounds(values):
    tiles, rounds = lax.axis_size("tile"), len(values)
    return [
        swap_tiles(value, range((number - SHIFTS[rounds]) % rounds, tiles - 1, rounds))
        for number, value in enumerate(values)
    ]


def per_device(
    src_prev,
    src_now,
    rec_prev,
    rec_now,
    speed_table,
    region_ids,
    source_cell,
    wavelet,
    receiver_cell,
    receiver_data,
):
    _, levels, extent, across = src_now.shape
    tiles = lax.axis_size("tile")
    width = extent * tiles
    shots = lax.axis_size("shot")
    share = levels // shots
    params = pltpu.CompilerParams(vmem_limit_bytes=LIMIT)

    def struct(*shape):
        return jax.ShapeDtypeStruct(shape, jnp.float32)

    def scratch(*shape, dtype=jnp.float32):
        return pltpu.VMEM(shape, dtype)

    wide_shape = (2, levels, extent + 2 * LEAD, across)
    message = struct(2 * levels + levels // 2, 2 * HALO, across)
    fields_shape = (2, levels, extent, across)
    amps, own, prev, ids, speeds, planes, *sent = pl.pallas_call(
        own_edges,
        out_shape=(
            struct(*wavelet.shape),
            struct(*wide_shape),
            struct(*fields_shape),
            jax.ShapeDtypeStruct(region_ids.shape, jnp.int32),
            struct(8, across),
            struct(2 * extent, across),
            *([message] * ROUNDS),
        ),
        in_specs=[HBM] * 9,
        out_specs=[VMEM] * (6 + ROUNDS),
        scratch_shapes=[
            scratch(1, speed_table.shape[0]),
            scratch(*receiver_cell.shape, dtype=jnp.int32),
            scratch(*receiver_data.shape),
            scratch(2, levels, 8, across),
            pltpu.SemaphoreType.DMA((14,)),
        ],
        compiler_params=params,
        name="own_edges",
    )(
        *(
            pltpu.with_memory_space_constraint(array, pltpu.HBM)
            for array in (
                speed_table.reshape(1, -1),
                receiver_cell,
                receiver_data,
                wavelet,
                region_ids,
                src_now,
                rec_now,
                src_prev,
                rec_prev,
            )
        )
    )
    came_sides = swap_rounds(sent)
    coef, steps, outside, source, sides, bits = pl.pallas_call(
        functools.partial(own_steps, width),
        out_shape=(
            struct(levels, extent, across),
            struct(*fields_shape),
            struct(2, levels, 2 * HALO, across),
            struct(levels, extent + 2 * LEAD, across),
            jax.ShapeDtypeStruct((4, 8, across), jnp.int32),
            jax.ShapeDtypeStruct((shots.bit_length() - 1, 8, across), jnp.int32),
        ),
        in_specs=[SMEM] + [VMEM] * 6,
        out_specs=[VMEM] * 6,
        scratch_shapes=[scratch(*wide_shape)],
        compiler_params=params,
        name="own_steps",
    )(source_cell, amps, own, prev, ids, speeds, planes)
    block = struct(2, share, extent, across)
    final, mine, *blocks = pl.pallas_call(
        neighbours_part,
        out_shape=(struct(*fields_shape), struct(2, *block.shape), *([block] * (shots - 2))),
        in_specs=[VMEM] * (6 + ROUNDS),
        out_specs=[VMEM] * shots,
        scratch_shapes=[
            scratch(*wide_shape),
            scratch(*wide_shape),
            scratch(2, levels, 8, across),
        ],
        compiler_params=params,
        name="neighbours_part",
    )(sides, bits, steps, outside, source, coef, *came_sides)
    def swap_shots(value, number):
        return lax.ppermute(value, "shot", [(shot, shot ^ number) for shot in range(shots)])

    came = [swap_shots(sent, 2 + i) for i, sent in enumerate(blocks)]
    weight = 1.0 / shots
    image_shape = (OFFS, share, extent, across)

    src_next, rec_next = pl.pallas_call(
        write_fields,
        out_shape=(struct(1, levels, extent, across), struct(1, levels, extent, across)),
        in_specs=[VMEM],
        out_specs=[HBM, HBM],
        scratch_shapes=[pltpu.SemaphoreType.DMA((2,))],
        compiler_params=params,
        name="write_fields",
    )(final)
    others = pl.pallas_call(
        stack,
        out_shape=struct(len(came), *block.shape),
        in_specs=[VMEM] * len(came),
        out_specs=VMEM,
        compiler_params=params,
        name="stack",
    )(*came[::-1])
    mine_sides = swap_rounds([mine] * ROUNDS)
    others_sides = swap_rounds([others] * ROUNDS)
    held = pl.pallas_call(
        hold,
        out_shape=block,
        in_specs=[VMEM] * 2,
        out_specs=VMEM,
        compiler_params=params,
        name="hold",
    )(mine[1], others)
    partner = [swap_shots(value, 1) for value in (held, *(side[1] for side in mine_sides))]
    operands = [others, *others_sides[::-1], mine, *mine_sides[::-1], *partner]
    image = pl.pallas_call(
        functools.partial(image_products, weight),
        out_shape=struct(*image_shape),
        in_specs=[VMEM] * (1 + len(operands)),
        out_specs=HBM,
        scratch_shapes=[
            scratch(shots, 2, share, 3 * extent, across),
            scratch(*image_shape),
            pltpu.SemaphoreType.DMA((11,)),
        ],
        compiler_params=params,
        name="image_products",
    )(sides, *operands)
    return src_next, rec_next, image


def solution(mesh):
    field = P(("groups", "shot"), None, "tile", None)
    return jax.shard_map(
        per_device,
        mesh=mesh,
        in_specs=(
            field,
            field,
            field,
            field,
            P("groups"),
            P(None, ("groups", "tile"), None),
            P(("groups", "shot")),
            P(("groups", "shot"), None),
            P(("groups", "shot"), "tile"),
            P(("groups", "shot"), None, "tile"),
        ),
        out_specs=(field, field, P(None, "shot", ("groups", "tile"), None)),
        check_vma=False,
    )
```

```python
import functools

import jax
import jax.numpy as jnp
from jax import lax
from jax.experimental import pallas as pl
from jax.experimental.pallas import tpu as pltpu
from jax.sharding import PartitionSpec as P

OFFS = 33
REACH = OFFS // 2
HALO = 4
LEAD = 8
ROUNDS = 3
SHIFTS = {2: 0, 3: 0}

COEFS = (-205.0 / 72.0, 8.0 / 5.0, -1.0 / 5.0, 8.0 / 315.0, -1.0 / 560.0)

VMEM = pl.BlockSpec(memory_space=pltpu.VMEM)
HBM = pl.BlockSpec(memory_space=pltpu.HBM)
SMEM = pl.BlockSpec(memory_space=pltpu.SMEM)
LIMIT = 16 * 1024 * 1024


def lane_weights(shape):
    lane = lax.broadcasted_iota(jnp.int32, shape, 1)
    across = shape[1]
    after = [jnp.where(lane < across - k, COEFS[k], 0.0) for k in range(1, HALO + 1)]
    before = [jnp.where(lane >= k, COEFS[k], 0.0) for k in range(1, HALO + 1)]
    return after, before


def lane_sum(centre, weights):
    after, before = weights
    across = centre.shape[1]
    total = 3.0 * COEFS[0] * centre
    for k in range(1, HALO + 1):
        total = total + after[k - 1] * pltpu.roll(centre, across - k, 1)
        total = total + before[k - 1] * pltpu.roll(centre, k, 1)
    return total


def beside_sum(wide, field, level, begin, count):
    total = None
    for k in range(1, HALO + 1):
        pair = (
            wide[field, level, begin + k : begin + k + count, :]
            + wide[field, level, begin - k : begin - k + count, :]
        )
        total = COEFS[k] * pair if total is None else total + COEFS[k] * pair
    return total


def depth_sum(rows_of, level, levels, total):
    for k in range(1, HALO + 1):
        for near in (level - k, level + k):
            if 0 <= near < levels:
                total = total + COEFS[k] * rows_of(near)
    return total


def laplace_level(wide, field, level, levels, extent, weights):
    def rows_of(near):
        return wide[field, near, LEAD : LEAD + extent, :]

    total = lane_sum(rows_of(level), weights) + beside_sum(wide, field, level, LEAD, extent)
    return depth_sum(rows_of, level, levels, total)


def is_low(across):
    return lax.broadcasted_iota(jnp.int32, (8, across), 0) < HALO


def own_edges(
    table_hbm,
    spots_hbm,
    traces_hbm,
    amps_hbm,
    ids_hbm,
    src_now,
    rec_now,
    src_prev,
    rec_prev,
    amps_ref,
    wide,
    prev_ref,
    ids_ref,
    speeds_ref,
    planes_ref,
    *rest,
):
    sent_refs, rest = rest[:ROUNDS], rest[ROUNDS:]
    table, spots_ref, traces_ref, edges, sems = rest
    levels, extent, across = ids_ref.shape
    regions = table_hbm.shape[1]
    end = LEAD + extent
    rows = pl.ds(LEAD, extent)
    moves = [(table_hbm, table), (spots_hbm, spots_ref), (traces_hbm, traces_ref)]
    for begin in range(0, levels, levels // 2):
        part = pl.ds(begin, levels // 2)
        moves += [
            (src_now.at[0, part], wide.at[0, part, rows, :]),
            (rec_now.at[0, part], wide.at[1, part, rows, :]),
            (ids_hbm.at[part], ids_ref.at[part]),
            (src_prev.at[0, part], prev_ref.at[0, part]),
            (rec_prev.at[0, part], prev_ref.at[1, part]),
        ]
    moves.append((amps_hbm, amps_ref))
    copies = [
        pltpu.make_async_copy(here, there, sems.at[i]) for i, (here, there) in enumerate(moves)
    ]
    for copy in copies:
        copy.start()
    zeros = jnp.zeros((LEAD, across), jnp.float32)
    for field in range(2):
        for level in range(levels):
            wide[field, level, 0:LEAD, :] = zeros
            wide[field, level, end : end + LEAD, :] = zeros
    weights = lane_weights((8, across))
    low_half = is_low(across)
    my_round = lax.rem(lax.axis_index("tile"), ROUNDS)
    for copy in copies:
        copy.wait()

    spots = spots_ref[...]
    column = lax.broadcasted_iota(jnp.int32, (extent, spots.shape[1]), 0) * across
    in_column = (spots >= column) & (spots < column + across)
    lane = lax.broadcasted_iota(jnp.int32, (across, spots.shape[1]), 0)
    in_row = jnp.where(lax.rem(spots, across) == lane, 1.0, 0.0)
    traces = jnp.concatenate(
        [jnp.where(in_column, traces_ref[0, t : t + 1, :], 0.0) for t in range(2)], axis=0
    )
    planes = lax.dot_general(
        traces,
        in_row,
        (((1,), (1,)), ((), ())),
        precision=lax.Precision.HIGHEST,
        preferred_element_type=jnp.float32,
    )
    planes_ref[...] = planes

    def send(place, low, high):
        for number, sent_ref in enumerate(sent_refs):
            sent_ref[place] = jnp.where(my_round == number, high, low)

    def halves(ref, *place):
        return jnp.where(
            low_half, ref[(*place, pl.ds(0, 8))], ref[(*place, pl.ds(extent - 8, 8))]
        )

    speeds = jnp.concatenate(
        [table[...], jnp.zeros((1, across - regions), jnp.float32)], axis=1
    )
    speeds = jnp.broadcast_to(speeds, (8, across))
    speeds_ref[...] = speeds
    coefs = [
        jnp.take_along_axis(speeds, halves(ids_ref, level), axis=1, mode="promise_in_bounds")
        for level in range(levels)
    ]
    for level in range(0, levels, 2):
        here, after = coefs[level], coefs[level + 1]
        send(
            2 * levels + level // 2,
            jnp.where(low_half, here, pltpu.roll(after, HALO, 0)),
            jnp.where(low_half, pltpu.roll(here, HALO, 0), after),
        )

    for field in range(2):
        for level in range(levels):
            edges[field, level] = jnp.where(
                low_half, wide[field, level, LEAD : LEAD + 8, :], wide[field, level, end - 8 : end, :]
            )
    for field in range(2):
        for level in range(levels):
            now = edges[field, level]
            total = lane_sum(now, weights) + jnp.where(
                low_half,
                beside_sum(wide, field, level, LEAD, 8),
                beside_sum(wide, field, level, end - 8, 8),
            )
            total = depth_sum(lambda near: edges[field, near], level, levels, total)
            value = 2.0 * now - halves(prev_ref, field, level) + coefs[level] * total
            if field == 1 and level == 0:
                value = value + jnp.where(low_half, planes[0:8, :], planes[extent - 8 : extent, :])
            send(
                field * levels + level,
                jnp.where(low_half, now, pltpu.roll(value, HALO, 0)),
                jnp.where(low_half, pltpu.roll(now, HALO, 0), value),
            )


def own_steps(
    width,
    cell_ref,
    amps_ref,
    own,
    prev_ref,
    ids_ref,
    speeds_ref,
    planes_ref,
    coef_ref,
    steps_ref,
    outside_ref,
    source_ref,
    sides_ref,
    bits_ref,
    middle,
):
    levels, extent, across = ids_ref.shape
    end = LEAD + extent
    cell = cell_ref[0]
    deep = lax.div(cell, width * across)
    row = lax.rem(lax.div(cell, across), width) - lax.axis_index("tile") * extent + LEAD
    shape = (extent + 2 * LEAD, across)
    rows = lax.broadcasted_iota(jnp.int32, shape, 0)
    lanes = lax.broadcasted_iota(jnp.int32, shape, 1)
    hit = jnp.where((rows == row) & (lanes == lax.rem(cell, across)), 1.0, 0.0)
    weights = lane_weights((extent, across))
    speeds = speeds_ref[...]
    zeros = jnp.zeros((LEAD, across), jnp.float32)
    for level in range(levels):
        here = hit * jnp.where(deep == level, 1.0, 0.0)
        source_ref[level] = here * amps_ref[0:1, 0:1]
        steps_ref[0, level] = here[LEAD:end, :] * amps_ref[0:1, 1:2] - own[0, level, LEAD:end, :]
        steps_ref[1, level] = -own[1, level, LEAD:end, :]
        for begin in range(0, extent, 8):
            coef_ref[level, begin : begin + 8, :] = jnp.take_along_axis(
                speeds, ids_ref[level, begin : begin + 8, :], axis=1, mode="promise_in_bounds"
            )
    steps_ref[1, 0] += planes_ref[extent:, :]
    for field in range(2):
        for level in range(levels):
            total = laplace_level(own, field, level, levels, extent, weights)
            value = 2.0 * own[field, level, LEAD:end, :] - prev_ref[field, level]
            value = value + coef_ref[level] * total
            if field == 0:
                value = value + source_ref[level, LEAD:end, :]
            elif level == 0:
                value = value + planes_ref[:extent, :]
            middle[field, level, 0:LEAD, :] = zeros
            middle[field, level, LEAD:end, :] = value
            middle[field, level, end : end + LEAD, :] = zeros
            below = above = jnp.zeros((HALO, across), jnp.float32)
            for k in range(1, HALO + 1):
                begin = LEAD - HALO + k
                below = below + COEFS[k] * own[field, level, begin : begin + HALO, :]
                above = above + COEFS[k] * own[field, level, end - k : end - k + HALO, :]
            outside_ref[field, level, 0:HALO, :] = below
            outside_ref[field, level, HALO : 2 * HALO, :] = above
    for field in range(2):
        for level in range(levels):
            total = laplace_level(middle, field, level, levels, extent, weights)
            steps_ref[field, level] += (
                2.0 * middle[field, level, LEAD:end, :] + coef_ref[level] * total
            )
    tile, tiles = lax.axis_index("tile"), lax.axis_size("tile")
    places = (jnp.where(tile > 0, 1, 0), jnp.where(tile < tiles - 1, 1, 0))
    places += tuple((tile + SHIFTS[rounds]) % rounds for rounds in (2, 3))
    for place, value in enumerate(places):
        sides_ref[place] = jnp.full(sides_ref.shape[1:], value, dtype=jnp.int32)
    shot = jnp.full(bits_ref.shape[1:], lax.axis_index("shot"), dtype=jnp.int32)
    for bit in range(bits_ref.shape[0]):
        bits_ref[bit] = shot & (1 << bit)


def both_sides(sides, came):
    has_low, has_high, my_round = sides[0], sides[1], sides[len(came)]
    low, high = came[-1], came[0]
    for number in range(1, len(came)):
        low = jnp.where(my_round == number, came[number - 1], low)
        high = jnp.where(my_round == number, came[number], high)
    return jnp.where(has_low != 0, low, 0.0), jnp.where(has_high != 0, high, 0.0)


def neighbours_part(
    sides_ref, bits_ref, steps_ref, outside_ref, source_ref, coef_ref, *rest
):
    came_refs, (final_ref, mine_ref, *blocks, other, change, edges) = rest[:ROUNDS], rest[ROUNDS:]
    blocks = [mine_ref.at[0], mine_ref.at[1], *blocks]
    levels, extent, across = coef_ref.shape
    share = mine_ref.shape[2]
    end = LEAD + extent
    low_half = is_low(across)
    weights = lane_weights((8, across))
    sides = [sides_ref[place] for place in range(4)]
    zeros = jnp.zeros((8, across), jnp.float32)

    def received(place):
        return both_sides(sides, [ref[place] for ref in came_refs])

    coefs = [received(2 * levels + pair) for pair in range(levels // 2)]
    for field in range(2):
        for level in range(levels):
            low, high = received(field * levels + level)
            other[field, level, LEAD : LEAD + 8, :] = zeros
            other[field, level, end - 8 : end, :] = zeros
            other[field, level, LEAD - HALO : LEAD, :] = low[0:HALO, :]
            other[field, level, end : end + HALO, :] = high[0:HALO, :]
            half = slice(level % 2 * HALO, level % 2 * HALO + HALO)
            low_coef, high_coef = (coef[half, :] for coef in coefs[level // 2])
            low = low[HALO:, :] + low_coef * outside_ref[field, level, 0:HALO, :]
            high = high[HALO:, :] + high_coef * outside_ref[field, level, HALO : 2 * HALO, :]
            if field == 0:
                low = low + source_ref[level, LEAD - HALO : LEAD, :]
                high = high + source_ref[level, end : end + HALO, :]
            change[field, level, LEAD - HALO : LEAD, :] = low
            change[field, level, end : end + HALO, :] = high
    for field in range(2):
        for level in range(levels):
            left = right = zeros
            for k in range(1, HALO + 1):
                left = left + COEFS[k] * other[field, level, LEAD - k : LEAD - k + 8, :]
                right = right + COEFS[k] * other[field, level, end - 8 + k : end + k, :]
            left = coef_ref[level, 0:8, :] * left
            right = coef_ref[level, extent - 8 : extent, :] * right
            change[field, level, LEAD : LEAD + 8, :] = left
            change[field, level, end - 8 : end, :] = right
            edges[field, level] = left + right
    for field in range(2):
        for level in range(levels):
            total = depth_sum(
                lambda near: edges[field, near],
                level,
                levels,
                lane_sum(edges[field, level], weights),
            )
            for begin, mine in ((0, low_half), (extent - 8, ~low_half)):
                part = beside_sum(change, field, level, LEAD + begin, 8)
                part = part + jnp.where(mine, total, 0.0)
                final_ref[field, level, begin : begin + 8, :] = (
                    steps_ref[field, level, begin : begin + 8, :]
                    + 2.0 * change[field, level, LEAD + begin : LEAD + begin + 8, :]
                    + coef_ref[level, begin : begin + 8, :] * part
                )
    masks = [
        jnp.concatenate([bits_ref[bit]] * (extent // 8), axis=0) != 0
        for bit in range(bits_ref.shape[0])
    ]
    for field in range(2):
        for level in range(share):
            parts = [final_ref[field, place * share + level] for place in range(len(blocks))]
            for bit, mask in enumerate(masks):
                parts = [
                    jnp.where(mask, parts[place ^ (1 << bit)], parts[place])
                    for place in range(len(blocks))
                ]
            for block, part in zip(blocks, parts):
                block[field, level] = part


def widen(weight, sides_ref, shot, mine_ref, came_refs, wide):
    _, share, extent, _ = mine_ref.shape
    sides = [
        jnp.concatenate([sides_ref[place]] * (extent // 8), axis=0) for place in range(4)
    ]
    for field in range(2):
        for level in range(share):
            scale = weight if field == 0 else 1.0
            low, high = both_sides(sides, [ref[field, level] for ref in came_refs])
            wide[shot, field, level, 0:extent, :] = scale * low
            wide[shot, field, level, extent : 2 * extent, :] = scale * mine_ref[field, level]
            wide[shot, field, level, 2 * extent : 3 * extent, :] = scale * high


def offset_product(wide, offset, level):
    extent = wide.shape[3] // 3
    lower = extent + REACH - offset
    upper = extent - REACH + offset
    total = None
    for shot in range(wide.shape[0]):
        product = (
            wide[shot, 0, level, lower : lower + extent, :]
            * wide[shot, 1, level, upper : upper + extent, :]
        )
        total = product if total is None else total + product
    return total


def stack(*refs):
    for place in range(len(refs) - 1):
        refs[-1][place] = refs[place][...]


def hold(mine_ref, _others_ref, held_ref):
    held_ref[...] = mine_ref[...]


def image_products(weight, sides_ref, others_ref, *rest):
    others_sides, rest = rest[ROUNDS - 1 :: -1], rest[ROUNDS:]
    mine_ref, rest = rest[0], rest[1:]
    mine_sides, rest = rest[ROUNDS - 1 :: -1], rest[ROUNDS:]
    partner_refs, rest = rest[: 1 + ROUNDS], rest[1 + ROUNDS :]
    final_ref, src_hbm, rec_hbm, image_hbm, wide, image_ref, field_sems, sems = rest
    copies = [
        pltpu.make_async_copy(final_ref.at[field], out.at[0], field_sems.at[field])
        for field, out in enumerate((src_hbm, rec_hbm))
    ]
    for copy in copies:
        copy.start()
    places = [
        (mine_ref.at[0], [ref.at[0] for ref in mine_sides]),
        (partner_refs[0], partner_refs[1:]),
    ]
    for place in range(others_ref.shape[0]):
        places.append((others_ref.at[place], [ref.at[place] for ref in others_sides]))
    for shot, (own_ref, came_refs) in enumerate(places):
        widen(weight, sides_ref, shot, own_ref, came_refs, wide)
    parts = sems.shape[0]
    for piece in range(parts):
        offsets = range(piece * OFFS // parts, (piece + 1) * OFFS // parts)
        for offset in offsets:
            for level in range(image_ref.shape[1]):
                image_ref[offset, level] = offset_product(wide, offset, level)
        rows = pl.ds(offsets[0], len(offsets))
        copy = pltpu.make_async_copy(image_ref.at[rows], image_hbm.at[rows], sems.at[piece])
        copy.start()
        copies.append(copy)
    for copy in copies:
        copy.wait()


def swap_tiles(value, lower):
    tiles, shots = lax.axis_size("tile"), lax.axis_size("shot")
    partner = {}
    for tile in lower:
        partner[tile], partner[tile + 1] = tile + 1, tile
    pairs = []
    for tile in range(tiles):
        for shot in range(shots):
            here = tile * shots + shot
            there = partner[tile] * shots + shot if tile in partner else here ^ 1
            pairs.append((here, there))
    return lax.ppermute(value, ("tile", "shot"), pairs)


def swap_rounds(values):
    tiles, rounds = lax.axis_size("tile"), len(values)
    return [
        swap_tiles(value, range((number - SHIFTS[rounds]) % rounds, tiles - 1, rounds))
        for number, value in enumerate(values)
    ]


def per_device(
    src_prev,
    src_now,
    rec_prev,
    rec_now,
    speed_table,
    region_ids,
    source_cell,
    wavelet,
    receiver_cell,
    receiver_data,
):
    _, levels, extent, across = src_now.shape
    tiles = lax.axis_size("tile")
    width = extent * tiles
    shots = lax.axis_size("shot")
    share = levels // shots
    params = pltpu.CompilerParams(vmem_limit_bytes=LIMIT)

    def struct(*shape):
        return jax.ShapeDtypeStruct(shape, jnp.float32)

    def scratch(*shape, dtype=jnp.float32):
        return pltpu.VMEM(shape, dtype)

    wide_shape = (2, levels, extent + 2 * LEAD, across)
    message = struct(2 * levels + levels // 2, 2 * HALO, across)
    fields_shape = (2, levels, extent, across)
    amps, own, prev, ids, speeds, planes, *sent = pl.pallas_call(
        own_edges,
        out_shape=(
            struct(*wavelet.shape),
            struct(*wide_shape),
            struct(*fields_shape),
            jax.ShapeDtypeStruct(region_ids.shape, jnp.int32),
            struct(8, across),
            struct(2 * extent, across),
            *([message] * ROUNDS),
        ),
        in_specs=[HBM] * 9,
        out_specs=[VMEM] * (6 + ROUNDS),
        scratch_shapes=[
            scratch(1, speed_table.shape[0]),
            scratch(*receiver_cell.shape, dtype=jnp.int32),
            scratch(*receiver_data.shape),
            scratch(2, levels, 8, across),
            pltpu.SemaphoreType.DMA((14,)),
        ],
        compiler_params=params,
        name="own_edges",
    )(
        *(
            pltpu.with_memory_space_constraint(array, pltpu.HBM)
            for array in (
                speed_table.reshape(1, -1),
                receiver_cell,
                receiver_data,
                wavelet,
                region_ids,
                src_now,
                rec_now,
                src_prev,
                rec_prev,
            )
        )
    )
    came_sides = swap_rounds(sent)
    coef, steps, outside, source, sides, bits = pl.pallas_call(
        functools.partial(own_steps, width),
        out_shape=(
            struct(levels, extent, across),
            struct(*fields_shape),
            struct(2, levels, 2 * HALO, across),
            struct(levels, extent + 2 * LEAD, across),
            jax.ShapeDtypeStruct((4, 8, across), jnp.int32),
            jax.ShapeDtypeStruct((shots.bit_length() - 1, 8, across), jnp.int32),
        ),
        in_specs=[SMEM] + [VMEM] * 6,
        out_specs=[VMEM] * 6,
        scratch_shapes=[scratch(*wide_shape)],
        compiler_params=params,
        name="own_steps",
    )(source_cell, amps, own, prev, ids, speeds, planes)
    block = struct(2, share, extent, across)
    final, mine, *blocks = pl.pallas_call(
        neighbours_part,
        out_shape=(struct(*fields_shape), struct(2, *block.shape), *([block] * (shots - 2))),
        in_specs=[VMEM] * (6 + ROUNDS),
        out_specs=[VMEM] * shots,
        scratch_shapes=[
            scratch(*wide_shape),
            scratch(*wide_shape),
            scratch(2, levels, 8, across),
        ],
        compiler_params=params,
        name="neighbours_part",
    )(sides, bits, steps, outside, source, coef, *came_sides)
    def swap_shots(value, number):
        return lax.ppermute(value, "shot", [(shot, shot ^ number) for shot in range(shots)])

    came = [swap_shots(sent, 2 + i) for i, sent in enumerate(blocks)]
    weight = 1.0 / shots
    image_shape = (OFFS, share, extent, across)

    others = pl.pallas_call(
        stack,
        out_shape=struct(len(came), *block.shape),
        in_specs=[VMEM] * len(came),
        out_specs=VMEM,
        compiler_params=params,
        name="stack",
    )(*came[::-1])
    mine_sides = swap_rounds([mine] * ROUNDS)
    others_sides = swap_rounds([others] * ROUNDS)
    held = pl.pallas_call(
        hold,
        out_shape=block,
        in_specs=[VMEM] * 2,
        out_specs=VMEM,
        compiler_params=params,
        name="hold",
    )(mine[1], others)
    partner = [swap_shots(value, 1) for value in (held, *(side[1] for side in mine_sides))]
    operands = [others, *others_sides[::-1], mine, *mine_sides[::-1], *partner]
    return pl.pallas_call(
        functools.partial(image_products, weight),
        out_shape=(
            struct(1, levels, extent, across),
            struct(1, levels, extent, across),
            struct(*image_shape),
        ),
        in_specs=[VMEM] * (2 + len(operands)),
        out_specs=[HBM] * 3,
        scratch_shapes=[
            scratch(shots, 2, share, 3 * extent, across),
            scratch(*image_shape),
            pltpu.SemaphoreType.DMA((2,)),
            pltpu.SemaphoreType.DMA((11,)),
        ],
        compiler_params=params,
        name="image_products",
    )(sides, *operands, final)


def solution(mesh):
    field = P(("groups", "shot"), None, "tile", None)
    return jax.shard_map(
        per_device,
        mesh=mesh,
        in_specs=(
            field,
            field,
            field,
            field,
            P("groups"),
            P(None, ("groups", "tile"), None),
            P(("groups", "shot")),
            P(("groups", "shot"), None),
            P(("groups", "shot"), "tile"),
            P(("groups", "shot"), None, "tile"),
        ),
        out_specs=(field, field, P(None, "shot", ("groups", "tile"), None)),
        check_vma=False,
    )
```

```python
import functools

import jax
import jax.numpy as jnp
from jax import lax
from jax.experimental import pallas as pl
from jax.experimental.pallas import tpu as pltpu
from jax.sharding import PartitionSpec as P

OFFS = 33
REACH = OFFS // 2
HALO = 4
LEAD = 8
ROUNDS = 3
SHIFTS = {2: 0, 3: 0}

COEFS = (-205.0 / 72.0, 8.0 / 5.0, -1.0 / 5.0, 8.0 / 315.0, -1.0 / 560.0)

VMEM = pl.BlockSpec(memory_space=pltpu.VMEM)
HBM = pl.BlockSpec(memory_space=pltpu.HBM)
SMEM = pl.BlockSpec(memory_space=pltpu.SMEM)
LIMIT = 16 * 1024 * 1024


def lane_weights(shape):
    lane = lax.broadcasted_iota(jnp.int32, shape, 1)
    across = shape[1]
    after = [jnp.where(lane < across - k, COEFS[k], 0.0) for k in range(1, HALO + 1)]
    before = [jnp.where(lane >= k, COEFS[k], 0.0) for k in range(1, HALO + 1)]
    return after, before


def lane_sum(centre, weights):
    after, before = weights
    across = centre.shape[1]
    total = 3.0 * COEFS[0] * centre
    for k in range(1, HALO + 1):
        total = total + after[k - 1] * pltpu.roll(centre, across - k, 1)
        total = total + before[k - 1] * pltpu.roll(centre, k, 1)
    return total


def beside_sum(wide, field, level, begin, count):
    total = None
    for k in range(1, HALO + 1):
        pair = (
            wide[field, level, begin + k : begin + k + count, :]
            + wide[field, level, begin - k : begin - k + count, :]
        )
        total = COEFS[k] * pair if total is None else total + COEFS[k] * pair
    return total


def depth_sum(rows_of, level, levels, total):
    for k in range(1, HALO + 1):
        for near in (level - k, level + k):
            if 0 <= near < levels:
                total = total + COEFS[k] * rows_of(near)
    return total


def laplace_level(wide, field, level, levels, extent, weights):
    def rows_of(near):
        return wide[field, near, LEAD : LEAD + extent, :]

    total = lane_sum(rows_of(level), weights) + beside_sum(wide, field, level, LEAD, extent)
    return depth_sum(rows_of, level, levels, total)


def is_low(across):
    return lax.broadcasted_iota(jnp.int32, (8, across), 0) < HALO


def own_edges(
    table_hbm,
    spots_hbm,
    traces_hbm,
    amps_hbm,
    ids_hbm,
    src_now,
    rec_now,
    src_prev,
    rec_prev,
    amps_ref,
    wide,
    prev_ref,
    ids_ref,
    speeds_ref,
    planes_ref,
    *rest,
):
    sent_refs, rest = rest[:ROUNDS], rest[ROUNDS:]
    table, spots_ref, traces_ref, edges, sems = rest
    levels, extent, across = ids_ref.shape
    regions = table_hbm.shape[1]
    end = LEAD + extent
    rows = pl.ds(LEAD, extent)
    moves = [(table_hbm, table), (spots_hbm, spots_ref), (traces_hbm, traces_ref)]
    for begin in range(0, levels, levels // 2):
        part = pl.ds(begin, levels // 2)
        moves += [
            (src_now.at[0, part], wide.at[0, part, rows, :]),
            (rec_now.at[0, part], wide.at[1, part, rows, :]),
            (ids_hbm.at[part], ids_ref.at[part]),
            (src_prev.at[0, part], prev_ref.at[0, part]),
            (rec_prev.at[0, part], prev_ref.at[1, part]),
        ]
    moves.append((amps_hbm, amps_ref))
    copies = [
        pltpu.make_async_copy(here, there, sems.at[i]) for i, (here, there) in enumerate(moves)
    ]
    for copy in copies:
        copy.start()
    zeros = jnp.zeros((LEAD, across), jnp.float32)
    for field in range(2):
        for level in range(levels):
            wide[field, level, 0:LEAD, :] = zeros
            wide[field, level, end : end + LEAD, :] = zeros
    weights = lane_weights((8, across))
    low_half = is_low(across)
    my_round = lax.rem(lax.axis_index("tile"), ROUNDS)
    for copy in copies:
        copy.wait()

    spots = spots_ref[...]
    column = lax.broadcasted_iota(jnp.int32, (extent, spots.shape[1]), 0) * across
    in_column = (spots >= column) & (spots < column + across)
    lane = lax.broadcasted_iota(jnp.int32, (across, spots.shape[1]), 0)
    in_row = jnp.where(lax.rem(spots, across) == lane, 1.0, 0.0)
    traces = jnp.concatenate(
        [jnp.where(in_column, traces_ref[0, t : t + 1, :], 0.0) for t in range(2)], axis=0
    )
    planes = lax.dot_general(
        traces,
        in_row,
        (((1,), (1,)), ((), ())),
        precision=lax.Precision.HIGHEST,
        preferred_element_type=jnp.float32,
    )
    planes_ref[...] = planes

    def send(place, low, high):
        for number, sent_ref in enumerate(sent_refs):
            sent_ref[place] = jnp.where(my_round == number, high, low)

    def halves(ref, *place):
        return jnp.where(
            low_half, ref[(*place, pl.ds(0, 8))], ref[(*place, pl.ds(extent - 8, 8))]
        )

    speeds = jnp.concatenate(
        [table[...], jnp.zeros((1, across - regions), jnp.float32)], axis=1
    )
    speeds = jnp.broadcast_to(speeds, (8, across))
    speeds_ref[...] = speeds
    coefs = [
        jnp.take_along_axis(speeds, halves(ids_ref, level), axis=1, mode="promise_in_bounds")
        for level in range(levels)
    ]
    for level in range(0, levels, 2):
        here, after = coefs[level], coefs[level + 1]
        send(
            2 * levels + level // 2,
            jnp.where(low_half, here, pltpu.roll(after, HALO, 0)),
            jnp.where(low_half, pltpu.roll(here, HALO, 0), after),
        )

    for field in range(2):
        for level in range(levels):
            edges[field, level] = jnp.where(
                low_half, wide[field, level, LEAD : LEAD + 8, :], wide[field, level, end - 8 : end, :]
            )
    for field in range(2):
        for level in range(levels):
            now = edges[field, level]
            total = lane_sum(now, weights) + jnp.where(
                low_half,
                beside_sum(wide, field, level, LEAD, 8),
                beside_sum(wide, field, level, end - 8, 8),
            )
            total = depth_sum(lambda near: edges[field, near], level, levels, total)
            value = 2.0 * now - halves(prev_ref, field, level) + coefs[level] * total
            if field == 1 and level == 0:
                value = value + jnp.where(low_half, planes[0:8, :], planes[extent - 8 : extent, :])
            send(
                field * levels + level,
                jnp.where(low_half, now, pltpu.roll(value, HALO, 0)),
                jnp.where(low_half, pltpu.roll(now, HALO, 0), value),
            )


def own_steps(
    width,
    cell_ref,
    amps_ref,
    own,
    prev_ref,
    ids_ref,
    speeds_ref,
    planes_ref,
    coef_ref,
    steps_ref,
    outside_ref,
    source_ref,
    sides_ref,
    bits_ref,
    middle,
):
    levels, extent, across = ids_ref.shape
    end = LEAD + extent
    cell = cell_ref[0]
    deep = lax.div(cell, width * across)
    row = lax.rem(lax.div(cell, across), width) - lax.axis_index("tile") * extent + LEAD
    shape = (extent + 2 * LEAD, across)
    rows = lax.broadcasted_iota(jnp.int32, shape, 0)
    lanes = lax.broadcasted_iota(jnp.int32, shape, 1)
    hit = jnp.where((rows == row) & (lanes == lax.rem(cell, across)), 1.0, 0.0)
    weights = lane_weights((extent, across))
    speeds = speeds_ref[...]
    zeros = jnp.zeros((LEAD, across), jnp.float32)
    for level in range(levels):
        here = hit * jnp.where(deep == level, 1.0, 0.0)
        source_ref[level] = here * amps_ref[0:1, 0:1]
        steps_ref[0, level] = here[LEAD:end, :] * amps_ref[0:1, 1:2] - own[0, level, LEAD:end, :]
        steps_ref[1, level] = -own[1, level, LEAD:end, :]
        for begin in range(0, extent, 8):
            coef_ref[level, begin : begin + 8, :] = jnp.take_along_axis(
                speeds, ids_ref[level, begin : begin + 8, :], axis=1, mode="promise_in_bounds"
            )
    steps_ref[1, 0] += planes_ref[extent:, :]
    for field in range(2):
        for level in range(levels):
            total = laplace_level(own, field, level, levels, extent, weights)
            value = 2.0 * own[field, level, LEAD:end, :] - prev_ref[field, level]
            value = value + coef_ref[level] * total
            if field == 0:
                value = value + source_ref[level, LEAD:end, :]
            elif level == 0:
                value = value + planes_ref[:extent, :]
            middle[field, level, 0:LEAD, :] = zeros
            middle[field, level, LEAD:end, :] = value
            middle[field, level, end : end + LEAD, :] = zeros
            below = above = jnp.zeros((HALO, across), jnp.float32)
            for k in range(1, HALO + 1):
                begin = LEAD - HALO + k
                below = below + COEFS[k] * own[field, level, begin : begin + HALO, :]
                above = above + COEFS[k] * own[field, level, end - k : end - k + HALO, :]
            outside_ref[field, level, 0:HALO, :] = below
            outside_ref[field, level, HALO : 2 * HALO, :] = above
    for field in range(2):
        for level in range(levels):
            total = laplace_level(middle, field, level, levels, extent, weights)
            steps_ref[field, level] += (
                2.0 * middle[field, level, LEAD:end, :] + coef_ref[level] * total
            )
    tile, tiles = lax.axis_index("tile"), lax.axis_size("tile")
    places = (jnp.where(tile > 0, 1, 0), jnp.where(tile < tiles - 1, 1, 0))
    places += tuple((tile + SHIFTS[rounds]) % rounds for rounds in (2, 3))
    for place, value in enumerate(places):
        sides_ref[place] = jnp.full(sides_ref.shape[1:], value, dtype=jnp.int32)
    shot = jnp.full(bits_ref.shape[1:], lax.axis_index("shot"), dtype=jnp.int32)
    for bit in range(bits_ref.shape[0]):
        bits_ref[bit] = shot & (1 << bit)


def both_sides(sides, came):
    has_low, has_high, my_round = sides[0], sides[1], sides[len(came)]
    low, high = came[-1], came[0]
    for number in range(1, len(came)):
        low = jnp.where(my_round == number, came[number - 1], low)
        high = jnp.where(my_round == number, came[number], high)
    return jnp.where(has_low != 0, low, 0.0), jnp.where(has_high != 0, high, 0.0)


def neighbours_part(
    sides_ref, bits_ref, steps_ref, outside_ref, source_ref, coef_ref, *rest
):
    came_refs, (final_ref, mine_ref, *blocks, other, change, edges) = rest[:ROUNDS], rest[ROUNDS:]
    blocks = [mine_ref.at[0], mine_ref.at[1], *blocks]
    levels, extent, across = coef_ref.shape
    share = mine_ref.shape[2]
    end = LEAD + extent
    low_half = is_low(across)
    weights = lane_weights((8, across))
    sides = [sides_ref[place] for place in range(4)]
    zeros = jnp.zeros((8, across), jnp.float32)

    def received(place):
        return both_sides(sides, [ref[place] for ref in came_refs])

    coefs = [received(2 * levels + pair) for pair in range(levels // 2)]
    for field in range(2):
        for level in range(levels):
            low, high = received(field * levels + level)
            other[field, level, LEAD : LEAD + 8, :] = zeros
            other[field, level, end - 8 : end, :] = zeros
            other[field, level, LEAD - HALO : LEAD, :] = low[0:HALO, :]
            other[field, level, end : end + HALO, :] = high[0:HALO, :]
            half = slice(level % 2 * HALO, level % 2 * HALO + HALO)
            low_coef, high_coef = (coef[half, :] for coef in coefs[level // 2])
            low = low[HALO:, :] + low_coef * outside_ref[field, level, 0:HALO, :]
            high = high[HALO:, :] + high_coef * outside_ref[field, level, HALO : 2 * HALO, :]
            if field == 0:
                low = low + source_ref[level, LEAD - HALO : LEAD, :]
                high = high + source_ref[level, end : end + HALO, :]
            change[field, level, LEAD - HALO : LEAD, :] = low
            change[field, level, end : end + HALO, :] = high
    for field in range(2):
        for level in range(levels):
            left = right = zeros
            for k in range(1, HALO + 1):
                left = left + COEFS[k] * other[field, level, LEAD - k : LEAD - k + 8, :]
                right = right + COEFS[k] * other[field, level, end - 8 + k : end + k, :]
            left = coef_ref[level, 0:8, :] * left
            right = coef_ref[level, extent - 8 : extent, :] * right
            change[field, level, LEAD : LEAD + 8, :] = left
            change[field, level, end - 8 : end, :] = right
            edges[field, level] = left + right
    for field in range(2):
        for level in range(levels):
            total = depth_sum(
                lambda near: edges[field, near],
                level,
                levels,
                lane_sum(edges[field, level], weights),
            )
            for begin, mine in ((0, low_half), (extent - 8, ~low_half)):
                part = beside_sum(change, field, level, LEAD + begin, 8)
                part = part + jnp.where(mine, total, 0.0)
                final_ref[field, level, begin : begin + 8, :] = (
                    steps_ref[field, level, begin : begin + 8, :]
                    + 2.0 * change[field, level, LEAD + begin : LEAD + begin + 8, :]
                    + coef_ref[level, begin : begin + 8, :] * part
                )
    masks = [
        jnp.concatenate([bits_ref[bit]] * (extent // 8), axis=0) != 0
        for bit in range(bits_ref.shape[0])
    ]
    for field in range(2):
        for level in range(share):
            parts = [final_ref[field, place * share + level] for place in range(len(blocks))]
            for bit, mask in enumerate(masks):
                parts = [
                    jnp.where(mask, parts[place ^ (1 << bit)], parts[place])
                    for place in range(len(blocks))
                ]
            for block, part in zip(blocks, parts):
                block[field, level] = part


def widen(weight, sides_ref, shot, mine_ref, came_refs, wide):
    _, share, extent, _ = mine_ref.shape
    sides = [
        jnp.concatenate([sides_ref[place]] * (extent // 8), axis=0) for place in range(4)
    ]
    for field in range(2):
        for level in range(share):
            scale = weight if field == 0 else 1.0
            low, high = both_sides(sides, [ref[field, level] for ref in came_refs])
            wide[shot, field, level, 0:extent, :] = scale * low
            wide[shot, field, level, extent : 2 * extent, :] = scale * mine_ref[field, level]
            wide[shot, field, level, 2 * extent : 3 * extent, :] = scale * high


def offset_product(wide, offset, level):
    extent = wide.shape[3] // 3
    lower = extent + REACH - offset
    upper = extent - REACH + offset
    total = None
    for shot in range(wide.shape[0]):
        product = (
            wide[shot, 0, level, lower : lower + extent, :]
            * wide[shot, 1, level, upper : upper + extent, :]
        )
        total = product if total is None else total + product
    return total


def stack(*refs):
    for place in range(len(refs) - 1):
        refs[-1][place] = refs[place][...]


def hold(mine_ref, _others_ref, held_ref):
    held_ref[...] = mine_ref[...]


def image_products(weight, sides_ref, others_ref, *rest):
    others_sides, rest = rest[ROUNDS - 1 :: -1], rest[ROUNDS:]
    mine_ref, rest = rest[0], rest[1:]
    mine_sides, rest = rest[ROUNDS - 1 :: -1], rest[ROUNDS:]
    (own_first_ref, second_third_ref), rest = rest[:2], rest[2:]
    partner_refs = [ref.at[place] for ref in (own_first_ref, second_third_ref) for place in range(2)]
    final_ref, src_hbm, rec_hbm, image_hbm, wide, image_ref, field_sems, sems = rest
    copies = [
        pltpu.make_async_copy(final_ref.at[field], out.at[0], field_sems.at[field])
        for field, out in enumerate((src_hbm, rec_hbm))
    ]
    for copy in copies:
        copy.start()
    places = [
        (mine_ref.at[0], [ref.at[0] for ref in mine_sides]),
        (partner_refs[0], partner_refs[1:]),
    ]
    for place in range(others_ref.shape[0]):
        places.append((others_ref.at[place], [ref.at[place] for ref in others_sides]))
    for shot, (own_ref, came_refs) in enumerate(places):
        widen(weight, sides_ref, shot, own_ref, came_refs, wide)
    parts = sems.shape[0]
    for piece in range(parts):
        offsets = range(piece * OFFS // parts, (piece + 1) * OFFS // parts)
        for offset in offsets:
            for level in range(image_ref.shape[1]):
                image_ref[offset, level] = offset_product(wide, offset, level)
        rows = pl.ds(offsets[0], len(offsets))
        copy = pltpu.make_async_copy(image_ref.at[rows], image_hbm.at[rows], sems.at[piece])
        copy.start()
        copies.append(copy)
    for copy in copies:
        copy.wait()


def swap_tiles(value, lower):
    tiles, shots = lax.axis_size("tile"), lax.axis_size("shot")
    partner = {}
    for tile in lower:
        partner[tile], partner[tile + 1] = tile + 1, tile
    pairs = []
    for tile in range(tiles):
        for shot in range(shots):
            here = tile * shots + shot
            there = partner[tile] * shots + shot if tile in partner else here ^ 1
            pairs.append((here, there))
    return lax.ppermute(value, ("tile", "shot"), pairs)


def swap_rounds(values):
    tiles, rounds = lax.axis_size("tile"), len(values)
    return [
        swap_tiles(value, range((number - SHIFTS[rounds]) % rounds, tiles - 1, rounds))
        for number, value in enumerate(values)
    ]


def per_device(
    src_prev,
    src_now,
    rec_prev,
    rec_now,
    speed_table,
    region_ids,
    source_cell,
    wavelet,
    receiver_cell,
    receiver_data,
):
    _, levels, extent, across = src_now.shape
    tiles = lax.axis_size("tile")
    width = extent * tiles
    shots = lax.axis_size("shot")
    share = levels // shots
    params = pltpu.CompilerParams(vmem_limit_bytes=LIMIT)

    def struct(*shape):
        return jax.ShapeDtypeStruct(shape, jnp.float32)

    def scratch(*shape, dtype=jnp.float32):
        return pltpu.VMEM(shape, dtype)

    wide_shape = (2, levels, extent + 2 * LEAD, across)
    message = struct(2 * levels + levels // 2, 2 * HALO, across)
    fields_shape = (2, levels, extent, across)
    amps, own, prev, ids, speeds, planes, *sent = pl.pallas_call(
        own_edges,
        out_shape=(
            struct(*wavelet.shape),
            struct(*wide_shape),
            struct(*fields_shape),
            jax.ShapeDtypeStruct(region_ids.shape, jnp.int32),
            struct(8, across),
            struct(2 * extent, across),
            *([message] * ROUNDS),
        ),
        in_specs=[HBM] * 9,
        out_specs=[VMEM] * (6 + ROUNDS),
        scratch_shapes=[
            scratch(1, speed_table.shape[0]),
            scratch(*receiver_cell.shape, dtype=jnp.int32),
            scratch(*receiver_data.shape),
            scratch(2, levels, 8, across),
            pltpu.SemaphoreType.DMA((14,)),
        ],
        compiler_params=params,
        name="own_edges",
    )(
        *(
            pltpu.with_memory_space_constraint(array, pltpu.HBM)
            for array in (
                speed_table.reshape(1, -1),
                receiver_cell,
                receiver_data,
                wavelet,
                region_ids,
                src_now,
                rec_now,
                src_prev,
                rec_prev,
            )
        )
    )
    came_sides = swap_rounds(sent)
    coef, steps, outside, source, sides, bits = pl.pallas_call(
        functools.partial(own_steps, width),
        out_shape=(
            struct(levels, extent, across),
            struct(*fields_shape),
            struct(2, levels, 2 * HALO, across),
            struct(levels, extent + 2 * LEAD, across),
            jax.ShapeDtypeStruct((4, 8, across), jnp.int32),
            jax.ShapeDtypeStruct((shots.bit_length() - 1, 8, across), jnp.int32),
        ),
        in_specs=[SMEM] + [VMEM] * 6,
        out_specs=[VMEM] * 6,
        scratch_shapes=[scratch(*wide_shape)],
        compiler_params=params,
        name="own_steps",
    )(source_cell, amps, own, prev, ids, speeds, planes)
    block = struct(2, share, extent, across)
    final, mine, *blocks = pl.pallas_call(
        neighbours_part,
        out_shape=(struct(*fields_shape), struct(2, *block.shape), *([block] * (shots - 2))),
        in_specs=[VMEM] * (6 + ROUNDS),
        out_specs=[VMEM] * shots,
        scratch_shapes=[
            scratch(*wide_shape),
            scratch(*wide_shape),
            scratch(2, levels, 8, across),
        ],
        compiler_params=params,
        name="neighbours_part",
    )(sides, bits, steps, outside, source, coef, *came_sides)
    def swap_shots(value, number):
        return lax.ppermute(value, "shot", [(shot, shot ^ number) for shot in range(shots)])

    came = [swap_shots(sent, 2 + i) for i, sent in enumerate(blocks)]
    weight = 1.0 / shots
    image_shape = (OFFS, share, extent, across)

    def stacked(blocks):
        return pl.pallas_call(
            stack,
            out_shape=struct(len(blocks), *block.shape),
            in_specs=[VMEM] * len(blocks),
            out_specs=VMEM,
            compiler_params=params,
            name="stack",
        )(*blocks)

    others = stacked(came[::-1])
    mine_sides = swap_rounds([mine] * ROUNDS)
    others_sides = swap_rounds([others] * ROUNDS)
    held = pl.pallas_call(
        hold,
        out_shape=block,
        in_specs=[VMEM] * 2,
        out_specs=VMEM,
        compiler_params=params,
        name="hold",
    )(mine[1], others)
    pieces = [held, *(side[1] for side in mine_sides)]
    partner = [
        swap_shots(stacked(pieces[begin : begin + 2]), 1) for begin in range(0, len(pieces), 2)
    ]
    operands = [others, *others_sides[::-1], mine, *mine_sides[::-1], *partner]
    return pl.pallas_call(
        functools.partial(image_products, weight),
        out_shape=(
            struct(1, levels, extent, across),
            struct(1, levels, extent, across),
            struct(*image_shape),
        ),
        in_specs=[VMEM] * (2 + len(operands)),
        out_specs=[HBM] * 3,
        scratch_shapes=[
            scratch(shots, 2, share, 3 * extent, across),
            scratch(*image_shape),
            pltpu.SemaphoreType.DMA((2,)),
            pltpu.SemaphoreType.DMA((11,)),
        ],
        compiler_params=params,
        name="image_products",
    )(sides, *operands, final)


def solution(mesh):
    field = P(("groups", "shot"), None, "tile", None)
    return jax.shard_map(
        per_device,
        mesh=mesh,
        in_specs=(
            field,
            field,
            field,
            field,
            P("groups"),
            P(None, ("groups", "tile"), None),
            P(("groups", "shot")),
            P(("groups", "shot"), None),
            P(("groups", "shot"), "tile"),
            P(("groups", "shot"), None, "tile"),
        ),
        out_specs=(field, field, P(None, "shot", ("groups", "tile"), None)),
        check_vma=False,
    )
```

```python
import functools

import jax
import jax.numpy as jnp
from jax import lax
from jax.experimental import pallas as pl
from jax.experimental.pallas import tpu as pltpu
from jax.sharding import PartitionSpec as P

OFFS = 33
REACH = OFFS // 2
HALO = 4
LEAD = 8
ROUNDS = 3
SHIFTS = {2: 0, 3: 0}

COEFS = (-205.0 / 72.0, 8.0 / 5.0, -1.0 / 5.0, 8.0 / 315.0, -1.0 / 560.0)

VMEM = pl.BlockSpec(memory_space=pltpu.VMEM)
HBM = pl.BlockSpec(memory_space=pltpu.HBM)
SMEM = pl.BlockSpec(memory_space=pltpu.SMEM)
LIMIT = 16 * 1024 * 1024


def lane_weights(shape):
    lane = lax.broadcasted_iota(jnp.int32, shape, 1)
    across = shape[1]
    after = [jnp.where(lane < across - k, COEFS[k], 0.0) for k in range(1, HALO + 1)]
    before = [jnp.where(lane >= k, COEFS[k], 0.0) for k in range(1, HALO + 1)]
    return after, before


def lane_sum(centre, weights):
    after, before = weights
    across = centre.shape[1]
    total = 3.0 * COEFS[0] * centre
    for k in range(1, HALO + 1):
        total = total + after[k - 1] * pltpu.roll(centre, across - k, 1)
        total = total + before[k - 1] * pltpu.roll(centre, k, 1)
    return total


def beside_sum(wide, field, level, begin, count):
    total = None
    for k in range(1, HALO + 1):
        pair = (
            wide[field, level, begin + k : begin + k + count, :]
            + wide[field, level, begin - k : begin - k + count, :]
        )
        total = COEFS[k] * pair if total is None else total + COEFS[k] * pair
    return total


def depth_sum(rows_of, level, levels, total):
    for k in range(1, HALO + 1):
        for near in (level - k, level + k):
            if 0 <= near < levels:
                total = total + COEFS[k] * rows_of(near)
    return total


def laplace_level(wide, field, level, levels, extent, weights):
    def rows_of(near):
        return wide[field, near, LEAD : LEAD + extent, :]

    total = lane_sum(rows_of(level), weights) + beside_sum(wide, field, level, LEAD, extent)
    return depth_sum(rows_of, level, levels, total)


def is_low(across):
    return lax.broadcasted_iota(jnp.int32, (8, across), 0) < HALO


def own_edges(
    table_hbm,
    spots_hbm,
    traces_hbm,
    amps_hbm,
    ids_hbm,
    src_now,
    rec_now,
    src_prev,
    rec_prev,
    amps_ref,
    wide,
    prev_ref,
    ids_ref,
    speeds_ref,
    planes_ref,
    *rest,
):
    sent_refs, rest = rest[:ROUNDS], rest[ROUNDS:]
    table, spots_ref, traces_ref, edges, sems = rest
    levels, extent, across = ids_ref.shape
    regions = table_hbm.shape[1]
    end = LEAD + extent
    rows = pl.ds(LEAD, extent)
    moves = [(table_hbm, table), (spots_hbm, spots_ref), (traces_hbm, traces_ref)]
    for begin in range(0, levels, levels // 2):
        part = pl.ds(begin, levels // 2)
        moves += [
            (src_now.at[0, part], wide.at[0, part, rows, :]),
            (rec_now.at[0, part], wide.at[1, part, rows, :]),
            (ids_hbm.at[part], ids_ref.at[part]),
            (src_prev.at[0, part], prev_ref.at[0, part]),
            (rec_prev.at[0, part], prev_ref.at[1, part]),
        ]
    moves.append((amps_hbm, amps_ref))
    copies = [
        pltpu.make_async_copy(here, there, sems.at[i]) for i, (here, there) in enumerate(moves)
    ]
    for copy in copies:
        copy.start()
    zeros = jnp.zeros((LEAD, across), jnp.float32)
    for field in range(2):
        for level in range(levels):
            wide[field, level, 0:LEAD, :] = zeros
            wide[field, level, end : end + LEAD, :] = zeros
    weights = lane_weights((8, across))
    low_half = is_low(across)
    my_round = lax.rem(lax.axis_index("tile"), ROUNDS)
    for copy in copies:
        copy.wait()

    spots = spots_ref[...]
    column = lax.broadcasted_iota(jnp.int32, (extent, spots.shape[1]), 0) * across
    in_column = (spots >= column) & (spots < column + across)
    lane = lax.broadcasted_iota(jnp.int32, (across, spots.shape[1]), 0)
    in_row = jnp.where(lax.rem(spots, across) == lane, 1.0, 0.0)
    traces = jnp.concatenate(
        [jnp.where(in_column, traces_ref[0, t : t + 1, :], 0.0) for t in range(2)], axis=0
    )
    planes = lax.dot_general(
        traces,
        in_row,
        (((1,), (1,)), ((), ())),
        precision=lax.Precision.HIGHEST,
        preferred_element_type=jnp.float32,
    )
    planes_ref[...] = planes

    def send(place, low, high):
        for number, sent_ref in enumerate(sent_refs):
            sent_ref[place] = jnp.where(my_round == number, high, low)

    def halves(ref, *place):
        return jnp.where(
            low_half, ref[(*place, pl.ds(0, 8))], ref[(*place, pl.ds(extent - 8, 8))]
        )

    speeds = jnp.concatenate(
        [table[...], jnp.zeros((1, across - regions), jnp.float32)], axis=1
    )
    speeds = jnp.broadcast_to(speeds, (8, across))
    speeds_ref[...] = speeds
    coefs = [
        jnp.take_along_axis(speeds, halves(ids_ref, level), axis=1, mode="promise_in_bounds")
        for level in range(levels)
    ]
    for level in range(0, levels, 2):
        here, after = coefs[level], coefs[level + 1]
        send(
            2 * levels + level // 2,
            jnp.where(low_half, here, pltpu.roll(after, HALO, 0)),
            jnp.where(low_half, pltpu.roll(here, HALO, 0), after),
        )

    for field in range(2):
        for level in range(levels):
            edges[field, level] = jnp.where(
                low_half, wide[field, level, LEAD : LEAD + 8, :], wide[field, level, end - 8 : end, :]
            )
    for field in range(2):
        for level in range(levels):
            now = edges[field, level]
            total = lane_sum(now, weights) + jnp.where(
                low_half,
                beside_sum(wide, field, level, LEAD, 8),
                beside_sum(wide, field, level, end - 8, 8),
            )
            total = depth_sum(lambda near: edges[field, near], level, levels, total)
            value = 2.0 * now - halves(prev_ref, field, level) + coefs[level] * total
            if field == 1 and level == 0:
                value = value + jnp.where(low_half, planes[0:8, :], planes[extent - 8 : extent, :])
            send(
                field * levels + level,
                jnp.where(low_half, now, pltpu.roll(value, HALO, 0)),
                jnp.where(low_half, pltpu.roll(now, HALO, 0), value),
            )


def own_steps(
    width,
    cell_ref,
    amps_ref,
    own,
    prev_ref,
    ids_ref,
    speeds_ref,
    planes_ref,
    coef_ref,
    steps_ref,
    outside_ref,
    source_ref,
    sides_ref,
    bits_ref,
    middle,
):
    levels, extent, across = ids_ref.shape
    end = LEAD + extent
    cell = cell_ref[0]
    deep = lax.div(cell, width * across)
    row = lax.rem(lax.div(cell, across), width) - lax.axis_index("tile") * extent + LEAD
    shape = (extent + 2 * LEAD, across)
    rows = lax.broadcasted_iota(jnp.int32, shape, 0)
    lanes = lax.broadcasted_iota(jnp.int32, shape, 1)
    hit = jnp.where((rows == row) & (lanes == lax.rem(cell, across)), 1.0, 0.0)
    weights = lane_weights((extent, across))
    speeds = speeds_ref[...]
    zeros = jnp.zeros((LEAD, across), jnp.float32)
    for level in range(levels):
        here = hit * jnp.where(deep == level, 1.0, 0.0)
        source_ref[level] = here * amps_ref[0:1, 0:1]
        steps_ref[0, level] = here[LEAD:end, :] * amps_ref[0:1, 1:2] - own[0, level, LEAD:end, :]
        steps_ref[1, level] = -own[1, level, LEAD:end, :]
        for begin in range(0, extent, 8):
            coef_ref[level, begin : begin + 8, :] = jnp.take_along_axis(
                speeds, ids_ref[level, begin : begin + 8, :], axis=1, mode="promise_in_bounds"
            )
    steps_ref[1, 0] += planes_ref[extent:, :]
    for field in range(2):
        for level in range(levels):
            total = laplace_level(own, field, level, levels, extent, weights)
            value = 2.0 * own[field, level, LEAD:end, :] - prev_ref[field, level]
            value = value + coef_ref[level] * total
            if field == 0:
                value = value + source_ref[level, LEAD:end, :]
            elif level == 0:
                value = value + planes_ref[:extent, :]
            middle[field, level, 0:LEAD, :] = zeros
            middle[field, level, LEAD:end, :] = value
            middle[field, level, end : end + LEAD, :] = zeros
            below = above = jnp.zeros((HALO, across), jnp.float32)
            for k in range(1, HALO + 1):
                begin = LEAD - HALO + k
                below = below + COEFS[k] * own[field, level, begin : begin + HALO, :]
                above = above + COEFS[k] * own[field, level, end - k : end - k + HALO, :]
            outside_ref[field, level, 0:HALO, :] = below
            outside_ref[field, level, HALO : 2 * HALO, :] = above
    for field in range(2):
        for level in range(levels):
            total = laplace_level(middle, field, level, levels, extent, weights)
            steps_ref[field, level] += (
                2.0 * middle[field, level, LEAD:end, :] + coef_ref[level] * total
            )
    tile, tiles = lax.axis_index("tile"), lax.axis_size("tile")
    places = (jnp.where(tile > 0, 1, 0), jnp.where(tile < tiles - 1, 1, 0))
    places += tuple((tile + SHIFTS[rounds]) % rounds for rounds in (2, 3))
    for place, value in enumerate(places):
        sides_ref[place] = jnp.full(sides_ref.shape[1:], value, dtype=jnp.int32)
    shot = jnp.full(bits_ref.shape[1:], lax.axis_index("shot"), dtype=jnp.int32)
    for bit in range(bits_ref.shape[0]):
        bits_ref[bit] = shot & (1 << bit)


def both_sides(sides, came):
    has_low, has_high, my_round = sides[0], sides[1], sides[len(came)]
    low, high = came[-1], came[0]
    for number in range(1, len(came)):
        low = jnp.where(my_round == number, came[number - 1], low)
        high = jnp.where(my_round == number, came[number], high)
    return jnp.where(has_low != 0, low, 0.0), jnp.where(has_high != 0, high, 0.0)


def neighbours_part(
    sides_ref, bits_ref, steps_ref, outside_ref, source_ref, coef_ref, *rest
):
    came_refs, (final_ref, mine_ref, *blocks, other, change, edges) = rest[:ROUNDS], rest[ROUNDS:]
    blocks = [mine_ref.at[0], mine_ref.at[1], *blocks]
    levels, extent, across = coef_ref.shape
    share = mine_ref.shape[2]
    end = LEAD + extent
    low_half = is_low(across)
    weights = lane_weights((8, across))
    sides = [sides_ref[place] for place in range(4)]
    zeros = jnp.zeros((8, across), jnp.float32)

    def received(place):
        return both_sides(sides, [ref[place] for ref in came_refs])

    coefs = [received(2 * levels + pair) for pair in range(levels // 2)]
    for field in range(2):
        for level in range(levels):
            low, high = received(field * levels + level)
            other[field, level, LEAD : LEAD + 8, :] = zeros
            other[field, level, end - 8 : end, :] = zeros
            other[field, level, LEAD - HALO : LEAD, :] = low[0:HALO, :]
            other[field, level, end : end + HALO, :] = high[0:HALO, :]
            half = slice(level % 2 * HALO, level % 2 * HALO + HALO)
            low_coef, high_coef = (coef[half, :] for coef in coefs[level // 2])
            low = low[HALO:, :] + low_coef * outside_ref[field, level, 0:HALO, :]
            high = high[HALO:, :] + high_coef * outside_ref[field, level, HALO : 2 * HALO, :]
            if field == 0:
                low = low + source_ref[level, LEAD - HALO : LEAD, :]
                high = high + source_ref[level, end : end + HALO, :]
            change[field, level, LEAD - HALO : LEAD, :] = low
            change[field, level, end : end + HALO, :] = high
    for field in range(2):
        for level in range(levels):
            left = right = zeros
            for k in range(1, HALO + 1):
                left = left + COEFS[k] * other[field, level, LEAD - k : LEAD - k + 8, :]
                right = right + COEFS[k] * other[field, level, end - 8 + k : end + k, :]
            left = coef_ref[level, 0:8, :] * left
            right = coef_ref[level, extent - 8 : extent, :] * right
            change[field, level, LEAD : LEAD + 8, :] = left
            change[field, level, end - 8 : end, :] = right
            edges[field, level] = left + right
    for field in range(2):
        for level in range(levels):
            total = depth_sum(
                lambda near: edges[field, near],
                level,
                levels,
                lane_sum(edges[field, level], weights),
            )
            for begin, mine in ((0, low_half), (extent - 8, ~low_half)):
                part = beside_sum(change, field, level, LEAD + begin, 8)
                part = part + jnp.where(mine, total, 0.0)
                final_ref[field, level, begin : begin + 8, :] = (
                    steps_ref[field, level, begin : begin + 8, :]
                    + 2.0 * change[field, level, LEAD + begin : LEAD + begin + 8, :]
                    + coef_ref[level, begin : begin + 8, :] * part
                )
    masks = [
        jnp.concatenate([bits_ref[bit]] * (extent // 8), axis=0) != 0
        for bit in range(bits_ref.shape[0])
    ]
    for field in range(2):
        for level in range(share):
            parts = [final_ref[field, place * share + level] for place in range(len(blocks))]
            for bit, mask in enumerate(masks):
                parts = [
                    jnp.where(mask, parts[place ^ (1 << bit)], parts[place])
                    for place in range(len(blocks))
                ]
            for block, part in zip(blocks, parts):
                block[field, level] = part


def widen(weight, sides_ref, shot, mine_ref, came_refs, wide):
    _, share, extent, _ = mine_ref.shape
    sides = [
        jnp.concatenate([sides_ref[place]] * (extent // 8), axis=0) for place in range(4)
    ]
    for field in range(2):
        for level in range(share):
            scale = weight if field == 0 else 1.0
            low, high = both_sides(sides, [ref[field, level] for ref in came_refs])
            wide[shot, field, level, 0:extent, :] = scale * low
            wide[shot, field, level, extent : 2 * extent, :] = scale * mine_ref[field, level]
            wide[shot, field, level, 2 * extent : 3 * extent, :] = scale * high


def offset_product(wide, offset, level, total):
    extent = wide.shape[3] // 3
    lower = extent + REACH - offset
    upper = extent - REACH + offset
    for shot in range(wide.shape[0]):
        product = (
            wide[shot, 0, level, lower : lower + extent, :]
            * wide[shot, 1, level, upper : upper + extent, :]
        )
        total = product if total is None else total + product
    return total


def stack(*refs):
    for place in range(len(refs) - 1):
        refs[-1][place] = refs[place][...]


def hold(mine_ref, _others_ref, held_ref):
    held_ref[...] = mine_ref[...]


def early_products(weight, sides_ref, mine_ref, third_ref, second_ref, first_ref, final_ref, *rest):
    src_hbm, rec_hbm, image_ref, wide, sems = rest
    copies = [
        pltpu.make_async_copy(final_ref.at[field], out.at[0], sems.at[field])
        for field, out in enumerate((src_hbm, rec_hbm))
    ]
    for copy in copies:
        copy.start()
    came_refs = [ref.at[0] for ref in (first_ref, second_ref, third_ref)]
    widen(weight, sides_ref, 0, mine_ref.at[0], came_refs, wide)
    for offset in range(OFFS):
        for level in range(wide.shape[2]):
            image_ref[offset, level] = offset_product(wide, offset, level, None)
    for copy in copies:
        copy.wait()


def image_products(weight, sides_ref, others_ref, *rest):
    others_sides, rest = rest[ROUNDS - 1 :: -1], rest[ROUNDS:]
    (own_first_ref, second_third_ref, early_ref), rest = rest[:3], rest[3:]
    partner_refs = [ref.at[place] for ref in (own_first_ref, second_third_ref) for place in range(2)]
    image_hbm, wide, image_ref, sems = rest
    copies = []
    places = [(partner_refs[0], partner_refs[1:])]
    for place in range(others_ref.shape[0]):
        places.append((others_ref.at[place], [ref.at[place] for ref in others_sides]))
    for shot, (own_ref, came_refs) in enumerate(places):
        widen(weight, sides_ref, shot, own_ref, came_refs, wide)
    parts = sems.shape[0]
    for piece in range(parts):
        offsets = range(piece * OFFS // parts, (piece + 1) * OFFS // parts)
        for offset in offsets:
            for level in range(image_ref.shape[1]):
                image_ref[offset, level] = offset_product(
                    wide, offset, level, early_ref[offset, level]
                )
        rows = pl.ds(offsets[0], len(offsets))
        copy = pltpu.make_async_copy(image_ref.at[rows], image_hbm.at[rows], sems.at[piece])
        copy.start()
        copies.append(copy)
    for copy in copies:
        copy.wait()


def swap_tiles(value, lower):
    tiles, shots = lax.axis_size("tile"), lax.axis_size("shot")
    partner = {}
    for tile in lower:
        partner[tile], partner[tile + 1] = tile + 1, tile
    pairs = []
    for tile in range(tiles):
        for shot in range(shots):
            here = tile * shots + shot
            there = partner[tile] * shots + shot if tile in partner else here ^ 1
            pairs.append((here, there))
    return lax.ppermute(value, ("tile", "shot"), pairs)


def swap_rounds(values):
    tiles, rounds = lax.axis_size("tile"), len(values)
    return [
        swap_tiles(value, range((number - SHIFTS[rounds]) % rounds, tiles - 1, rounds))
        for number, value in enumerate(values)
    ]


def per_device(
    src_prev,
    src_now,
    rec_prev,
    rec_now,
    speed_table,
    region_ids,
    source_cell,
    wavelet,
    receiver_cell,
    receiver_data,
):
    _, levels, extent, across = src_now.shape
    tiles = lax.axis_size("tile")
    width = extent * tiles
    shots = lax.axis_size("shot")
    share = levels // shots
    params = pltpu.CompilerParams(vmem_limit_bytes=LIMIT)

    def struct(*shape):
        return jax.ShapeDtypeStruct(shape, jnp.float32)

    def scratch(*shape, dtype=jnp.float32):
        return pltpu.VMEM(shape, dtype)

    wide_shape = (2, levels, extent + 2 * LEAD, across)
    message = struct(2 * levels + levels // 2, 2 * HALO, across)
    fields_shape = (2, levels, extent, across)
    amps, own, prev, ids, speeds, planes, *sent = pl.pallas_call(
        own_edges,
        out_shape=(
            struct(*wavelet.shape),
            struct(*wide_shape),
            struct(*fields_shape),
            jax.ShapeDtypeStruct(region_ids.shape, jnp.int32),
            struct(8, across),
            struct(2 * extent, across),
            *([message] * ROUNDS),
        ),
        in_specs=[HBM] * 9,
        out_specs=[VMEM] * (6 + ROUNDS),
        scratch_shapes=[
            scratch(1, speed_table.shape[0]),
            scratch(*receiver_cell.shape, dtype=jnp.int32),
            scratch(*receiver_data.shape),
            scratch(2, levels, 8, across),
            pltpu.SemaphoreType.DMA((14,)),
        ],
        compiler_params=params,
        name="own_edges",
    )(
        *(
            pltpu.with_memory_space_constraint(array, pltpu.HBM)
            for array in (
                speed_table.reshape(1, -1),
                receiver_cell,
                receiver_data,
                wavelet,
                region_ids,
                src_now,
                rec_now,
                src_prev,
                rec_prev,
            )
        )
    )
    came_sides = swap_rounds(sent)
    coef, steps, outside, source, sides, bits = pl.pallas_call(
        functools.partial(own_steps, width),
        out_shape=(
            struct(levels, extent, across),
            struct(*fields_shape),
            struct(2, levels, 2 * HALO, across),
            struct(levels, extent + 2 * LEAD, across),
            jax.ShapeDtypeStruct((4, 8, across), jnp.int32),
            jax.ShapeDtypeStruct((shots.bit_length() - 1, 8, across), jnp.int32),
        ),
        in_specs=[SMEM] + [VMEM] * 6,
        out_specs=[VMEM] * 6,
        scratch_shapes=[scratch(*wide_shape)],
        compiler_params=params,
        name="own_steps",
    )(source_cell, amps, own, prev, ids, speeds, planes)
    block = struct(2, share, extent, across)
    final, mine, *blocks = pl.pallas_call(
        neighbours_part,
        out_shape=(struct(*fields_shape), struct(2, *block.shape), *([block] * (shots - 2))),
        in_specs=[VMEM] * (6 + ROUNDS),
        out_specs=[VMEM] * shots,
        scratch_shapes=[
            scratch(*wide_shape),
            scratch(*wide_shape),
            scratch(2, levels, 8, across),
        ],
        compiler_params=params,
        name="neighbours_part",
    )(sides, bits, steps, outside, source, coef, *came_sides)
    def swap_shots(value, number):
        return lax.ppermute(value, "shot", [(shot, shot ^ number) for shot in range(shots)])

    came = [swap_shots(sent, 2 + i) for i, sent in enumerate(blocks)]
    weight = 1.0 / shots
    image_shape = (OFFS, share, extent, across)

    def stacked(blocks):
        return pl.pallas_call(
            stack,
            out_shape=struct(len(blocks), *block.shape),
            in_specs=[VMEM] * len(blocks),
            out_specs=VMEM,
            compiler_params=params,
            name="stack",
        )(*blocks)

    others = stacked(came[::-1])
    mine_sides = swap_rounds([mine] * ROUNDS)
    others_sides = swap_rounds([others] * ROUNDS)
    held = pl.pallas_call(
        hold,
        out_shape=block,
        in_specs=[VMEM] * 2,
        out_specs=VMEM,
        compiler_params=params,
        name="hold",
    )(mine[1], others)
    pieces = [held, *(side[1] for side in mine_sides)]
    partner = [
        swap_shots(stacked(pieces[begin : begin + 2]), 1) for begin in range(0, len(pieces), 2)
    ]
    src_next, rec_next, early = pl.pallas_call(
        functools.partial(early_products, weight),
        out_shape=(
            struct(1, levels, extent, across),
            struct(1, levels, extent, across),
            struct(*image_shape),
        ),
        in_specs=[VMEM] * (3 + ROUNDS),
        out_specs=[HBM, HBM, VMEM],
        scratch_shapes=[
            scratch(1, 2, share, 3 * extent, across),
            pltpu.SemaphoreType.DMA((2,)),
        ],
        compiler_params=params,
        name="early_products",
    )(sides, mine, *mine_sides[::-1], final)
    operands = [others, *others_sides[::-1], *partner, early]
    image = pl.pallas_call(
        functools.partial(image_products, weight),
        out_shape=struct(*image_shape),
        in_specs=[VMEM] * (1 + len(operands)),
        out_specs=HBM,
        scratch_shapes=[
            scratch(shots - 1, 2, share, 3 * extent, across),
            scratch(*image_shape),
            pltpu.SemaphoreType.DMA((11,)),
        ],
        compiler_params=params,
        name="image_products",
    )(sides, *operands)
    return src_next, rec_next, image


def solution(mesh):
    field = P(("groups", "shot"), None, "tile", None)
    return jax.shard_map(
        per_device,
        mesh=mesh,
        in_specs=(
            field,
            field,
            field,
            field,
            P("groups"),
            P(None, ("groups", "tile"), None),
            P(("groups", "shot")),
            P(("groups", "shot"), None),
            P(("groups", "shot"), "tile"),
            P(("groups", "shot"), None, "tile"),
        ),
        out_specs=(field, field, P(None, "shot", ("groups", "tile"), None)),
        check_vma=False,
    )
```

```python
import functools

import jax
import jax.numpy as jnp
from jax import lax
from jax.experimental import pallas as pl
from jax.experimental.pallas import tpu as pltpu
from jax.sharding import PartitionSpec as P

OFFS = 33
REACH = OFFS // 2
HALO = 4
LEAD = 8
ROUNDS = 3
SHIFTS = {2: 0, 3: 0}

COEFS = (-205.0 / 72.0, 8.0 / 5.0, -1.0 / 5.0, 8.0 / 315.0, -1.0 / 560.0)

VMEM = pl.BlockSpec(memory_space=pltpu.VMEM)
HBM = pl.BlockSpec(memory_space=pltpu.HBM)
SMEM = pl.BlockSpec(memory_space=pltpu.SMEM)
LIMIT = 16 * 1024 * 1024


def lane_weights(shape):
    lane = lax.broadcasted_iota(jnp.int32, shape, 1)
    across = shape[1]
    after = [jnp.where(lane < across - k, COEFS[k], 0.0) for k in range(1, HALO + 1)]
    before = [jnp.where(lane >= k, COEFS[k], 0.0) for k in range(1, HALO + 1)]
    return after, before


def lane_sum(centre, weights):
    after, before = weights
    across = centre.shape[1]
    total = 3.0 * COEFS[0] * centre
    for k in range(1, HALO + 1):
        total = total + after[k - 1] * pltpu.roll(centre, across - k, 1)
        total = total + before[k - 1] * pltpu.roll(centre, k, 1)
    return total


def beside_sum(wide, field, level, begin, count):
    total = None
    for k in range(1, HALO + 1):
        pair = (
            wide[field, level, begin + k : begin + k + count, :]
            + wide[field, level, begin - k : begin - k + count, :]
        )
        total = COEFS[k] * pair if total is None else total + COEFS[k] * pair
    return total


def depth_sum(rows_of, level, levels, total):
    for k in range(1, HALO + 1):
        for near in (level - k, level + k):
            if 0 <= near < levels:
                total = total + COEFS[k] * rows_of(near)
    return total


def laplace_level(wide, field, level, levels, extent, weights):
    def rows_of(near):
        return wide[field, near, LEAD : LEAD + extent, :]

    total = lane_sum(rows_of(level), weights) + beside_sum(wide, field, level, LEAD, extent)
    return depth_sum(rows_of, level, levels, total)


def is_low(across):
    return lax.broadcasted_iota(jnp.int32, (8, across), 0) < HALO


def own_edges(
    table_hbm,
    spots_hbm,
    traces_hbm,
    amps_hbm,
    ids_hbm,
    src_now,
    rec_now,
    src_prev,
    rec_prev,
    amps_ref,
    wide,
    prev_ref,
    ids_ref,
    speeds_ref,
    planes_ref,
    *rest,
):
    sent_refs, rest = rest[:ROUNDS], rest[ROUNDS:]
    table, spots_ref, traces_ref, edges, sums, sems = rest
    levels, extent, across = ids_ref.shape
    regions = table_hbm.shape[1]
    end = LEAD + extent
    rows = pl.ds(LEAD, extent)
    moves = [
        (src_now.at[0], wide.at[0, :, rows, :]),
        (rec_now.at[0], wide.at[1, :, rows, :]),
        (ids_hbm, ids_ref),
        (src_prev.at[0], prev_ref.at[0]),
        (rec_prev.at[0], prev_ref.at[1]),
        (table_hbm, table),
        (spots_hbm, spots_ref),
        (traces_hbm, traces_ref),
        (amps_hbm, amps_ref),
    ]
    copies = [
        pltpu.make_async_copy(here, there, sems.at[i]) for i, (here, there) in enumerate(moves)
    ]
    for copy in copies:
        copy.start()
    zeros = jnp.zeros((LEAD, across), jnp.float32)
    for field in range(2):
        for level in range(levels):
            wide[field, level, 0:LEAD, :] = zeros
            wide[field, level, end : end + LEAD, :] = zeros
    weights = lane_weights((8, across))
    low_half = is_low(across)
    my_round = lax.rem(lax.axis_index("tile"), ROUNDS)
    for copy in copies[:2]:
        copy.wait()
    for field in range(2):
        for level in range(levels):
            edges[field, level] = jnp.where(
                low_half, wide[field, level, LEAD : LEAD + 8, :], wide[field, level, end - 8 : end, :]
            )
    for field in range(2):
        for level in range(levels):
            total = lane_sum(edges[field, level], weights) + jnp.where(
                low_half,
                beside_sum(wide, field, level, LEAD, 8),
                beside_sum(wide, field, level, end - 8, 8),
            )
            sums[field, level] = depth_sum(lambda near: edges[field, near], level, levels, total)
    for copy in copies[2:]:
        copy.wait()

    spots = spots_ref[...]
    column = lax.broadcasted_iota(jnp.int32, (extent, spots.shape[1]), 0) * across
    in_column = (spots >= column) & (spots < column + across)
    lane = lax.broadcasted_iota(jnp.int32, (across, spots.shape[1]), 0)
    in_row = jnp.where(lax.rem(spots, across) == lane, 1.0, 0.0)
    traces = jnp.concatenate(
        [jnp.where(in_column, traces_ref[0, t : t + 1, :], 0.0) for t in range(2)], axis=0
    )
    planes = lax.dot_general(
        traces,
        in_row,
        (((1,), (1,)), ((), ())),
        precision=lax.Precision.HIGHEST,
        preferred_element_type=jnp.float32,
    )
    planes_ref[...] = planes

    def send(place, low, high):
        for number, sent_ref in enumerate(sent_refs):
            sent_ref[place] = jnp.where(my_round == number, high, low)

    def halves(ref, *place):
        return jnp.where(
            low_half, ref[(*place, pl.ds(0, 8))], ref[(*place, pl.ds(extent - 8, 8))]
        )

    speeds = jnp.concatenate(
        [table[...], jnp.zeros((1, across - regions), jnp.float32)], axis=1
    )
    speeds = jnp.broadcast_to(speeds, (8, across))
    speeds_ref[...] = speeds
    coefs = [
        jnp.take_along_axis(speeds, halves(ids_ref, level), axis=1, mode="promise_in_bounds")
        for level in range(levels)
    ]
    for level in range(0, levels, 2):
        here, after = coefs[level], coefs[level + 1]
        send(
            2 * levels + level // 2,
            jnp.where(low_half, here, pltpu.roll(after, HALO, 0)),
            jnp.where(low_half, pltpu.roll(here, HALO, 0), after),
        )

    for field in range(2):
        for level in range(levels):
            now, total = edges[field, level], sums[field, level]
            value = 2.0 * now - halves(prev_ref, field, level) + coefs[level] * total
            if field == 1 and level == 0:
                value = value + jnp.where(low_half, planes[0:8, :], planes[extent - 8 : extent, :])
            send(
                field * levels + level,
                jnp.where(low_half, now, pltpu.roll(value, HALO, 0)),
                jnp.where(low_half, pltpu.roll(now, HALO, 0), value),
            )


def own_steps(
    width,
    cell_ref,
    amps_ref,
    own,
    prev_ref,
    ids_ref,
    speeds_ref,
    planes_ref,
    coef_ref,
    steps_ref,
    outside_ref,
    source_ref,
    sides_ref,
    bits_ref,
    middle,
):
    levels, extent, across = ids_ref.shape
    end = LEAD + extent
    cell = cell_ref[0]
    deep = lax.div(cell, width * across)
    row = lax.rem(lax.div(cell, across), width) - lax.axis_index("tile") * extent + LEAD
    shape = (extent + 2 * LEAD, across)
    rows = lax.broadcasted_iota(jnp.int32, shape, 0)
    lanes = lax.broadcasted_iota(jnp.int32, shape, 1)
    hit = jnp.where((rows == row) & (lanes == lax.rem(cell, across)), 1.0, 0.0)
    weights = lane_weights((extent, across))
    speeds = speeds_ref[...]
    zeros = jnp.zeros((LEAD, across), jnp.float32)
    for level in range(levels):
        here = hit * jnp.where(deep == level, 1.0, 0.0)
        source_ref[level] = here * amps_ref[0:1, 0:1]
        steps_ref[0, level] = here[LEAD:end, :] * amps_ref[0:1, 1:2] - own[0, level, LEAD:end, :]
        steps_ref[1, level] = -own[1, level, LEAD:end, :]
        for begin in range(0, extent, 8):
            coef_ref[level, begin : begin + 8, :] = jnp.take_along_axis(
                speeds, ids_ref[level, begin : begin + 8, :], axis=1, mode="promise_in_bounds"
            )
    steps_ref[1, 0] += planes_ref[extent:, :]
    for field in range(2):
        for level in range(levels):
            total = laplace_level(own, field, level, levels, extent, weights)
            value = 2.0 * own[field, level, LEAD:end, :] - prev_ref[field, level]
            value = value + coef_ref[level] * total
            if field == 0:
                value = value + source_ref[level, LEAD:end, :]
            elif level == 0:
                value = value + planes_ref[:extent, :]
            middle[field, level, 0:LEAD, :] = zeros
            middle[field, level, LEAD:end, :] = value
            middle[field, level, end : end + LEAD, :] = zeros
            below = above = jnp.zeros((HALO, across), jnp.float32)
            for k in range(1, HALO + 1):
                begin = LEAD - HALO + k
                below = below + COEFS[k] * own[field, level, begin : begin + HALO, :]
                above = above + COEFS[k] * own[field, level, end - k : end - k + HALO, :]
            outside_ref[field, level, 0:HALO, :] = below
            outside_ref[field, level, HALO : 2 * HALO, :] = above
    for field in range(2):
        for level in range(levels):
            total = laplace_level(middle, field, level, levels, extent, weights)
            steps_ref[field, level] += (
                2.0 * middle[field, level, LEAD:end, :] + coef_ref[level] * total
            )
    tile, tiles = lax.axis_index("tile"), lax.axis_size("tile")
    places = (jnp.where(tile > 0, 1, 0), jnp.where(tile < tiles - 1, 1, 0))
    places += tuple((tile + SHIFTS[rounds]) % rounds for rounds in (2, 3))
    for place, value in enumerate(places):
        sides_ref[place] = jnp.full(sides_ref.shape[1:], value, dtype=jnp.int32)
    shot = jnp.full(bits_ref.shape[1:], lax.axis_index("shot"), dtype=jnp.int32)
    for bit in range(bits_ref.shape[0]):
        bits_ref[bit] = shot & (1 << bit)


def both_sides(sides, came):
    has_low, has_high, my_round = sides[0], sides[1], sides[len(came)]
    low, high = came[-1], came[0]
    for number in range(1, len(came)):
        low = jnp.where(my_round == number, came[number - 1], low)
        high = jnp.where(my_round == number, came[number], high)
    return jnp.where(has_low != 0, low, 0.0), jnp.where(has_high != 0, high, 0.0)


def neighbours_part(
    sides_ref, bits_ref, steps_ref, outside_ref, source_ref, coef_ref, *rest
):
    came_refs, (final_ref, mine_ref, *blocks, other, change, edges) = rest[:ROUNDS], rest[ROUNDS:]
    blocks = [mine_ref.at[0], mine_ref.at[1], *blocks]
    levels, extent, across = coef_ref.shape
    share = mine_ref.shape[2]
    end = LEAD + extent
    low_half = is_low(across)
    weights = lane_weights((8, across))
    sides = [sides_ref[place] for place in range(4)]
    zeros = jnp.zeros((8, across), jnp.float32)

    def received(place):
        return both_sides(sides, [ref[place] for ref in came_refs])

    coefs = [received(2 * levels + pair) for pair in range(levels // 2)]
    for field in range(2):
        for level in range(levels):
            low, high = received(field * levels + level)
            other[field, level, LEAD : LEAD + 8, :] = zeros
            other[field, level, end - 8 : end, :] = zeros
            other[field, level, LEAD - HALO : LEAD, :] = low[0:HALO, :]
            other[field, level, end : end + HALO, :] = high[0:HALO, :]
            half = slice(level % 2 * HALO, level % 2 * HALO + HALO)
            low_coef, high_coef = (coef[half, :] for coef in coefs[level // 2])
            low = low[HALO:, :] + low_coef * outside_ref[field, level, 0:HALO, :]
            high = high[HALO:, :] + high_coef * outside_ref[field, level, HALO : 2 * HALO, :]
            if field == 0:
                low = low + source_ref[level, LEAD - HALO : LEAD, :]
                high = high + source_ref[level, end : end + HALO, :]
            change[field, level, LEAD - HALO : LEAD, :] = low
            change[field, level, end : end + HALO, :] = high
    for field in range(2):
        for level in range(levels):
            left = right = zeros
            for k in range(1, HALO + 1):
                left = left + COEFS[k] * other[field, level, LEAD - k : LEAD - k + 8, :]
                right = right + COEFS[k] * other[field, level, end - 8 + k : end + k, :]
            left = coef_ref[level, 0:8, :] * left
            right = coef_ref[level, extent - 8 : extent, :] * right
            change[field, level, LEAD : LEAD + 8, :] = left
            change[field, level, end - 8 : end, :] = right
            edges[field, level] = left + right
    for field in range(2):
        for level in range(levels):
            total = depth_sum(
                lambda near: edges[field, near],
                level,
                levels,
                lane_sum(edges[field, level], weights),
            )
            for begin, mine in ((0, low_half), (extent - 8, ~low_half)):
                part = beside_sum(change, field, level, LEAD + begin, 8)
                part = part + jnp.where(mine, total, 0.0)
                final_ref[field, level, begin : begin + 8, :] = (
                    steps_ref[field, level, begin : begin + 8, :]
                    + 2.0 * change[field, level, LEAD + begin : LEAD + begin + 8, :]
                    + coef_ref[level, begin : begin + 8, :] * part
                )
    masks = [
        jnp.concatenate([bits_ref[bit]] * (extent // 8), axis=0) != 0
        for bit in range(bits_ref.shape[0])
    ]
    for field in range(2):
        for level in range(share):
            parts = [final_ref[field, place * share + level] for place in range(len(blocks))]
            for bit, mask in enumerate(masks):
                parts = [
                    jnp.where(mask, parts[place ^ (1 << bit)], parts[place])
                    for place in range(len(blocks))
                ]
            for block, part in zip(blocks, parts):
                block[field, level] = part


def widen(weight, sides_ref, shot, mine_ref, came_refs, wide):
    _, share, extent, _ = mine_ref.shape
    sides = [
        jnp.concatenate([sides_ref[place]] * (extent // 8), axis=0) for place in range(4)
    ]
    for field in range(2):
        for level in range(share):
            scale = weight if field == 0 else 1.0
            low, high = both_sides(sides, [ref[field, level] for ref in came_refs])
            wide[shot, field, level, 0:extent, :] = scale * low
            wide[shot, field, level, extent : 2 * extent, :] = scale * mine_ref[field, level]
            wide[shot, field, level, 2 * extent : 3 * extent, :] = scale * high


def offset_product(wide, offset, level, total):
    extent = wide.shape[3] // 3
    lower = extent + REACH - offset
    upper = extent - REACH + offset
    for shot in range(wide.shape[0]):
        product = (
            wide[shot, 0, level, lower : lower + extent, :]
            * wide[shot, 1, level, upper : upper + extent, :]
        )
        total = product if total is None else total + product
    return total


def stack(*refs):
    for place in range(len(refs) - 1):
        refs[-1][place] = refs[place][...]


def hold(mine_ref, _others_ref, held_ref):
    held_ref[...] = mine_ref[...]


def early_products(weight, sides_ref, mine_ref, third_ref, second_ref, first_ref, final_ref, *rest):
    src_hbm, rec_hbm, image_ref, wide, sems = rest
    copies = [
        pltpu.make_async_copy(final_ref.at[field], out.at[0], sems.at[field])
        for field, out in enumerate((src_hbm, rec_hbm))
    ]
    for copy in copies:
        copy.start()
    came_refs = [ref.at[0] for ref in (first_ref, second_ref, third_ref)]
    widen(weight, sides_ref, 0, mine_ref.at[0], came_refs, wide)
    for offset in range(OFFS):
        for level in range(wide.shape[2]):
            image_ref[offset, level] = offset_product(wide, offset, level, None)
    for copy in copies:
        copy.wait()


def image_products(weight, sides_ref, others_ref, *rest):
    others_sides, rest = rest[ROUNDS - 1 :: -1], rest[ROUNDS:]
    (own_first_ref, second_third_ref, early_ref), rest = rest[:3], rest[3:]
    partner_refs = [ref.at[place] for ref in (own_first_ref, second_third_ref) for place in range(2)]
    image_hbm, wide, image_ref, sems = rest
    copies = []
    places = [(partner_refs[0], partner_refs[1:])]
    for place in range(others_ref.shape[0]):
        places.append((others_ref.at[place], [ref.at[place] for ref in others_sides]))
    for shot, (own_ref, came_refs) in enumerate(places):
        widen(weight, sides_ref, shot, own_ref, came_refs, wide)
    parts = sems.shape[0]
    for piece in range(parts):
        offsets = range(piece * OFFS // parts, (piece + 1) * OFFS // parts)
        for offset in offsets:
            for level in range(image_ref.shape[1]):
                image_ref[offset, level] = offset_product(
                    wide, offset, level, early_ref[offset, level]
                )
        rows = pl.ds(offsets[0], len(offsets))
        copy = pltpu.make_async_copy(image_ref.at[rows], image_hbm.at[rows], sems.at[piece])
        copy.start()
        copies.append(copy)
    for copy in copies:
        copy.wait()


def swap_tiles(value, lower):
    tiles, shots = lax.axis_size("tile"), lax.axis_size("shot")
    partner = {}
    for tile in lower:
        partner[tile], partner[tile + 1] = tile + 1, tile
    pairs = []
    for tile in range(tiles):
        for shot in range(shots):
            here = tile * shots + shot
            there = partner[tile] * shots + shot if tile in partner else here ^ 1
            pairs.append((here, there))
    return lax.ppermute(value, ("tile", "shot"), pairs)


def swap_rounds(values):
    tiles, rounds = lax.axis_size("tile"), len(values)
    return [
        swap_tiles(value, range((number - SHIFTS[rounds]) % rounds, tiles - 1, rounds))
        for number, value in enumerate(values)
    ]


def per_device(
    src_prev,
    src_now,
    rec_prev,
    rec_now,
    speed_table,
    region_ids,
    source_cell,
    wavelet,
    receiver_cell,
    receiver_data,
):
    _, levels, extent, across = src_now.shape
    tiles = lax.axis_size("tile")
    width = extent * tiles
    shots = lax.axis_size("shot")
    share = levels // shots
    params = pltpu.CompilerParams(vmem_limit_bytes=LIMIT)

    def struct(*shape):
        return jax.ShapeDtypeStruct(shape, jnp.float32)

    def scratch(*shape, dtype=jnp.float32):
        return pltpu.VMEM(shape, dtype)

    wide_shape = (2, levels, extent + 2 * LEAD, across)
    message = struct(2 * levels + levels // 2, 2 * HALO, across)
    fields_shape = (2, levels, extent, across)
    amps, own, prev, ids, speeds, planes, *sent = pl.pallas_call(
        own_edges,
        out_shape=(
            struct(*wavelet.shape),
            struct(*wide_shape),
            struct(*fields_shape),
            jax.ShapeDtypeStruct(region_ids.shape, jnp.int32),
            struct(8, across),
            struct(2 * extent, across),
            *([message] * ROUNDS),
        ),
        in_specs=[HBM] * 9,
        out_specs=[VMEM] * (6 + ROUNDS),
        scratch_shapes=[
            scratch(1, speed_table.shape[0]),
            scratch(*receiver_cell.shape, dtype=jnp.int32),
            scratch(*receiver_data.shape),
            scratch(2, levels, 8, across),
            scratch(2, levels, 8, across),
            pltpu.SemaphoreType.DMA((9,)),
        ],
        compiler_params=params,
        name="own_edges",
    )(
        *(
            pltpu.with_memory_space_constraint(array, pltpu.HBM)
            for array in (
                speed_table.reshape(1, -1),
                receiver_cell,
                receiver_data,
                wavelet,
                region_ids,
                src_now,
                rec_now,
                src_prev,
                rec_prev,
            )
        )
    )
    came_sides = swap_rounds(sent)
    coef, steps, outside, source, sides, bits = pl.pallas_call(
        functools.partial(own_steps, width),
        out_shape=(
            struct(levels, extent, across),
            struct(*fields_shape),
            struct(2, levels, 2 * HALO, across),
            struct(levels, extent + 2 * LEAD, across),
            jax.ShapeDtypeStruct((4, 8, across), jnp.int32),
            jax.ShapeDtypeStruct((shots.bit_length() - 1, 8, across), jnp.int32),
        ),
        in_specs=[SMEM] + [VMEM] * 6,
        out_specs=[VMEM] * 6,
        scratch_shapes=[scratch(*wide_shape)],
        compiler_params=params,
        name="own_steps",
    )(source_cell, amps, own, prev, ids, speeds, planes)
    block = struct(2, share, extent, across)
    final, mine, *blocks = pl.pallas_call(
        neighbours_part,
        out_shape=(struct(*fields_shape), struct(2, *block.shape), *([block] * (shots - 2))),
        in_specs=[VMEM] * (6 + ROUNDS),
        out_specs=[VMEM] * shots,
        scratch_shapes=[
            scratch(*wide_shape),
            scratch(*wide_shape),
            scratch(2, levels, 8, across),
        ],
        compiler_params=params,
        name="neighbours_part",
    )(sides, bits, steps, outside, source, coef, *came_sides)
    def swap_shots(value, number):
        return lax.ppermute(value, "shot", [(shot, shot ^ number) for shot in range(shots)])

    came = [swap_shots(sent, 2 + i) for i, sent in enumerate(blocks)]
    weight = 1.0 / shots
    image_shape = (OFFS, share, extent, across)

    def stacked(blocks):
        return pl.pallas_call(
            stack,
            out_shape=struct(len(blocks), *block.shape),
            in_specs=[VMEM] * len(blocks),
            out_specs=VMEM,
            compiler_params=params,
            name="stack",
        )(*blocks)

    others = stacked(came[::-1])
    mine_sides = swap_rounds([mine] * ROUNDS)
    others_sides = swap_rounds([others] * ROUNDS)
    held = pl.pallas_call(
        hold,
        out_shape=block,
        in_specs=[VMEM] * 2,
        out_specs=VMEM,
        compiler_params=params,
        name="hold",
    )(mine[1], others)
    pieces = [held, *(side[1] for side in mine_sides)]
    partner = [
        swap_shots(stacked(pieces[begin : begin + 2]), 1) for begin in range(0, len(pieces), 2)
    ]
    src_next, rec_next, early = pl.pallas_call(
        functools.partial(early_products, weight),
        out_shape=(
            struct(1, levels, extent, across),
            struct(1, levels, extent, across),
            struct(*image_shape),
        ),
        in_specs=[VMEM] * (3 + ROUNDS),
        out_specs=[HBM, HBM, VMEM],
        scratch_shapes=[
            scratch(1, 2, share, 3 * extent, across),
            pltpu.SemaphoreType.DMA((2,)),
        ],
        compiler_params=params,
        name="early_products",
    )(sides, mine, *mine_sides[::-1], final)
    operands = [others, *others_sides[::-1], *partner, early]
    image = pl.pallas_call(
        functools.partial(image_products, weight),
        out_shape=struct(*image_shape),
        in_specs=[VMEM] * (1 + len(operands)),
        out_specs=HBM,
        scratch_shapes=[
            scratch(shots - 1, 2, share, 3 * extent, across),
            scratch(*image_shape),
            pltpu.SemaphoreType.DMA((11,)),
        ],
        compiler_params=params,
        name="image_products",
    )(sides, *operands)
    return src_next, rec_next, image


def solution(mesh):
    field = P(("groups", "shot"), None, "tile", None)
    return jax.shard_map(
        per_device,
        mesh=mesh,
        in_specs=(
            field,
            field,
            field,
            field,
            P("groups"),
            P(None, ("groups", "tile"), None),
            P(("groups", "shot")),
            P(("groups", "shot"), None),
            P(("groups", "shot"), "tile"),
            P(("groups", "shot"), None, "tile"),
        ),
        out_specs=(field, field, P(None, "shot", ("groups", "tile"), None)),
        check_vma=False,
    )
```

```python
import functools

import jax
import jax.numpy as jnp
from jax import lax
from jax.experimental import pallas as pl
from jax.experimental.pallas import tpu as pltpu
from jax.sharding import PartitionSpec as P

OFFS = 33
REACH = OFFS // 2
HALO = 4
LEAD = 8
ROUNDS = 3
SHIFTS = {2: 0, 3: 0}

COEFS = (-205.0 / 72.0, 8.0 / 5.0, -1.0 / 5.0, 8.0 / 315.0, -1.0 / 560.0)

VMEM = pl.BlockSpec(memory_space=pltpu.VMEM)
HBM = pl.BlockSpec(memory_space=pltpu.HBM)
SMEM = pl.BlockSpec(memory_space=pltpu.SMEM)
LIMIT = 16 * 1024 * 1024


def lane_weights(shape):
    lane = lax.broadcasted_iota(jnp.int32, shape, 1)
    across = shape[1]
    after = [jnp.where(lane < across - k, COEFS[k], 0.0) for k in range(1, HALO + 1)]
    before = [jnp.where(lane >= k, COEFS[k], 0.0) for k in range(1, HALO + 1)]
    return after, before


def lane_sum(centre, weights):
    after, before = weights
    across = centre.shape[1]
    total = 3.0 * COEFS[0] * centre
    for k in range(1, HALO + 1):
        total = total + after[k - 1] * pltpu.roll(centre, across - k, 1)
        total = total + before[k - 1] * pltpu.roll(centre, k, 1)
    return total


def beside_sum(wide, field, level, begin, count):
    total = None
    for k in range(1, HALO + 1):
        pair = (
            wide[field, level, begin + k : begin + k + count, :]
            + wide[field, level, begin - k : begin - k + count, :]
        )
        total = COEFS[k] * pair if total is None else total + COEFS[k] * pair
    return total


def depth_sum(rows_of, level, levels, total):
    for k in range(1, HALO + 1):
        for near in (level - k, level + k):
            if 0 <= near < levels:
                total = total + COEFS[k] * rows_of(near)
    return total


def laplace_level(wide, field, level, levels, extent, weights):
    def rows_of(near):
        return wide[field, near, LEAD : LEAD + extent, :]

    total = lane_sum(rows_of(level), weights) + beside_sum(wide, field, level, LEAD, extent)
    return depth_sum(rows_of, level, levels, total)


def is_low(across):
    return lax.broadcasted_iota(jnp.int32, (8, across), 0) < HALO


def own_edges(
    table_hbm,
    spots_hbm,
    traces_hbm,
    amps_hbm,
    ids_hbm,
    src_now,
    rec_now,
    src_prev,
    rec_prev,
    amps_ref,
    wide,
    prev_ref,
    ids_ref,
    speeds_ref,
    planes_ref,
    *rest,
):
    sent_refs, rest = rest[:ROUNDS], rest[ROUNDS:]
    table, spots_ref, traces_ref, edges, sems = rest
    levels, extent, across = ids_ref.shape
    regions = table_hbm.shape[1]
    end = LEAD + extent
    rows = pl.ds(LEAD, extent)
    moves = [(table_hbm, table), (spots_hbm, spots_ref), (traces_hbm, traces_ref)]
    for begin in range(0, levels, levels // 2):
        part = pl.ds(begin, levels // 2)
        moves += [
            (src_now.at[0, part], wide.at[0, part, rows, :]),
            (rec_now.at[0, part], wide.at[1, part, rows, :]),
            (ids_hbm.at[part], ids_ref.at[part]),
            (src_prev.at[0, part], prev_ref.at[0, part]),
            (rec_prev.at[0, part], prev_ref.at[1, part]),
        ]
    moves.append((amps_hbm, amps_ref))
    copies = [
        pltpu.make_async_copy(here, there, sems.at[i]) for i, (here, there) in enumerate(moves)
    ]
    for copy in copies:
        copy.start()
    zeros = jnp.zeros((LEAD, across), jnp.float32)
    for field in range(2):
        for level in range(levels):
            wide[field, level, 0:LEAD, :] = zeros
            wide[field, level, end : end + LEAD, :] = zeros
    weights = lane_weights((8, across))
    low_half = is_low(across)
    my_round = lax.rem(lax.axis_index("tile"), ROUNDS)
    for copy in copies:
        copy.wait()

    spots = spots_ref[...]
    column = lax.broadcasted_iota(jnp.int32, (extent, spots.shape[1]), 0) * across
    in_column = (spots >= column) & (spots < column + across)
    lane = lax.broadcasted_iota(jnp.int32, (across, spots.shape[1]), 0)
    in_row = jnp.where(lax.rem(spots, across) == lane, 1.0, 0.0)
    traces = jnp.concatenate(
        [jnp.where(in_column, traces_ref[0, t : t + 1, :], 0.0) for t in range(2)], axis=0
    )
    planes = lax.dot_general(
        traces,
        in_row,
        (((1,), (1,)), ((), ())),
        precision=lax.Precision.HIGHEST,
        preferred_element_type=jnp.float32,
    )
    planes_ref[...] = planes

    def send(place, low, high):
        for number, sent_ref in enumerate(sent_refs):
            sent_ref[place] = jnp.where(my_round == number, high, low)

    def halves(ref, *place):
        return jnp.where(
            low_half, ref[(*place, pl.ds(0, 8))], ref[(*place, pl.ds(extent - 8, 8))]
        )

    speeds = jnp.concatenate(
        [table[...], jnp.zeros((1, across - regions), jnp.float32)], axis=1
    )
    speeds = jnp.broadcast_to(speeds, (8, across))
    speeds_ref[...] = speeds
    coefs = [
        jnp.take_along_axis(speeds, halves(ids_ref, level), axis=1, mode="promise_in_bounds")
        for level in range(levels)
    ]
    for level in range(0, levels, 2):
        here, after = coefs[level], coefs[level + 1]
        send(
            2 * levels + level // 2,
            jnp.where(low_half, here, pltpu.roll(after, HALO, 0)),
            jnp.where(low_half, pltpu.roll(here, HALO, 0), after),
        )

    for field in range(2):
        for level in range(levels):
            edges[field, level] = jnp.where(
                low_half, wide[field, level, LEAD : LEAD + 8, :], wide[field, level, end - 8 : end, :]
            )
    for field in range(2):
        for level in range(levels):
            now = edges[field, level]
            total = lane_sum(now, weights) + jnp.where(
                low_half,
                beside_sum(wide, field, level, LEAD, 8),
                beside_sum(wide, field, level, end - 8, 8),
            )
            total = depth_sum(lambda near: edges[field, near], level, levels, total)
            value = 2.0 * now - halves(prev_ref, field, level) + coefs[level] * total
            if field == 1 and level == 0:
                value = value + jnp.where(low_half, planes[0:8, :], planes[extent - 8 : extent, :])
            send(
                field * levels + level,
                jnp.where(low_half, now, pltpu.roll(value, HALO, 0)),
                jnp.where(low_half, pltpu.roll(now, HALO, 0), value),
            )


def own_steps(
    width,
    cell_ref,
    amps_ref,
    own,
    prev_ref,
    ids_ref,
    speeds_ref,
    planes_ref,
    coef_ref,
    steps_ref,
    outside_ref,
    source_ref,
    sides_ref,
    bits_ref,
    middle,
):
    levels, extent, across = ids_ref.shape
    end = LEAD + extent
    cell = cell_ref[0]
    deep = lax.div(cell, width * across)
    row = lax.rem(lax.div(cell, across), width) - lax.axis_index("tile") * extent + LEAD
    shape = (extent + 2 * LEAD, across)
    rows = lax.broadcasted_iota(jnp.int32, shape, 0)
    lanes = lax.broadcasted_iota(jnp.int32, shape, 1)
    hit = jnp.where((rows == row) & (lanes == lax.rem(cell, across)), 1.0, 0.0)
    weights = lane_weights((extent, across))
    speeds = speeds_ref[...]
    zeros = jnp.zeros((LEAD, across), jnp.float32)
    for level in range(levels):
        here = hit * jnp.where(deep == level, 1.0, 0.0)
        source_ref[level] = here * amps_ref[0:1, 0:1]
        steps_ref[0, level] = here[LEAD:end, :] * amps_ref[0:1, 1:2] - own[0, level, LEAD:end, :]
        steps_ref[1, level] = -own[1, level, LEAD:end, :]
        for begin in range(0, extent, 8):
            coef_ref[level, begin : begin + 8, :] = jnp.take_along_axis(
                speeds, ids_ref[level, begin : begin + 8, :], axis=1, mode="promise_in_bounds"
            )
    steps_ref[1, 0] += planes_ref[extent:, :]
    for field in range(2):
        for level in range(levels):
            total = laplace_level(own, field, level, levels, extent, weights)
            value = 2.0 * own[field, level, LEAD:end, :] - prev_ref[field, level]
            value = value + coef_ref[level] * total
            if field == 0:
                value = value + source_ref[level, LEAD:end, :]
            elif level == 0:
                value = value + planes_ref[:extent, :]
            middle[field, level, 0:LEAD, :] = zeros
            middle[field, level, LEAD:end, :] = value
            middle[field, level, end : end + LEAD, :] = zeros
            below = above = jnp.zeros((HALO, across), jnp.float32)
            for k in range(1, HALO + 1):
                begin = LEAD - HALO + k
                below = below + COEFS[k] * own[field, level, begin : begin + HALO, :]
                above = above + COEFS[k] * own[field, level, end - k : end - k + HALO, :]
            outside_ref[field, level, 0:HALO, :] = below
            outside_ref[field, level, HALO : 2 * HALO, :] = above
    for field in range(2):
        for level in range(levels):
            total = laplace_level(middle, field, level, levels, extent, weights)
            steps_ref[field, level] += (
                2.0 * middle[field, level, LEAD:end, :] + coef_ref[level] * total
            )
    tile, tiles = lax.axis_index("tile"), lax.axis_size("tile")
    places = (jnp.where(tile > 0, 1, 0), jnp.where(tile < tiles - 1, 1, 0))
    places += tuple((tile + SHIFTS[rounds]) % rounds for rounds in (2, 3))
    for place, value in enumerate(places):
        sides_ref[place] = jnp.full(sides_ref.shape[1:], value, dtype=jnp.int32)
    shot = jnp.full(bits_ref.shape[1:], lax.axis_index("shot"), dtype=jnp.int32)
    for bit in range(bits_ref.shape[0]):
        bits_ref[bit] = shot & (1 << bit)


def both_sides(sides, came):
    has_low, has_high, my_round = sides[0], sides[1], sides[len(came)]
    low, high = came[-1], came[0]
    for number in range(1, len(came)):
        low = jnp.where(my_round == number, came[number - 1], low)
        high = jnp.where(my_round == number, came[number], high)
    return jnp.where(has_low != 0, low, 0.0), jnp.where(has_high != 0, high, 0.0)


def neighbours_part(
    sides_ref, bits_ref, steps_ref, outside_ref, source_ref, coef_ref, *rest
):
    came_refs, (final_ref, mine_ref, *blocks, other, change, edges) = rest[:ROUNDS], rest[ROUNDS:]
    blocks = [mine_ref.at[0], mine_ref.at[1], *blocks]
    levels, extent, across = coef_ref.shape
    share = mine_ref.shape[2]
    end = LEAD + extent
    low_half = is_low(across)
    weights = lane_weights((8, across))
    sides = [sides_ref[place] for place in range(4)]
    zeros = jnp.zeros((8, across), jnp.float32)

    def received(place):
        return both_sides(sides, [ref[place] for ref in came_refs])

    coefs = [received(2 * levels + pair) for pair in range(levels // 2)]
    for field in range(2):
        for level in range(levels):
            low, high = received(field * levels + level)
            other[field, level, LEAD : LEAD + 8, :] = zeros
            other[field, level, end - 8 : end, :] = zeros
            other[field, level, LEAD - HALO : LEAD, :] = low[0:HALO, :]
            other[field, level, end : end + HALO, :] = high[0:HALO, :]
            half = slice(level % 2 * HALO, level % 2 * HALO + HALO)
            low_coef, high_coef = (coef[half, :] for coef in coefs[level // 2])
            low = low[HALO:, :] + low_coef * outside_ref[field, level, 0:HALO, :]
            high = high[HALO:, :] + high_coef * outside_ref[field, level, HALO : 2 * HALO, :]
            if field == 0:
                low = low + source_ref[level, LEAD - HALO : LEAD, :]
                high = high + source_ref[level, end : end + HALO, :]
            change[field, level, LEAD - HALO : LEAD, :] = low
            change[field, level, end : end + HALO, :] = high
    for field in range(2):
        for level in range(levels):
            left = right = zeros
            for k in range(1, HALO + 1):
                left = left + COEFS[k] * other[field, level, LEAD - k : LEAD - k + 8, :]
                right = right + COEFS[k] * other[field, level, end - 8 + k : end + k, :]
            left = coef_ref[level, 0:8, :] * left
            right = coef_ref[level, extent - 8 : extent, :] * right
            change[field, level, LEAD : LEAD + 8, :] = left
            change[field, level, end - 8 : end, :] = right
            edges[field, level] = left + right
    for field in range(2):
        for level in range(levels):
            total = depth_sum(
                lambda near: edges[field, near],
                level,
                levels,
                lane_sum(edges[field, level], weights),
            )
            for begin, mine in ((0, low_half), (extent - 8, ~low_half)):
                part = beside_sum(change, field, level, LEAD + begin, 8)
                part = part + jnp.where(mine, total, 0.0)
                final_ref[field, level, begin : begin + 8, :] = (
                    steps_ref[field, level, begin : begin + 8, :]
                    + 2.0 * change[field, level, LEAD + begin : LEAD + begin + 8, :]
                    + coef_ref[level, begin : begin + 8, :] * part
                )
    masks = [
        jnp.concatenate([bits_ref[bit]] * (extent // 8), axis=0) != 0
        for bit in range(bits_ref.shape[0])
    ]
    for field in range(2):
        for level in range(share):
            parts = [final_ref[field, place * share + level] for place in range(len(blocks))]
            for bit, mask in enumerate(masks):
                parts = [
                    jnp.where(mask, parts[place ^ (1 << bit)], parts[place])
                    for place in range(len(blocks))
                ]
            for block, part in zip(blocks, parts):
                block[field, level] = part


def widen(weight, sides_ref, shot, mine_ref, came_refs, wide):
    _, share, extent, _ = mine_ref.shape
    sides = [
        jnp.concatenate([sides_ref[place]] * (extent // 8), axis=0) for place in range(4)
    ]
    for field in range(2):
        for level in range(share):
            scale = weight if field == 0 else 1.0
            low, high = both_sides(sides, [ref[field, level] for ref in came_refs])
            wide[shot, field, level, 0:extent, :] = scale * low
            wide[shot, field, level, extent : 2 * extent, :] = scale * mine_ref[field, level]
            wide[shot, field, level, 2 * extent : 3 * extent, :] = scale * high


def offset_product(wide, offset, level):
    extent = wide.shape[3] // 3
    lower = extent + REACH - offset
    upper = extent - REACH + offset
    total = None
    for shot in range(wide.shape[0]):
        product = (
            wide[shot, 0, level, lower : lower + extent, :]
            * wide[shot, 1, level, upper : upper + extent, :]
        )
        total = product if total is None else total + product
    return total


def stack(*refs):
    for place in range(len(refs) - 1):
        refs[-1][place] = refs[place][...]


def hold(mine_ref, _others_ref, held_ref):
    held_ref[...] = mine_ref[...]


def image_products(weight, sides_ref, others_ref, *rest):
    others_sides, rest = rest[ROUNDS - 1 :: -1], rest[ROUNDS:]
    mine_ref, rest = rest[0], rest[1:]
    mine_sides, rest = rest[ROUNDS - 1 :: -1], rest[ROUNDS:]
    (own_first_ref, second_third_ref), rest = rest[:2], rest[2:]
    partner_refs = [ref.at[place] for ref in (own_first_ref, second_third_ref) for place in range(2)]
    final_ref, src_hbm, rec_hbm, image_hbm, wide, image_ref, field_sems, sems = rest
    copies = [
        pltpu.make_async_copy(final_ref.at[field], out.at[0], field_sems.at[field])
        for field, out in enumerate((src_hbm, rec_hbm))
    ]
    for copy in copies:
        copy.start()
    places = [
        (mine_ref.at[0], [ref.at[0] for ref in mine_sides]),
        (partner_refs[0], partner_refs[1:]),
    ]
    for place in range(others_ref.shape[0]):
        places.append((others_ref.at[place], [ref.at[place] for ref in others_sides]))
    for shot, (own_ref, came_refs) in enumerate(places):
        widen(weight, sides_ref, shot, own_ref, came_refs, wide)
    parts = sems.shape[0]
    for piece in range(parts):
        offsets = range(piece * OFFS // parts, (piece + 1) * OFFS // parts)
        for offset in offsets:
            for level in range(image_ref.shape[1]):
                image_ref[offset, level] = offset_product(wide, offset, level)
        rows = pl.ds(offsets[0], len(offsets))
        copy = pltpu.make_async_copy(image_ref.at[rows], image_hbm.at[rows], sems.at[piece])
        copy.start()
        copies.append(copy)
    for copy in copies:
        copy.wait()


def swap_tiles(value, lower):
    tiles, shots = lax.axis_size("tile"), lax.axis_size("shot")
    partner = {}
    for tile in lower:
        partner[tile], partner[tile + 1] = tile + 1, tile
    pairs = []
    for tile in range(tiles):
        for shot in range(shots):
            here = tile * shots + shot
            there = partner[tile] * shots + shot if tile in partner else here ^ 1
            pairs.append((here, there))
    return lax.ppermute(value, ("tile", "shot"), pairs)


def swap_rounds(values):
    tiles, rounds = lax.axis_size("tile"), len(values)
    return [
        swap_tiles(value, range((number - SHIFTS[rounds]) % rounds, tiles - 1, rounds))
        for number, value in enumerate(values)
    ]


def per_device(
    src_prev,
    src_now,
    rec_prev,
    rec_now,
    speed_table,
    region_ids,
    source_cell,
    wavelet,
    receiver_cell,
    receiver_data,
):
    _, levels, extent, across = src_now.shape
    tiles = lax.axis_size("tile")
    width = extent * tiles
    shots = lax.axis_size("shot")
    share = levels // shots
    params = pltpu.CompilerParams(vmem_limit_bytes=LIMIT)

    def struct(*shape):
        return jax.ShapeDtypeStruct(shape, jnp.float32)

    def scratch(*shape, dtype=jnp.float32):
        return pltpu.VMEM(shape, dtype)

    wide_shape = (2, levels, extent + 2 * LEAD, across)
    message = struct(2 * levels + levels // 2, 2 * HALO, across)
    fields_shape = (2, levels, extent, across)
    amps, own, prev, ids, speeds, planes, *sent = pl.pallas_call(
        own_edges,
        out_shape=(
            struct(*wavelet.shape),
            struct(*wide_shape),
            struct(*fields_shape),
            jax.ShapeDtypeStruct(region_ids.shape, jnp.int32),
            struct(8, across),
            struct(2 * extent, across),
            *([message] * ROUNDS),
        ),
        in_specs=[HBM] * 9,
        out_specs=[VMEM] * (6 + ROUNDS),
        scratch_shapes=[
            scratch(1, speed_table.shape[0]),
            scratch(*receiver_cell.shape, dtype=jnp.int32),
            scratch(*receiver_data.shape),
            scratch(2, levels, 8, across),
            pltpu.SemaphoreType.DMA((14,)),
        ],
        compiler_params=params,
        name="own_edges",
    )(
        *(
            pltpu.with_memory_space_constraint(array, pltpu.HBM)
            for array in (
                speed_table.reshape(1, -1),
                receiver_cell,
                receiver_data,
                wavelet,
                region_ids,
                src_now,
                rec_now,
                src_prev,
                rec_prev,
            )
        )
    )
    came_sides = swap_rounds(sent)
    coef, steps, outside, source, sides, bits = pl.pallas_call(
        functools.partial(own_steps, width),
        out_shape=(
            struct(levels, extent, across),
            struct(*fields_shape),
            struct(2, levels, 2 * HALO, across),
            struct(levels, extent + 2 * LEAD, across),
            jax.ShapeDtypeStruct((4, 8, across), jnp.int32),
            jax.ShapeDtypeStruct((shots.bit_length() - 1, 8, across), jnp.int32),
        ),
        in_specs=[SMEM] + [VMEM] * 6,
        out_specs=[VMEM] * 6,
        scratch_shapes=[scratch(*wide_shape)],
        compiler_params=params,
        name="own_steps",
    )(source_cell, amps, own, prev, ids, speeds, planes)
    block = struct(2, share, extent, across)
    final, mine, *blocks = pl.pallas_call(
        neighbours_part,
        out_shape=(struct(*fields_shape), struct(2, *block.shape), *([block] * (shots - 2))),
        in_specs=[VMEM] * (6 + ROUNDS),
        out_specs=[VMEM] * shots,
        scratch_shapes=[
            scratch(*wide_shape),
            scratch(*wide_shape),
            scratch(2, levels, 8, across),
        ],
        compiler_params=params,
        name="neighbours_part",
    )(sides, bits, steps, outside, source, coef, *came_sides)
    def swap_shots(value, number):
        return lax.ppermute(value, "shot", [(shot, shot ^ number) for shot in range(shots)])

    came = [swap_shots(sent, 2 + i) for i, sent in enumerate(blocks)]
    weight = 1.0 / shots
    image_shape = (OFFS, share, extent, across)

    def stacked(blocks):
        return pl.pallas_call(
            stack,
            out_shape=struct(len(blocks), *block.shape),
            in_specs=[VMEM] * len(blocks),
            out_specs=VMEM,
            compiler_params=params,
            name="stack",
        )(*blocks)

    others = stacked(came[::-1])
    mine_sides = swap_rounds([mine] * ROUNDS)
    others_sides = swap_rounds([others] * ROUNDS)
    held = pl.pallas_call(
        hold,
        out_shape=block,
        in_specs=[VMEM] * 2,
        out_specs=VMEM,
        compiler_params=params,
        name="hold",
    )(mine[1], others)
    pieces = [held, *(side[1] for side in mine_sides)]
    partner = [
        swap_shots(stacked(pieces[begin : begin + 2]), 1) for begin in range(0, len(pieces), 2)
    ]
    operands = [others, *others_sides[::-1], mine, *mine_sides[::-1], *partner]
    return pl.pallas_call(
        functools.partial(image_products, weight),
        out_shape=(
            struct(1, levels, extent, across),
            struct(1, levels, extent, across),
            struct(*image_shape),
        ),
        in_specs=[VMEM] * (2 + len(operands)),
        out_specs=[HBM] * 3,
        scratch_shapes=[
            scratch(shots, 2, share, 3 * extent, across),
            scratch(*image_shape),
            pltpu.SemaphoreType.DMA((2,)),
            pltpu.SemaphoreType.DMA((OFFS,)),
        ],
        compiler_params=params,
        name="image_products",
    )(sides, *operands, final)


def solution(mesh):
    field = P(("groups", "shot"), None, "tile", None)
    return jax.shard_map(
        per_device,
        mesh=mesh,
        in_specs=(
            field,
            field,
            field,
            field,
            P("groups"),
            P(None, ("groups", "tile"), None),
            P(("groups", "shot")),
            P(("groups", "shot"), None),
            P(("groups", "shot"), "tile"),
            P(("groups", "shot"), None, "tile"),
        ),
        out_specs=(field, field, P(None, "shot", ("groups", "tile"), None)),
        check_vma=False,
    )
```
